32 devices in a mesh: dp: 2 (over y), ctx: 16 (over z, x, core).
Axes of the slice: x: 2, y: 2, z: 4, core: 2. Of those that a mesh axis runs over, the one named last changes fastest.
Arguments:
- tokens: bfloat16 [8192, 1024], P(('dp', 'ctx')), may hold values from -6 to 6
- lengths: int32 [2, 3], P('dp'), may hold values from 1 to 3840, as said below
- cotangent: bfloat16 [8192, 1024], P(('dp', 'ctx')), may hold values from -6 to 6
- mixgain: bfloat16 [1024], replicated, may hold values from 0.5 to 1.5
- mixentry: bfloat16 [1024, 3072], replicated, may hold values from -0.1875 to 0.1875
- mixtaps: bfloat16 [3, 1024], replicated, may hold values from -3.5 to 3.5
- mixexit: bfloat16 [1024, 1024], replicated, may hold values from -0.1875 to 0.1875
- lowgain: bfloat16 [1024], replicated, may hold values from 0.5 to 1.5
- lowgate: bfloat16 [1024, 4608], replicated, may hold values from -0.1875 to 0.1875
- lowlift: bfloat16 [1024, 4608], replicated, may hold values from -0.1875 to 0.1875
- lowdrop: bfloat16 [4608, 1024], replicated, may hold values from -0.09375 to 0.09375
- attgain: bfloat16 [1024], replicated, may hold values from 0.5 to 1.5
- attquery: bfloat16 [1024, 1024], replicated, may hold values from -0.1875 to 0.1875
- attkeys: bfloat16 [1024, 512], replicated, may hold values from -0.1875 to 0.1875
- attvalues: bfloat16 [1024, 512], replicated, may hold values from -0.1875 to 0.1875
- querygain: bfloat16 [64], replicated, may hold values from 1.1953125 to 2
- keysgain: bfloat16 [64], replicated, may hold values from 1.1953125 to 2
- attexit: bfloat16 [1024, 1024], replicated, may hold values from -0.75 to 0.75
- topgain: bfloat16 [1024], replicated, may hold values from 0.5 to 1.5
- topgate: bfloat16 [1024, 4608], replicated, may hold values from -0.1875 to 0.1875
- toplift: bfloat16 [1024, 4608], replicated, may hold values from -0.1875 to 0.1875
- topdrop: bfloat16 [4608, 1024], replicated, may hold values from -0.09375 to 0.09375
Outputs:
- output: float32 [8192, 1024], P(('dp', 'ctx'))
- tokens_grad: float32 [8192, 1024], P(('dp', 'ctx'))
- mixgain_grad: float32 [1024], replicated
- mixentry_grad: float32 [1024, 3072], P('ctx')
- mixtaps_grad: float32 [3, 1024], replicated
- mixexit_grad: float32 [1024, 1024], P('ctx')
- lowgain_grad: float32 [1024], replicated
- lowgate_grad: float32 [1024, 4608], P('ctx')
- lowlift_grad: float32 [1024, 4608], P('ctx')
- lowdrop_grad: float32 [4608, 1024], P('ctx')
- attgain_grad: float32 [1024], replicated
- attquery_grad: float32 [1024, 1024], P('ctx')
- attkeys_grad: float32 [1024, 512], P('ctx')
- attvalues_grad: float32 [1024, 512], P('ctx')
- querygain_grad: float32 [64], replicated
- keysgain_grad: float32 [64], replicated
- attexit_grad: float32 [1024, 1024], P('ctx')
- topgain_grad: float32 [1024], replicated
- topgate_grad: float32 [1024, 4608], P('ctx')
- toplift_grad: float32 [1024, 4608], P('ctx')
- topdrop_grad: float32 [4608, 1024], P('ctx')
The draws below stay inside these ranges and needn't reach their ends.
Inputs may be any that keep to these rules, and one draw needn't show every extreme that they name: `lengths`: each group holds three documents in order: the first shorter than 256 tokens, the second of 3840 tokens, the third of 256 minus the first's length.
All inputs are finite; a program needn't handle non-finite values.
Results may differ from the reference program's by a relative error of at most 0.04.
Values may be sent and summed in bfloat16 or wider, within the bound.
A program may use at most 384 MiB of HBM per device.

```python
import math
import jax
import jax.numpy as jnp
from jax import lax

MODEL_WIDTH = 1024
FF = 4608
QUERY_HEADS = 16
KEY_VALUE_HEADS = 8
HEAD_WIDTH = 64
KERNEL = 3
TOK_DEV = 256
GROUP_TOKENS = 4096
TOKEN_COUNT = 8192
N_DP = 2


def draw_lengths(key, part):
    leading = jax.random.randint(key, (N_DP, 1), 1, TOK_DEV, dtype=jnp.int32)
    middle = jnp.full((N_DP, 1), GROUP_TOKENS - TOK_DEV, jnp.int32)
    trailing = TOK_DEV - leading
    return jnp.concatenate([leading, middle, trailing], axis=1)


def levels(stream_key, shape, cuts, least, top_value):
    loudness, own = 1.0, jax.random.fold_in(stream_key, 6)
    for dim, shards_of in cuts:
        steps = jnp.exp(jax.random.uniform(jax.random.fold_in(own, dim), (shards_of,), jnp.float32, least / len(cuts), top_value / len(cuts)))
        loudness = loudness * jnp.repeat(steps, shape[dim] // shards_of).reshape([-1 if axis == dim else 1 for axis in range(len(shape))])
    return loudness


def bell_draw(rng, dims, scale, reach, shards=(), kind=jnp.bfloat16):
    entries = jax.random.normal(rng, dims, jnp.float32) * scale
    if len(shards) > 0:
        entries = levels(rng, dims, shards, -0.22, 0.18) * entries
    return jnp.clip(entries, min=-reach, max=reach).astype(kind)


def setup_inputs(seed: int = 0) -> dict:
    seeds = jax.random.split(jax.random.key(seed), 23)
    tokens = bell_draw(seeds[0], (TOKEN_COUNT, MODEL_WIDTH), 1.0, 6.0, ((0, 32),))
    lengths = draw_lengths(jax.random.fold_in(seeds[22], 71), 0)
    cotangent = bell_draw(seeds[2], (TOKEN_COUNT, MODEL_WIDTH), 1.0, 6.0, ((0, 32),))
    mixgain = jnp.clip(1.0 + 0.1 * jax.random.normal(seeds[3], (MODEL_WIDTH,), jnp.float32), 0.5, 1.5).astype(jnp.bfloat16)
    mixentry = bell_draw(seeds[4], (MODEL_WIDTH, 3 * MODEL_WIDTH), MODEL_WIDTH ** -0.5, 0.1875)
    mixtaps = bell_draw(seeds[5], (KERNEL, MODEL_WIDTH), KERNEL ** -0.5, 3.5)
    mixexit = bell_draw(seeds[6], (MODEL_WIDTH, MODEL_WIDTH), MODEL_WIDTH ** -0.5, 0.1875)
    lowgain = jnp.clip(1.0 + 0.1 * jax.random.normal(seeds[7], (MODEL_WIDTH,), jnp.float32), 0.5, 1.5).astype(jnp.bfloat16)
    lowgate = bell_draw(seeds[8], (MODEL_WIDTH, FF), MODEL_WIDTH ** -0.5, 0.1875)
    lowlift = bell_draw(seeds[9], (MODEL_WIDTH, FF), MODEL_WIDTH ** -0.5, 0.1875)
    lowdrop = bell_draw(seeds[10], (FF, MODEL_WIDTH), FF ** -0.5, 0.09375)
    attgain = jnp.clip(1.0 + 0.1 * jax.random.normal(seeds[11], (MODEL_WIDTH,), jnp.float32), 0.5, 1.5).astype(jnp.bfloat16)
    attquery = bell_draw(seeds[12], (MODEL_WIDTH, QUERY_HEADS * HEAD_WIDTH), MODEL_WIDTH ** -0.5, 0.1875)
    attkeys = bell_draw(seeds[13], (MODEL_WIDTH, KEY_VALUE_HEADS * HEAD_WIDTH), MODEL_WIDTH ** -0.5, 0.1875)
    attvalues = bell_draw(seeds[14], (MODEL_WIDTH, KEY_VALUE_HEADS * HEAD_WIDTH), MODEL_WIDTH ** -0.5, 0.1875)
    querygain = jnp.clip(jax.random.uniform(seeds[15], (HEAD_WIDTH,), jnp.float32, 1.1953125, 2.0), 1.1953125, 2.0).astype(jnp.bfloat16)
    keysgain = jnp.clip(jax.random.uniform(seeds[16], (HEAD_WIDTH,), jnp.float32, 1.1953125, 2.0), 1.1953125, 2.0).astype(jnp.bfloat16)
    attexit = bell_draw(seeds[17], (QUERY_HEADS * HEAD_WIDTH, MODEL_WIDTH), (MODEL_WIDTH / 16) ** -0.5, 0.75)
    topgain = jnp.clip(1.0 + 0.1 * jax.random.normal(seeds[18], (MODEL_WIDTH,), jnp.float32), 0.5, 1.5).astype(jnp.bfloat16)
    topgate = bell_draw(seeds[19], (MODEL_WIDTH, FF), MODEL_WIDTH ** -0.5, 0.1875)
    toplift = bell_draw(seeds[20], (MODEL_WIDTH, FF), MODEL_WIDTH ** -0.5, 0.1875)
    topdrop = bell_draw(seeds[21], (FF, MODEL_WIDTH), FF ** -0.5, 0.09375)
    return {"tokens": tokens, "lengths": lengths, "cotangent": cotangent, "mixgain": mixgain, "mixentry": mixentry, "mixtaps": mixtaps, "mixexit": mixexit, "lowgain": lowgain, "lowgate": lowgate, "lowlift": lowlift, "lowdrop": lowdrop, "attgain": attgain, "attquery": attquery, "attkeys": attkeys, "attvalues": attvalues, "querygain": querygain, "keysgain": keysgain, "attexit": attexit, "topgain": topgain, "topgate": topgate, "toplift": toplift, "topdrop": topdrop}


EPS = 1e-05
THETA = 1000000.0
NEGATIVE = -1e+30
HIGH = lax.Precision.HIGHEST

@jax.custom_vjp
def low(v):
    return lax.optimization_barrier(v.astype(jnp.bfloat16)).astype(jnp.float32)

@jax.custom_vjp
def low_back(v):
    return v

def low_keep(v):
    return (low(v), None)

def low_pass(kept, grad):
    return (grad,)

def back_keep(v):
    return (v, None)

def back_low(kept, grad):
    return (low(grad),)
low.defvjp(low_keep, low_pass)
low_back.defvjp(back_keep, back_low)

def matrix_product(left, right):
    return jnp.dot(left, right, precision=HIGH, preferred_element_type=jnp.float32)

def root_mean_square_scale(hidden, gain):
    return hidden * lax.rsqrt(lax.optimization_barrier(jnp.mean(hidden * hidden, axis=-1, keepdims=True)) + EPS) * gain

def rotary_embed(value_rows, position_index):
    half = value_rows.shape[-1] // 2
    freq = THETA ** (-jnp.arange(half, dtype=jnp.float32) * 2.0 / value_rows.shape[-1])
    angle = position_index.astype(jnp.float32)[:, None] * freq[None, :]
    cosine = jnp.cos(angle)[:, None, :]
    sine = jnp.sin(angle)[:, None, :]
    front = value_rows[..., :half]
    behind = value_rows[..., half:]
    return jnp.concatenate([front * cosine - behind * sine, behind * cosine + front * sine], axis=-1)

def segment_of(where, first, second):
    return (where >= first).astype(jnp.int32) + (where >= second).astype(jnp.int32)

def attend(query, key_rows, value_rows, segment, where, scale):
    count = query.shape[0]
    width = math.gcd(count, 512)
    blocks = count // width

    def one_block(args):
        query_part, seg_part, where_part = args
        raw = low_back(jnp.einsum('tkgd,pkd->kgtp', query_part, key_rows, precision=HIGH) * scale)
        allowed = (seg_part[:, None] == segment[None, :]) & (where_part[:, None] >= where[None, :])
        masked = jnp.where(allowed, raw, NEGATIVE)
        peak = lax.optimization_barrier(jnp.max(masked, axis=-1, keepdims=True))
        raised = jnp.where(allowed, jnp.exp(masked - peak), 0.0)
        prob = low(raised / lax.optimization_barrier(jnp.sum(raised, axis=-1, keepdims=True)))
        return jnp.einsum('kgtp,pkd->tkgd', prob, value_rows, precision=HIGH)
    shaped = query.reshape((blocks, width) + query.shape[1:])
    result = lax.map(jax.checkpoint(one_block), (shaped, segment.reshape(blocks, width), where.reshape(blocks, width)))
    return result.reshape(count, -1)

def reference(tokens, lengths, cotangent, mixgain, mixentry, mixtaps, mixexit, lowgain, lowgate, lowlift, lowdrop, attgain, attquery, attkeys, attvalues, querygain, keysgain, attexit, topgain, topgate, toplift, topdrop):
    where = jnp.arange(GROUP_TOKENS, dtype=jnp.int32)[None, :]
    first = lengths[:, 0:1]
    second = first + lengths[:, 1:2]
    segment = segment_of(where, first, second)
    begin = jnp.where(segment == 0, 0, jnp.where(segment == 1, first, second))
    position_index = (where - begin).reshape(TOKEN_COUNT).astype(jnp.int32)
    fits_one = ((where >= 1) & (segment_of(where - 1, first, second) == segment)).astype(jnp.float32)[..., None]
    fits_two = ((where >= 2) & (segment_of(where - 2, first, second) == segment)).astype(jnp.float32)[..., None]
    shared_gradient = QUERY_HEADS // KEY_VALUE_HEADS
    scale = 1.0 / math.sqrt(HEAD_WIDTH)

    def feed(hidden, gain, gate_weight, lift_weight, drop_weight):
        fnormed = low(root_mean_square_scale(hidden, gain))
        gate_act = low_back(matrix_product(fnormed, gate_weight))
        lift_act = low_back(matrix_product(fnormed, lift_weight))
        inner = low(jax.nn.silu(gate_act) * lift_act)
        return hidden + low_back(matrix_product(inner, drop_weight))

    def forward(hidden, mixgain, mixentry, mixtaps, mixexit, lowgain, lowgate, lowlift, lowdrop, attgain, attquery, attkeys, attvalues, querygain, keysgain, attexit, topgain, topgate, toplift, topdrop):
        norm_output = low(root_mean_square_scale(hidden, mixgain))
        mixed = low_back(matrix_product(norm_output, mixentry))
        part_b = mixed[:, :MODEL_WIDTH]
        part_c = mixed[:, MODEL_WIDTH:2 * MODEL_WIDTH]
        part_x = mixed[:, 2 * MODEL_WIDTH:]
        product = low(part_b * part_x).reshape(N_DP, GROUP_TOKENS, MODEL_WIDTH)
        zeros_one = jnp.zeros((N_DP, 1, MODEL_WIDTH), jnp.float32)
        before_one = jnp.concatenate([zeros_one, product[:, :-1]], axis=1)
        before_two = jnp.concatenate([zeros_one, zeros_one, product[:, :-2]], axis=1)
        conved = (mixtaps[2] * product + mixtaps[1] * before_one * fits_one + mixtaps[0] * before_two * fits_two).reshape(TOKEN_COUNT, MODEL_WIDTH)
        gated = low(part_c * conved)
        hidden = hidden + low_back(matrix_product(gated, mixexit))
        hidden = feed(hidden, lowgain, lowgate, lowlift, lowdrop)
        norm_output = low(root_mean_square_scale(hidden, attgain))
        query_unrotated = low_back(matrix_product(norm_output, attquery)).reshape(TOKEN_COUNT, QUERY_HEADS, HEAD_WIDTH)
        key_unrotated = low_back(matrix_product(norm_output, attkeys)).reshape(TOKEN_COUNT, KEY_VALUE_HEADS, HEAD_WIDTH)
        value_projected = low_back(matrix_product(norm_output, attvalues))
        query_rows = low(rotary_embed(root_mean_square_scale(query_unrotated, querygain), position_index)).reshape(N_DP, GROUP_TOKENS, KEY_VALUE_HEADS, shared_gradient, HEAD_WIDTH)
        key_rows = low(rotary_embed(root_mean_square_scale(key_unrotated, keysgain), position_index)).reshape(N_DP, GROUP_TOKENS, KEY_VALUE_HEADS, HEAD_WIDTH)
        value_rows = low(value_projected).reshape(N_DP, GROUP_TOKENS, KEY_VALUE_HEADS, HEAD_WIDTH)
        pieces = [attend(query_rows[group_index], key_rows[group_index], value_rows[group_index], segment[group_index], where[0], scale) for group_index in range(N_DP)]
        attended = low(low_back(jnp.concatenate(pieces, axis=0)))
        hidden = hidden + low_back(matrix_product(attended, attexit))
        return feed(hidden, topgain, topgate, toplift, topdrop)
    params = tuple((weight.astype(jnp.float32) for weight in (mixgain, mixentry, mixtaps, mixexit, lowgain, lowgate, lowlift, lowdrop, attgain, attquery, attkeys, attvalues, querygain, keysgain, attexit, topgain, topgate, toplift, topdrop)))
    result, pull = jax.vjp(forward, tokens.astype(jnp.float32), *params)
    grads = pull(cotangent.astype(jnp.float32))
    return (result, grads[0], grads[1], grads[2], grads[3], grads[4], grads[5], grads[6], grads[7], grads[8], grads[9], grads[10], grads[11], grads[12], grads[13], grads[14], grads[15], grads[16], grads[17], grads[18], grads[19])
```

```python
import functools
import math

import jax
import jax.numpy as jnp
from jax import lax
from jax.experimental import pallas as pl
from jax.experimental.pallas import tpu as pltpu
from jax.sharding import PartitionSpec as P

EPS = 1e-05
THETA = 1000000.0
NEGATIVE = -1e30


def passed_along(value, axis, steps):
    count = lax.axis_size(axis)
    first, last = (max(0, -steps), min(count, count - steps))
    return lax.ppermute(value, axis, [(source, source + steps) for source in range(first, last)])


def passed_along_2(block, axis, distance):
    devices = range(lax.axis_size(axis))
    route = [((i - distance) % len(devices), i) for i in devices]
    return lax.ppermute(block, axis, route)


def root_mean_square_scale(hidden, gain):
    return hidden * lax.rsqrt(jnp.mean(hidden * hidden, axis=-1, keepdims=True) + EPS) * gain


def rotary_embed(value_rows, position_index):
    half = value_rows.shape[-1] // 2
    freq = THETA ** (-jnp.arange(half, dtype=jnp.float32) * 2.0 / value_rows.shape[-1])
    angle = position_index.astype(jnp.float32)[:, None] * freq[None, :]
    cosine = jnp.cos(angle)[:, None, :]
    sine = jnp.sin(angle)[:, None, :]
    front = value_rows[..., :half]
    behind = value_rows[..., half:]
    return jnp.concatenate(
        [front * cosine - behind * sine, behind * cosine + front * sine], axis=-1
    )


def head_prep(raw, gain, position_index, heads):
    shaped = raw.reshape(raw.shape[0], heads, -1)
    return rotary_embed(root_mean_square_scale(shaped, gain), position_index)


def segment_of(where, first, second):
    return (where >= first).astype(jnp.int32) + (where >= second).astype(jnp.int32)


def block_width(count):
    best = 1
    for candidate in range(1, min(count, 1024) + 1):
        if count % candidate == 0:
            best = candidate
    return best


def sweep(carry, count, visit):
    width = block_width(count)
    return lax.fori_loop(
        0, count // width, lambda index, inner: visit(inner, index * width, width), carry
    )


def inner_dot(left, right):
    return lax.dot_general(
        left, right, (((0,), (0,)), ((), ())), preferred_element_type=jnp.float32
    )


def outer_dot(left, right):
    return lax.dot_general(
        left, right, (((1,), (1,)), ((), ())), preferred_element_type=jnp.float32
    )


def scores_of(query_part, key_part, query_where, key_where, query_seg, key_seg, scale):
    raw = (
        jnp.einsum("tkgd,pkd->kgtp", query_part, key_part, preferred_element_type=jnp.float32)
        * scale
    )
    allowed = (query_seg[:, None] == key_seg[None, :]) & (
        query_where[:, None] >= key_where[None, :]
    )
    return (raw, allowed)


def grad_block(
    query_part,
    grad_part,
    logsum_part,
    delta_part,
    key_part,
    value_part,
    query_where,
    key_where,
    query_seg,
    key_seg,
    scale,
):
    raw, allowed = scores_of(
        query_part, key_part, query_where, key_where, query_seg, key_seg, scale
    )
    prob = jnp.where(allowed, jnp.exp(raw - logsum_part[..., None]), 0.0)
    prob_grad = jnp.einsum(
        "tkgd,pkd->kgtp", grad_part, value_part, preferred_element_type=jnp.float32
    )
    score_grad = (prob * (prob_grad - delta_part[..., None])).astype(jnp.bfloat16)
    query_grad = (
        jnp.einsum("kgtp,pkd->tkgd", score_grad, key_part, preferred_element_type=jnp.float32)
        * scale
    )
    key_grad = (
        jnp.einsum("kgtp,tkgd->pkd", score_grad, query_part, preferred_element_type=jnp.float32)
        * scale
    )
    value_grad = jnp.einsum(
        "kgtp,tkgd->pkd", prob.astype(jnp.bfloat16), grad_part, preferred_element_type=jnp.float32
    )
    return (query_grad, key_grad, value_grad)


def conv_local(extended, taps, fits_one, fits_two):
    rows = extended.shape[0] - 2
    return (
        taps[2] * extended[2:]
        + taps[1] * extended[1 : rows + 1] * fits_one
        + taps[0] * extended[:rows] * fits_two
    )


def feed_forward(hidden, gain, gate_weight, lift_weight, drop_weight):
    fnormed = root_mean_square_scale(hidden, gain).astype(jnp.bfloat16)
    gate_act = jnp.dot(fnormed, gate_weight, preferred_element_type=jnp.float32)
    lift_act = jnp.dot(fnormed, lift_weight, preferred_element_type=jnp.float32)
    inner = (jax.nn.silu(gate_act) * lift_act).astype(jnp.bfloat16)
    result = hidden + jnp.dot(inner, drop_weight, preferred_element_type=jnp.float32)
    return (result, (fnormed, gate_act, lift_act, inner))


def feed_back(grad, hidden, gain, kept, gate_weight, lift_weight, drop_weight):
    fnormed, gate_act, lift_act, inner = kept
    grad_low = grad.astype(jnp.bfloat16)
    drop_grad = inner_dot(inner, grad_low)
    inner_grad = outer_dot(grad_low, drop_weight)
    _, pull_gate = jax.vjp(
        lambda gate_in, lift_in: jax.nn.silu(gate_in) * lift_in, gate_act, lift_act
    )
    gate_grad, lift_grad = pull_gate(inner_grad)
    gate_low = gate_grad.astype(jnp.bfloat16)
    lift_low = lift_grad.astype(jnp.bfloat16)
    gate_wgrad = inner_dot(fnormed, gate_low)
    lift_wgrad = inner_dot(fnormed, lift_low)
    normed_grad = outer_dot(gate_low, gate_weight) + outer_dot(lift_low, lift_weight)
    _, pull_norm = jax.vjp(root_mean_square_scale, hidden, gain)
    hidden_grad, gain_grad = pull_norm(normed_grad)
    return (grad + hidden_grad, (gain_grad, gate_wgrad, lift_wgrad, drop_grad))


def per_device(
    tokens,
    lengths,
    cotangent,
    mixgain,
    mixentry,
    mixtaps,
    mixexit,
    lowgain,
    lowgate,
    lowlift,
    lowdrop,
    attgain,
    attquery,
    attkeys,
    attvalues,
    querygain,
    keysgain,
    attexit,
    topgain,
    topgate,
    toplift,
    topdrop,
):
    rows = tokens.shape[0]
    width_model = tokens.shape[1]
    head_size = querygain.shape[0]
    query_heads = attquery.shape[1] // head_size
    kv_heads = attkeys.shape[1] // head_size
    shared_gradient = query_heads // kv_heads
    scale = 1.0 / math.sqrt(head_size)
    place = lax.axis_index("ctx")
    first = lengths[0, 0]
    second = first + lengths[0, 1]
    mine = place * rows + jnp.arange(rows, dtype=jnp.int32)
    my_seg = segment_of(mine, first, second)
    begin = jnp.where(my_seg == 0, 0, jnp.where(my_seg == 1, first, second))
    position_index = mine - begin
    last_row = place * rows + rows - 1
    mixgain_f = mixgain.astype(jnp.float32)
    taps_f = mixtaps.astype(jnp.float32)
    lowgain_f = lowgain.astype(jnp.float32)
    attgain_f = attgain.astype(jnp.float32)
    querygain_f = querygain.astype(jnp.float32)
    keysgain_f = keysgain.astype(jnp.float32)
    topgain_f = topgain.astype(jnp.float32)
    hidden = tokens.astype(jnp.float32)
    normed_one = root_mean_square_scale(hidden, mixgain_f).astype(jnp.bfloat16)
    mixed = jnp.dot(normed_one, mixentry, preferred_element_type=jnp.float32)
    part_b = mixed[:, :width_model]
    part_c = mixed[:, width_model : 2 * width_model]
    part_x = mixed[:, 2 * width_model :]
    product = (part_b * part_x).astype(jnp.bfloat16)
    borrowed = passed_along(product[rows - 2 :], "ctx", 1)
    extended = jnp.concatenate([borrowed, product], axis=0).astype(jnp.float32)
    fits_one = ((mine >= 1) & (segment_of(mine - 1, first, second) == my_seg)).astype(jnp.float32)[
        :, None
    ]
    fits_two = ((mine >= 2) & (segment_of(mine - 2, first, second) == my_seg)).astype(jnp.float32)[
        :, None
    ]
    conved = conv_local(extended, taps_f, fits_one, fits_two)
    gated = (part_c * conved).astype(jnp.bfloat16)
    hidden_one = hidden + jnp.dot(gated, mixexit, preferred_element_type=jnp.float32)
    hidden_two, kept_low = feed_forward(hidden_one, lowgain_f, lowgate, lowlift, lowdrop)
    normed_two = root_mean_square_scale(hidden_two, attgain_f).astype(jnp.bfloat16)
    query_unrotated = jnp.dot(normed_two, attquery, preferred_element_type=jnp.float32)
    key_unrotated = jnp.dot(normed_two, attkeys, preferred_element_type=jnp.float32)
    value_projected = jnp.dot(normed_two, attvalues, preferred_element_type=jnp.float32)
    query_low = head_prep(query_unrotated, querygain_f, position_index, query_heads).astype(
        jnp.bfloat16
    )
    key_low = head_prep(key_unrotated, keysgain_f, position_index, kv_heads).astype(jnp.bfloat16)
    value_low = value_projected.astype(jnp.bfloat16).reshape(rows, kv_heads, head_size)
    query_grouped = query_low.reshape(rows, kv_heads, shared_gradient, head_size)

    def stat_visit(carry, keys_in, start, offset, width):
        top, total = carry
        key_part = lax.dynamic_slice_in_dim(keys_in, offset, width, 0)
        key_where = start + offset + jnp.arange(width, dtype=jnp.int32)
        raw, allowed = scores_of(
            query_grouped,
            key_part,
            mine,
            key_where,
            my_seg,
            segment_of(key_where, first, second),
            scale,
        )
        new_top = jnp.maximum(top, jnp.max(jnp.where(allowed, raw, NEGATIVE), axis=-1))
        weights = jnp.where(allowed, jnp.exp(raw - new_top[..., None]), 0.0)
        total = total * jnp.exp(top - new_top) + jnp.sum(weights, axis=-1)
        return (new_top, total)

    stat_state = (
        jnp.full((kv_heads, shared_gradient, rows), NEGATIVE, jnp.float32),
        jnp.zeros((kv_heads, shared_gradient, rows), jnp.float32),
    )
    piece = lax.all_gather(key_low, "ctx", axis=0, tiled=True)
    start = jnp.int32(0)
    count = piece.shape[0]

    def stat_running(inner):
        return sweep(
            inner, count, lambda acc, offset, width: stat_visit(acc, piece, start, offset, width)
        )

    top, total = lax.cond(start > last_row, lambda inner: inner, stat_running, stat_state)
    logsum = top + jnp.log(total)

    def forward_visit(accum, keys_in, values_in, start, offset, width):
        key_part = lax.dynamic_slice_in_dim(keys_in, offset, width, 0)
        value_part = lax.dynamic_slice_in_dim(values_in, offset, width, 0)
        key_where = start + offset + jnp.arange(width, dtype=jnp.int32)
        raw, allowed = scores_of(
            query_grouped,
            key_part,
            mine,
            key_where,
            my_seg,
            segment_of(key_where, first, second),
            scale,
        )
        prob_low = jnp.where(allowed, jnp.exp(raw - logsum[..., None]), 0.0).astype(jnp.bfloat16)
        return accum + jnp.einsum(
            "kgtp,pkd->kgtd", prob_low, value_part, preferred_element_type=jnp.float32
        )

    forward_start = jnp.int32(0)
    keys_in = lax.all_gather(key_low, "ctx", axis=0, tiled=True)
    values_in = lax.all_gather(value_low, "ctx", axis=0, tiled=True)
    forward_count = keys_in.shape[0]

    def forward_running(inner):
        return sweep(
            inner,
            forward_count,
            lambda acc, offset, width: forward_visit(
                acc, keys_in, values_in, forward_start, offset, width
            ),
        )

    accum = lax.cond(
        forward_start > last_row,
        lambda inner: inner,
        forward_running,
        jnp.zeros((kv_heads, shared_gradient, rows, head_size), jnp.float32),
    )
    attended = accum.transpose(2, 0, 1, 3).reshape(rows, -1)
    attended_low = attended.astype(jnp.bfloat16)
    hidden_three = hidden_two + jnp.dot(attended_low, attexit, preferred_element_type=jnp.float32)
    output, kept_top = feed_forward(hidden_three, topgain_f, topgate, toplift, topdrop)
    grad = cotangent.astype(jnp.float32)
    grad, top_grads = feed_back(grad, hidden_three, topgain_f, kept_top, topgate, toplift, topdrop)
    grad_low = grad.astype(jnp.bfloat16)
    attexit_grad = inner_dot(attended_low, grad_low)
    out_grads = (
        outer_dot(grad_low, attexit)
        .astype(jnp.bfloat16)
        .reshape(rows, kv_heads, shared_gradient, head_size)
    )
    delta = jnp.einsum(
        "tkgd,tkgd->kgt",
        out_grads.astype(jnp.float32),
        attended.reshape(rows, kv_heads, shared_gradient, head_size),
    )
    cycle_size = lax.axis_size("ctx")

    def cycle_visit(state, keys_in, values_in, start, offset, width):
        query_acc, key_acc, value_acc = state
        key_part = lax.dynamic_slice_in_dim(keys_in, offset, width, 0)
        value_part = lax.dynamic_slice_in_dim(values_in, offset, width, 0)
        key_where = start + offset + jnp.arange(width, dtype=jnp.int32)
        query_grad, key_grad, value_grad = grad_block(
            query_grouped,
            out_grads,
            logsum,
            delta,
            key_part,
            value_part,
            mine,
            key_where,
            my_seg,
            segment_of(key_where, first, second),
            scale,
        )
        key_acc = lax.dynamic_update_slice_in_dim(
            key_acc, lax.dynamic_slice_in_dim(key_acc, offset, width, 0) + key_grad, offset, 0
        )
        value_acc = lax.dynamic_update_slice_in_dim(
            value_acc, lax.dynamic_slice_in_dim(value_acc, offset, width, 0) + value_grad, offset, 0
        )
        return (query_acc + query_grad, key_acc, value_acc)

    def cycle_step(step, carry):
        keys_cur, values_cur, key_acc, value_acc, query_acc = carry
        anchor = (place - step + cycle_size) % cycle_size
        start = anchor * rows

        def cycle_running(state):
            return sweep(
                state,
                rows,
                lambda acc, offset, width: cycle_visit(
                    acc, keys_cur, values_cur, start, offset, width
                ),
            )

        query_acc, key_acc, value_acc = lax.cond(
            start > last_row, lambda state: state, cycle_running, (query_acc, key_acc, value_acc)
        )
        keys_cur, values_cur = passed_along((keys_cur, values_cur), "ctx", 1)
        key_acc, value_acc = (
            passed_along_2(key_acc.astype(jnp.bfloat16), "ctx", 1).astype(key_acc.dtype),
            passed_along_2(value_acc.astype(jnp.bfloat16), "ctx", 1).astype(value_acc.dtype),
        )
        return (keys_cur, values_cur, key_acc, value_acc, query_acc)

    cycle_state = (
        key_low,
        value_low,
        jnp.zeros((rows, kv_heads, head_size), jnp.float32),
        jnp.zeros((rows, kv_heads, head_size), jnp.float32),
        jnp.zeros((rows, kv_heads, shared_gradient, head_size), jnp.float32),
    )
    _, _, key_grads, value_grads, query_acc = lax.fori_loop(0, cycle_size, cycle_step, cycle_state)
    _, pull_query = jax.vjp(
        lambda raw, gain: head_prep(raw, gain, position_index, query_heads),
        query_unrotated,
        querygain_f,
    )
    query_raw_grad, querygain_grad = pull_query(query_acc.reshape(rows, query_heads, head_size))
    _, pull_key = jax.vjp(
        lambda raw, gain: head_prep(raw, gain, position_index, kv_heads), key_unrotated, keysgain_f
    )
    key_raw_grad, keysgain_grad = pull_key(key_grads)
    query_raw_low = query_raw_grad.astype(jnp.bfloat16)
    key_raw_low = key_raw_grad.astype(jnp.bfloat16)
    value_raw_low = value_grads.reshape(rows, -1).astype(jnp.bfloat16)
    attquery_grad = inner_dot(normed_two, query_raw_low)
    attkeys_grad = inner_dot(normed_two, key_raw_low)
    attvalues_grad = inner_dot(normed_two, value_raw_low)
    normed_two_grad = (
        outer_dot(query_raw_low, attquery)
        + outer_dot(key_raw_low, attkeys)
        + outer_dot(value_raw_low, attvalues)
    )
    _, pull_att = jax.vjp(root_mean_square_scale, hidden_two, attgain_f)
    hidden_two_grad, attgain_grad = pull_att(normed_two_grad)
    grad = grad + hidden_two_grad
    grad, low_grads = feed_back(grad, hidden_one, lowgain_f, kept_low, lowgate, lowlift, lowdrop)
    grad_low = grad.astype(jnp.bfloat16)
    mixexit_grad = inner_dot(gated, grad_low)
    gated_grad = outer_dot(grad_low, mixexit)
    part_c_grad = gated_grad * conved
    conved_grad = gated_grad * part_c
    _, pull_conv = jax.vjp(
        lambda ext, taps: conv_local(ext, taps, fits_one, fits_two), extended, taps_f
    )
    extended_grad, mixtaps_grad = pull_conv(conved_grad)
    returned_rim = passed_along(extended_grad[:2], "ctx", -1)
    product_grad = extended_grad[2:].at[rows - 2 :].add(returned_rim)
    mixed_grad = jnp.concatenate(
        [product_grad * part_x, part_c_grad, product_grad * part_b], axis=1
    ).astype(jnp.bfloat16)
    mixentry_grad = inner_dot(normed_one, mixed_grad)
    normed_one_grad = outer_dot(mixed_grad, mixentry)
    _, pull_mix = jax.vjp(root_mean_square_scale, hidden, mixgain_f)
    hidden_grad, mixgain_grad = pull_mix(normed_one_grad)
    tokens_grad = grad + hidden_grad
    lowgain_grad, lowgate_grad, lowlift_grad, lowdrop_grad = low_grads
    topgain_grad, topgate_grad, toplift_grad, topdrop_grad = top_grads
    shares = (
        lax.psum_scatter(mixentry_grad, "ctx", scatter_dimension=0, tiled=True),
        lax.psum_scatter(mixexit_grad, "ctx", scatter_dimension=0, tiled=True),
        lax.psum_scatter(lowgate_grad, "ctx", scatter_dimension=0, tiled=True),
        lax.psum_scatter(lowlift_grad, "ctx", scatter_dimension=0, tiled=True),
        lax.psum_scatter(lowdrop_grad, "ctx", scatter_dimension=0, tiled=True),
        lax.psum_scatter(attquery_grad, "ctx", scatter_dimension=0, tiled=True),
        lax.psum_scatter(attkeys_grad, "ctx", scatter_dimension=0, tiled=True),
        lax.psum_scatter(attvalues_grad, "ctx", scatter_dimension=0, tiled=True),
        lax.psum_scatter(attexit_grad, "ctx", scatter_dimension=0, tiled=True),
        lax.psum_scatter(topgate_grad, "ctx", scatter_dimension=0, tiled=True),
        lax.psum_scatter(toplift_grad, "ctx", scatter_dimension=0, tiled=True),
        lax.psum_scatter(topdrop_grad, "ctx", scatter_dimension=0, tiled=True),
    )
    smalls = lax.psum(
        (
            mixgain_grad,
            mixtaps_grad,
            lowgain_grad,
            attgain_grad,
            querygain_grad,
            keysgain_grad,
            topgain_grad,
        ),
        "ctx",
    )
    summed = (
        lax.psum(shares[0].astype(jnp.bfloat16), "dp").astype(jnp.float32),
        lax.psum(shares[1].astype(jnp.bfloat16), "dp").astype(jnp.float32),
        lax.psum(shares[2].astype(jnp.bfloat16), "dp").astype(jnp.float32),
        lax.psum(shares[3].astype(jnp.bfloat16), "dp").astype(jnp.float32),
        lax.psum(shares[4].astype(jnp.bfloat16), "dp").astype(jnp.float32),
        lax.psum(shares[5].astype(jnp.bfloat16), "dp").astype(jnp.float32),
        lax.psum(shares[6].astype(jnp.bfloat16), "dp").astype(jnp.float32),
        lax.psum(shares[7].astype(jnp.bfloat16), "dp").astype(jnp.float32),
        lax.psum(shares[8].astype(jnp.bfloat16), "dp").astype(jnp.float32),
        lax.psum(shares[9].astype(jnp.bfloat16), "dp").astype(jnp.float32),
        lax.psum(shares[10].astype(jnp.bfloat16), "dp").astype(jnp.float32),
        lax.psum(shares[11].astype(jnp.bfloat16), "dp").astype(jnp.float32),
        lax.psum(smalls[0].astype(jnp.bfloat16), "dp").astype(jnp.float32),
        lax.psum(smalls[1].astype(jnp.bfloat16), "dp").astype(jnp.float32),
        lax.psum(smalls[2].astype(jnp.bfloat16), "dp").astype(jnp.float32),
        lax.psum(smalls[3].astype(jnp.bfloat16), "dp").astype(jnp.float32),
        lax.psum(smalls[4].astype(jnp.bfloat16), "dp").astype(jnp.float32),
        lax.psum(smalls[5].astype(jnp.bfloat16), "dp").astype(jnp.float32),
        lax.psum(smalls[6].astype(jnp.bfloat16), "dp").astype(jnp.float32),
    )
    return (
        output,
        tokens_grad,
        summed[12],
        summed[0],
        summed[13],
        summed[1],
        summed[14],
        summed[2],
        summed[3],
        summed[4],
        summed[15],
        summed[5],
        summed[6],
        summed[7],
        summed[16],
        summed[17],
        summed[8],
        summed[18],
        summed[9],
        summed[10],
        summed[11],
    )


LANES = 128
BF = jnp.bfloat16
F32 = jnp.float32
ONES_NT = (((1,), (1,)), ((), ()))
ONES_TN = (((0,), (0,)), ((), ()))
VMEM_LIMIT = 60 * 1024 * 1024


def vmem_specs(count):
    return [pl.BlockSpec(memory_space=pltpu.VMEM)] * count


def lane_of(shape):
    return lax.broadcasted_iota(jnp.int32, shape, len(shape) - 1)


def same_head(head):
    row = lax.broadcasted_iota(jnp.int32, (LANES, LANES), 0) // head
    column = lax.broadcasted_iota(jnp.int32, (LANES, LANES), 1) // head
    return jnp.where(row == column, 1.0 / head, 0.0).astype(F32)


def head_mean(value, blocks):
    return jnp.dot(value, blocks, precision=lax.Precision.HIGHEST, preferred_element_type=F32)


def other_half(value, head):
    lane = lane_of(value.shape)
    ahead = pltpu.roll(value, LANES - head // 2, 1)
    behind = pltpu.roll(value, head // 2, 1)
    return jnp.where(lane % head < head // 2, ahead, behind)


def swap_heads(value, head):
    return pltpu.roll(value, head, 1)


def three_parts(value):
    high = value.astype(BF)
    rest = value - high.astype(F32)
    middle = rest.astype(BF)
    low = (rest - middle.astype(F32)).astype(BF)
    return high.astype(F32), middle.astype(F32), low.astype(F32)


def project_kernel(head, hid_ref, gain_ref, wq_ref, wk_ref, wv_ref, cos_ref, sin_ref, qg_ref, kg_ref,
                   msg_ref, normed_ref, qraw_ref, kraw_ref):
    hid = hid_ref[...]
    scale = lax.rsqrt(jnp.mean(hid * hid, axis=-1, keepdims=True) + EPS)
    normed = (hid * scale * gain_ref[...]).astype(BF)
    normed_ref[...] = normed
    blocks = same_head(head)
    cosine, sine = cos_ref[...], sin_ref[...]
    half_rows = msg_ref.shape[1]
    lane = lane_of(cosine.shape)

    def prepared(raw, gain):
        unit = raw * lax.rsqrt(head_mean(raw * raw, blocks) + EPS) * gain
        return unit * cosine + other_half(unit, head) * sine

    def put(dest, start, tile):
        low = tile.astype(BF)
        for part in range(2):
            msg_ref[2 * dest + part, :, start:start + LANES] = low[part * half_rows:(part + 1) * half_rows]

    qraw = jnp.dot(normed, wq_ref[...], preferred_element_type=F32)
    qraw_ref[...] = qraw
    for tile in range(qraw.shape[1] // LANES):
        put(tile, 0, prepared(qraw[:, tile * LANES:(tile + 1) * LANES], qg_ref[...]))
    kraw = jnp.dot(normed, wk_ref[...], preferred_element_type=F32)
    kraw_ref[...] = kraw
    vraw = jnp.dot(normed, wv_ref[...], preferred_element_type=F32)
    for tile in range(kraw.shape[1] // LANES):
        keys = prepared(kraw[:, tile * LANES:(tile + 1) * LANES], kg_ref[...])
        values = vraw[:, tile * LANES:(tile + 1) * LANES]
        put(2 * tile, LANES, jnp.where(lane < head, keys, swap_heads(values, head)))
        put(2 * tile + 1, LANES, jnp.where(lane < head, swap_heads(keys, head), values))


def project_back_kernel(head, back_ref, hid_ref, gain_ref, wq_ref, wk_ref, wv_ref, cos_ref, sin_ref, qg_ref,
                        kg_ref, qraw_ref, kraw_ref, grad_ref,
                        raw_ref, two_ref, again_ref, qgain_ref, kgain_ref):
    blocks = same_head(head)
    cosine, sine = cos_ref[...], sin_ref[...]
    half_rows = back_ref.shape[1]
    lane = lane_of(cosine.shape)

    def fetch(dest, start):
        return jnp.concatenate(
            [back_ref[2 * dest + part, :, start:start + LANES] for part in range(2)], axis=0).astype(F32)

    def through(grad, raw, gain):
        scale = lax.rsqrt(head_mean(raw * raw, blocks) + EPS)
        unit = raw * scale
        turned = grad * cosine - other_half(grad, head) * sine
        gain_part = jnp.sum(turned * unit, axis=0, keepdims=True)
        inward = turned * gain
        return scale * (inward - unit * head_mean(inward * unit, blocks)), gain_part

    width_q = wq_ref.shape[1]
    width_k = wk_ref.shape[1]
    gain_total = jnp.zeros((1, LANES), F32)
    for tile in range(width_q // LANES):
        got, part = through(fetch(tile, 0), qraw_ref[:, tile * LANES:(tile + 1) * LANES], qg_ref[...])
        gain_total = gain_total + part
        raw_ref[:, tile * LANES:(tile + 1) * LANES] = got.astype(BF)
    qgain_ref[...] = gain_total
    gain_total = jnp.zeros((1, LANES), F32)
    for tile in range(width_k // LANES):
        even, odd = fetch(2 * tile, LANES), fetch(2 * tile + 1, LANES)
        keys = jnp.where(lane < head, even, swap_heads(odd, head))
        values = jnp.where(lane < head, swap_heads(even, head), odd)
        got, part = through(keys, kraw_ref[:, tile * LANES:(tile + 1) * LANES], kg_ref[...])
        gain_total = gain_total + part
        raw_ref[:, width_q + tile * LANES:width_q + (tile + 1) * LANES] = got.astype(BF)
        raw_ref[:, width_q + width_k + tile * LANES:width_q + width_k + (tile + 1) * LANES] = values.astype(BF)
    kgain_ref[...] = gain_total
    normed_grad = lax.dot_general(raw_ref[:, :width_q], wq_ref[...], ONES_NT, preferred_element_type=F32)
    normed_grad += lax.dot_general(raw_ref[:, width_q:width_q + width_k], wk_ref[...], ONES_NT,
                                   preferred_element_type=F32)
    normed_grad += lax.dot_general(raw_ref[:, width_q + width_k:], wv_ref[...], ONES_NT,
                                   preferred_element_type=F32)
    hid = hid_ref[...]
    scale = lax.rsqrt(jnp.mean(hid * hid, axis=-1, keepdims=True) + EPS)
    unit = hid * scale
    again_ref[...] = jnp.sum(normed_grad * unit, axis=0, keepdims=True)
    inward = normed_grad * gain_ref[...]
    two_ref[...] = grad_ref[...] + scale * (inward - unit * jnp.mean(inward * unit, axis=-1, keepdims=True))


def allowed_block(row_axis, key_axis, shape, first, second, part, base, start, rows, half_rows):
    row = lax.broadcasted_iota(jnp.int32, shape, row_axis)
    token = (base + row // (2 * half_rows)) * rows + part * half_rows + row % half_rows
    key = start + lax.broadcasted_iota(jnp.int32, shape, key_axis)
    begin = jnp.where(token >= second, second, jnp.where(token >= first, first, 0))
    return (key >= begin) & (key <= token)


def need_mask(first, second, part, base, start, rows, half_rows, keys, sources):
    lowest = base * rows + part * half_rows
    highest = (base + sources - 1) * rows + (part + 1) * half_rows - 1
    begin = jnp.where(highest >= second, second, jnp.where(highest >= first, first, 0))
    return (start + keys - 1 > lowest) | (start < begin)


def attend_kernel(head, rows, keys, sources, info_ref, q_ref, kv_ref, out_ref, aug_ref, ones_ref, acc_ref):
    first, second, part = info_ref[0], info_ref[1], info_ref[2]
    half_rows = q_ref.shape[1]
    wide = sources * 2 * half_rows
    factor = math.log2(math.e) / math.sqrt(head)
    ones_ref[...] = jnp.where(lane_of(kv_ref.shape) < head, jnp.ones_like(kv_ref), kv_ref[...])
    lane = lane_of((half_rows, LANES))

    def block(index, _):
        base = index * sources
        stack = []
        for source in range(sources):
            tile = q_ref[base + source][:, :LANES].astype(F32)
            stack.append(jnp.where(lane < head, tile, 0.0))
            stack.append(jnp.where(lane < head, swap_heads(tile, head), 0.0))
        queries = jnp.concatenate(stack, axis=0).astype(BF)
        acc_ref[...] = jnp.zeros_like(acc_ref)
        last = (base + sources - 1) * rows + (part + 1) * half_rows
        count = (last + keys - 1) // keys

        def visit(step, _):
            start = pl.multiple_of(step * keys, keys)
            raw = lax.dot_general(queries, kv_ref[pl.ds(start, keys)], ONES_NT, preferred_element_type=F32)
            raised = jnp.exp2(raw * factor)
            masked = need_mask(first, second, part, base, start, rows, half_rows, keys, sources)

            @pl.when(masked)
            def _():
                ok = allowed_block(0, 1, (wide, keys), first, second, part, base, start, rows, half_rows)
                acc_ref[...] += jnp.dot(jnp.where(ok, raised, 0.0).astype(BF), ones_ref[pl.ds(start, keys)],
                                        preferred_element_type=F32)

            @pl.when(jnp.logical_not(masked))
            def _():
                acc_ref[...] += jnp.dot(raised.astype(BF), ones_ref[pl.ds(start, keys)],
                                        preferred_element_type=F32)

        lax.fori_loop(0, count, visit, None)
        for source in range(sources):
            tile = q_ref[base + source][:, :LANES].astype(F32)
            outs = []
            for which in range(2):
                place = (2 * source + which) * half_rows
                acc = acc_ref[place:place + half_rows]
                turned = swap_heads(acc, head)
                outs.append(turned / acc if which == 0 else acc / turned)
                high, middle, low = three_parts(-math.sqrt(head) * jnp.log(turned))
                query = tile if which == 0 else swap_heads(tile, head)
                extra = jnp.where(lane == head, high, jnp.where(lane == head + 1, middle,
                                                                jnp.where(lane == head + 2, low, 0.0)))
                aug_ref[base + source, which] = jnp.where(lane < head, query, extra).astype(BF)
            out_ref[base + source] = jnp.where(lane < head, outs[0], outs[1])

    lax.fori_loop(0, q_ref.shape[0] // sources, block, None)


def attend_back_kernel(head, rows, keys, sources, info_ref, aug_ref, out_ref, grad_ref, kv_ref,
                       dq_ref, dkv_ref, kone_ref, vone_ref, dk_ref, dv_ref, acc_ref):
    first, second, part = info_ref[0], info_ref[1], info_ref[2]
    half_rows = grad_ref.shape[1]
    wide = sources * 2 * half_rows
    factor = math.log2(math.e) / math.sqrt(head)
    whole = lane_of(kv_ref.shape)
    vone_ref[...] = jnp.where(whole < head, jnp.ones_like(kv_ref), kv_ref[...])
    kone_ref[...] = jnp.where(whole < head, kv_ref[...], jnp.ones_like(kv_ref))
    dk_ref[...] = jnp.zeros_like(dk_ref)
    dv_ref[...] = jnp.zeros_like(dv_ref)
    lane = lane_of((half_rows, LANES))

    def block(index, _):
        base = index * sources
        stack_q, stack_d = [], []
        for source in range(sources):
            grad = grad_ref[base + source].astype(F32)
            spread = grad * out_ref[base + source]
            for which in range(2):
                stack_q.append(aug_ref[base + source, which])
                mine = (lane < head) if which == 0 else (lane >= head)
                delta = jnp.sum(jnp.where(mine, spread, 0.0), axis=1, keepdims=True)
                high, middle, low = three_parts(-delta)
                extra = jnp.where(lane == 0, high, jnp.where(lane == 1, middle, jnp.where(lane == 2, low, 0.0)))
                moved = swap_heads(grad, head) if which == 0 else grad
                stack_d.append(jnp.where(lane < head, extra, moved).astype(BF))
        queries = jnp.concatenate(stack_q, axis=0)
        grads = jnp.concatenate(stack_d, axis=0)
        acc_ref[...] = jnp.zeros_like(acc_ref)
        last = (base + sources - 1) * rows + (part + 1) * half_rows
        count = (last + keys - 1) // keys

        def visit(step, _):
            start = pl.multiple_of(step * keys, keys)
            here = pl.ds(start, keys)

            def finish(prob):
                along = lax.dot_general(vone_ref[here], grads, ONES_NT, preferred_element_type=F32)
                score = (prob * along).astype(BF)
                dv_ref[here] += jnp.dot(prob.astype(BF), grads, preferred_element_type=F32)
                dk_ref[here] += jnp.dot(score, queries, preferred_element_type=F32)
                acc_ref[...] += lax.dot_general(score, kone_ref[here], ONES_TN, preferred_element_type=F32)

            raw = lax.dot_general(kone_ref[here], queries, ONES_NT, preferred_element_type=F32)
            masked = need_mask(first, second, part, base, start, rows, half_rows, keys, sources)

            @pl.when(masked)
            def _():
                ok = allowed_block(1, 0, (keys, wide), first, second, part, base, start, rows, half_rows)
                finish(jnp.where(ok, jnp.exp2(jnp.where(ok, raw, 0.0) * factor), 0.0))

            @pl.when(jnp.logical_not(masked))
            def _():
                finish(jnp.exp2(raw * factor))

        lax.fori_loop(0, count, visit, None)
        for source in range(sources):
            place = 2 * source * half_rows
            one = acc_ref[place:place + half_rows]
            two = acc_ref[place + half_rows:place + 2 * half_rows]
            both = jnp.where(lane < head, one, swap_heads(two, head)) * (1.0 / math.sqrt(head))
            dq_ref[base + source] = both.astype(BF)

    lax.fori_loop(0, grad_ref.shape[0] // sources, block, None)
    dkv_ref[...] = jnp.where(whole < head, dk_ref[...] * (1.0 / math.sqrt(head)), dv_ref[...]).astype(BF)


SUB = 64
STRIP = 256
RING = 8
LAG = 2


def sum_kernel(jobs, lines, *refs):
    count = len(jobs)
    lefts, rights, out_ref = refs[:count], refs[count:2 * count], refs[2 * count]
    (lbuf, rbuf, xp, xr, yp, yr, zp, us, ur, ds_, dr, fs, fr, stage,
     lsem, rsem, xs, xv, ys, yv, uss, urv, dss, drv, fss, frv, osem) = refs[2 * count + 1:]
    steps = sum(job[2] for job in jobs)
    last = steps - 1 + LAG
    half = STRIP // 2
    quarter = SUB // 2
    tall = SUB + quarter
    me = lax.axis_index("ctx")
    y = lax.axis_index("dp")
    z = me // 4
    x = (me // 2) % 2
    c = me % 2
    across_x = {"ctx": me + 2 - 4 * x}
    across_y = {"dp": 1 - y}
    above = {"ctx": jnp.minimum(me + 4, 4 * lines - 4 + me % 4)}
    below = {"ctx": jnp.maximum(me - 4, me % 4)}
    top = lines - 1

    for buf in (xp, ur, dr, zp):
        buf[...] = jnp.zeros_like(buf)

    barrier = pltpu.get_barrier_semaphore()
    pl.semaphore_signal(barrier, inc=1, device_id=across_x, device_id_type=MESH)
    pl.semaphore_signal(barrier, inc=1, device_id=across_y, device_id_type=MESH)

    @pl.when(z < top)
    def _():
        pl.semaphore_signal(barrier, inc=1, device_id=above, device_id_type=MESH)

    @pl.when(z > 0)
    def _():
        pl.semaphore_signal(barrier, inc=1, device_id=below, device_id_type=MESH)

    pl.semaphore_wait(barrier, 2 + (z < top).astype(jnp.int32) + (z > 0).astype(jnp.int32))

    def remote(src, dst, send, recv, where):
        return pltpu.make_async_remote_copy(src_ref=src, dst_ref=dst, send_sem=send, recv_sem=recv,
                                            device_id=where, device_id_type=MESH)

    def x_copy(j):
        s = j % RING
        return remote(xp.at[s, 1 - x], xr.at[s], xs.at[s], xv.at[s], across_x)

    def y_copy(j):
        s = j % RING
        return remote(yp.at[s, 1 - y], yr.at[s], ys.at[s], yv.at[s], across_y)

    def up_copy(j):
        s = j % RING
        return remote(us.at[s], ur.at[s], uss.at[s], urv.at[s], above)

    def down_copy(j):
        s = j % RING
        return remote(ds_.at[s], dr.at[s], dss.at[s], drv.at[s], below)

    def f_copy(j):
        s = j % RING
        return remote(fs.at[s], fr.at[s], fss.at[s], frv.at[s], across_y)

    def l_wait(j):
        s = j % 2
        pltpu.make_async_copy(lefts[0].at[:, pl.ds(0, SUB), :], lbuf.at[s], lsem.at[s]).wait()
        pltpu.make_async_copy(rights[0].at[:, pl.ds(0, STRIP)], rbuf.at[s], rsem.at[s]).wait()

    def load(j):
        s = j % 2
        begin = 0
        for number, (subs, strips, total) in enumerate(jobs):
            @pl.when((j >= begin) & (j < begin + total))
            def _(number=number, subs=subs, begin=begin):
                k = j - begin
                row = pl.multiple_of((k % subs) * SUB, SUB)
                column = pl.multiple_of((k // subs) * STRIP, STRIP)
                pltpu.make_async_copy(lefts[number].at[:, pl.ds(row, SUB), :], lbuf.at[s], lsem.at[s]).start()
                pltpu.make_async_copy(rights[number].at[:, pl.ds(column, STRIP)], rbuf.at[s], rsem.at[s]).start()
            begin += total

    def out_copy(j):
        s = j % 2
        return pltpu.make_async_copy(stage.at[s], out_ref.at[j], osem.at[s])

    load(0)

    def step(t, _):
        slot = t % RING

        @pl.when(t < steps)
        def _():
            l_wait(t)

            @pl.when(t + 1 < steps)
            def _():
                load(t + 1)

            left = lbuf[t % 2].reshape(2 * lines * SUB, lbuf.shape[-1])
            got = jnp.dot(left, rbuf[t % 2], preferred_element_type=F32).astype(BF)
            for line in range(lines):
                for side in range(2):
                    row = (2 * line + side) * SUB
                    xp[slot, side, line, :SUB] = got[row:row + SUB, :half]
                    for part in range(2):
                        yp[slot, part, side, line] = got[row + part * quarter:row + (part + 1) * quarter, half:]

        @pl.when((t >= LAG) & (t <= last))
        def _():
            y_copy(t - LAG).wait()
            s = (t - LAG) % RING
            xp[slot, :, :, SUB:] = yp[s, y] + yr[s]

        @pl.when(t < steps)
        def _():
            y_copy(t).start()

        @pl.when(t <= last)
        def _():
            x_copy(t).start()

        @pl.when((t >= LAG) & (t - LAG <= last))
        def _():
            x_copy(t - LAG).wait()
            s = (t - LAG) % RING
            zp[(t - LAG) % (2 * RING)] = xp[s, x] + xr[s]

        ju = t - LAG * (1 + z)

        @pl.when((ju >= 0) & (ju <= last))
        def _():
            s = ju % RING
            held = ju % (2 * RING)

            @pl.when(z > 0)
            def _():
                up_copy(ju).wait_recv()
                zp[held, z] = zp[held, z] + ur[s, 0]

            @pl.when(z < top)
            def _():
                @pl.when(ju >= RING)
                def _():
                    up_copy(ju).wait_send()

                for m in range(top):
                    own = zp[held, jnp.minimum(z + 1 + m, top)]
                    if m + 1 < top:
                        own = own + ur[s, m + 1]
                    us[s, m] = own
                up_copy(ju).start()

        jd = t - LAG * (1 + top - z)

        @pl.when((jd >= 0) & (jd <= last))
        def _():
            s = jd % RING
            held = jd % (2 * RING)

            @pl.when(z < top)
            def _():
                down_copy(jd).wait_recv()
                zp[held, z] = zp[held, z] + dr[s, 0]

            @pl.when(z > 0)
            def _():
                @pl.when(jd >= RING)
                def _():
                    down_copy(jd).wait_send()

                for m in range(top):
                    own = zp[held, jnp.maximum(z - 1 - m, 0)]
                    if m + 1 < top:
                        own = own + dr[s, m + 1]
                    ds_[s, m] = own
                down_copy(jd).start()

        jf = t - LAG * (1 + top)

        @pl.when((jf >= 0) & (jf <= last))
        def _():
            fs[jf % RING] = zp[jf % (2 * RING), z]
            f_copy(jf).start()

        jo = jf - LAG

        @pl.when((jo >= 0) & (jo <= last))
        def _():
            f_copy(jo).wait()
            s = jo % RING
            o = jo % 2

            @pl.when(jo >= 2)
            def _():
                out_copy(jo).wait()

            stage[o, :SUB] = fs[s, :SUB] + fr[s, :SUB]
            mine, other = fs[s, SUB:].astype(F32), fr[s, SUB:].astype(F32)
            stage[o, SUB:tall] = jnp.where(y == 0, mine, other).astype(BF)
            stage[o, tall:] = jnp.where(y == 0, other, mine).astype(BF)
            out_copy(jo).start()

    lax.fori_loop(0, last + LAG * (top + 2) + 1, step, None)
    for j in (last - 1, last):
        out_copy(j).wait()
    for back in range(RING):
        j = last - back

        @pl.when(z < top)
        def _(j=j):
            up_copy(j).wait_send()

        @pl.when(z > 0)
        def _(j=j):
            down_copy(j).wait_send()


def sum_over_chips(pairs, lines, collective_id):
    jobs = []
    lefts, rights = [], []
    for left, right in pairs:
        rows = left.shape[0] // (2 * lines)
        subs, strips = rows // SUB, right.shape[1] // STRIP
        jobs.append((subs, strips, subs * strips))
        lefts.append(left.reshape(2 * lines, rows, left.shape[1]))
        rights.append(right)
    steps = sum(job[2] for job in jobs)
    tokens = pairs[0][0].shape[1]
    half, quarter = STRIP // 2, SUB // 2
    tall = SUB + quarter
    top = lines - 1
    dma = pltpu.SemaphoreType.DMA
    scratch = [
        pltpu.VMEM((2, 2 * lines, SUB, tokens), BF),
        pltpu.VMEM((2, tokens, STRIP), BF),
        pltpu.VMEM((RING, 2, lines, tall, half), BF),
        pltpu.VMEM((RING, lines, tall, half), BF),
        pltpu.VMEM((RING, 2, 2, lines, quarter, half), BF),
        pltpu.VMEM((RING, 2, lines, quarter, half), BF),
        pltpu.VMEM((2 * RING, lines, tall, half), BF),
        pltpu.VMEM((RING, top, tall, half), BF),
        pltpu.VMEM((RING, top, tall, half), BF),
        pltpu.VMEM((RING, top, tall, half), BF),
        pltpu.VMEM((RING, top, tall, half), BF),
        pltpu.VMEM((RING, tall, half), BF),
        pltpu.VMEM((RING, tall, half), BF),
        pltpu.VMEM((2, 2 * SUB, half), BF),
        dma((2,)), dma((2,)),
        dma((RING,)), dma((RING,)), dma((RING,)), dma((RING,)),
        dma((RING,)), dma((RING,)), dma((RING,)), dma((RING,)),
        dma((RING,)), dma((RING,)),
        dma((2,)),
    ]
    flops = 2 * steps * 2 * lines * SUB * STRIP * tokens
    out = pl.pallas_call(
        functools.partial(sum_kernel, jobs, lines),
        out_shape=jax.ShapeDtypeStruct((steps + LAG, 2 * SUB, half), BF),
        in_specs=[pl.BlockSpec(memory_space=pl.ANY)] * (2 * len(pairs)),
        out_specs=pl.BlockSpec(memory_space=pl.ANY),
        scratch_shapes=scratch,
        compiler_params=pltpu.CompilerParams(collective_id=collective_id, has_side_effects=True,
                                             vmem_limit_bytes=VMEM_LIMIT),
        cost_estimate=pl.CostEstimate(flops=flops, bytes_accessed=steps * 800_000, transcendentals=0),
        name="sum_over_chips",
    )(*lefts, *rights)
    results = []
    begin = 0
    for (subs, strips, total) in jobs:
        one = out[begin:begin + total, :SUB].reshape(strips, subs * SUB, half)
        two = out[begin + LAG:begin + total + LAG, SUB:].reshape(strips, subs * SUB, half)
        both = jnp.concatenate([one, two], axis=2)
        results.append(both.transpose(1, 0, 2).reshape(subs * SUB, strips * STRIP))
        begin += total
    return results


MESH = pl.DeviceIdType.MESH


def call_plain(kernel, outs, args, smem=0, scratch=(), flops=0, moved=0, name=None):
    specs = [pl.BlockSpec(memory_space=pltpu.SMEM)] * smem + vmem_specs(len(args) - smem)
    many = isinstance(outs, (tuple, list))
    return pl.pallas_call(
        kernel,
        out_shape=tuple(outs) if many else outs,
        in_specs=specs,
        out_specs=tuple(vmem_specs(len(outs))) if many else vmem_specs(1)[0],
        scratch_shapes=list(scratch),
        compiler_params=pltpu.CompilerParams(vmem_limit_bytes=VMEM_LIMIT),
        cost_estimate=pl.CostEstimate(flops=flops, bytes_accessed=moved, transcendentals=0),
        name=name,
    )(*args)


def shape_of(shape, kind):
    return jax.ShapeDtypeStruct(shape, kind)


def sibling(value):
    count = lax.axis_size("ctx")
    return lax.ppermute(value, "ctx", [(i, i ^ 1) for i in range(count)])


def halves(value, core):
    width = value.shape[1] // 2
    mine = lax.dynamic_slice_in_dim(value, core * width, width, 1)
    send = lax.dynamic_slice_in_dim(value, (1 - core) * width, width, 1)
    return mine, send


def left_side(value):
    return jnp.concatenate([value, sibling(value)], axis=0).T


def right_side(values, core):
    mine, send = zip(*[halves(value, core) for value in values])
    mine, send = (jnp.concatenate(part, axis=1) for part in (mine, send))
    return jnp.concatenate([mine, sibling(send)], axis=0)


def silu_parts(gate_act, lift_act, inner_grad):
    sigma = jax.nn.sigmoid(gate_act)
    gate_grad = inner_grad * lift_act * sigma * (1 + gate_act * (1 - sigma))
    return gate_grad.astype(BF), (inner_grad * gate_act * sigma).astype(BF)


def norm_back(grad, hidden, gain):
    scale = lax.rsqrt(jnp.mean(hidden * hidden, axis=-1, keepdims=True) + EPS)
    unit = hidden * scale
    inward = grad * gain
    gain_grad = jnp.sum(grad * unit, axis=0)
    return scale * (inward - unit * jnp.mean(inward * unit, axis=-1, keepdims=True)), gain_grad


def feed_fwd(hidden, gain, gate_weight, lift_weight, drop_weight):
    fnormed = root_mean_square_scale(hidden, gain).astype(BF)
    gate_act = jnp.dot(fnormed, gate_weight, preferred_element_type=F32)
    lift_act = jnp.dot(fnormed, lift_weight, preferred_element_type=F32)
    inner = (jax.nn.silu(gate_act) * lift_act).astype(BF)
    result = hidden + jnp.dot(inner, drop_weight, preferred_element_type=F32)
    return result, (fnormed, gate_act.astype(BF), lift_act.astype(BF), inner)


def feed_bwd(grad, hidden, gain, kept, gate_weight, lift_weight, drop_weight):
    fnormed, gate_act, lift_act, inner = kept
    grad_low = grad.astype(BF)
    inner_grad = outer_dot(grad_low, drop_weight)
    gate_low, lift_low = silu_parts(gate_act.astype(F32), lift_act.astype(F32), inner_grad)
    normed_grad = outer_dot(gate_low, gate_weight) + outer_dot(lift_low, lift_weight)
    hidden_grad, gain_grad = norm_back(normed_grad, hidden, gain)
    return grad + hidden_grad, gain_grad, grad_low, gate_low, lift_low


def fast_device(tokens, lengths, cotangent, mixgain, mixentry, mixtaps, mixexit, lowgain, lowgate, lowlift,
                lowdrop, attgain, attquery, attkeys, attvalues, querygain, keysgain, attexit, topgain, topgate,
                toplift, topdrop):
    rows, width = tokens.shape
    head = querygain.shape[0]
    devices = lax.axis_size("ctx")
    lines = devices // 4
    half_rows = rows // 2
    group = devices * rows
    place = lax.axis_index("ctx")
    core = place % 2
    first = lengths[0, 0]
    second = first + lengths[0, 1]
    mine = place * rows + jnp.arange(rows, dtype=jnp.int32)
    my_seg = segment_of(mine, first, second)
    begin = jnp.where(my_seg == 0, 0, jnp.where(my_seg == 1, first, second))
    position = (mine - begin).astype(F32)
    gains = [value.astype(F32) for value in (mixgain, lowgain, attgain, topgain)]
    mixgain_f, lowgain_f, attgain_f, topgain_f = gains
    taps_f = mixtaps.astype(F32)
    twice = lambda gain: jnp.tile(gain.astype(F32), LANES // head)[None, :]
    querygain_2, keysgain_2 = twice(querygain), twice(keysgain)
    spot = jnp.arange(LANES, dtype=jnp.int32) % (head // 2)
    angle = position[:, None] * (THETA ** (-spot.astype(F32) * 2.0 / head))[None, :]
    cosine = jnp.cos(angle)
    sine = jnp.sin(angle) * jnp.where(jnp.arange(LANES) % head < head // 2, -1.0, 1.0)[None, :]
    info = jnp.stack([first, second, core, core]).astype(jnp.int32)

    hidden = tokens.astype(F32)
    normed_one = root_mean_square_scale(hidden, mixgain_f).astype(BF)
    mixed = jnp.dot(normed_one, mixentry, preferred_element_type=F32)
    part_b, part_c, part_x = (mixed[:, i * width:(i + 1) * width] for i in range(3))
    product = (part_b * part_x).astype(BF)
    borrowed = passed_along(product[rows - 2:], "ctx", 1)
    extended = jnp.concatenate([borrowed, product], axis=0).astype(F32)
    fits_one = ((mine >= 1) & (segment_of(mine - 1, first, second) == my_seg)).astype(F32)[:, None]
    fits_two = ((mine >= 2) & (segment_of(mine - 2, first, second) == my_seg)).astype(F32)[:, None]
    conved = conv_local(extended, taps_f, fits_one, fits_two)
    gated = (part_c * conved).astype(BF)
    hidden_one = hidden + jnp.dot(gated, mixexit, preferred_element_type=F32)
    hidden_two, kept_low = feed_fwd(hidden_one, lowgain_f, lowgate, lowlift, lowdrop)

    heads_q, heads_k = attquery.shape[1] // head, attkeys.shape[1] // head
    msg, normed_two, query_raw, key_raw = call_plain(
        functools.partial(project_kernel, head),
        (shape_of((devices, half_rows, 2 * LANES), BF), shape_of((rows, width), BF),
         shape_of((rows, attquery.shape[1]), F32), shape_of((rows, attkeys.shape[1]), F32)),
        (hidden_two, attgain_f[None, :], attquery, attkeys, attvalues, cosine, sine, querygain_2, keysgain_2),
        flops=2 * rows * width * 2 * width, moved=6 << 20, name="project")
    held = lax.all_to_all(msg, "ctx", 0, 0)
    held_kv = held[:, :, LANES:]
    other_kv = sibling(held_kv)
    pair = jnp.where(core == 0, jnp.stack([held_kv, other_kv], axis=1), jnp.stack([other_kv, held_kv], axis=1))
    all_kv = pair.reshape(group, LANES)
    keys, sources = 512, 2
    wide = sources * rows
    area = group * group // 2 // 2 * 2
    attended_f, augmented = call_plain(
        functools.partial(attend_kernel, head, rows, keys, sources),
        (shape_of((devices, half_rows, LANES), F32), shape_of((devices, 2, half_rows, LANES), BF)),
        (info, held, all_kv), smem=1,
        scratch=[pltpu.VMEM((group, LANES), BF), pltpu.VMEM((wide, LANES), F32)],
        flops=4 * area * LANES, moved=5 << 20, name="attend")
    got = lax.all_to_all(attended_f.astype(BF), "ctx", 0, 0)
    attended_low = got.reshape(devices // 2, rows, LANES).transpose(1, 0, 2).reshape(rows, width)
    hidden_three = hidden_two + jnp.dot(attended_low, attexit, preferred_element_type=F32)
    output, kept_top = feed_fwd(hidden_three, topgain_f, topgate, toplift, topdrop)

    grad = cotangent.astype(F32)
    grad, topgain_grad, gb_top, gate_top, lift_top = feed_bwd(
        grad, hidden_three, topgain_f, kept_top, topgate, toplift, topdrop)
    grad_low3 = grad.astype(BF)
    dattn = outer_dot(grad_low3, attexit).astype(BF)
    send = dattn.reshape(2, half_rows, devices // 2, LANES).transpose(2, 0, 1, 3).reshape(devices, half_rows, LANES)
    held_grad = lax.all_to_all(send, "ctx", 0, 0)
    dq, dkv = call_plain(
        functools.partial(attend_back_kernel, head, rows, keys, sources),
        (shape_of((devices, half_rows, LANES), BF), shape_of((group, LANES), BF)),
        (info, augmented, attended_f, held_grad, all_kv), smem=1,
        scratch=[pltpu.VMEM((group, LANES), BF), pltpu.VMEM((group, LANES), BF),
                 pltpu.VMEM((group, LANES), F32), pltpu.VMEM((group, LANES), F32), pltpu.VMEM((wide, LANES), F32)],
        flops=10 * area * LANES, moved=8 << 20, name="attend_back")
    dkv = dkv.reshape(devices, 2, half_rows, LANES)
    mine_kv = lax.dynamic_index_in_dim(dkv, core, 1, keepdims=False)
    send_kv = lax.dynamic_index_in_dim(dkv, 1 - core, 1, keepdims=False)
    dkv_sum = (mine_kv.astype(F32) + sibling(send_kv).astype(F32)).astype(BF)
    back = lax.all_to_all(jnp.concatenate([dq, dkv_sum], axis=2), "ctx", 0, 0)
    raw_low, grad_two, attgain_grad, querygain_grad, keysgain_grad = call_plain(
        functools.partial(project_back_kernel, head),
        (shape_of((rows, 2 * width), BF), shape_of((rows, width), F32), shape_of((1, width), F32),
         shape_of((1, LANES), F32), shape_of((1, LANES), F32)),
        (back, hidden_two, attgain_f[None, :], attquery, attkeys, attvalues, cosine, sine, querygain_2, keysgain_2,
         query_raw, key_raw, grad),
        flops=2 * rows * width * 2 * width, moved=8 << 20, name="project_back")
    fold = lambda value: value.reshape(LANES // head, head).sum(axis=0)
    querygain_grad, keysgain_grad = fold(querygain_grad), fold(keysgain_grad)
    grad, lowgain_grad, gb_low, gate_low, lift_low = feed_bwd(
        grad_two, hidden_one, lowgain_f, kept_low, lowgate, lowlift, lowdrop)
    grad_low1 = grad.astype(BF)
    gated_grad = outer_dot(grad_low1, mixexit)
    part_c_grad = gated_grad * conved
    conved_grad = gated_grad * part_c
    _, pull_conv = jax.vjp(lambda ext, taps: conv_local(ext, taps, fits_one, fits_two), extended, taps_f)
    extended_grad, mixtaps_grad = pull_conv(conved_grad)
    returned_rim = passed_along(extended_grad[:2], "ctx", -1)
    product_grad = extended_grad[2:].at[rows - 2:].add(returned_rim)
    mixed_grad = jnp.concatenate(
        [product_grad * part_x, part_c_grad, product_grad * part_b], axis=1).astype(BF)
    hidden_grad, mixgain_grad = norm_back(outer_dot(mixed_grad, mixentry), hidden, mixgain_f)
    tokens_grad = grad + hidden_grad

    kq, kk = attquery.shape[1], attkeys.shape[1]
    pairs = [
        (left_side(kept_top[3]), right_side([gb_top], core)),
        (left_side(kept_top[0]), right_side([gate_top, lift_top], core)),
        (left_side(attended_low), right_side([grad_low3], core)),
        (left_side(normed_two), right_side([raw_low[:, :kq], raw_low[:, kq:kq + kk], raw_low[:, kq + kk:]], core)),
        (left_side(kept_low[3]), right_side([gb_low], core)),
        (left_side(kept_low[0]), right_side([gate_low, lift_low], core)),
        (left_side(gated), right_side([grad_low1], core)),
        (left_side(normed_one), right_side([mixed_grad], core)),
    ]
    sums = sum_over_chips(pairs, lines, 1)

    def finish(value, cuts):
        size = value.shape[0] // 2
        own = lax.dynamic_slice_in_dim(value, core * size, size, 0)
        away = sibling(lax.dynamic_slice_in_dim(value, (1 - core) * size, size, 0))
        results, start = [], 0
        for cut in cuts:
            a, b = own[:, start:start + cut], away[:, start:start + cut]
            results.append(jnp.where(core == 0, jnp.concatenate([a, b], axis=1),
                                     jnp.concatenate([b, a], axis=1)).astype(F32))
            start += cut
        return results

    ff = lowgate.shape[1]
    (topdrop_grad,) = finish(sums[0], [width // 2])
    topgate_grad, toplift_grad = finish(sums[1], [ff // 2, ff // 2])
    (attexit_grad,) = finish(sums[2], [width // 2])
    attquery_grad, attkeys_grad, attvalues_grad = finish(sums[3], [kq // 2, kk // 2, kk // 2])
    (lowdrop_grad,) = finish(sums[4], [width // 2])
    lowgate_grad, lowlift_grad = finish(sums[5], [ff // 2, ff // 2])
    (mixexit_grad,) = finish(sums[6], [width // 2])
    (mixentry_grad,) = finish(sums[7], [mixentry.shape[1] // 2])
    smalls = lax.psum((mixgain_grad, mixtaps_grad, lowgain_grad, attgain_grad[0], querygain_grad, keysgain_grad,
                       topgain_grad), ("dp", "ctx"))
    return (output, tokens_grad, smalls[0], mixentry_grad, smalls[1], mixexit_grad, smalls[2], lowgate_grad,
            lowlift_grad, lowdrop_grad, smalls[3], attquery_grad, attkeys_grad, attvalues_grad, smalls[4],
            smalls[5], attexit_grad, smalls[6], topgate_grad, toplift_grad, topdrop_grad)


def solution(mesh):
    placed = (P(("dp", "ctx"), None), P("dp", None), P(("dp", "ctx"), None)) + (P(),) * 19
    split = {0: P(("dp", "ctx"), None), 1: P(("dp", "ctx"), None)}
    whole = (2, 4, 6, 10, 14, 15, 17)
    outs = tuple(split.get(i, P() if i in whole else P("ctx", None)) for i in range(21))
    small = mesh.shape["ctx"] == 16 and mesh.shape["dp"] == 2
    return jax.shard_map(fast_device if small else per_device, mesh=mesh, in_specs=placed, out_specs=outs,
                         check_vma=False)
```

```python
import functools
import math

import jax
import jax.numpy as jnp
from jax import lax
from jax.experimental import pallas as pl
from jax.experimental.pallas import tpu as pltpu
from jax.sharding import PartitionSpec as P

EPS = 1e-05
THETA = 1000000.0
NEGATIVE = -1e30


def passed_along(value, axis, steps):
    count = lax.axis_size(axis)
    first, last = (max(0, -steps), min(count, count - steps))
    return lax.ppermute(value, axis, [(source, source + steps) for source in range(first, last)])


def passed_along_2(block, axis, distance):
    devices = range(lax.axis_size(axis))
    route = [((i - distance) % len(devices), i) for i in devices]
    return lax.ppermute(block, axis, route)


def root_mean_square_scale(hidden, gain):
    return hidden * lax.rsqrt(jnp.mean(hidden * hidden, axis=-1, keepdims=True) + EPS) * gain


def rotary_embed(value_rows, position_index):
    half = value_rows.shape[-1] // 2
    freq = THETA ** (-jnp.arange(half, dtype=jnp.float32) * 2.0 / value_rows.shape[-1])
    angle = position_index.astype(jnp.float32)[:, None] * freq[None, :]
    cosine = jnp.cos(angle)[:, None, :]
    sine = jnp.sin(angle)[:, None, :]
    front = value_rows[..., :half]
    behind = value_rows[..., half:]
    return jnp.concatenate(
        [front * cosine - behind * sine, behind * cosine + front * sine], axis=-1
    )


def head_prep(raw, gain, position_index, heads):
    shaped = raw.reshape(raw.shape[0], heads, -1)
    return rotary_embed(root_mean_square_scale(shaped, gain), position_index)


def segment_of(where, first, second):
    return (where >= first).astype(jnp.int32) + (where >= second).astype(jnp.int32)


def block_width(count):
    best = 1
    for candidate in range(1, min(count, 1024) + 1):
        if count % candidate == 0:
            best = candidate
    return best


def sweep(carry, count, visit):
    width = block_width(count)
    return lax.fori_loop(
        0, count // width, lambda index, inner: visit(inner, index * width, width), carry
    )


def inner_dot(left, right):
    return lax.dot_general(
        left, right, (((0,), (0,)), ((), ())), preferred_element_type=jnp.float32
    )


def outer_dot(left, right):
    return lax.dot_general(
        left, right, (((1,), (1,)), ((), ())), preferred_element_type=jnp.float32
    )


def scores_of(query_part, key_part, query_where, key_where, query_seg, key_seg, scale):
    raw = (
        jnp.einsum("tkgd,pkd->kgtp", query_part, key_part, preferred_element_type=jnp.float32)
        * scale
    )
    allowed = (query_seg[:, None] == key_seg[None, :]) & (
        query_where[:, None] >= key_where[None, :]
    )
    return (raw, allowed)


def grad_block(
    query_part,
    grad_part,
    logsum_part,
    delta_part,
    key_part,
    value_part,
    query_where,
    key_where,
    query_seg,
    key_seg,
    scale,
):
    raw, allowed = scores_of(
        query_part, key_part, query_where, key_where, query_seg, key_seg, scale
    )
    prob = jnp.where(allowed, jnp.exp(raw - logsum_part[..., None]), 0.0)
    prob_grad = jnp.einsum(
        "tkgd,pkd->kgtp", grad_part, value_part, preferred_element_type=jnp.float32
    )
    score_grad = (prob * (prob_grad - delta_part[..., None])).astype(jnp.bfloat16)
    query_grad = (
        jnp.einsum("kgtp,pkd->tkgd", score_grad, key_part, preferred_element_type=jnp.float32)
        * scale
    )
    key_grad = (
        jnp.einsum("kgtp,tkgd->pkd", score_grad, query_part, preferred_element_type=jnp.float32)
        * scale
    )
    value_grad = jnp.einsum(
        "kgtp,tkgd->pkd", prob.astype(jnp.bfloat16), grad_part, preferred_element_type=jnp.float32
    )
    return (query_grad, key_grad, value_grad)


def conv_local(extended, taps, fits_one, fits_two):
    rows = extended.shape[0] - 2
    return (
        taps[2] * extended[2:]
        + taps[1] * extended[1 : rows + 1] * fits_one
        + taps[0] * extended[:rows] * fits_two
    )


def feed_forward(hidden, gain, gate_weight, lift_weight, drop_weight):
    fnormed = root_mean_square_scale(hidden, gain).astype(jnp.bfloat16)
    gate_act = jnp.dot(fnormed, gate_weight, preferred_element_type=jnp.float32)
    lift_act = jnp.dot(fnormed, lift_weight, preferred_element_type=jnp.float32)
    inner = (jax.nn.silu(gate_act) * lift_act).astype(jnp.bfloat16)
    result = hidden + jnp.dot(inner, drop_weight, preferred_element_type=jnp.float32)
    return (result, (fnormed, gate_act, lift_act, inner))


def feed_back(grad, hidden, gain, kept, gate_weight, lift_weight, drop_weight):
    fnormed, gate_act, lift_act, inner = kept
    grad_low = grad.astype(jnp.bfloat16)
    drop_grad = inner_dot(inner, grad_low)
    inner_grad = outer_dot(grad_low, drop_weight)
    _, pull_gate = jax.vjp(
        lambda gate_in, lift_in: jax.nn.silu(gate_in) * lift_in, gate_act, lift_act
    )
    gate_grad, lift_grad = pull_gate(inner_grad)
    gate_low = gate_grad.astype(jnp.bfloat16)
    lift_low = lift_grad.astype(jnp.bfloat16)
    gate_wgrad = inner_dot(fnormed, gate_low)
    lift_wgrad = inner_dot(fnormed, lift_low)
    normed_grad = outer_dot(gate_low, gate_weight) + outer_dot(lift_low, lift_weight)
    _, pull_norm = jax.vjp(root_mean_square_scale, hidden, gain)
    hidden_grad, gain_grad = pull_norm(normed_grad)
    return (grad + hidden_grad, (gain_grad, gate_wgrad, lift_wgrad, drop_grad))


def per_device(
    tokens,
    lengths,
    cotangent,
    mixgain,
    mixentry,
    mixtaps,
    mixexit,
    lowgain,
    lowgate,
    lowlift,
    lowdrop,
    attgain,
    attquery,
    attkeys,
    attvalues,
    querygain,
    keysgain,
    attexit,
    topgain,
    topgate,
    toplift,
    topdrop,
):
    rows = tokens.shape[0]
    width_model = tokens.shape[1]
    head_size = querygain.shape[0]
    query_heads = attquery.shape[1] // head_size
    kv_heads = attkeys.shape[1] // head_size
    shared_gradient = query_heads // kv_heads
    scale = 1.0 / math.sqrt(head_size)
    place = lax.axis_index("ctx")
    first = lengths[0, 0]
    second = first + lengths[0, 1]
    mine = place * rows + jnp.arange(rows, dtype=jnp.int32)
    my_seg = segment_of(mine, first, second)
    begin = jnp.where(my_seg == 0, 0, jnp.where(my_seg == 1, first, second))
    position_index = mine - begin
    last_row = place * rows + rows - 1
    mixgain_f = mixgain.astype(jnp.float32)
    taps_f = mixtaps.astype(jnp.float32)
    lowgain_f = lowgain.astype(jnp.float32)
    attgain_f = attgain.astype(jnp.float32)
    querygain_f = querygain.astype(jnp.float32)
    keysgain_f = keysgain.astype(jnp.float32)
    topgain_f = topgain.astype(jnp.float32)
    hidden = tokens.astype(jnp.float32)
    normed_one = root_mean_square_scale(hidden, mixgain_f).astype(jnp.bfloat16)
    mixed = jnp.dot(normed_one, mixentry, preferred_element_type=jnp.float32)
    part_b = mixed[:, :width_model]
    part_c = mixed[:, width_model : 2 * width_model]
    part_x = mixed[:, 2 * width_model :]
    product = (part_b * part_x).astype(jnp.bfloat16)
    borrowed = passed_along(product[rows - 2 :], "ctx", 1)
    extended = jnp.concatenate([borrowed, product], axis=0).astype(jnp.float32)
    fits_one = ((mine >= 1) & (segment_of(mine - 1, first, second) == my_seg)).astype(jnp.float32)[
        :, None
    ]
    fits_two = ((mine >= 2) & (segment_of(mine - 2, first, second) == my_seg)).astype(jnp.float32)[
        :, None
    ]
    conved = conv_local(extended, taps_f, fits_one, fits_two)
    gated = (part_c * conved).astype(jnp.bfloat16)
    hidden_one = hidden + jnp.dot(gated, mixexit, preferred_element_type=jnp.float32)
    hidden_two, kept_low = feed_forward(hidden_one, lowgain_f, lowgate, lowlift, lowdrop)
    normed_two = root_mean_square_scale(hidden_two, attgain_f).astype(jnp.bfloat16)
    query_unrotated = jnp.dot(normed_two, attquery, preferred_element_type=jnp.float32)
    key_unrotated = jnp.dot(normed_two, attkeys, preferred_element_type=jnp.float32)
    value_projected = jnp.dot(normed_two, attvalues, preferred_element_type=jnp.float32)
    query_low = head_prep(query_unrotated, querygain_f, position_index, query_heads).astype(
        jnp.bfloat16
    )
    key_low = head_prep(key_unrotated, keysgain_f, position_index, kv_heads).astype(jnp.bfloat16)
    value_low = value_projected.astype(jnp.bfloat16).reshape(rows, kv_heads, head_size)
    query_grouped = query_low.reshape(rows, kv_heads, shared_gradient, head_size)

    def stat_visit(carry, keys_in, start, offset, width):
        top, total = carry
        key_part = lax.dynamic_slice_in_dim(keys_in, offset, width, 0)
        key_where = start + offset + jnp.arange(width, dtype=jnp.int32)
        raw, allowed = scores_of(
            query_grouped,
            key_part,
            mine,
            key_where,
            my_seg,
            segment_of(key_where, first, second),
            scale,
        )
        new_top = jnp.maximum(top, jnp.max(jnp.where(allowed, raw, NEGATIVE), axis=-1))
        weights = jnp.where(allowed, jnp.exp(raw - new_top[..., None]), 0.0)
        total = total * jnp.exp(top - new_top) + jnp.sum(weights, axis=-1)
        return (new_top, total)

    stat_state = (
        jnp.full((kv_heads, shared_gradient, rows), NEGATIVE, jnp.float32),
        jnp.zeros((kv_heads, shared_gradient, rows), jnp.float32),
    )
    piece = lax.all_gather(key_low, "ctx", axis=0, tiled=True)
    start = jnp.int32(0)
    count = piece.shape[0]

    def stat_running(inner):
        return sweep(
            inner, count, lambda acc, offset, width: stat_visit(acc, piece, start, offset, width)
        )

    top, total = lax.cond(start > last_row, lambda inner: inner, stat_running, stat_state)
    logsum = top + jnp.log(total)

    def forward_visit(accum, keys_in, values_in, start, offset, width):
        key_part = lax.dynamic_slice_in_dim(keys_in, offset, width, 0)
        value_part = lax.dynamic_slice_in_dim(values_in, offset, width, 0)
        key_where = start + offset + jnp.arange(width, dtype=jnp.int32)
        raw, allowed = scores_of(
            query_grouped,
            key_part,
            mine,
            key_where,
            my_seg,
            segment_of(key_where, first, second),
            scale,
        )
        prob_low = jnp.where(allowed, jnp.exp(raw - logsum[..., None]), 0.0).astype(jnp.bfloat16)
        return accum + jnp.einsum(
            "kgtp,pkd->kgtd", prob_low, value_part, preferred_element_type=jnp.float32
        )

    forward_start = jnp.int32(0)
    keys_in = lax.all_gather(key_low, "ctx", axis=0, tiled=True)
    values_in = lax.all_gather(value_low, "ctx", axis=0, tiled=True)
    forward_count = keys_in.shape[0]

    def forward_running(inner):
        return sweep(
            inner,
            forward_count,
            lambda acc, offset, width: forward_visit(
                acc, keys_in, values_in, forward_start, offset, width
            ),
        )

    accum = lax.cond(
        forward_start > last_row,
        lambda inner: inner,
        forward_running,
        jnp.zeros((kv_heads, shared_gradient, rows, head_size), jnp.float32),
    )
    attended = accum.transpose(2, 0, 1, 3).reshape(rows, -1)
    attended_low = attended.astype(jnp.bfloat16)
    hidden_three = hidden_two + jnp.dot(attended_low, attexit, preferred_element_type=jnp.float32)
    output, kept_top = feed_forward(hidden_three, topgain_f, topgate, toplift, topdrop)
    grad = cotangent.astype(jnp.float32)
    grad, top_grads = feed_back(grad, hidden_three, topgain_f, kept_top, topgate, toplift, topdrop)
    grad_low = grad.astype(jnp.bfloat16)
    attexit_grad = inner_dot(attended_low, grad_low)
    out_grads = (
        outer_dot(grad_low, attexit)
        .astype(jnp.bfloat16)
        .reshape(rows, kv_heads, shared_gradient, head_size)
    )
    delta = jnp.einsum(
        "tkgd,tkgd->kgt",
        out_grads.astype(jnp.float32),
        attended.reshape(rows, kv_heads, shared_gradient, head_size),
    )
    cycle_size = lax.axis_size("ctx")

    def cycle_visit(state, keys_in, values_in, start, offset, width):
        query_acc, key_acc, value_acc = state
        key_part = lax.dynamic_slice_in_dim(keys_in, offset, width, 0)
        value_part = lax.dynamic_slice_in_dim(values_in, offset, width, 0)
        key_where = start + offset + jnp.arange(width, dtype=jnp.int32)
        query_grad, key_grad, value_grad = grad_block(
            query_grouped,
            out_grads,
            logsum,
            delta,
            key_part,
            value_part,
            mine,
            key_where,
            my_seg,
            segment_of(key_where, first, second),
            scale,
        )
        key_acc = lax.dynamic_update_slice_in_dim(
            key_acc, lax.dynamic_slice_in_dim(key_acc, offset, width, 0) + key_grad, offset, 0
        )
        value_acc = lax.dynamic_update_slice_in_dim(
            value_acc, lax.dynamic_slice_in_dim(value_acc, offset, width, 0) + value_grad, offset, 0
        )
        return (query_acc + query_grad, key_acc, value_acc)

    def cycle_step(step, carry):
        keys_cur, values_cur, key_acc, value_acc, query_acc = carry
        anchor = (place - step + cycle_size) % cycle_size
        start = anchor * rows

        def cycle_running(state):
            return sweep(
                state,
                rows,
                lambda acc, offset, width: cycle_visit(
                    acc, keys_cur, values_cur, start, offset, width
                ),
            )

        query_acc, key_acc, value_acc = lax.cond(
            start > last_row, lambda state: state, cycle_running, (query_acc, key_acc, value_acc)
        )
        keys_cur, values_cur = passed_along((keys_cur, values_cur), "ctx", 1)
        key_acc, value_acc = (
            passed_along_2(key_acc.astype(jnp.bfloat16), "ctx", 1).astype(key_acc.dtype),
            passed_along_2(value_acc.astype(jnp.bfloat16), "ctx", 1).astype(value_acc.dtype),
        )
        return (keys_cur, values_cur, key_acc, value_acc, query_acc)

    cycle_state = (
        key_low,
        value_low,
        jnp.zeros((rows, kv_heads, head_size), jnp.float32),
        jnp.zeros((rows, kv_heads, head_size), jnp.float32),
        jnp.zeros((rows, kv_heads, shared_gradient, head_size), jnp.float32),
    )
    _, _, key_grads, value_grads, query_acc = lax.fori_loop(0, cycle_size, cycle_step, cycle_state)
    _, pull_query = jax.vjp(
        lambda raw, gain: head_prep(raw, gain, position_index, query_heads),
        query_unrotated,
        querygain_f,
    )
    query_raw_grad, querygain_grad = pull_query(query_acc.reshape(rows, query_heads, head_size))
    _, pull_key = jax.vjp(
        lambda raw, gain: head_prep(raw, gain, position_index, kv_heads), key_unrotated, keysgain_f
    )
    key_raw_grad, keysgain_grad = pull_key(key_grads)
    query_raw_low = query_raw_grad.astype(jnp.bfloat16)
    key_raw_low = key_raw_grad.astype(jnp.bfloat16)
    value_raw_low = value_grads.reshape(rows, -1).astype(jnp.bfloat16)
    attquery_grad = inner_dot(normed_two, query_raw_low)
    attkeys_grad = inner_dot(normed_two, key_raw_low)
    attvalues_grad = inner_dot(normed_two, value_raw_low)
    normed_two_grad = (
        outer_dot(query_raw_low, attquery)
        + outer_dot(key_raw_low, attkeys)
        + outer_dot(value_raw_low, attvalues)
    )
    _, pull_att = jax.vjp(root_mean_square_scale, hidden_two, attgain_f)
    hidden_two_grad, attgain_grad = pull_att(normed_two_grad)
    grad = grad + hidden_two_grad
    grad, low_grads = feed_back(grad, hidden_one, lowgain_f, kept_low, lowgate, lowlift, lowdrop)
    grad_low = grad.astype(jnp.bfloat16)
    mixexit_grad = inner_dot(gated, grad_low)
    gated_grad = outer_dot(grad_low, mixexit)
    part_c_grad = gated_grad * conved
    conved_grad = gated_grad * part_c
    _, pull_conv = jax.vjp(
        lambda ext, taps: conv_local(ext, taps, fits_one, fits_two), extended, taps_f
    )
    extended_grad, mixtaps_grad = pull_conv(conved_grad)
    returned_rim = passed_along(extended_grad[:2], "ctx", -1)
    product_grad = extended_grad[2:].at[rows - 2 :].add(returned_rim)
    mixed_grad = jnp.concatenate(
        [product_grad * part_x, part_c_grad, product_grad * part_b], axis=1
    ).astype(jnp.bfloat16)
    mixentry_grad = inner_dot(normed_one, mixed_grad)
    normed_one_grad = outer_dot(mixed_grad, mixentry)
    _, pull_mix = jax.vjp(root_mean_square_scale, hidden, mixgain_f)
    hidden_grad, mixgain_grad = pull_mix(normed_one_grad)
    tokens_grad = grad + hidden_grad
    lowgain_grad, lowgate_grad, lowlift_grad, lowdrop_grad = low_grads
    topgain_grad, topgate_grad, toplift_grad, topdrop_grad = top_grads
    shares = (
        lax.psum_scatter(mixentry_grad, "ctx", scatter_dimension=0, tiled=True),
        lax.psum_scatter(mixexit_grad, "ctx", scatter_dimension=0, tiled=True),
        lax.psum_scatter(lowgate_grad, "ctx", scatter_dimension=0, tiled=True),
        lax.psum_scatter(lowlift_grad, "ctx", scatter_dimension=0, tiled=True),
        lax.psum_scatter(lowdrop_grad, "ctx", scatter_dimension=0, tiled=True),
        lax.psum_scatter(attquery_grad, "ctx", scatter_dimension=0, tiled=True),
        lax.psum_scatter(attkeys_grad, "ctx", scatter_dimension=0, tiled=True),
        lax.psum_scatter(attvalues_grad, "ctx", scatter_dimension=0, tiled=True),
        lax.psum_scatter(attexit_grad, "ctx", scatter_dimension=0, tiled=True),
        lax.psum_scatter(topgate_grad, "ctx", scatter_dimension=0, tiled=True),
        lax.psum_scatter(toplift_grad, "ctx", scatter_dimension=0, tiled=True),
        lax.psum_scatter(topdrop_grad, "ctx", scatter_dimension=0, tiled=True),
    )
    smalls = lax.psum(
        (
            mixgain_grad,
            mixtaps_grad,
            lowgain_grad,
            attgain_grad,
            querygain_grad,
            keysgain_grad,
            topgain_grad,
        ),
        "ctx",
    )
    summed = (
        lax.psum(shares[0].astype(jnp.bfloat16), "dp").astype(jnp.float32),
        lax.psum(shares[1].astype(jnp.bfloat16), "dp").astype(jnp.float32),
        lax.psum(shares[2].astype(jnp.bfloat16), "dp").astype(jnp.float32),
        lax.psum(shares[3].astype(jnp.bfloat16), "dp").astype(jnp.float32),
        lax.psum(shares[4].astype(jnp.bfloat16), "dp").astype(jnp.float32),
        lax.psum(shares[5].astype(jnp.bfloat16), "dp").astype(jnp.float32),
        lax.psum(shares[6].astype(jnp.bfloat16), "dp").astype(jnp.float32),
        lax.psum(shares[7].astype(jnp.bfloat16), "dp").astype(jnp.float32),
        lax.psum(shares[8].astype(jnp.bfloat16), "dp").astype(jnp.float32),
        lax.psum(shares[9].astype(jnp.bfloat16), "dp").astype(jnp.float32),
        lax.psum(shares[10].astype(jnp.bfloat16), "dp").astype(jnp.float32),
        lax.psum(shares[11].astype(jnp.bfloat16), "dp").astype(jnp.float32),
        lax.psum(smalls[0].astype(jnp.bfloat16), "dp").astype(jnp.float32),
        lax.psum(smalls[1].astype(jnp.bfloat16), "dp").astype(jnp.float32),
        lax.psum(smalls[2].astype(jnp.bfloat16), "dp").astype(jnp.float32),
        lax.psum(smalls[3].astype(jnp.bfloat16), "dp").astype(jnp.float32),
        lax.psum(smalls[4].astype(jnp.bfloat16), "dp").astype(jnp.float32),
        lax.psum(smalls[5].astype(jnp.bfloat16), "dp").astype(jnp.float32),
        lax.psum(smalls[6].astype(jnp.bfloat16), "dp").astype(jnp.float32),
    )
    return (
        output,
        tokens_grad,
        summed[12],
        summed[0],
        summed[13],
        summed[1],
        summed[14],
        summed[2],
        summed[3],
        summed[4],
        summed[15],
        summed[5],
        summed[6],
        summed[7],
        summed[16],
        summed[17],
        summed[8],
        summed[18],
        summed[9],
        summed[10],
        summed[11],
    )


LANES = 128
BF = jnp.bfloat16
F32 = jnp.float32
ONES_NT = (((1,), (1,)), ((), ()))
ONES_TN = (((0,), (0,)), ((), ()))
VMEM_LIMIT = 60 * 1024 * 1024


def vmem_specs(count):
    return [pl.BlockSpec(memory_space=pltpu.VMEM)] * count


def lane_of(shape):
    return lax.broadcasted_iota(jnp.int32, shape, len(shape) - 1)


def same_head(head):
    row = lax.broadcasted_iota(jnp.int32, (LANES, LANES), 0) // head
    column = lax.broadcasted_iota(jnp.int32, (LANES, LANES), 1) // head
    return jnp.where(row == column, 1.0 / head, 0.0).astype(F32)


def head_mean(value, blocks):
    return jnp.dot(value, blocks, precision=lax.Precision.HIGHEST, preferred_element_type=F32)


def other_half(value, head):
    lane = lane_of(value.shape)
    ahead = pltpu.roll(value, LANES - head // 2, 1)
    behind = pltpu.roll(value, head // 2, 1)
    return jnp.where(lane % head < head // 2, ahead, behind)


def swap_heads(value, head):
    return pltpu.roll(value, head, 1)


def three_parts(value):
    high = value.astype(BF)
    rest = value - high.astype(F32)
    middle = rest.astype(BF)
    low = (rest - middle.astype(F32)).astype(BF)
    return high.astype(F32), middle.astype(F32), low.astype(F32)


def project_kernel(head, hid_ref, gain_ref, wq_ref, wk_ref, wv_ref, cos_ref, sin_ref, qg_ref, kg_ref,
                   msg_ref, normt_ref, qraw_ref, kraw_ref):
    hid = hid_ref[...]
    scale = lax.rsqrt(jnp.mean(hid * hid, axis=-1, keepdims=True) + EPS)
    normed = hid * scale * gain_ref[...]
    normt_ref[...] = turned(normed)
    normed = normed.astype(BF)
    blocks = same_head(head)
    cosine, sine = cos_ref[...], sin_ref[...]
    half_rows = msg_ref.shape[1]
    lane = lane_of(cosine.shape)

    def prepared(raw, gain):
        unit = raw * lax.rsqrt(head_mean(raw * raw, blocks) + EPS) * gain
        return unit * cosine + other_half(unit, head) * sine

    def put(dest, start, tile):
        low = tile.astype(BF)
        for part in range(2):
            msg_ref[2 * dest + part, :, start:start + LANES] = low[part * half_rows:(part + 1) * half_rows]

    qraw = jnp.dot(normed, wq_ref[...], preferred_element_type=F32)
    qraw_ref[...] = qraw
    for tile in range(qraw.shape[1] // LANES):
        put(tile, 0, prepared(qraw[:, tile * LANES:(tile + 1) * LANES], qg_ref[...]))
    kraw = jnp.dot(normed, wk_ref[...], preferred_element_type=F32)
    kraw_ref[...] = kraw
    vraw = jnp.dot(normed, wv_ref[...], preferred_element_type=F32)
    for tile in range(kraw.shape[1] // LANES):
        keys = prepared(kraw[:, tile * LANES:(tile + 1) * LANES], kg_ref[...])
        values = vraw[:, tile * LANES:(tile + 1) * LANES]
        put(2 * tile, LANES, jnp.where(lane < head, keys, swap_heads(values, head)))
        put(2 * tile + 1, LANES, jnp.where(lane < head, swap_heads(keys, head), values))


def project_back_kernel(head, back_ref, hid_ref, gain_ref, wq_ref, wk_ref, wv_ref, cos_ref, sin_ref, qg_ref,
                        kg_ref, qraw_ref, kraw_ref, grad_ref,
                        rawq_ref, rawk_ref, rawv_ref, two_ref, again_ref, qgain_ref, kgain_ref):
    blocks = same_head(head)
    cosine, sine = cos_ref[...], sin_ref[...]
    half_rows = back_ref.shape[1]
    lane = lane_of(cosine.shape)

    def fetch(dest, start):
        return jnp.concatenate(
            [back_ref[2 * dest + part, :, start:start + LANES] for part in range(2)], axis=0).astype(F32)

    def through(grad, raw, gain):
        scale = lax.rsqrt(head_mean(raw * raw, blocks) + EPS)
        unit = raw * scale
        turned = grad * cosine - other_half(grad, head) * sine
        gain_part = jnp.sum(turned * unit, axis=0, keepdims=True)
        inward = turned * gain
        return scale * (inward - unit * head_mean(inward * unit, blocks)), gain_part

    width_q = wq_ref.shape[1]
    width_k = wk_ref.shape[1]
    gain_total = jnp.zeros((1, LANES), F32)
    for tile in range(width_q // LANES):
        got, part = through(fetch(tile, 0), qraw_ref[:, tile * LANES:(tile + 1) * LANES], qg_ref[...])
        gain_total = gain_total + part
        rawq_ref[:, tile * LANES:(tile + 1) * LANES] = got.astype(BF)
    qgain_ref[...] = gain_total
    gain_total = jnp.zeros((1, LANES), F32)
    for tile in range(width_k // LANES):
        even, odd = fetch(2 * tile, LANES), fetch(2 * tile + 1, LANES)
        keys = jnp.where(lane < head, even, swap_heads(odd, head))
        values = jnp.where(lane < head, swap_heads(even, head), odd)
        got, part = through(keys, kraw_ref[:, tile * LANES:(tile + 1) * LANES], kg_ref[...])
        gain_total = gain_total + part
        rawk_ref[:, tile * LANES:(tile + 1) * LANES] = got.astype(BF)
        rawv_ref[:, tile * LANES:(tile + 1) * LANES] = values.astype(BF)
    kgain_ref[...] = gain_total
    normed_grad = nt_dot(rawq_ref[...], wq_ref[...]) + nt_dot(rawk_ref[...], wk_ref[...])
    normed_grad += nt_dot(rawv_ref[...], wv_ref[...])
    hid = hid_ref[...]
    scale = lax.rsqrt(jnp.mean(hid * hid, axis=-1, keepdims=True) + EPS)
    unit = hid * scale
    again_ref[...] = jnp.sum(normed_grad * unit, axis=0, keepdims=True)
    inward = normed_grad * gain_ref[...]
    two_ref[...] = grad_ref[...] + scale * (inward - unit * jnp.mean(inward * unit, axis=-1, keepdims=True))


def allowed_block(row_axis, key_axis, shape, first, second, part, base, start, rows, half_rows):
    row = lax.broadcasted_iota(jnp.int32, shape, row_axis)
    token = (base + row // (2 * half_rows)) * rows + part * half_rows + row % half_rows
    key = start + lax.broadcasted_iota(jnp.int32, shape, key_axis)
    begin = jnp.where(token >= second, second, jnp.where(token >= first, first, 0))
    return (key >= begin) & (key <= token)


def need_mask(first, second, part, base, start, rows, half_rows, keys, sources):
    lowest = base * rows + part * half_rows
    highest = (base + sources - 1) * rows + (part + 1) * half_rows - 1
    begin = jnp.where(highest >= second, second, jnp.where(highest >= first, first, 0))
    return (start + keys - 1 > lowest) | (start < begin)


def attend_kernel(head, rows, keys, sources, info_ref, q_ref, kv_ref, out_ref, aug_ref, ones_ref, acc_ref):
    first, second, part = info_ref[0], info_ref[1], info_ref[2]
    half_rows = q_ref.shape[1]
    wide = sources * 2 * half_rows
    factor = math.log2(math.e) / math.sqrt(head)
    ones_ref[...] = jnp.where(lane_of(kv_ref.shape) < head, jnp.ones_like(kv_ref), kv_ref[...])
    lane = lane_of((half_rows, LANES))

    def block(index, _):
        base = index * sources
        stack = []
        for source in range(sources):
            tile = q_ref[base + source][:, :LANES].astype(F32)
            stack.append(jnp.where(lane < head, tile, 0.0))
            stack.append(jnp.where(lane < head, swap_heads(tile, head), 0.0))
        queries = jnp.concatenate(stack, axis=0).astype(BF)
        acc_ref[...] = jnp.zeros_like(acc_ref)
        last = (base + sources - 1) * rows + (part + 1) * half_rows
        count = (last + keys - 1) // keys

        def visit(step, _):
            start = pl.multiple_of(step * keys, keys)
            raw = lax.dot_general(queries, kv_ref[pl.ds(start, keys)], ONES_NT, preferred_element_type=F32)
            raised = jnp.exp2(raw * factor)
            masked = need_mask(first, second, part, base, start, rows, half_rows, keys, sources)

            @pl.when(masked)
            def _():
                ok = allowed_block(0, 1, (wide, keys), first, second, part, base, start, rows, half_rows)
                acc_ref[...] += jnp.dot(jnp.where(ok, raised, 0.0).astype(BF), ones_ref[pl.ds(start, keys)],
                                        preferred_element_type=F32)

            @pl.when(jnp.logical_not(masked))
            def _():
                acc_ref[...] += jnp.dot(raised.astype(BF), ones_ref[pl.ds(start, keys)],
                                        preferred_element_type=F32)

        lax.fori_loop(0, count, visit, None)
        for source in range(sources):
            tile = q_ref[base + source][:, :LANES].astype(F32)
            outs = []
            for which in range(2):
                place = (2 * source + which) * half_rows
                acc = acc_ref[place:place + half_rows]
                turned = swap_heads(acc, head)
                outs.append(turned / acc if which == 0 else acc / turned)
                high, middle, low = three_parts(-math.sqrt(head) * jnp.log(turned))
                query = tile if which == 0 else swap_heads(tile, head)
                extra = jnp.where(lane == head, high, jnp.where(lane == head + 1, middle,
                                                                jnp.where(lane == head + 2, low, 0.0)))
                aug_ref[base + source, which] = jnp.where(lane < head, query, extra).astype(BF)
            out_ref[base + source] = jnp.where(lane < head, outs[0], outs[1])

    lax.fori_loop(0, q_ref.shape[0] // sources, block, None)


def attend_back_kernel(head, rows, keys, sources, info_ref, aug_ref, out_ref, grad_ref, kv_ref,
                       dq_ref, dkv_ref, kone_ref, vone_ref, dk_ref, dv_ref, acc_ref):
    first, second, part = info_ref[0], info_ref[1], info_ref[2]
    half_rows = grad_ref.shape[1]
    wide = sources * 2 * half_rows
    factor = math.log2(math.e) / math.sqrt(head)
    whole = lane_of(kv_ref.shape)
    vone_ref[...] = jnp.where(whole < head, jnp.ones_like(kv_ref), kv_ref[...])
    kone_ref[...] = jnp.where(whole < head, kv_ref[...], jnp.ones_like(kv_ref))
    dk_ref[...] = jnp.zeros_like(dk_ref)
    dv_ref[...] = jnp.zeros_like(dv_ref)
    lane = lane_of((half_rows, LANES))

    def block(index, _):
        base = index * sources
        stack_q, stack_d = [], []
        for source in range(sources):
            grad = grad_ref[base + source].astype(F32)
            spread = grad * out_ref[base + source]
            for which in range(2):
                stack_q.append(aug_ref[base + source, which])
                mine = (lane < head) if which == 0 else (lane >= head)
                delta = jnp.sum(jnp.where(mine, spread, 0.0), axis=1, keepdims=True)
                high, middle, low = three_parts(-delta)
                extra = jnp.where(lane == 0, high, jnp.where(lane == 1, middle, jnp.where(lane == 2, low, 0.0)))
                moved = swap_heads(grad, head) if which == 0 else grad
                stack_d.append(jnp.where(lane < head, extra, moved).astype(BF))
        queries = jnp.concatenate(stack_q, axis=0)
        grads = jnp.concatenate(stack_d, axis=0)
        acc_ref[...] = jnp.zeros_like(acc_ref)
        last = (base + sources - 1) * rows + (part + 1) * half_rows
        count = (last + keys - 1) // keys

        def visit(step, _):
            start = pl.multiple_of(step * keys, keys)
            here = pl.ds(start, keys)

            def finish(prob):
                along = lax.dot_general(vone_ref[here], grads, ONES_NT, preferred_element_type=F32)
                score = (prob * along).astype(BF)
                dv_ref[here] += jnp.dot(prob.astype(BF), grads, preferred_element_type=F32)
                dk_ref[here] += jnp.dot(score, queries, preferred_element_type=F32)
                acc_ref[...] += lax.dot_general(score, kone_ref[here], ONES_TN, preferred_element_type=F32)

            raw = lax.dot_general(kone_ref[here], queries, ONES_NT, preferred_element_type=F32)
            masked = need_mask(first, second, part, base, start, rows, half_rows, keys, sources)

            @pl.when(masked)
            def _():
                ok = allowed_block(1, 0, (keys, wide), first, second, part, base, start, rows, half_rows)
                finish(jnp.where(ok, jnp.exp2(jnp.where(ok, raw, 0.0) * factor), 0.0))

            @pl.when(jnp.logical_not(masked))
            def _():
                finish(jnp.exp2(raw * factor))

        lax.fori_loop(0, count, visit, None)
        for source in range(sources):
            place = 2 * source * half_rows
            one = acc_ref[place:place + half_rows]
            two = acc_ref[place + half_rows:place + 2 * half_rows]
            both = jnp.where(lane < head, one, swap_heads(two, head)) * (1.0 / math.sqrt(head))
            dq_ref[base + source] = both.astype(BF)

    lax.fori_loop(0, grad_ref.shape[0] // sources, block, None)
    dkv_ref[...] = jnp.where(whole < head, dk_ref[...] * (1.0 / math.sqrt(head)), dv_ref[...]).astype(BF)


MESH = pl.DeviceIdType.MESH


def turned(value):
    return value.astype(F32).T.astype(BF)


def norm_scale(hidden):
    return lax.rsqrt(jnp.mean(hidden * hidden, axis=-1, keepdims=True) + EPS)


def norm_pull(normed_grad, hidden, gain):
    scale = norm_scale(hidden)
    unit = hidden * scale
    inward = normed_grad * gain
    back = scale * (inward - unit * jnp.mean(inward * unit, axis=-1, keepdims=True))
    return back, jnp.sum(normed_grad * unit, axis=0, keepdims=True)


def nt_dot(left, right):
    return lax.dot_general(left, right, ONES_NT, preferred_element_type=F32)


def nn_dot(left, right):
    return jnp.dot(left, right, preferred_element_type=F32)


def activation_pull(gate_act, lift_act, sigma, inner_grad):
    gate_grad = inner_grad * lift_act * sigma * (1 + gate_act * (1 - sigma))
    return gate_grad.astype(BF), (inner_grad * gate_act * sigma).astype(BF)


def low_kernel(hid_ref, gain_ref, gate_ref, lift_ref, drop_ref,
               out_ref, normt_ref, gact_ref, lact_ref, innert_ref, norm_ref):
    step = pl.program_id(0)

    @pl.when(step == 0)
    def _():
        hid = hid_ref[...]
        normed = hid * norm_scale(hid) * gain_ref[...]
        norm_ref[...] = normed.astype(BF)
        normt_ref[...] = turned(normed)
        out_ref[...] = hid

    normed = norm_ref[...]
    gate_act = nn_dot(normed, gate_ref[...])
    lift_act = nn_dot(normed, lift_ref[...])
    inner = gate_act * jax.nn.sigmoid(gate_act) * lift_act
    gact_ref[...] = gate_act.astype(BF)
    lact_ref[...] = lift_act.astype(BF)
    innert_ref[...] = turned(inner)
    out_ref[...] += nn_dot(inner.astype(BF), drop_ref[...])


def low_back_kernel(grad_ref, hid_ref, gain_ref, gact_ref, lact_ref, gate_ref, lift_ref, drop_ref,
                    out_ref, again_ref, low_ref, outlow_ref, glow_ref, llow_ref, acc_ref):
    step = pl.program_id(0)

    @pl.when(step == 0)
    def _():
        low_ref[...] = grad_ref[...].astype(BF)
        acc_ref[...] = jnp.zeros_like(acc_ref)

    gate_act, lift_act = gact_ref[...].astype(F32), lact_ref[...].astype(F32)
    inner_grad = nt_dot(low_ref[...], drop_ref[...])
    gate_low, lift_low = activation_pull(gate_act, lift_act, jax.nn.sigmoid(gate_act), inner_grad)
    glow_ref[...] = gate_low
    llow_ref[...] = lift_low
    acc_ref[...] += nt_dot(gate_low, gate_ref[...]) + nt_dot(lift_low, lift_ref[...])

    @pl.when(step == pl.num_programs(0) - 1)
    def _():
        back, gain_part = norm_pull(acc_ref[...], hid_ref[...], gain_ref[...])
        again_ref[...] = gain_part
        out = grad_ref[...] + back
        out_ref[...] = out
        outlow_ref[...] = out.astype(BF)


def top_kernel(got_ref, two_ref, exit_ref, cot_ref, gain_ref, gate_ref, lift_ref, drop_ref,
               out_ref, grad_ref, gradlow_ref, send_ref, attt_ref, again_ref, normt_ref, innert_ref, glow_ref,
               llow_ref, hid_ref, norm_ref, acc_ref):
    step = pl.program_id(0)
    half_rows = got_ref.shape[1]

    @pl.when(step == 0)
    def _():
        tiles = []
        for tile in range(got_ref.shape[0] // 2):
            tiles.append(jnp.concatenate([got_ref[2 * tile], got_ref[2 * tile + 1]], axis=0))
        attended = jnp.concatenate(tiles, axis=1)
        attt_ref[...] = turned(attended)
        hid = two_ref[...] + nn_dot(attended, exit_ref[...])
        hid_ref[...] = hid
        normed = hid * norm_scale(hid) * gain_ref[...]
        norm_ref[...] = normed.astype(BF)
        normt_ref[...] = turned(normed)
        out_ref[...] = hid
        acc_ref[...] = jnp.zeros_like(acc_ref)

    normed = norm_ref[...]
    gate_act = nn_dot(normed, gate_ref[...])
    lift_act = nn_dot(normed, lift_ref[...])
    sigma = jax.nn.sigmoid(gate_act)
    inner = gate_act * sigma * lift_act
    innert_ref[...] = turned(inner)
    out_ref[...] += nn_dot(inner.astype(BF), drop_ref[...])
    inner_grad = nt_dot(cot_ref[...], drop_ref[...])
    gate_low, lift_low = activation_pull(gate_act, lift_act, sigma, inner_grad)
    glow_ref[...] = gate_low
    llow_ref[...] = lift_low
    acc_ref[...] += nt_dot(gate_low, gate_ref[...]) + nt_dot(lift_low, lift_ref[...])

    @pl.when(step == pl.num_programs(0) - 1)
    def _():
        back, gain_part = norm_pull(acc_ref[...], hid_ref[...], gain_ref[...])
        again_ref[...] = gain_part
        grad = cot_ref[...].astype(F32) + back
        grad_ref[...] = grad
        low = grad.astype(BF)
        gradlow_ref[...] = low
        sent = nt_dot(low, exit_ref[...]).astype(BF)
        for tile in range(send_ref.shape[0] // 2):
            for part in range(2):
                send_ref[2 * tile + part] = sent[part * half_rows:(part + 1) * half_rows,
                                                 tile * LANES:(tile + 1) * LANES]


TILE = 512


def whole_block(shape):
    return pl.BlockSpec(shape, lambda step, rank=len(shape): (0,) * rank)


def column_block(rows):
    return pl.BlockSpec((rows, TILE), lambda step: (0, step))


def row_block(columns):
    return pl.BlockSpec((TILE, columns), lambda step: (step, 0))


def call_tiled(kernel, tiles, ins, outs, scratch, flops, moved, name):
    return pl.pallas_call(
        kernel,
        grid=(tiles,),
        in_specs=[spec for _, spec in ins],
        out_specs=tuple(spec for _, spec in outs),
        out_shape=tuple(shape for shape, _ in outs),
        scratch_shapes=scratch,
        compiler_params=pltpu.CompilerParams(vmem_limit_bytes=VMEM_LIMIT, dimension_semantics=("arbitrary",)),
        cost_estimate=pl.CostEstimate(flops=flops, bytes_accessed=moved, transcendentals=0),
        name=name,
    )(*[value for value, _ in ins])


def feed_low(hidden, gain, gate, lift, drop):
    rows, width = hidden.shape
    ff = gate.shape[1]
    S = jax.ShapeDtypeStruct
    return call_tiled(
        low_kernel, ff // TILE,
        [(hidden, whole_block((rows, width))), (gain, whole_block((1, width))), (gate, column_block(width)),
         (lift, column_block(width)), (drop, row_block(width))],
        [(S((rows, width), F32), whole_block((rows, width))), (S((width, rows), BF), whole_block((width, rows))),
         (S((rows, ff), BF), column_block(rows)), (S((rows, ff), BF), column_block(rows)),
         (S((ff, rows), BF), row_block(rows))],
        [pltpu.VMEM((rows, width), BF)], 6 * rows * width * ff, 38 << 20, "feed_low")


def feed_low_back(grad, hidden, gain, gact, lact, gate, lift, drop):
    rows, width = hidden.shape
    ff = gate.shape[1]
    S = jax.ShapeDtypeStruct
    full = whole_block((rows, width))
    return call_tiled(
        low_back_kernel, ff // TILE,
        [(grad, full), (hidden, full), (gain, whole_block((1, width))), (gact, column_block(rows)),
         (lact, column_block(rows)), (gate, column_block(width)), (lift, column_block(width)),
         (drop, row_block(width))],
        [(S((rows, width), F32), full), (S((1, width), F32), whole_block((1, width))), (S((rows, width), BF), full),
         (S((rows, width), BF), full), (S((rows, ff), BF), column_block(rows)), (S((rows, ff), BF), column_block(rows))],
        [pltpu.VMEM((rows, width), F32)], 6 * rows * width * ff, 40 << 20, "feed_low_back")


def feed_top(got, two, exit_weight, cotangent, gain, gate, lift, drop):
    rows, width = two.shape
    ff = gate.shape[1]
    S = jax.ShapeDtypeStruct
    full = whole_block((rows, width))
    flat = whole_block((1, width))
    standing = whole_block((width, rows))
    return call_tiled(
        top_kernel, ff // TILE,
        [(got, whole_block(got.shape)), (two, full), (exit_weight, whole_block(exit_weight.shape)), (cotangent, full),
         (gain, flat), (gate, column_block(width)), (lift, column_block(width)), (drop, row_block(width))],
        [(S((rows, width), F32), full), (S((rows, width), F32), full), (S((rows, width), BF), full),
         (S(got.shape, BF), whole_block(got.shape)), (S((width, rows), BF), standing), (S((1, width), F32), flat),
         (S((width, rows), BF), standing), (S((ff, rows), BF), row_block(rows)), (S((rows, ff), BF), column_block(rows)),
         (S((rows, ff), BF), column_block(rows))],
        [pltpu.VMEM((rows, width), F32), pltpu.VMEM((rows, width), BF), pltpu.VMEM((rows, width), F32)],
        12 * rows * width * ff, 45 << 20, "feed_top")


PIECE = 32
SUB = 2 * PIECE
STRIP = 256
RING = 8
LAG = 2


def sum_kernel(jobs, sides, lines, *refs):
    count = len(jobs)
    refs = list(refs)
    take = lambda number: [refs.pop(0) for _ in range(number)]
    lefts, rights, (small_ref,) = take(sides), take(count), take(1)
    outs, (small_out,), lefts_b, rights_b = take(count), take(1), take(sides), take(count)
    (lbuf, rbuf, xp, xr, yp, yr, zp, us, ur, ds_, dr, fs, fr, cs, cr, stage, sm_s, sm_r,
     lsem, rsem, xs, xv, ys, yv, uss, urv, dss, drv, fss, frv, css, crv, osem, sms, smv, els, elv, ers, erv) = refs
    steps = sum(job[3] for job in jobs)
    last = steps - 1 + LAG
    half = STRIP // 2
    tall = SUB + PIECE
    tokens = lbuf.shape[-1] // 2
    me = lax.axis_index("ctx")
    y = lax.axis_index("dp")
    z = me // 4
    x = (me // 2) % 2
    c = me % 2
    top = lines - 1
    twin = {"ctx": me + 1 - 2 * c}
    across_x = {"ctx": me + 2 - 4 * x}
    across_y = {"dp": 1 - y}
    above = {"ctx": jnp.minimum(me + 4, 4 * top + me % 4)}
    below = {"ctx": jnp.maximum(me - 4, me % 4)}
    near = {"ctx": me + 4 - 8 * (z % 2)}
    far = {"ctx": me + 8 - 16 * (z // 2)}
    rounds = [twin, across_x, across_y, near, far]

    for buf in (xp, ur, dr, zp):
        buf[...] = jnp.zeros_like(buf)
    sm_s[0] = small_ref[...]

    barrier = pltpu.get_barrier_semaphore()
    for where in (twin, across_x, across_y, far):
        pl.semaphore_signal(barrier, inc=1, device_id=where, device_id_type=MESH)

    @pl.when(z < top)
    def _():
        pl.semaphore_signal(barrier, inc=1, device_id=above, device_id_type=MESH)

    @pl.when(z > 0)
    def _():
        pl.semaphore_signal(barrier, inc=1, device_id=below, device_id_type=MESH)

    pl.semaphore_wait(barrier, 4 + (z < top).astype(jnp.int32) + (z > 0).astype(jnp.int32))

    def remote(src, dst, send, recv, where):
        return pltpu.make_async_remote_copy(src_ref=src, dst_ref=dst, send_sem=send, recv_sem=recv,
                                            device_id=where, device_id_type=MESH)

    def left_copy(number):
        return remote(lefts[number], lefts_b[number], els.at[number], elv.at[number], twin)

    def right_copy(number):
        width = rights_b[number].shape[1]
        start = pl.multiple_of((1 - c) * width, width)
        return remote(rights[number].at[:, pl.ds(start, width)], rights_b[number], ers.at[number], erv.at[number], twin)

    seen = []
    for number, job in enumerate(jobs):
        if job[0] not in seen:
            seen.append(job[0])
            left_copy(job[0]).start()
        right_copy(number).start()

    def x_copy(j):
        s = j % RING
        return remote(xp.at[s, 1 - x], xr.at[s], xs.at[s], xv.at[s], across_x)

    def y_copy(j):
        s = j % RING
        return remote(yp.at[s, 1 - y], yr.at[s], ys.at[s], yv.at[s], across_y)

    def up_copy(j):
        s = j % RING
        return remote(us.at[s], ur.at[s], uss.at[s], urv.at[s], above)

    def down_copy(j):
        s = j % RING
        return remote(ds_.at[s], dr.at[s], dss.at[s], drv.at[s], below)

    def f_copy(j):
        s = j % RING
        return remote(fs.at[s], fr.at[s], fss.at[s], frv.at[s], across_y)

    def c_copy(j):
        s = j % RING
        return remote(cs.at[s], cr.at[s], css.at[s], crv.at[s], twin)

    def small_copy(k):
        return remote(sm_s.at[k], sm_r.at[k], sms.at[k], smv.at[k], rounds[k])

    def loads(number, row, column, s):
        left = jobs[number][0]
        width = rights_b[number].shape[1]
        mine = pl.multiple_of(c * width + column, STRIP)
        rows = pl.ds(row, PIECE)
        return [
            pltpu.make_async_copy(lefts[left].at[:, :, rows, :], lbuf.at[s, :, :, :, pl.ds(0, tokens)], lsem.at[s, 0]),
            pltpu.make_async_copy(lefts_b[left].at[:, :, rows, :], lbuf.at[s, :, :, :, pl.ds(tokens, tokens)],
                                  lsem.at[s, 1]),
            pltpu.make_async_copy(rights[number].at[:, pl.ds(mine, STRIP)], rbuf.at[s, pl.ds(0, tokens)], rsem.at[s, 0]),
            pltpu.make_async_copy(rights_b[number].at[:, pl.ds(column, STRIP)], rbuf.at[s, pl.ds(tokens, tokens)],
                                  rsem.at[s, 1]),
        ]

    def load(j):
        begin = 0
        done = []
        for number, (left, subs, strips, total) in enumerate(jobs):
            fresh = left not in done
            done.append(left)

            @pl.when(j == begin)
            def _(number=number, left=left, fresh=fresh):
                if fresh:
                    left_copy(left).wait()
                right_copy(number).wait()

            @pl.when((j >= begin) & (j < begin + total))
            def _(number=number, subs=subs, begin=begin):
                k = j - begin
                row = pl.multiple_of((k % subs) * PIECE, PIECE)
                column = pl.multiple_of((k // subs) * STRIP, STRIP)
                for copy in loads(number, row, column, j % 2):
                    copy.start()
            begin += total

    def out_copies(number, j, row, column):
        width = rights_b[number].shape[1]
        o = j % RING
        rows = pl.ds(row, PIECE)
        mine = pl.multiple_of(c * width + column, STRIP)
        other = pl.multiple_of((1 - c) * width + column, STRIP)
        return [
            pltpu.make_async_copy(stage.at[o, 0], outs[number].at[rows, pl.ds(mine, STRIP)], osem.at[o, 0]),
            pltpu.make_async_copy(stage.at[o, 1], outs[number].at[rows, pl.ds(other, STRIP)], osem.at[o, 1]),
        ]

    def store(j):
        begin = 0
        for number, (left, subs, strips, total) in enumerate(jobs):
            @pl.when((j >= begin) & (j < begin + total))
            def _(number=number, subs=subs, begin=begin):
                k = j - begin
                row = pl.multiple_of((k % subs) * PIECE, PIECE)
                column = pl.multiple_of((k // subs) * STRIP, STRIP)
                for copy in out_copies(number, j, row, column):
                    copy.start()
            begin += total

    load(0)

    def step(t, _):
        slot = t % RING

        for k in range(len(rounds) + 1):
            @pl.when(t == LAG * k)
            def _(k=k):
                if k > 0:
                    small_copy(k - 1).wait()
                    total = sm_s[k - 1] + sm_r[k - 1]
                    if k == len(rounds):
                        small_out[...] = total
                    else:
                        sm_s[k] = total
                if k < len(rounds):
                    small_copy(k).start()

        @pl.when(t < steps)
        def _():
            for copy in loads(0, 0, 0, t % 2):
                copy.wait()

            @pl.when(t + 1 < steps)
            def _():
                load(t + 1)

            left = lbuf[t % 2].reshape(2 * lines * SUB, 2 * tokens)
            got = jnp.dot(left, rbuf[t % 2], preferred_element_type=F32).astype(BF)
            for line in range(lines):
                for side in range(2):
                    row = (2 * line + side) * SUB
                    xp[slot, side, line, :SUB] = got[row:row + SUB, :half]
                    for part in range(2):
                        yp[slot, part, side, line] = got[row + part * PIECE:row + (part + 1) * PIECE, half:]

        @pl.when((t >= LAG) & (t <= last))
        def _():
            y_copy(t - LAG).wait()
            s = (t - LAG) % RING
            xp[slot, :, :, SUB:] = yp[s, y] + yr[s]

        @pl.when(t < steps)
        def _():
            y_copy(t).start()

        @pl.when(t <= last)
        def _():
            x_copy(t).start()

        @pl.when((t >= LAG) & (t - LAG <= last))
        def _():
            x_copy(t - LAG).wait()
            s = (t - LAG) % RING
            zp[(t - LAG) % (2 * RING)] = xp[s, x] + xr[s]

        ju = t - LAG * (1 + z)

        @pl.when((ju >= 0) & (ju <= last))
        def _():
            s = ju % RING
            held = ju % (2 * RING)

            @pl.when(z > 0)
            def _():
                up_copy(ju).wait_recv()
                zp[held, z] = zp[held, z] + ur[s, 0]

            @pl.when(z < top)
            def _():
                @pl.when(ju >= RING)
                def _():
                    up_copy(ju).wait_send()

                for m in range(top):
                    own = zp[held, jnp.minimum(z + 1 + m, top)]
                    if m + 1 < top:
                        own = own + ur[s, m + 1]
                    us[s, m] = own
                up_copy(ju).start()

        jd = t - LAG * (1 + top - z)

        @pl.when((jd >= 0) & (jd <= last))
        def _():
            s = jd % RING
            held = jd % (2 * RING)

            @pl.when(z < top)
            def _():
                down_copy(jd).wait_recv()
                zp[held, z] = zp[held, z] + dr[s, 0]

            @pl.when(z > 0)
            def _():
                @pl.when(jd >= RING)
                def _():
                    down_copy(jd).wait_send()

                for m in range(top):
                    own = zp[held, jnp.maximum(z - 1 - m, 0)]
                    if m + 1 < top:
                        own = own + dr[s, m + 1]
                    ds_[s, m] = own
                down_copy(jd).start()

        jf = t - LAG * (1 + top)

        @pl.when((jf >= 0) & (jf <= last))
        def _():
            fs[jf % RING] = zp[jf % (2 * RING), z]
            f_copy(jf).start()

        jo = jf - LAG

        @pl.when((jo >= 0) & (jo <= last))
        def _():
            f_copy(jo).wait()
            s = jo % RING
            fs[s, :SUB] = fs[s, :SUB] + fr[s, :SUB]
            mine = pl.ds(pl.multiple_of(c * PIECE, PIECE), PIECE)
            away = pl.ds(pl.multiple_of((1 - c) * PIECE, PIECE), PIECE)
            cs[s, :, :half] = fs[s, away]
            own, far_rows = fs[s, SUB:].astype(F32), fr[s, SUB:].astype(F32)
            cs[s, :, half:] = jnp.where(y == c, far_rows, own).astype(BF)
            c_copy(jo).start()
            stage[jo % RING, 0, :, :half] = fs[s, mine].astype(F32)

            @pl.when(jo >= LAG)
            def _():
                stage[(jo - LAG) % RING, 0, :, half:] = jnp.where(y == c, own, far_rows)

        jc = jo - LAG

        @pl.when((jc >= 0) & (jc <= last))
        def _():
            c_copy(jc).wait()
            s = jc % RING
            stage[jc % RING, 1, :, :half] = cr[s, :, :half].astype(F32)

            @pl.when(jc >= LAG)
            def _():
                chunk = jc - LAG
                stage[chunk % RING, 1, :, half:] = cr[s, :, half:].astype(F32)
                store(chunk)

            @pl.when(jc >= 2 * LAG)
            def _():
                for copy in out_copies(0, jc - 2 * LAG, 0, 0):
                    copy.wait()

    lax.fori_loop(0, last + LAG * (top + 3) + 1, step, None)
    for back in range(LAG):
        for copy in out_copies(0, steps - 1 - back, 0, 0):
            copy.wait()
    for back in range(RING):
        j = last - back

        @pl.when(z < top)
        def _(j=j):
            up_copy(j).wait_send()

        @pl.when(z > 0)
        def _(j=j):
            down_copy(j).wait_send()


def sum_over_chips(lefts, works, small, lines, collective_id):
    shaped, jobs, landing_l, landing_r, outs = [], [], [], [], []
    for left in lefts:
        rows, tokens = left.shape
        shaped.append(left.reshape(2 * lines, 2, rows // (4 * lines), tokens))
        landing_l.append(jax.ShapeDtypeStruct(shaped[-1].shape, BF))
    for number, right in works:
        rows = shaped[number].shape[2]
        subs, strips = rows // PIECE, right.shape[1] // 2 // STRIP
        jobs.append((number, subs, strips, subs * strips))
        landing_r.append(jax.ShapeDtypeStruct((tokens, right.shape[1] // 2), BF))
        outs.append(jax.ShapeDtypeStruct((rows, right.shape[1]), F32))
    steps = sum(job[3] for job in jobs)
    half = STRIP // 2
    tall = SUB + PIECE
    top = lines - 1
    dma = pltpu.SemaphoreType.DMA
    scratch = [
        pltpu.VMEM((2, 2 * lines, 2, PIECE, 2 * tokens), BF),
        pltpu.VMEM((2, 2 * tokens, STRIP), BF),
        pltpu.VMEM((RING, 2, lines, tall, half), BF),
        pltpu.VMEM((RING, lines, tall, half), BF),
        pltpu.VMEM((RING, 2, 2, lines, PIECE, half), BF),
        pltpu.VMEM((RING, 2, lines, PIECE, half), BF),
        pltpu.VMEM((2 * RING, lines, tall, half), BF),
        pltpu.VMEM((RING, top, tall, half), BF),
        pltpu.VMEM((RING, top, tall, half), BF),
        pltpu.VMEM((RING, top, tall, half), BF),
        pltpu.VMEM((RING, top, tall, half), BF),
        pltpu.VMEM((RING, tall, half), BF),
        pltpu.VMEM((RING, tall, half), BF),
        pltpu.VMEM((RING, PIECE, STRIP), BF),
        pltpu.VMEM((RING, PIECE, STRIP), BF),
        pltpu.VMEM((RING, 2, PIECE, STRIP), F32),
        pltpu.VMEM((5,) + small.shape, F32),
        pltpu.VMEM((5,) + small.shape, F32),
        dma((2, 2)), dma((2, 2)),
    ] + [dma((RING,))] * 12 + [
        dma((RING, 2)), dma((5,)), dma((5,)),
        dma((len(lefts),)), dma((len(lefts),)), dma((len(works),)), dma((len(works),)),
    ]
    anywhere = pl.BlockSpec(memory_space=pl.ANY)
    inside = pl.BlockSpec(memory_space=pltpu.VMEM)
    flops = 2 * steps * 2 * lines * SUB * STRIP * 2 * tokens
    got = pl.pallas_call(
        functools.partial(sum_kernel, jobs, len(lefts), lines),
        out_shape=tuple(outs) + (jax.ShapeDtypeStruct(small.shape, F32),) + tuple(landing_l) + tuple(landing_r),
        in_specs=[anywhere] * (len(lefts) + len(works)) + [inside],
        out_specs=tuple([anywhere] * len(works) + [inside] + [anywhere] * (len(lefts) + len(works))),
        scratch_shapes=scratch,
        compiler_params=pltpu.CompilerParams(collective_id=collective_id, has_side_effects=True,
                                             vmem_limit_bytes=VMEM_LIMIT),
        cost_estimate=pl.CostEstimate(flops=flops, bytes_accessed=steps * 800_000, transcendentals=0),
        name="sum_over_chips",
    )(*shaped, *[right for _, right in works], small)
    return got[:len(works)], got[len(works)]


def call_plain(kernel, outs, args, smem=0, scratch=(), flops=0, moved=0, name=None):
    specs = [pl.BlockSpec(memory_space=pltpu.SMEM)] * smem + vmem_specs(len(args) - smem)
    many = isinstance(outs, (tuple, list))
    return pl.pallas_call(
        kernel,
        out_shape=tuple(outs) if many else outs,
        in_specs=specs,
        out_specs=tuple(vmem_specs(len(outs))) if many else vmem_specs(1)[0],
        scratch_shapes=list(scratch),
        compiler_params=pltpu.CompilerParams(vmem_limit_bytes=VMEM_LIMIT),
        cost_estimate=pl.CostEstimate(flops=flops, bytes_accessed=moved, transcendentals=0),
        name=name,
    )(*args)


def shape_of(shape, kind):
    return jax.ShapeDtypeStruct(shape, kind)


def sibling(value):
    count = lax.axis_size("ctx")
    return lax.ppermute(value, "ctx", [(i, i ^ 1) for i in range(count)])


def norm_back(grad, hidden, gain):
    scale = lax.rsqrt(jnp.mean(hidden * hidden, axis=-1, keepdims=True) + EPS)
    unit = hidden * scale
    inward = grad * gain
    gain_grad = jnp.sum(grad * unit, axis=0)
    return scale * (inward - unit * jnp.mean(inward * unit, axis=-1, keepdims=True)), gain_grad


def fast_device(tokens, lengths, cotangent, mixgain, mixentry, mixtaps, mixexit, lowgain, lowgate, lowlift,
                lowdrop, attgain, attquery, attkeys, attvalues, querygain, keysgain, attexit, topgain, topgate,
                toplift, topdrop):
    rows, width = tokens.shape
    head = querygain.shape[0]
    devices = lax.axis_size("ctx")
    lines = devices // 4
    half_rows = rows // 2
    group = devices * rows
    place = lax.axis_index("ctx")
    core = place % 2
    first = lengths[0, 0]
    second = first + lengths[0, 1]
    mine = place * rows + jnp.arange(rows, dtype=jnp.int32)
    my_seg = segment_of(mine, first, second)
    begin = jnp.where(my_seg == 0, 0, jnp.where(my_seg == 1, first, second))
    position = (mine - begin).astype(F32)
    gains = [value.astype(F32) for value in (mixgain, lowgain, attgain, topgain)]
    mixgain_f, lowgain_f, attgain_f, topgain_f = gains
    taps_f = mixtaps.astype(F32)
    twice = lambda gain: jnp.tile(gain.astype(F32), LANES // head)[None, :]
    querygain_2, keysgain_2 = twice(querygain), twice(keysgain)
    spot = jnp.arange(LANES, dtype=jnp.int32) % (head // 2)
    angle = position[:, None] * (THETA ** (-spot.astype(F32) * 2.0 / head))[None, :]
    cosine = jnp.cos(angle)
    sine = jnp.sin(angle) * jnp.where(jnp.arange(LANES) % head < head // 2, -1.0, 1.0)[None, :]
    info = jnp.stack([first, second, core, core]).astype(jnp.int32)

    hidden = tokens.astype(F32)
    normed_one = root_mean_square_scale(hidden, mixgain_f).astype(BF)
    mixed = jnp.dot(normed_one, mixentry, preferred_element_type=F32)
    part_b, part_c, part_x = (mixed[:, i * width:(i + 1) * width] for i in range(3))
    product = (part_b * part_x).astype(BF)
    borrowed = passed_along(product[rows - 2:], "ctx", 1)
    extended = jnp.concatenate([borrowed, product], axis=0).astype(F32)
    fits_one = ((mine >= 1) & (segment_of(mine - 1, first, second) == my_seg)).astype(F32)[:, None]
    fits_two = ((mine >= 2) & (segment_of(mine - 2, first, second) == my_seg)).astype(F32)[:, None]
    conved = conv_local(extended, taps_f, fits_one, fits_two)
    gated = (part_c * conved).astype(BF)
    hidden_one = hidden + jnp.dot(gated, mixexit, preferred_element_type=F32)
    hidden_two, lownorm_t, gact_low, lact_low, lowinner_t = feed_low(
        hidden_one, lowgain_f[None, :], lowgate, lowlift, lowdrop)

    heads_q, heads_k = attquery.shape[1] // head, attkeys.shape[1] // head
    msg, normed_two_t, query_raw, key_raw = call_plain(
        functools.partial(project_kernel, head),
        (shape_of((devices, half_rows, 2 * LANES), BF), shape_of((width, rows), BF),
         shape_of((rows, attquery.shape[1]), F32), shape_of((rows, attkeys.shape[1]), F32)),
        (hidden_two, attgain_f[None, :], attquery, attkeys, attvalues, cosine, sine, querygain_2, keysgain_2),
        flops=2 * rows * width * 2 * width, moved=6 << 20, name="project")
    held = lax.all_to_all(msg, "ctx", 0, 0)
    held_kv = held[:, :, LANES:]
    other_kv = sibling(held_kv)
    pair = jnp.where(core == 0, jnp.stack([held_kv, other_kv], axis=1), jnp.stack([other_kv, held_kv], axis=1))
    all_kv = pair.reshape(group, LANES)
    keys, sources = 512, 2
    wide = sources * rows
    area = group * group // 2 // 2 * 2
    attended_f, augmented = call_plain(
        functools.partial(attend_kernel, head, rows, keys, sources),
        (shape_of((devices, half_rows, LANES), F32), shape_of((devices, 2, half_rows, LANES), BF)),
        (info, held, all_kv), smem=1,
        scratch=[pltpu.VMEM((group, LANES), BF), pltpu.VMEM((wide, LANES), F32)],
        flops=4 * area * LANES, moved=5 << 20, name="attend")
    got = lax.all_to_all(attended_f.astype(BF), "ctx", 0, 0)
    (output, grad, grad_low3, send, attended_t, topgain_grad, topnorm_t, topinner_t, gate_top, lift_top) = feed_top(
        got, hidden_two, attexit, cotangent, topgain_f[None, :], topgate, toplift, topdrop)
    held_grad = lax.all_to_all(send, "ctx", 0, 0)
    dq, dkv = call_plain(
        functools.partial(attend_back_kernel, head, rows, keys, sources),
        (shape_of((devices, half_rows, LANES), BF), shape_of((group, LANES), BF)),
        (info, augmented, attended_f, held_grad, all_kv), smem=1,
        scratch=[pltpu.VMEM((group, LANES), BF), pltpu.VMEM((group, LANES), BF),
                 pltpu.VMEM((group, LANES), F32), pltpu.VMEM((group, LANES), F32), pltpu.VMEM((wide, LANES), F32)],
        flops=10 * area * LANES, moved=8 << 20, name="attend_back")
    dkv = dkv.reshape(devices, 2, half_rows, LANES)
    mine_kv = lax.dynamic_index_in_dim(dkv, core, 1, keepdims=False)
    send_kv = lax.dynamic_index_in_dim(dkv, 1 - core, 1, keepdims=False)
    dkv_sum = (mine_kv.astype(F32) + sibling(send_kv).astype(F32)).astype(BF)
    back = lax.all_to_all(jnp.concatenate([dq, dkv_sum], axis=2), "ctx", 0, 0)
    rawq_low, rawk_low, rawv_low, grad_two, attgain_grad, querygain_grad, keysgain_grad = call_plain(
        functools.partial(project_back_kernel, head),
        (shape_of((rows, attquery.shape[1]), BF), shape_of((rows, attkeys.shape[1]), BF),
         shape_of((rows, attkeys.shape[1]), BF), shape_of((rows, width), F32), shape_of((1, width), F32),
         shape_of((1, LANES), F32), shape_of((1, LANES), F32)),
        (back, hidden_two, attgain_f[None, :], attquery, attkeys, attvalues, cosine, sine, querygain_2, keysgain_2,
         query_raw, key_raw, grad),
        flops=2 * rows * width * 2 * width, moved=8 << 20, name="project_back")
    fold = lambda value: value.reshape(LANES // head, head).sum(axis=0)
    querygain_grad, keysgain_grad = fold(querygain_grad), fold(keysgain_grad)
    grad, lowgain_grad, gb_low, grad_low1, gate_low, lift_low = feed_low_back(
        grad_two, hidden_one, lowgain_f[None, :], gact_low, lact_low, lowgate, lowlift, lowdrop)
    gated_grad = outer_dot(grad_low1, mixexit)
    part_c_grad = gated_grad * conved
    conved_grad = gated_grad * part_c
    _, pull_conv = jax.vjp(lambda ext, taps: conv_local(ext, taps, fits_one, fits_two), extended, taps_f)
    extended_grad, mixtaps_grad = pull_conv(conved_grad)
    returned_rim = passed_along(extended_grad[:2], "ctx", -1)
    product_grad = extended_grad[2:].at[rows - 2:].add(returned_rim)
    mixed_grad = jnp.concatenate(
        [product_grad * part_x, part_c_grad, product_grad * part_b], axis=1).astype(BF)
    hidden_grad, mixgain_grad = norm_back(outer_dot(mixed_grad, mixentry), hidden, mixgain_f)
    tokens_grad = grad + hidden_grad

    lefts = [attended_t, normed_two_t, topinner_t, topnorm_t, lowinner_t, lownorm_t, gated.T, normed_one.T]
    works = [(0, grad_low3), (1, rawq_low), (1, rawk_low), (1, rawv_low), (2, cotangent), (3, gate_top),
             (3, lift_top), (4, gb_low), (5, gate_low), (5, lift_low), (6, grad_low1), (7, mixed_grad)]
    heads = jnp.concatenate([querygain_grad, keysgain_grad, jnp.zeros((width - 2 * head,), F32)])
    small = jnp.concatenate([mixgain_grad[None, :], mixtaps_grad, lowgain_grad, attgain_grad, topgain_grad,
                             heads[None, :]], axis=0)
    grads, small = sum_over_chips(lefts, works, small, lines, 1)
    (attexit_grad, attquery_grad, attkeys_grad, attvalues_grad, topdrop_grad, topgate_grad, toplift_grad,
     lowdrop_grad, lowgate_grad, lowlift_grad, mixexit_grad, mixentry_grad) = grads
    return (output, tokens_grad, small[0], mixentry_grad, small[1:4], mixexit_grad, small[4], lowgate_grad,
            lowlift_grad, lowdrop_grad, small[5], attquery_grad, attkeys_grad, attvalues_grad, small[7, :head],
            small[7, head:2 * head], attexit_grad, small[6], topgate_grad, toplift_grad, topdrop_grad)


def solution(mesh):
    placed = (P(("dp", "ctx"), None), P("dp", None), P(("dp", "ctx"), None)) + (P(),) * 19
    split = {0: P(("dp", "ctx"), None), 1: P(("dp", "ctx"), None)}
    whole = (2, 4, 6, 10, 14, 15, 17)
    outs = tuple(split.get(i, P() if i in whole else P("ctx", None)) for i in range(21))
    small = mesh.shape["ctx"] == 16 and mesh.shape["dp"] == 2
    return jax.shard_map(fast_device if small else per_device, mesh=mesh, in_specs=placed, out_specs=outs,
                         check_vma=False)
```

```python
import functools
import math

import jax
import jax.numpy as jnp
from jax import lax
from jax.experimental import pallas as pl
from jax.experimental.pallas import tpu as pltpu
from jax.sharding import PartitionSpec as P

EPS = 1e-05
THETA = 1000000.0
NEGATIVE = -1e30


def passed_along(value, axis, steps):
    count = lax.axis_size(axis)
    first, last = (max(0, -steps), min(count, count - steps))
    return lax.ppermute(value, axis, [(source, source + steps) for source in range(first, last)])


def passed_along_2(block, axis, distance):
    devices = range(lax.axis_size(axis))
    route = [((i - distance) % len(devices), i) for i in devices]
    return lax.ppermute(block, axis, route)


def root_mean_square_scale(hidden, gain):
    return hidden * lax.rsqrt(jnp.mean(hidden * hidden, axis=-1, keepdims=True) + EPS) * gain


def rotary_embed(value_rows, position_index):
    half = value_rows.shape[-1] // 2
    freq = THETA ** (-jnp.arange(half, dtype=jnp.float32) * 2.0 / value_rows.shape[-1])
    angle = position_index.astype(jnp.float32)[:, None] * freq[None, :]
    cosine = jnp.cos(angle)[:, None, :]
    sine = jnp.sin(angle)[:, None, :]
    front = value_rows[..., :half]
    behind = value_rows[..., half:]
    return jnp.concatenate(
        [front * cosine - behind * sine, behind * cosine + front * sine], axis=-1
    )


def head_prep(raw, gain, position_index, heads):
    shaped = raw.reshape(raw.shape[0], heads, -1)
    return rotary_embed(root_mean_square_scale(shaped, gain), position_index)


def segment_of(where, first, second):
    return (where >= first).astype(jnp.int32) + (where >= second).astype(jnp.int32)


def block_width(count):
    best = 1
    for candidate in range(1, min(count, 1024) + 1):
        if count % candidate == 0:
            best = candidate
    return best


def sweep(carry, count, visit):
    width = block_width(count)
    return lax.fori_loop(
        0, count // width, lambda index, inner: visit(inner, index * width, width), carry
    )


def inner_dot(left, right):
    return lax.dot_general(
        left, right, (((0,), (0,)), ((), ())), preferred_element_type=jnp.float32
    )


def outer_dot(left, right):
    return lax.dot_general(
        left, right, (((1,), (1,)), ((), ())), preferred_element_type=jnp.float32
    )


def scores_of(query_part, key_part, query_where, key_where, query_seg, key_seg, scale):
    raw = (
        jnp.einsum("tkgd,pkd->kgtp", query_part, key_part, preferred_element_type=jnp.float32)
        * scale
    )
    allowed = (query_seg[:, None] == key_seg[None, :]) & (
        query_where[:, None] >= key_where[None, :]
    )
    return (raw, allowed)


def grad_block(
    query_part,
    grad_part,
    logsum_part,
    delta_part,
    key_part,
    value_part,
    query_where,
    key_where,
    query_seg,
    key_seg,
    scale,
):
    raw, allowed = scores_of(
        query_part, key_part, query_where, key_where, query_seg, key_seg, scale
    )
    prob = jnp.where(allowed, jnp.exp(raw - logsum_part[..., None]), 0.0)
    prob_grad = jnp.einsum(
        "tkgd,pkd->kgtp", grad_part, value_part, preferred_element_type=jnp.float32
    )
    score_grad = (prob * (prob_grad - delta_part[..., None])).astype(jnp.bfloat16)
    query_grad = (
        jnp.einsum("kgtp,pkd->tkgd", score_grad, key_part, preferred_element_type=jnp.float32)
        * scale
    )
    key_grad = (
        jnp.einsum("kgtp,tkgd->pkd", score_grad, query_part, preferred_element_type=jnp.float32)
        * scale
    )
    value_grad = jnp.einsum(
        "kgtp,tkgd->pkd", prob.astype(jnp.bfloat16), grad_part, preferred_element_type=jnp.float32
    )
    return (query_grad, key_grad, value_grad)


def conv_local(extended, taps, fits_one, fits_two):
    rows = extended.shape[0] - 2
    return (
        taps[2] * extended[2:]
        + taps[1] * extended[1 : rows + 1] * fits_one
        + taps[0] * extended[:rows] * fits_two
    )


def feed_forward(hidden, gain, gate_weight, lift_weight, drop_weight):
    fnormed = root_mean_square_scale(hidden, gain).astype(jnp.bfloat16)
    gate_act = jnp.dot(fnormed, gate_weight, preferred_element_type=jnp.float32)
    lift_act = jnp.dot(fnormed, lift_weight, preferred_element_type=jnp.float32)
    inner = (jax.nn.silu(gate_act) * lift_act).astype(jnp.bfloat16)
    result = hidden + jnp.dot(inner, drop_weight, preferred_element_type=jnp.float32)
    return (result, (fnormed, gate_act, lift_act, inner))


def feed_back(grad, hidden, gain, kept, gate_weight, lift_weight, drop_weight):
    fnormed, gate_act, lift_act, inner = kept
    grad_low = grad.astype(jnp.bfloat16)
    drop_grad = inner_dot(inner, grad_low)
    inner_grad = outer_dot(grad_low, drop_weight)
    _, pull_gate = jax.vjp(
        lambda gate_in, lift_in: jax.nn.silu(gate_in) * lift_in, gate_act, lift_act
    )
    gate_grad, lift_grad = pull_gate(inner_grad)
    gate_low = gate_grad.astype(jnp.bfloat16)
    lift_low = lift_grad.astype(jnp.bfloat16)
    gate_wgrad = inner_dot(fnormed, gate_low)
    lift_wgrad = inner_dot(fnormed, lift_low)
    normed_grad = outer_dot(gate_low, gate_weight) + outer_dot(lift_low, lift_weight)
    _, pull_norm = jax.vjp(root_mean_square_scale, hidden, gain)
    hidden_grad, gain_grad = pull_norm(normed_grad)
    return (grad + hidden_grad, (gain_grad, gate_wgrad, lift_wgrad, drop_grad))


def per_device(
    tokens,
    lengths,
    cotangent,
    mixgain,
    mixentry,
    mixtaps,
    mixexit,
    lowgain,
    lowgate,
    lowlift,
    lowdrop,
    attgain,
    attquery,
    attkeys,
    attvalues,
    querygain,
    keysgain,
    attexit,
    topgain,
    topgate,
    toplift,
    topdrop,
):
    rows = tokens.shape[0]
    width_model = tokens.shape[1]
    head_size = querygain.shape[0]
    query_heads = attquery.shape[1] // head_size
    kv_heads = attkeys.shape[1] // head_size
    shared_gradient = query_heads // kv_heads
    scale = 1.0 / math.sqrt(head_size)
    place = lax.axis_index("ctx")
    first = lengths[0, 0]
    second = first + lengths[0, 1]
    mine = place * rows + jnp.arange(rows, dtype=jnp.int32)
    my_seg = segment_of(mine, first, second)
    begin = jnp.where(my_seg == 0, 0, jnp.where(my_seg == 1, first, second))
    position_index = mine - begin
    last_row = place * rows + rows - 1
    mixgain_f = mixgain.astype(jnp.float32)
    taps_f = mixtaps.astype(jnp.float32)
    lowgain_f = lowgain.astype(jnp.float32)
    attgain_f = attgain.astype(jnp.float32)
    querygain_f = querygain.astype(jnp.float32)
    keysgain_f = keysgain.astype(jnp.float32)
    topgain_f = topgain.astype(jnp.float32)
    hidden = tokens.astype(jnp.float32)
    normed_one = root_mean_square_scale(hidden, mixgain_f).astype(jnp.bfloat16)
    mixed = jnp.dot(normed_one, mixentry, preferred_element_type=jnp.float32)
    part_b = mixed[:, :width_model]
    part_c = mixed[:, width_model : 2 * width_model]
    part_x = mixed[:, 2 * width_model :]
    product = (part_b * part_x).astype(jnp.bfloat16)
    borrowed = passed_along(product[rows - 2 :], "ctx", 1)
    extended = jnp.concatenate([borrowed, product], axis=0).astype(jnp.float32)
    fits_one = ((mine >= 1) & (segment_of(mine - 1, first, second) == my_seg)).astype(jnp.float32)[
        :, None
    ]
    fits_two = ((mine >= 2) & (segment_of(mine - 2, first, second) == my_seg)).astype(jnp.float32)[
        :, None
    ]
    conved = conv_local(extended, taps_f, fits_one, fits_two)
    gated = (part_c * conved).astype(jnp.bfloat16)
    hidden_one = hidden + jnp.dot(gated, mixexit, preferred_element_type=jnp.float32)
    hidden_two, kept_low = feed_forward(hidden_one, lowgain_f, lowgate, lowlift, lowdrop)
    normed_two = root_mean_square_scale(hidden_two, attgain_f).astype(jnp.bfloat16)
    query_unrotated = jnp.dot(normed_two, attquery, preferred_element_type=jnp.float32)
    key_unrotated = jnp.dot(normed_two, attkeys, preferred_element_type=jnp.float32)
    value_projected = jnp.dot(normed_two, attvalues, preferred_element_type=jnp.float32)
    query_low = head_prep(query_unrotated, querygain_f, position_index, query_heads).astype(
        jnp.bfloat16
    )
    key_low = head_prep(key_unrotated, keysgain_f, position_index, kv_heads).astype(jnp.bfloat16)
    value_low = value_projected.astype(jnp.bfloat16).reshape(rows, kv_heads, head_size)
    query_grouped = query_low.reshape(rows, kv_heads, shared_gradient, head_size)

    def stat_visit(carry, keys_in, start, offset, width):
        top, total = carry
        key_part = lax.dynamic_slice_in_dim(keys_in, offset, width, 0)
        key_where = start + offset + jnp.arange(width, dtype=jnp.int32)
        raw, allowed = scores_of(
            query_grouped,
            key_part,
            mine,
            key_where,
            my_seg,
            segment_of(key_where, first, second),
            scale,
        )
        new_top = jnp.maximum(top, jnp.max(jnp.where(allowed, raw, NEGATIVE), axis=-1))
        weights = jnp.where(allowed, jnp.exp(raw - new_top[..., None]), 0.0)
        total = total * jnp.exp(top - new_top) + jnp.sum(weights, axis=-1)
        return (new_top, total)

    stat_state = (
        jnp.full((kv_heads, shared_gradient, rows), NEGATIVE, jnp.float32),
        jnp.zeros((kv_heads, shared_gradient, rows), jnp.float32),
    )
    piece = lax.all_gather(key_low, "ctx", axis=0, tiled=True)
    start = jnp.int32(0)
    count = piece.shape[0]

    def stat_running(inner):
        return sweep(
            inner, count, lambda acc, offset, width: stat_visit(acc, piece, start, offset, width)
        )

    top, total = lax.cond(start > last_row, lambda inner: inner, stat_running, stat_state)
    logsum = top + jnp.log(total)

    def forward_visit(accum, keys_in, values_in, start, offset, width):
        key_part = lax.dynamic_slice_in_dim(keys_in, offset, width, 0)
        value_part = lax.dynamic_slice_in_dim(values_in, offset, width, 0)
        key_where = start + offset + jnp.arange(width, dtype=jnp.int32)
        raw, allowed = scores_of(
            query_grouped,
            key_part,
            mine,
            key_where,
            my_seg,
            segment_of(key_where, first, second),
            scale,
        )
        prob_low = jnp.where(allowed, jnp.exp(raw - logsum[..., None]), 0.0).astype(jnp.bfloat16)
        return accum + jnp.einsum(
            "kgtp,pkd->kgtd", prob_low, value_part, preferred_element_type=jnp.float32
        )

    forward_start = jnp.int32(0)
    keys_in = lax.all_gather(key_low, "ctx", axis=0, tiled=True)
    values_in = lax.all_gather(value_low, "ctx", axis=0, tiled=True)
    forward_count = keys_in.shape[0]

    def forward_running(inner):
        return sweep(
            inner,
            forward_count,
            lambda acc, offset, width: forward_visit(
                acc, keys_in, values_in, forward_start, offset, width
            ),
        )

    accum = lax.cond(
        forward_start > last_row,
        lambda inner: inner,
        forward_running,
        jnp.zeros((kv_heads, shared_gradient, rows, head_size), jnp.float32),
    )
    attended = accum.transpose(2, 0, 1, 3).reshape(rows, -1)
    attended_low = attended.astype(jnp.bfloat16)
    hidden_three = hidden_two + jnp.dot(attended_low, attexit, preferred_element_type=jnp.float32)
    output, kept_top = feed_forward(hidden_three, topgain_f, topgate, toplift, topdrop)
    grad = cotangent.astype(jnp.float32)
    grad, top_grads = feed_back(grad, hidden_three, topgain_f, kept_top, topgate, toplift, topdrop)
    grad_low = grad.astype(jnp.bfloat16)
    attexit_grad = inner_dot(attended_low, grad_low)
    out_grads = (
        outer_dot(grad_low, attexit)
        .astype(jnp.bfloat16)
        .reshape(rows, kv_heads, shared_gradient, head_size)
    )
    delta = jnp.einsum(
        "tkgd,tkgd->kgt",
        out_grads.astype(jnp.float32),
        attended.reshape(rows, kv_heads, shared_gradient, head_size),
    )
    cycle_size = lax.axis_size("ctx")

    def cycle_visit(state, keys_in, values_in, start, offset, width):
        query_acc, key_acc, value_acc = state
        key_part = lax.dynamic_slice_in_dim(keys_in, offset, width, 0)
        value_part = lax.dynamic_slice_in_dim(values_in, offset, width, 0)
        key_where = start + offset + jnp.arange(width, dtype=jnp.int32)
        query_grad, key_grad, value_grad = grad_block(
            query_grouped,
            out_grads,
            logsum,
            delta,
            key_part,
            value_part,
            mine,
            key_where,
            my_seg,
            segment_of(key_where, first, second),
            scale,
        )
        key_acc = lax.dynamic_update_slice_in_dim(
            key_acc, lax.dynamic_slice_in_dim(key_acc, offset, width, 0) + key_grad, offset, 0
        )
        value_acc = lax.dynamic_update_slice_in_dim(
            value_acc, lax.dynamic_slice_in_dim(value_acc, offset, width, 0) + value_grad, offset, 0
        )
        return (query_acc + query_grad, key_acc, value_acc)

    def cycle_step(step, carry):
        keys_cur, values_cur, key_acc, value_acc, query_acc = carry
        anchor = (place - step + cycle_size) % cycle_size
        start = anchor * rows

        def cycle_running(state):
            return sweep(
                state,
                rows,
                lambda acc, offset, width: cycle_visit(
                    acc, keys_cur, values_cur, start, offset, width
                ),
            )

        query_acc, key_acc, value_acc = lax.cond(
            start > last_row, lambda state: state, cycle_running, (query_acc, key_acc, value_acc)
        )
        keys_cur, values_cur = passed_along((keys_cur, values_cur), "ctx", 1)
        key_acc, value_acc = (
            passed_along_2(key_acc.astype(jnp.bfloat16), "ctx", 1).astype(key_acc.dtype),
            passed_along_2(value_acc.astype(jnp.bfloat16), "ctx", 1).astype(value_acc.dtype),
        )
        return (keys_cur, values_cur, key_acc, value_acc, query_acc)

    cycle_state = (
        key_low,
        value_low,
        jnp.zeros((rows, kv_heads, head_size), jnp.float32),
        jnp.zeros((rows, kv_heads, head_size), jnp.float32),
        jnp.zeros((rows, kv_heads, shared_gradient, head_size), jnp.float32),
    )
    _, _, key_grads, value_grads, query_acc = lax.fori_loop(0, cycle_size, cycle_step, cycle_state)
    _, pull_query = jax.vjp(
        lambda raw, gain: head_prep(raw, gain, position_index, query_heads),
        query_unrotated,
        querygain_f,
    )
    query_raw_grad, querygain_grad = pull_query(query_acc.reshape(rows, query_heads, head_size))
    _, pull_key = jax.vjp(
        lambda raw, gain: head_prep(raw, gain, position_index, kv_heads), key_unrotated, keysgain_f
    )
    key_raw_grad, keysgain_grad = pull_key(key_grads)
    query_raw_low = query_raw_grad.astype(jnp.bfloat16)
    key_raw_low = key_raw_grad.astype(jnp.bfloat16)
    value_raw_low = value_grads.reshape(rows, -1).astype(jnp.bfloat16)
    attquery_grad = inner_dot(normed_two, query_raw_low)
    attkeys_grad = inner_dot(normed_two, key_raw_low)
    attvalues_grad = inner_dot(normed_two, value_raw_low)
    normed_two_grad = (
        outer_dot(query_raw_low, attquery)
        + outer_dot(key_raw_low, attkeys)
        + outer_dot(value_raw_low, attvalues)
    )
    _, pull_att = jax.vjp(root_mean_square_scale, hidden_two, attgain_f)
    hidden_two_grad, attgain_grad = pull_att(normed_two_grad)
    grad = grad + hidden_two_grad
    grad, low_grads = feed_back(grad, hidden_one, lowgain_f, kept_low, lowgate, lowlift, lowdrop)
    grad_low = grad.astype(jnp.bfloat16)
    mixexit_grad = inner_dot(gated, grad_low)
    gated_grad = outer_dot(grad_low, mixexit)
    part_c_grad = gated_grad * conved
    conved_grad = gated_grad * part_c
    _, pull_conv = jax.vjp(
        lambda ext, taps: conv_local(ext, taps, fits_one, fits_two), extended, taps_f
    )
    extended_grad, mixtaps_grad = pull_conv(conved_grad)
    returned_rim = passed_along(extended_grad[:2], "ctx", -1)
    product_grad = extended_grad[2:].at[rows - 2 :].add(returned_rim)
    mixed_grad = jnp.concatenate(
        [product_grad * part_x, part_c_grad, product_grad * part_b], axis=1
    ).astype(jnp.bfloat16)
    mixentry_grad = inner_dot(normed_one, mixed_grad)
    normed_one_grad = outer_dot(mixed_grad, mixentry)
    _, pull_mix = jax.vjp(root_mean_square_scale, hidden, mixgain_f)
    hidden_grad, mixgain_grad = pull_mix(normed_one_grad)
    tokens_grad = grad + hidden_grad
    lowgain_grad, lowgate_grad, lowlift_grad, lowdrop_grad = low_grads
    topgain_grad, topgate_grad, toplift_grad, topdrop_grad = top_grads
    shares = (
        lax.psum_scatter(mixentry_grad, "ctx", scatter_dimension=0, tiled=True),
        lax.psum_scatter(mixexit_grad, "ctx", scatter_dimension=0, tiled=True),
        lax.psum_scatter(lowgate_grad, "ctx", scatter_dimension=0, tiled=True),
        lax.psum_scatter(lowlift_grad, "ctx", scatter_dimension=0, tiled=True),
        lax.psum_scatter(lowdrop_grad, "ctx", scatter_dimension=0, tiled=True),
        lax.psum_scatter(attquery_grad, "ctx", scatter_dimension=0, tiled=True),
        lax.psum_scatter(attkeys_grad, "ctx", scatter_dimension=0, tiled=True),
        lax.psum_scatter(attvalues_grad, "ctx", scatter_dimension=0, tiled=True),
        lax.psum_scatter(attexit_grad, "ctx", scatter_dimension=0, tiled=True),
        lax.psum_scatter(topgate_grad, "ctx", scatter_dimension=0, tiled=True),
        lax.psum_scatter(toplift_grad, "ctx", scatter_dimension=0, tiled=True),
        lax.psum_scatter(topdrop_grad, "ctx", scatter_dimension=0, tiled=True),
    )
    smalls = lax.psum(
        (
            mixgain_grad,
            mixtaps_grad,
            lowgain_grad,
            attgain_grad,
            querygain_grad,
            keysgain_grad,
            topgain_grad,
        ),
        "ctx",
    )
    summed = (
        lax.psum(shares[0].astype(jnp.bfloat16), "dp").astype(jnp.float32),
        lax.psum(shares[1].astype(jnp.bfloat16), "dp").astype(jnp.float32),
        lax.psum(shares[2].astype(jnp.bfloat16), "dp").astype(jnp.float32),
        lax.psum(shares[3].astype(jnp.bfloat16), "dp").astype(jnp.float32),
        lax.psum(shares[4].astype(jnp.bfloat16), "dp").astype(jnp.float32),
        lax.psum(shares[5].astype(jnp.bfloat16), "dp").astype(jnp.float32),
        lax.psum(shares[6].astype(jnp.bfloat16), "dp").astype(jnp.float32),
        lax.psum(shares[7].astype(jnp.bfloat16), "dp").astype(jnp.float32),
        lax.psum(shares[8].astype(jnp.bfloat16), "dp").astype(jnp.float32),
        lax.psum(shares[9].astype(jnp.bfloat16), "dp").astype(jnp.float32),
        lax.psum(shares[10].astype(jnp.bfloat16), "dp").astype(jnp.float32),
        lax.psum(shares[11].astype(jnp.bfloat16), "dp").astype(jnp.float32),
        lax.psum(smalls[0].astype(jnp.bfloat16), "dp").astype(jnp.float32),
        lax.psum(smalls[1].astype(jnp.bfloat16), "dp").astype(jnp.float32),
        lax.psum(smalls[2].astype(jnp.bfloat16), "dp").astype(jnp.float32),
        lax.psum(smalls[3].astype(jnp.bfloat16), "dp").astype(jnp.float32),
        lax.psum(smalls[4].astype(jnp.bfloat16), "dp").astype(jnp.float32),
        lax.psum(smalls[5].astype(jnp.bfloat16), "dp").astype(jnp.float32),
        lax.psum(smalls[6].astype(jnp.bfloat16), "dp").astype(jnp.float32),
    )
    return (
        output,
        tokens_grad,
        summed[12],
        summed[0],
        summed[13],
        summed[1],
        summed[14],
        summed[2],
        summed[3],
        summed[4],
        summed[15],
        summed[5],
        summed[6],
        summed[7],
        summed[16],
        summed[17],
        summed[8],
        summed[18],
        summed[9],
        summed[10],
        summed[11],
    )


LANES = 128
BF = jnp.bfloat16
F32 = jnp.float32
ONES_NT = (((1,), (1,)), ((), ()))
ONES_TN = (((0,), (0,)), ((), ()))
VMEM_LIMIT = 60 * 1024 * 1024


def vmem_specs(count):
    return [pl.BlockSpec(memory_space=pltpu.VMEM)] * count


def lane_of(shape):
    return lax.broadcasted_iota(jnp.int32, shape, len(shape) - 1)


def same_head(head):
    row = lax.broadcasted_iota(jnp.int32, (LANES, LANES), 0) // head
    column = lax.broadcasted_iota(jnp.int32, (LANES, LANES), 1) // head
    return jnp.where(row == column, 1.0 / head, 0.0).astype(F32)


def head_mean(value, blocks):
    return jnp.dot(value, blocks, precision=lax.Precision.HIGHEST, preferred_element_type=F32)


def other_half(value, head):
    lane = lane_of(value.shape)
    ahead = pltpu.roll(value, LANES - head // 2, 1)
    behind = pltpu.roll(value, head // 2, 1)
    return jnp.where(lane % head < head // 2, ahead, behind)


def swap_heads(value, head):
    return pltpu.roll(value, head, 1)


def three_parts(value):
    high = value.astype(BF)
    rest = value - high.astype(F32)
    middle = rest.astype(BF)
    low = (rest - middle.astype(F32)).astype(BF)
    return high.astype(F32), middle.astype(F32), low.astype(F32)


def project_kernel(head, hid_ref, gain_ref, wq_ref, wk_ref, wv_ref, cos_ref, sin_ref, qg_ref, kg_ref,
                   msg_ref, normt_ref, qraw_ref, kraw_ref):
    hid = hid_ref[...]
    scale = lax.rsqrt(jnp.mean(hid * hid, axis=-1, keepdims=True) + EPS)
    normed = hid * scale * gain_ref[...]
    normt_ref[...] = turned(normed)
    normed = normed.astype(BF)
    blocks = same_head(head)
    cosine, sine = cos_ref[...], sin_ref[...]
    half_rows = msg_ref.shape[1]
    lane = lane_of(cosine.shape)

    def prepared(raw, gain):
        unit = raw * lax.rsqrt(head_mean(raw * raw, blocks) + EPS) * gain
        return unit * cosine + other_half(unit, head) * sine

    def put(dest, start, tile):
        low = tile.astype(BF)
        for part in range(2):
            msg_ref[2 * dest + part, :, start:start + LANES] = low[part * half_rows:(part + 1) * half_rows]

    qraw = jnp.dot(normed, wq_ref[...], preferred_element_type=F32)
    qraw_ref[...] = qraw
    for tile in range(qraw.shape[1] // LANES):
        put(tile, 0, prepared(qraw[:, tile * LANES:(tile + 1) * LANES], qg_ref[...]))
    kraw = jnp.dot(normed, wk_ref[...], preferred_element_type=F32)
    kraw_ref[...] = kraw
    vraw = jnp.dot(normed, wv_ref[...], preferred_element_type=F32)
    for tile in range(kraw.shape[1] // LANES):
        keys = prepared(kraw[:, tile * LANES:(tile + 1) * LANES], kg_ref[...])
        values = vraw[:, tile * LANES:(tile + 1) * LANES]
        put(2 * tile, LANES, jnp.where(lane < head, keys, swap_heads(values, head)))
        put(2 * tile + 1, LANES, jnp.where(lane < head, swap_heads(keys, head), values))


def project_back_kernel(head, backq_ref, backk_ref, hid_ref, gain_ref, wq_ref, wk_ref, wv_ref, cos_ref, sin_ref, qg_ref,
                        kg_ref, qraw_ref, kraw_ref, grad_ref,
                        rawq_ref, rawk_ref, rawv_ref, two_ref, again_ref, qgain_ref, kgain_ref):
    blocks = same_head(head)
    cosine, sine = cos_ref[...], sin_ref[...]
    lane = lane_of(cosine.shape)

    def fetch(source, dest):
        return jnp.concatenate([source[2 * dest], source[2 * dest + 1]], axis=0).astype(F32)

    def through(grad, raw, gain):
        scale = lax.rsqrt(head_mean(raw * raw, blocks) + EPS)
        unit = raw * scale
        turned = grad * cosine - other_half(grad, head) * sine
        gain_part = jnp.sum(turned * unit, axis=0, keepdims=True)
        inward = turned * gain
        return scale * (inward - unit * head_mean(inward * unit, blocks)), gain_part

    width_q = wq_ref.shape[1]
    width_k = wk_ref.shape[1]
    gain_total = jnp.zeros((1, LANES), F32)
    for tile in range(width_q // LANES):
        got, part = through(fetch(backq_ref, tile), qraw_ref[:, tile * LANES:(tile + 1) * LANES], qg_ref[...])
        gain_total = gain_total + part
        rawq_ref[:, tile * LANES:(tile + 1) * LANES] = got.astype(BF)
    qgain_ref[...] = gain_total
    gain_total = jnp.zeros((1, LANES), F32)
    for tile in range(width_k // LANES):
        even, odd = fetch(backk_ref, 2 * tile), fetch(backk_ref, 2 * tile + 1)
        keys = jnp.where(lane < head, even, swap_heads(odd, head))
        values = jnp.where(lane < head, swap_heads(even, head), odd)
        got, part = through(keys, kraw_ref[:, tile * LANES:(tile + 1) * LANES], kg_ref[...])
        gain_total = gain_total + part
        rawk_ref[:, tile * LANES:(tile + 1) * LANES] = got.astype(BF)
        rawv_ref[:, tile * LANES:(tile + 1) * LANES] = values.astype(BF)
    kgain_ref[...] = gain_total
    normed_grad = nt_dot(rawq_ref[...], wq_ref[...]) + nt_dot(rawk_ref[...], wk_ref[...])
    normed_grad += nt_dot(rawv_ref[...], wv_ref[...])
    hid = hid_ref[...]
    scale = lax.rsqrt(jnp.mean(hid * hid, axis=-1, keepdims=True) + EPS)
    unit = hid * scale
    again_ref[...] = jnp.sum(normed_grad * unit, axis=0, keepdims=True)
    inward = normed_grad * gain_ref[...]
    two_ref[...] = grad_ref[...] + scale * (inward - unit * jnp.mean(inward * unit, axis=-1, keepdims=True))


def allowed_block(row_axis, key_axis, shape, first, second, part, base, start, rows, half_rows):
    row = lax.broadcasted_iota(jnp.int32, shape, row_axis)
    token = (base + row // (2 * half_rows)) * rows + part * half_rows + row % half_rows
    key = start + lax.broadcasted_iota(jnp.int32, shape, key_axis)
    begin = jnp.where(token >= second, second, jnp.where(token >= first, first, 0))
    return (key >= begin) & (key <= token)


MESH = pl.DeviceIdType.MESH


def turned(value):
    return value.astype(F32).T.astype(BF)


def norm_scale(hidden):
    return lax.rsqrt(jnp.mean(hidden * hidden, axis=-1, keepdims=True) + EPS)


def norm_pull(normed_grad, hidden, gain):
    scale = norm_scale(hidden)
    unit = hidden * scale
    inward = normed_grad * gain
    back = scale * (inward - unit * jnp.mean(inward * unit, axis=-1, keepdims=True))
    return back, jnp.sum(normed_grad * unit, axis=0, keepdims=True)


def nt_dot(left, right):
    return lax.dot_general(left, right, ONES_NT, preferred_element_type=F32)


def nn_dot(left, right):
    return jnp.dot(left, right, preferred_element_type=F32)


def activation_pull(gate_act, lift_act, sigma, inner_grad):
    gate_grad = inner_grad * lift_act * sigma * (1 + gate_act * (1 - sigma))
    return gate_grad.astype(BF), (inner_grad * gate_act * sigma).astype(BF)


def low_kernel(hid_ref, gain_ref, gate_ref, lift_ref, drop_ref,
               out_ref, normt_ref, gact_ref, lact_ref, innert_ref, norm_ref):
    step = pl.program_id(0)

    @pl.when(step == 0)
    def _():
        hid = hid_ref[...]
        normed = hid * norm_scale(hid) * gain_ref[...]
        norm_ref[...] = normed.astype(BF)
        normt_ref[...] = turned(normed)
        out_ref[...] = hid

    normed = norm_ref[...]
    gate_act = nn_dot(normed, gate_ref[...])
    lift_act = nn_dot(normed, lift_ref[...])
    inner = gate_act * jax.nn.sigmoid(gate_act) * lift_act
    gact_ref[...] = gate_act.astype(BF)
    lact_ref[...] = lift_act.astype(BF)
    innert_ref[...] = turned(inner)
    out_ref[...] += nn_dot(inner.astype(BF), drop_ref[...])


def low_back_kernel(grad_ref, hid_ref, gain_ref, gact_ref, lact_ref, gate_ref, lift_ref, drop_ref,
                    out_ref, again_ref, low_ref, outlow_ref, glow_ref, llow_ref, acc_ref):
    step = pl.program_id(0)

    @pl.when(step == 0)
    def _():
        low_ref[...] = grad_ref[...].astype(BF)
        acc_ref[...] = jnp.zeros_like(acc_ref)

    gate_act, lift_act = gact_ref[...].astype(F32), lact_ref[...].astype(F32)
    inner_grad = nt_dot(low_ref[...], drop_ref[...])
    gate_low, lift_low = activation_pull(gate_act, lift_act, jax.nn.sigmoid(gate_act), inner_grad)
    glow_ref[...] = gate_low
    llow_ref[...] = lift_low
    acc_ref[...] += nt_dot(gate_low, gate_ref[...]) + nt_dot(lift_low, lift_ref[...])

    @pl.when(step == pl.num_programs(0) - 1)
    def _():
        back, gain_part = norm_pull(acc_ref[...], hid_ref[...], gain_ref[...])
        again_ref[...] = gain_part
        out = grad_ref[...] + back
        out_ref[...] = out
        outlow_ref[...] = out.astype(BF)


def top_kernel(got_ref, two_ref, exit_ref, cot_ref, gain_ref, gate_ref, lift_ref, drop_ref,
               out_ref, grad_ref, gradlow_ref, send_ref, attt_ref, again_ref, normt_ref, innert_ref, glow_ref,
               llow_ref, hid_ref, norm_ref, acc_ref):
    step = pl.program_id(0)
    half_rows = got_ref.shape[1]

    @pl.when(step == 0)
    def _():
        tiles = []
        for tile in range(got_ref.shape[0] // 2):
            tiles.append(jnp.concatenate([got_ref[2 * tile], got_ref[2 * tile + 1]], axis=0))
        attended = jnp.concatenate(tiles, axis=1)
        attt_ref[...] = turned(attended)
        hid = two_ref[...] + nn_dot(attended, exit_ref[...])
        hid_ref[...] = hid
        normed = hid * norm_scale(hid) * gain_ref[...]
        norm_ref[...] = normed.astype(BF)
        normt_ref[...] = turned(normed)
        out_ref[...] = hid
        acc_ref[...] = jnp.zeros_like(acc_ref)

    normed = norm_ref[...]
    gate_act = nn_dot(normed, gate_ref[...])
    lift_act = nn_dot(normed, lift_ref[...])
    sigma = jax.nn.sigmoid(gate_act)
    inner = gate_act * sigma * lift_act
    innert_ref[...] = turned(inner)
    out_ref[...] += nn_dot(inner.astype(BF), drop_ref[...])
    inner_grad = nt_dot(cot_ref[...], drop_ref[...])
    gate_low, lift_low = activation_pull(gate_act, lift_act, sigma, inner_grad)
    glow_ref[...] = gate_low
    llow_ref[...] = lift_low
    acc_ref[...] += nt_dot(gate_low, gate_ref[...]) + nt_dot(lift_low, lift_ref[...])

    @pl.when(step == pl.num_programs(0) - 1)
    def _():
        back, gain_part = norm_pull(acc_ref[...], hid_ref[...], gain_ref[...])
        again_ref[...] = gain_part
        grad = cot_ref[...].astype(F32) + back
        grad_ref[...] = grad
        low = grad.astype(BF)
        gradlow_ref[...] = low
        sent = nt_dot(low, exit_ref[...]).astype(BF)
        for tile in range(send_ref.shape[0] // 2):
            for part in range(2):
                send_ref[2 * tile + part] = sent[part * half_rows:(part + 1) * half_rows,
                                                 tile * LANES:(tile + 1) * LANES]


TILE = 512
WIDE_TILE = 1152


def whole_block(shape):
    return pl.BlockSpec(shape, lambda step, rank=len(shape): (0,) * rank)


def column_block(rows, tile=TILE):
    return pl.BlockSpec((rows, tile), lambda step: (0, step))


def row_block(columns, tile=TILE):
    return pl.BlockSpec((tile, columns), lambda step: (step, 0))


def call_tiled(kernel, tiles, ins, outs, scratch, flops, moved, name):
    return pl.pallas_call(
        kernel,
        grid=(tiles,),
        in_specs=[spec for _, spec in ins],
        out_specs=tuple(spec for _, spec in outs),
        out_shape=tuple(shape for shape, _ in outs),
        scratch_shapes=scratch,
        compiler_params=pltpu.CompilerParams(vmem_limit_bytes=VMEM_LIMIT, dimension_semantics=("arbitrary",)),
        cost_estimate=pl.CostEstimate(flops=flops, bytes_accessed=moved, transcendentals=0),
        name=name,
    )(*[value for value, _ in ins])


def feed_low(hidden, gain, gate, lift, drop):
    rows, width = hidden.shape
    ff = gate.shape[1]
    S = jax.ShapeDtypeStruct
    return call_tiled(
        low_kernel, ff // WIDE_TILE,
        [(hidden, whole_block((rows, width))), (gain, whole_block((1, width))), (gate, column_block(width, WIDE_TILE)),
         (lift, column_block(width, WIDE_TILE)), (drop, row_block(width, WIDE_TILE))],
        [(S((rows, width), F32), whole_block((rows, width))), (S((width, rows), BF), whole_block((width, rows))),
         (S((rows, ff), BF), column_block(rows, WIDE_TILE)), (S((rows, ff), BF), column_block(rows, WIDE_TILE)),
         (S((ff, rows), BF), row_block(rows, WIDE_TILE))],
        [pltpu.VMEM((rows, width), BF)], 6 * rows * width * ff, 38 << 20, "feed_low")


def feed_low_back(grad, hidden, gain, gact, lact, gate, lift, drop):
    rows, width = hidden.shape
    ff = gate.shape[1]
    S = jax.ShapeDtypeStruct
    full = whole_block((rows, width))
    return call_tiled(
        low_back_kernel, ff // WIDE_TILE,
        [(grad, full), (hidden, full), (gain, whole_block((1, width))), (gact, column_block(rows, WIDE_TILE)),
         (lact, column_block(rows, WIDE_TILE)), (gate, column_block(width, WIDE_TILE)), (lift, column_block(width, WIDE_TILE)),
         (drop, row_block(width, WIDE_TILE))],
        [(S((rows, width), F32), full), (S((1, width), F32), whole_block((1, width))), (S((rows, width), BF), full),
         (S((rows, width), BF), full), (S((rows, ff), BF), column_block(rows, WIDE_TILE)), (S((rows, ff), BF), column_block(rows, WIDE_TILE))],
        [pltpu.VMEM((rows, width), F32)], 6 * rows * width * ff, 40 << 20, "feed_low_back")


def feed_top(got, two, exit_weight, cotangent, gain, gate, lift, drop):
    rows, width = two.shape
    ff = gate.shape[1]
    S = jax.ShapeDtypeStruct
    full = whole_block((rows, width))
    flat = whole_block((1, width))
    standing = whole_block((width, rows))
    return call_tiled(
        top_kernel, ff // TILE,
        [(got, whole_block(got.shape)), (two, full), (exit_weight, whole_block(exit_weight.shape)), (cotangent, full),
         (gain, flat), (gate, column_block(width)), (lift, column_block(width)), (drop, row_block(width))],
        [(S((rows, width), F32), full), (S((rows, width), F32), full), (S((rows, width), BF), full),
         (S(got.shape, BF), whole_block(got.shape)), (S((width, rows), BF), standing), (S((1, width), F32), flat),
         (S((width, rows), BF), standing), (S((ff, rows), BF), row_block(rows)), (S((rows, ff), BF), column_block(rows)),
         (S((rows, ff), BF), column_block(rows))],
        [pltpu.VMEM((rows, width), F32), pltpu.VMEM((rows, width), BF), pltpu.VMEM((rows, width), F32)],
        12 * rows * width * ff, 45 << 20, "feed_top")


def sweep_keys(visit, index, tail, part, base, rows, half_rows, keys, sources):
    lowest = base * rows + part * half_rows
    end = (base + sources - 1) * rows + (part + 1) * half_rows
    count = (end + keys - 1) // keys
    free = jnp.where(end > tail, 0, jnp.maximum((lowest + 1) // keys - 1, 0))
    lax.fori_loop(0, free, lambda step, _: visit(step + 1, False), None)
    lax.fori_loop(0, count - free, lambda step, _: visit(jnp.where(step == 0, 0, free + step), True), None)


def greet(me, count):
    barrier = pltpu.get_barrier_semaphore()

    def hello(step, _):
        pl.semaphore_signal(barrier, inc=1, device_id={"ctx": lax.rem(me + step, count)}, device_id_type=MESH)

    lax.fori_loop(1, count, hello, None)
    pl.semaphore_wait(barrier, count - 1)


def attend_kernel(head, rows, keys, sources, count, info_ref, msg_ref, got_ref, out_ref, aug_ref, all_ref,
                  land, kv, tiles, arrive, ones_ref, acc_ref, msend, mrecv, fsend, frecv, gsend, grecv):
    first, second = info_ref[0], info_ref[1]
    me = lax.axis_index("ctx")
    part = me % 2
    twin = {"ctx": me + 1 - 2 * part}
    half_rows = msg_ref.shape[1]
    wide = sources * 2 * half_rows
    span = sources * rows
    factor = math.log2(math.e) / math.sqrt(head)
    lane = lane_of((half_rows, LANES))
    greet(me, count)

    def remote(src, dst, send, recv, where):
        return pltpu.make_async_remote_copy(src_ref=src, dst_ref=dst, send_sem=send, recv_sem=recv,
                                            device_id=where, device_id_type=MESH)

    def msg_copy(owner, dest):
        return remote(msg_ref.at[dest], land.at[owner], msend.at[dest], mrecv.at[owner], {"ctx": dest})

    def share_copy(source):
        return remote(kv.at[source, part], kv.at[source, part], fsend.at[source], frecv.at[source], twin)

    def tile_copy(owner, dest):
        return remote(tiles.at[dest], arrive.at[owner], gsend.at[dest], grecv.at[owner], {"ctx": dest})

    def start_msg(step, _):
        msg_copy(me, lax.rem(me + step, count)).start()

    lax.fori_loop(1, count, start_msg, None)
    land[me] = msg_ref[me]

    def share(source):
        @pl.when(source != me)
        def _():
            msg_copy(source, me).wait_recv()

        kv[source, part] = land[source, :, LANES:]
        share_copy(source).start()

    def compute(index):
        base = index * sources
        stack = []
        for source in range(sources):
            share_copy(base + source).wait_recv()
            both = kv[base + source].reshape(rows, LANES)
            place = pl.ds(pl.multiple_of((base + source) * rows, rows), rows)
            all_ref[place] = both
            ones_ref[place] = jnp.where(lane_of(both.shape) < head, jnp.ones_like(both), both)
            tile = land[base + source, :, :LANES].astype(F32)
            stack.append(jnp.where(lane < head, tile, 0.0))
            stack.append(jnp.where(lane < head, swap_heads(tile, head), 0.0))
        queries = jnp.concatenate(stack, axis=0).astype(BF)
        acc_ref[...] = jnp.zeros_like(acc_ref)

        def visit(step, masked):
            start = pl.multiple_of(step * keys, keys)
            here = pl.ds(start, keys)
            raised = jnp.exp2(lax.dot_general(queries, all_ref[here], ONES_NT, preferred_element_type=F32) * factor)
            if masked:
                ok = allowed_block(0, 1, (wide, keys), first, second, part, base, start, rows, half_rows)
                raised = jnp.where(ok, raised, 0.0)
            acc_ref[...] += jnp.dot(raised.astype(BF), ones_ref[here], preferred_element_type=F32)

        sweep_keys(visit, index, count * rows - rows, part, base, rows, half_rows, keys, sources)
        for source in range(sources):
            tile = land[base + source, :, :LANES].astype(F32)
            outs = []
            for which in range(2):
                place = (2 * source + which) * half_rows
                acc = acc_ref[place:place + half_rows]
                turn = swap_heads(acc, head)
                outs.append(turn / acc if which == 0 else acc / turn)
                high, middle, low = three_parts(-math.sqrt(head) * jnp.log(turn))
                query = tile if which == 0 else swap_heads(tile, head)
                extra = jnp.where(lane == head, high, jnp.where(lane == head + 1, middle,
                                                                jnp.where(lane == head + 2, low, 0.0)))
                aug_ref[base + source, which] = jnp.where(lane < head, query, extra).astype(BF)
            out = jnp.where(lane < head, outs[0], outs[1])
            out_ref[base + source] = out
            tiles[base + source] = out.astype(BF)

            @pl.when(base + source != me)
            def _(source=source):
                tile_copy(me, base + source).start()

    def block(index, _):
        @pl.when(index < count // sources)
        def _():
            for source in range(sources):
                share(index * sources + source)

        @pl.when(index > 0)
        def _():
            compute(index - 1)

    lax.fori_loop(0, count // sources + 1, block, None)
    arrive[me] = tiles[me]

    def drain(other, _):
        share_copy(other).wait_send()

        @pl.when(other != me)
        def _():
            msg_copy(me, other).wait_send()
            tile_copy(me, other).wait_send()
            tile_copy(other, me).wait_recv()

    lax.fori_loop(0, count, drain, None)
    got_ref[...] = arrive[...]


def attend_back_kernel(head, rows, keys, sources, count, info_ref, aug_ref, out_ref, kv_ref, msg_ref,
                       gotq_ref, gotk_ref,
                       land, tiles, away, near, sums, arrive_q, arrive_k, kone_ref, vone_ref, kturn_ref, dk_ref,
                       dv_ref, acc_ref, msend, mrecv, fsend, frecv, gsend, grecv, ksend, krecv):
    first, second = info_ref[0], info_ref[1]
    me = lax.axis_index("ctx")
    part = me % 2
    twin = {"ctx": me + 1 - 2 * part}
    half_rows = msg_ref.shape[1]
    wide = sources * 2 * half_rows
    factor = math.log2(math.e) / math.sqrt(head)
    shrink = 1.0 / math.sqrt(head)
    lane = lane_of((half_rows, LANES))
    greet(me, count)

    def remote(src, dst, send, recv, where):
        return pltpu.make_async_remote_copy(src_ref=src, dst_ref=dst, send_sem=send, recv_sem=recv,
                                            device_id=where, device_id_type=MESH)

    def msg_copy(owner, dest):
        return remote(msg_ref.at[dest], land.at[owner], msend.at[dest], mrecv.at[owner], {"ctx": dest})

    def share_copy(source):
        return remote(away.at[source], near.at[source], fsend.at[source], frecv.at[source], twin)

    def q_copy(owner, dest):
        return remote(tiles.at[dest], arrive_q.at[owner], gsend.at[dest], grecv.at[owner], {"ctx": dest})

    def k_copy(owner, dest):
        return remote(sums.at[dest], arrive_k.at[owner], ksend.at[dest], krecv.at[owner], {"ctx": dest})

    def start_msg(step, _):
        msg_copy(me, lax.rem(me + count - step, count)).start()

    lax.fori_loop(1, count, start_msg, None)
    land[me] = msg_ref[me]
    whole = lane_of(kv_ref.shape)
    vone_ref[...] = jnp.where(whole < head, jnp.ones_like(kv_ref), kv_ref[...])
    kone_ref[...] = jnp.where(whole < head, kv_ref[...], jnp.ones_like(kv_ref))
    kturn_ref[...] = turned(kv_ref[...])
    dk_ref[...] = jnp.zeros_like(dk_ref)
    dv_ref[...] = jnp.zeros_like(dv_ref)

    def rows_of(source, which):
        return pl.ds(pl.multiple_of(source * rows + which * half_rows, half_rows), half_rows)

    def key_tile(source, which):
        here = rows_of(source, which)
        return jnp.where(lane < head, dk_ref[here] * shrink, dv_ref[here])

    def compute(index):
        base = index * sources
        stack_q, stack_d = [], []
        for source in range(sources):
            @pl.when(base + source != me)
            def _(source=source):
                msg_copy(base + source, me).wait_recv()

            grad = land[base + source].astype(F32)
            spread = grad * out_ref[base + source]
            for which in range(2):
                stack_q.append(aug_ref[base + source, which])
                mine = (lane < head) if which == 0 else (lane >= head)
                delta = jnp.sum(jnp.where(mine, spread, 0.0), axis=1, keepdims=True)
                high, middle, low = three_parts(-delta)
                extra = jnp.where(lane == 0, high, jnp.where(lane == 1, middle, jnp.where(lane == 2, low, 0.0)))
                moved = swap_heads(grad, head) if which == 0 else grad
                stack_d.append(jnp.where(lane < head, extra, moved).astype(BF))
        queries = jnp.concatenate(stack_q, axis=0)
        grads = jnp.concatenate(stack_d, axis=0)
        acc_ref[...] = jnp.zeros_like(acc_ref)

        def visit(step, masked):
            start = pl.multiple_of(step * keys, keys)
            here = pl.ds(start, keys)
            raw = lax.dot_general(kone_ref[here], queries, ONES_NT, preferred_element_type=F32)
            if masked:
                ok = allowed_block(1, 0, (keys, wide), first, second, part, base, start, rows, half_rows)
                prob = jnp.where(ok, jnp.exp2(jnp.where(ok, raw, 0.0) * factor), 0.0)
            else:
                prob = jnp.exp2(raw * factor)
            along = lax.dot_general(vone_ref[here], grads, ONES_NT, preferred_element_type=F32)
            score = (prob * along).astype(BF)
            dv_ref[here] += jnp.dot(prob.astype(BF), grads, preferred_element_type=F32)
            dk_ref[here] += jnp.dot(score, queries, preferred_element_type=F32)
            acc_ref[...] += jnp.dot(kturn_ref[:, here], score, preferred_element_type=F32)

        sweep_keys(visit, index, count * rows - rows, part, base, rows, half_rows, keys, sources)
        acc = acc_ref[...].T
        for source in range(sources):
            place = 2 * source * half_rows
            one = acc[place:place + half_rows]
            two = acc[place + half_rows:place + 2 * half_rows]
            tiles[base + source] = (jnp.where(lane < head, one, swap_heads(two, head)) * shrink).astype(BF)

            @pl.when(base + source != me)
            def _(source=source):
                q_copy(me, base + source).start()

            away[base + source] = key_tile(base + source, 1 - part).astype(BF)
            share_copy(base + source).start()

    def finish(index):
        for source in range(sources):
            block = index * sources + source
            share_copy(block).wait_recv()
            sums[block] = (key_tile(block, part) + near[block].astype(F32)).astype(BF)

            @pl.when(block != me)
            def _(block=block):
                k_copy(me, block).start()

    def sweep(step, _):
        index = count // sources - 1 - step

        @pl.when(index >= 0)
        def _():
            compute(jnp.maximum(index, 0))

        @pl.when(step > 0)
        def _():
            finish(index + 1)

    lax.fori_loop(0, count // sources + 1, sweep, None)
    arrive_q[me] = tiles[me]
    arrive_k[me] = sums[me]

    def drain(other, _):
        share_copy(other).wait_send()

        @pl.when(other != me)
        def _():
            msg_copy(me, other).wait_send()
            q_copy(me, other).wait_send()
            k_copy(me, other).wait_send()
            q_copy(other, me).wait_recv()
            k_copy(other, me).wait_recv()

    lax.fori_loop(0, count, drain, None)
    gotq_ref[...] = arrive_q[...]
    gotk_ref[...] = arrive_k[...]


def exchange_attend(msg, info, head, rows, collective_id):
    count, half_rows = msg.shape[0], msg.shape[1]
    keys, sources = 512, 2
    group = count * rows
    dma = pltpu.SemaphoreType.DMA((count,))
    S = jax.ShapeDtypeStruct
    tile = (count, half_rows, LANES)
    return pl.pallas_call(
        functools.partial(attend_kernel, head, rows, keys, sources, count),
        out_shape=(S(tile, BF), S(tile, F32), S((count, 2, half_rows, LANES), BF), S((group, LANES), BF)),
        in_specs=[pl.BlockSpec(memory_space=pltpu.SMEM)] + vmem_specs(1),
        out_specs=tuple(vmem_specs(4)),
        scratch_shapes=[pltpu.VMEM((count, half_rows, 2 * LANES), BF), pltpu.VMEM((count, 2, half_rows, LANES), BF),
                        pltpu.VMEM(tile, BF), pltpu.VMEM(tile, BF), pltpu.VMEM((group, LANES), BF),
                        pltpu.VMEM((sources * rows, LANES), F32)] + [dma] * 6,
        compiler_params=pltpu.CompilerParams(collective_id=collective_id, has_side_effects=True,
                                             vmem_limit_bytes=VMEM_LIMIT),
        cost_estimate=pl.CostEstimate(flops=2 * group * group * LANES, bytes_accessed=6 << 20, transcendentals=0),
        name="attend",
    )(info, msg)


def exchange_attend_back(msg, info, augmented, attended, all_kv, head, rows, collective_id):
    count, half_rows = msg.shape[0], msg.shape[1]
    keys, sources = 512, 2
    group = count * rows
    dma = pltpu.SemaphoreType.DMA((count,))
    S = jax.ShapeDtypeStruct
    tile = (count, half_rows, LANES)
    long = (group, LANES)
    return pl.pallas_call(
        functools.partial(attend_back_kernel, head, rows, keys, sources, count),
        out_shape=(S(tile, BF), S(tile, BF)),
        in_specs=[pl.BlockSpec(memory_space=pltpu.SMEM)] + vmem_specs(4),
        out_specs=tuple(vmem_specs(2)),
        scratch_shapes=[pltpu.VMEM(tile, BF)] * 7 + [
            pltpu.VMEM(long, BF), pltpu.VMEM(long, BF), pltpu.VMEM((LANES, group), BF), pltpu.VMEM(long, F32),
            pltpu.VMEM(long, F32), pltpu.VMEM((LANES, sources * rows), F32)] + [dma] * 8,
        compiler_params=pltpu.CompilerParams(collective_id=collective_id, has_side_effects=True,
                                             vmem_limit_bytes=VMEM_LIMIT),
        cost_estimate=pl.CostEstimate(flops=5 * group * group * LANES, bytes_accessed=8 << 20, transcendentals=0),
        name="attend_back",
    )(info, augmented, attended, all_kv, msg)


PIECE = 32
SUB = 2 * PIECE
STRIP = 256
RING = 8
LAG = 2


def sum_kernel(jobs, sides, lines, *refs):
    count = len(jobs)
    refs = list(refs)
    take = lambda number: [refs.pop(0) for _ in range(number)]
    lefts, rights, (small_ref,) = take(sides), take(count), take(1)
    outs, (small_out,), lefts_b, rights_b = take(count), take(1), take(sides), take(count)
    (lbuf, rbuf, xp, xr, yp, yr, zp, us, ur, ds_, dr, fs, fr, cs, cr, stage, sm_s, sm_r,
     lsem, rsem, xs, xv, ys, yv, uss, urv, dss, drv, fss, frv, css, crv, osem, sms, smv, els, elv, ers, erv) = refs
    steps = sum(job[3] for job in jobs)
    last = steps - 1 + LAG
    half = STRIP // 2
    tall = SUB + PIECE
    tokens = lbuf.shape[-1] // 2
    me = lax.axis_index("ctx")
    y = lax.axis_index("dp")
    z = me // 4
    x = (me // 2) % 2
    c = me % 2
    top = lines - 1
    twin = {"ctx": me + 1 - 2 * c}
    across_x = {"ctx": me + 2 - 4 * x}
    across_y = {"dp": 1 - y}
    above = {"ctx": jnp.minimum(me + 4, 4 * top + me % 4)}
    below = {"ctx": jnp.maximum(me - 4, me % 4)}
    near = {"ctx": me + 4 - 8 * (z % 2)}
    far = {"ctx": me + 8 - 16 * (z // 2)}
    rounds = [twin, across_x, across_y, near, far]

    for buf in (xp, ur, dr, zp):
        buf[...] = jnp.zeros_like(buf)
    sm_s[0] = small_ref[...]

    barrier = pltpu.get_barrier_semaphore()
    for where in (twin, across_x, across_y, far):
        pl.semaphore_signal(barrier, inc=1, device_id=where, device_id_type=MESH)

    @pl.when(z < top)
    def _():
        pl.semaphore_signal(barrier, inc=1, device_id=above, device_id_type=MESH)

    @pl.when(z > 0)
    def _():
        pl.semaphore_signal(barrier, inc=1, device_id=below, device_id_type=MESH)

    pl.semaphore_wait(barrier, 4 + (z < top).astype(jnp.int32) + (z > 0).astype(jnp.int32))

    def remote(src, dst, send, recv, where):
        return pltpu.make_async_remote_copy(src_ref=src, dst_ref=dst, send_sem=send, recv_sem=recv,
                                            device_id=where, device_id_type=MESH)

    def left_copy(number):
        return remote(lefts[number], lefts_b[number], els.at[number], elv.at[number], twin)

    def right_copy(number):
        width = rights_b[number].shape[1]
        start = pl.multiple_of((1 - c) * width, width)
        return remote(rights[number].at[:, pl.ds(start, width)], rights_b[number], ers.at[number], erv.at[number], twin)

    seen = []
    for number, job in enumerate(jobs):
        if job[0] not in seen:
            seen.append(job[0])
            left_copy(job[0]).start()
        right_copy(number).start()

    def x_copy(j):
        s = j % RING
        return remote(xp.at[s, 1 - x], xr.at[s], xs.at[s], xv.at[s], across_x)

    def y_copy(j):
        s = j % RING
        return remote(yp.at[s, 1 - y], yr.at[s], ys.at[s], yv.at[s], across_y)

    def up_copy(j):
        s = j % RING
        return remote(us.at[s], ur.at[s], uss.at[s], urv.at[s], above)

    def down_copy(j):
        s = j % RING
        return remote(ds_.at[s], dr.at[s], dss.at[s], drv.at[s], below)

    def f_copy(j):
        s = j % RING
        return remote(fs.at[s], fr.at[s], fss.at[s], frv.at[s], across_y)

    def c_copy(j):
        s = j % RING
        return remote(cs.at[s], cr.at[s], css.at[s], crv.at[s], twin)

    def small_copy(k):
        return remote(sm_s.at[k], sm_r.at[k], sms.at[k], smv.at[k], rounds[k])

    def loads(number, row, column, s):
        left = jobs[number][0]
        width = rights_b[number].shape[1]
        mine = pl.multiple_of(c * width + column, STRIP)
        rows = pl.ds(row, PIECE)
        return [
            pltpu.make_async_copy(lefts[left].at[:, :, rows, :], lbuf.at[s, :, :, :, pl.ds(0, tokens)], lsem.at[s, 0]),
            pltpu.make_async_copy(lefts_b[left].at[:, :, rows, :], lbuf.at[s, :, :, :, pl.ds(tokens, tokens)],
                                  lsem.at[s, 1]),
            pltpu.make_async_copy(rights[number].at[:, pl.ds(mine, STRIP)], rbuf.at[s, pl.ds(0, tokens)], rsem.at[s, 0]),
            pltpu.make_async_copy(rights_b[number].at[:, pl.ds(column, STRIP)], rbuf.at[s, pl.ds(tokens, tokens)],
                                  rsem.at[s, 1]),
        ]

    def load(j):
        begin = 0
        done = []
        for number, (left, subs, strips, total) in enumerate(jobs):
            fresh = left not in done
            done.append(left)

            @pl.when(j == begin)
            def _(number=number, left=left, fresh=fresh):
                if fresh:
                    left_copy(left).wait()
                right_copy(number).wait()

            @pl.when((j >= begin) & (j < begin + total))
            def _(number=number, subs=subs, begin=begin):
                k = j - begin
                row = pl.multiple_of((k % subs) * PIECE, PIECE)
                column = pl.multiple_of((k // subs) * STRIP, STRIP)
                for copy in loads(number, row, column, j % 2):
                    copy.start()
            begin += total

    def out_copies(number, j, row, column):
        width = rights_b[number].shape[1]
        o = j % RING
        rows = pl.ds(row, PIECE)
        mine = pl.multiple_of(c * width + column, STRIP)
        other = pl.multiple_of((1 - c) * width + column, STRIP)
        return [
            pltpu.make_async_copy(stage.at[o, 0], outs[number].at[rows, pl.ds(mine, STRIP)], osem.at[o, 0]),
            pltpu.make_async_copy(stage.at[o, 1], outs[number].at[rows, pl.ds(other, STRIP)], osem.at[o, 1]),
        ]

    def store(j):
        begin = 0
        for number, (left, subs, strips, total) in enumerate(jobs):
            @pl.when((j >= begin) & (j < begin + total))
            def _(number=number, subs=subs, begin=begin):
                k = j - begin
                row = pl.multiple_of((k % subs) * PIECE, PIECE)
                column = pl.multiple_of((k // subs) * STRIP, STRIP)
                for copy in out_copies(number, j, row, column):
                    copy.start()
            begin += total

    load(0)

    def step(t, _):
        slot = t % RING

        for k in range(len(rounds) + 1):
            @pl.when(t == LAG * k)
            def _(k=k):
                if k > 0:
                    small_copy(k - 1).wait()
                    total = sm_s[k - 1] + sm_r[k - 1]
                    if k == len(rounds):
                        small_out[...] = total
                    else:
                        sm_s[k] = total
                if k < len(rounds):
                    small_copy(k).start()

        @pl.when(t < steps)
        def _():
            for copy in loads(0, 0, 0, t % 2):
                copy.wait()

            @pl.when(t + 1 < steps)
            def _():
                load(t + 1)

            left = lbuf[t % 2].reshape(2 * lines * SUB, 2 * tokens)
            got = jnp.dot(left, rbuf[t % 2], preferred_element_type=F32).astype(BF)
            for line in range(lines):
                for side in range(2):
                    row = (2 * line + side) * SUB
                    xp[slot, side, line, :SUB] = got[row:row + SUB, :half]
                    for part in range(2):
                        yp[slot, part, side, line] = got[row + part * PIECE:row + (part + 1) * PIECE, half:]

        @pl.when((t >= LAG) & (t <= last))
        def _():
            y_copy(t - LAG).wait()
            s = (t - LAG) % RING
            xp[slot, :, :, SUB:] = yp[s, y] + yr[s]

        @pl.when(t < steps)
        def _():
            y_copy(t).start()

        @pl.when(t <= last)
        def _():
            x_copy(t).start()

        @pl.when((t >= LAG) & (t - LAG <= last))
        def _():
            x_copy(t - LAG).wait()
            s = (t - LAG) % RING
            zp[(t - LAG) % (2 * RING)] = xp[s, x] + xr[s]

        ju = t - LAG * (1 + z)

        @pl.when((ju >= 0) & (ju <= last))
        def _():
            s = ju % RING
            held = ju % (2 * RING)

            @pl.when(z > 0)
            def _():
                up_copy(ju).wait_recv()
                zp[held, z] = zp[held, z] + ur[s, 0]

            @pl.when(z < top)
            def _():
                @pl.when(ju >= RING)
                def _():
                    up_copy(ju).wait_send()

                for m in range(top):
                    own = zp[held, jnp.minimum(z + 1 + m, top)]
                    if m + 1 < top:
                        own = own + ur[s, m + 1]
                    us[s, m] = own
                up_copy(ju).start()

        jd = t - LAG * (1 + top - z)

        @pl.when((jd >= 0) & (jd <= last))
        def _():
            s = jd % RING
            held = jd % (2 * RING)

            @pl.when(z < top)
            def _():
                down_copy(jd).wait_recv()
                zp[held, z] = zp[held, z] + dr[s, 0]

            @pl.when(z > 0)
            def _():
                @pl.when(jd >= RING)
                def _():
                    down_copy(jd).wait_send()

                for m in range(top):
                    own = zp[held, jnp.maximum(z - 1 - m, 0)]
                    if m + 1 < top:
                        own = own + dr[s, m + 1]
                    ds_[s, m] = own
                down_copy(jd).start()

        jf = t - LAG * (1 + top)

        @pl.when((jf >= 0) & (jf <= last))
        def _():
            fs[jf % RING] = zp[jf % (2 * RING), z]
            f_copy(jf).start()

        jo = jf - LAG

        @pl.when((jo >= 0) & (jo <= last))
        def _():
            f_copy(jo).wait()
            s = jo % RING
            fs[s, :SUB] = fs[s, :SUB] + fr[s, :SUB]
            mine = pl.ds(pl.multiple_of(c * PIECE, PIECE), PIECE)
            away = pl.ds(pl.multiple_of((1 - c) * PIECE, PIECE), PIECE)
            cs[s, :, :half] = fs[s, away]
            own, far_rows = fs[s, SUB:].astype(F32), fr[s, SUB:].astype(F32)
            cs[s, :, half:] = jnp.where(y == c, far_rows, own).astype(BF)
            c_copy(jo).start()
            stage[jo % RING, 0, :, :half] = fs[s, mine].astype(F32)

            @pl.when(jo >= LAG)
            def _():
                stage[(jo - LAG) % RING, 0, :, half:] = jnp.where(y == c, own, far_rows)

        jc = jo - LAG

        @pl.when((jc >= 0) & (jc <= last))
        def _():
            c_copy(jc).wait()
            s = jc % RING
            stage[jc % RING, 1, :, :half] = cr[s, :, :half].astype(F32)

            @pl.when(jc >= LAG)
            def _():
                chunk = jc - LAG
                stage[chunk % RING, 1, :, half:] = cr[s, :, half:].astype(F32)
                store(chunk)

            @pl.when(jc >= 2 * LAG)
            def _():
                for copy in out_copies(0, jc - 2 * LAG, 0, 0):
                    copy.wait()

    lax.fori_loop(0, last + LAG * (top + 3) + 1, step, None)
    for back in range(LAG):
        for copy in out_copies(0, steps - 1 - back, 0, 0):
            copy.wait()
    for back in range(RING):
        j = last - back

        @pl.when(z < top)
        def _(j=j):
            up_copy(j).wait_send()

        @pl.when(z > 0)
        def _(j=j):
            down_copy(j).wait_send()


def sum_over_chips(lefts, works, small, lines, collective_id):
    shaped, jobs, landing_l, landing_r, outs = [], [], [], [], []
    for left in lefts:
        rows, tokens = left.shape
        shaped.append(left.reshape(2 * lines, 2, rows // (4 * lines), tokens))
        landing_l.append(jax.ShapeDtypeStruct(shaped[-1].shape, BF))
    for number, right in works:
        rows = shaped[number].shape[2]
        subs, strips = rows // PIECE, right.shape[1] // 2 // STRIP
        jobs.append((number, subs, strips, subs * strips))
        landing_r.append(jax.ShapeDtypeStruct((tokens, right.shape[1] // 2), BF))
        outs.append(jax.ShapeDtypeStruct((rows, right.shape[1]), F32))
    steps = sum(job[3] for job in jobs)
    half = STRIP // 2
    tall = SUB + PIECE
    top = lines - 1
    dma = pltpu.SemaphoreType.DMA
    scratch = [
        pltpu.VMEM((2, 2 * lines, 2, PIECE, 2 * tokens), BF),
        pltpu.VMEM((2, 2 * tokens, STRIP), BF),
        pltpu.VMEM((RING, 2, lines, tall, half), BF),
        pltpu.VMEM((RING, lines, tall, half), BF),
        pltpu.VMEM((RING, 2, 2, lines, PIECE, half), BF),
        pltpu.VMEM((RING, 2, lines, PIECE, half), BF),
        pltpu.VMEM((2 * RING, lines, tall, half), BF),
        pltpu.VMEM((RING, top, tall, half), BF),
        pltpu.VMEM((RING, top, tall, half), BF),
        pltpu.VMEM((RING, top, tall, half), BF),
        pltpu.VMEM((RING, top, tall, half), BF),
        pltpu.VMEM((RING, tall, half), BF),
        pltpu.VMEM((RING, tall, half), BF),
        pltpu.VMEM((RING, PIECE, STRIP), BF),
        pltpu.VMEM((RING, PIECE, STRIP), BF),
        pltpu.VMEM((RING, 2, PIECE, STRIP), F32),
        pltpu.VMEM((5,) + small.shape, F32),
        pltpu.VMEM((5,) + small.shape, F32),
        dma((2, 2)), dma((2, 2)),
    ] + [dma((RING,))] * 12 + [
        dma((RING, 2)), dma((5,)), dma((5,)),
        dma((len(lefts),)), dma((len(lefts),)), dma((len(works),)), dma((len(works),)),
    ]
    anywhere = pl.BlockSpec(memory_space=pl.ANY)
    inside = pl.BlockSpec(memory_space=pltpu.VMEM)
    flops = 2 * steps * 2 * lines * SUB * STRIP * 2 * tokens
    got = pl.pallas_call(
        functools.partial(sum_kernel, jobs, len(lefts), lines),
        out_shape=tuple(outs) + (jax.ShapeDtypeStruct(small.shape, F32),) + tuple(landing_l) + tuple(landing_r),
        in_specs=[anywhere] * (len(lefts) + len(works)) + [inside],
        out_specs=tuple([anywhere] * len(works) + [inside] + [anywhere] * (len(lefts) + len(works))),
        scratch_shapes=scratch,
        compiler_params=pltpu.CompilerParams(collective_id=collective_id, has_side_effects=True,
                                             vmem_limit_bytes=VMEM_LIMIT),
        cost_estimate=pl.CostEstimate(flops=flops, bytes_accessed=steps * 800_000, transcendentals=0),
        name="sum_over_chips",
    )(*shaped, *[right for _, right in works], small)
    return got[:len(works)], got[len(works)]


def call_plain(kernel, outs, args, smem=0, scratch=(), flops=0, moved=0, name=None):
    specs = [pl.BlockSpec(memory_space=pltpu.SMEM)] * smem + vmem_specs(len(args) - smem)
    many = isinstance(outs, (tuple, list))
    return pl.pallas_call(
        kernel,
        out_shape=tuple(outs) if many else outs,
        in_specs=specs,
        out_specs=tuple(vmem_specs(len(outs))) if many else vmem_specs(1)[0],
        scratch_shapes=list(scratch),
        compiler_params=pltpu.CompilerParams(vmem_limit_bytes=VMEM_LIMIT),
        cost_estimate=pl.CostEstimate(flops=flops, bytes_accessed=moved, transcendentals=0),
        name=name,
    )(*args)


def shape_of(shape, kind):
    return jax.ShapeDtypeStruct(shape, kind)


def sibling(value):
    count = lax.axis_size("ctx")
    return lax.ppermute(value, "ctx", [(i, i ^ 1) for i in range(count)])


def norm_back(grad, hidden, gain):
    scale = lax.rsqrt(jnp.mean(hidden * hidden, axis=-1, keepdims=True) + EPS)
    unit = hidden * scale
    inward = grad * gain
    gain_grad = jnp.sum(grad * unit, axis=0)
    return scale * (inward - unit * jnp.mean(inward * unit, axis=-1, keepdims=True)), gain_grad


def fast_device(tokens, lengths, cotangent, mixgain, mixentry, mixtaps, mixexit, lowgain, lowgate, lowlift,
                lowdrop, attgain, attquery, attkeys, attvalues, querygain, keysgain, attexit, topgain, topgate,
                toplift, topdrop):
    rows, width = tokens.shape
    head = querygain.shape[0]
    devices = lax.axis_size("ctx")
    lines = devices // 4
    half_rows = rows // 2
    place = lax.axis_index("ctx")
    core = place % 2
    first = lengths[0, 0]
    second = first + lengths[0, 1]
    mine = place * rows + jnp.arange(rows, dtype=jnp.int32)
    my_seg = segment_of(mine, first, second)
    begin = jnp.where(my_seg == 0, 0, jnp.where(my_seg == 1, first, second))
    position = (mine - begin).astype(F32)
    gains = [value.astype(F32) for value in (mixgain, lowgain, attgain, topgain)]
    mixgain_f, lowgain_f, attgain_f, topgain_f = gains
    taps_f = mixtaps.astype(F32)
    twice = lambda gain: jnp.tile(gain.astype(F32), LANES // head)[None, :]
    querygain_2, keysgain_2 = twice(querygain), twice(keysgain)
    spot = jnp.arange(LANES, dtype=jnp.int32) % (head // 2)
    angle = position[:, None] * (THETA ** (-spot.astype(F32) * 2.0 / head))[None, :]
    cosine = jnp.cos(angle)
    sine = jnp.sin(angle) * jnp.where(jnp.arange(LANES) % head < head // 2, -1.0, 1.0)[None, :]
    info = jnp.stack([first, second]).astype(jnp.int32)

    hidden = tokens.astype(F32)
    normed_one = root_mean_square_scale(hidden, mixgain_f).astype(BF)
    mixed = jnp.dot(normed_one, mixentry, preferred_element_type=F32)
    part_b, part_c, part_x = (mixed[:, i * width:(i + 1) * width] for i in range(3))
    product = (part_b * part_x).astype(BF)
    borrowed = passed_along(product[rows - 2:], "ctx", 1)
    extended = jnp.concatenate([borrowed, product], axis=0).astype(F32)
    fits_one = ((mine >= 1) & (segment_of(mine - 1, first, second) == my_seg)).astype(F32)[:, None]
    fits_two = ((mine >= 2) & (segment_of(mine - 2, first, second) == my_seg)).astype(F32)[:, None]
    conved = conv_local(extended, taps_f, fits_one, fits_two)
    gated = (part_c * conved).astype(BF)
    hidden_one = hidden + jnp.dot(gated, mixexit, preferred_element_type=F32)
    hidden_two, lownorm_t, gact_low, lact_low, lowinner_t = feed_low(
        hidden_one, lowgain_f[None, :], lowgate, lowlift, lowdrop)

    heads_q, heads_k = attquery.shape[1] // head, attkeys.shape[1] // head
    msg, normed_two_t, query_raw, key_raw = call_plain(
        functools.partial(project_kernel, head),
        (shape_of((devices, half_rows, 2 * LANES), BF), shape_of((width, rows), BF),
         shape_of((rows, attquery.shape[1]), F32), shape_of((rows, attkeys.shape[1]), F32)),
        (hidden_two, attgain_f[None, :], attquery, attkeys, attvalues, cosine, sine, querygain_2, keysgain_2),
        flops=2 * rows * width * 2 * width, moved=6 << 20, name="project")
    got, attended_f, augmented, all_kv = exchange_attend(msg, info, head, rows, 2)
    (output, grad, grad_low3, send, attended_t, topgain_grad, topnorm_t, topinner_t, gate_top, lift_top) = feed_top(
        got, hidden_two, attexit, cotangent, topgain_f[None, :], topgate, toplift, topdrop)
    back_q, back_k = exchange_attend_back(send, info, augmented, attended_f, all_kv, head, rows, 3)
    rawq_low, rawk_low, rawv_low, grad_two, attgain_grad, querygain_grad, keysgain_grad = call_plain(
        functools.partial(project_back_kernel, head),
        (shape_of((rows, attquery.shape[1]), BF), shape_of((rows, attkeys.shape[1]), BF),
         shape_of((rows, attkeys.shape[1]), BF), shape_of((rows, width), F32), shape_of((1, width), F32),
         shape_of((1, LANES), F32), shape_of((1, LANES), F32)),
        (back_q, back_k, hidden_two, attgain_f[None, :], attquery, attkeys, attvalues, cosine, sine, querygain_2, keysgain_2,
         query_raw, key_raw, grad),
        flops=2 * rows * width * 2 * width, moved=8 << 20, name="project_back")
    fold = lambda value: value.reshape(LANES // head, head).sum(axis=0)
    querygain_grad, keysgain_grad = fold(querygain_grad), fold(keysgain_grad)
    grad, lowgain_grad, gb_low, grad_low1, gate_low, lift_low = feed_low_back(
        grad_two, hidden_one, lowgain_f[None, :], gact_low, lact_low, lowgate, lowlift, lowdrop)
    gated_grad = outer_dot(grad_low1, mixexit)
    part_c_grad = gated_grad * conved
    conved_grad = gated_grad * part_c
    _, pull_conv = jax.vjp(lambda ext, taps: conv_local(ext, taps, fits_one, fits_two), extended, taps_f)
    extended_grad, mixtaps_grad = pull_conv(conved_grad)
    returned_rim = passed_along(extended_grad[:2], "ctx", -1)
    product_grad = extended_grad[2:].at[rows - 2:].add(returned_rim)
    mixed_grad = jnp.concatenate(
        [product_grad * part_x, part_c_grad, product_grad * part_b], axis=1).astype(BF)
    hidden_grad, mixgain_grad = norm_back(outer_dot(mixed_grad, mixentry), hidden, mixgain_f)
    tokens_grad = grad + hidden_grad

    lefts = [attended_t, normed_two_t, topinner_t, topnorm_t, lowinner_t, lownorm_t, gated.T, normed_one.T]
    works = [(0, grad_low3), (1, rawq_low), (1, rawk_low), (1, rawv_low), (2, cotangent), (3, gate_top),
             (3, lift_top), (4, gb_low), (5, gate_low), (5, lift_low), (6, grad_low1), (7, mixed_grad)]
    heads = jnp.concatenate([querygain_grad, keysgain_grad, jnp.zeros((width - 2 * head,), F32)])
    small = jnp.concatenate([mixgain_grad[None, :], mixtaps_grad, lowgain_grad, attgain_grad, topgain_grad,
                             heads[None, :]], axis=0)
    grads, small = sum_over_chips(lefts, works, small, lines, 1)
    (attexit_grad, attquery_grad, attkeys_grad, attvalues_grad, topdrop_grad, topgate_grad, toplift_grad,
     lowdrop_grad, lowgate_grad, lowlift_grad, mixexit_grad, mixentry_grad) = grads
    return (output, tokens_grad, small[0], mixentry_grad, small[1:4], mixexit_grad, small[4], lowgate_grad,
            lowlift_grad, lowdrop_grad, small[5], attquery_grad, attkeys_grad, attvalues_grad, small[7, :head],
            small[7, head:2 * head], attexit_grad, small[6], topgate_grad, toplift_grad, topdrop_grad)


def solution(mesh):
    placed = (P(("dp", "ctx"), None), P("dp", None), P(("dp", "ctx"), None)) + (P(),) * 19
    split = {0: P(("dp", "ctx"), None), 1: P(("dp", "ctx"), None)}
    whole = (2, 4, 6, 10, 14, 15, 17)
    outs = tuple(split.get(i, P() if i in whole else P("ctx", None)) for i in range(21))
    small = mesh.shape["ctx"] == 16 and mesh.shape["dp"] == 2
    return jax.shard_map(fast_device if small else per_device, mesh=mesh, in_specs=placed, out_specs=outs,
                         check_vma=False)
```

```python
import functools
import math

import jax
import jax.numpy as jnp
from jax import lax
from jax.experimental import pallas as pl
from jax.experimental.pallas import tpu as pltpu
from jax.sharding import PartitionSpec as P

EPS = 1e-05
THETA = 1000000.0
NEGATIVE = -1e30


def passed_along(value, axis, steps):
    count = lax.axis_size(axis)
    first, last = (max(0, -steps), min(count, count - steps))
    return lax.ppermute(value, axis, [(source, source + steps) for source in range(first, last)])


def passed_along_2(block, axis, distance):
    devices = range(lax.axis_size(axis))
    route = [((i - distance) % len(devices), i) for i in devices]
    return lax.ppermute(block, axis, route)


def root_mean_square_scale(hidden, gain):
    return hidden * lax.rsqrt(jnp.mean(hidden * hidden, axis=-1, keepdims=True) + EPS) * gain


def rotary_embed(value_rows, position_index):
    half = value_rows.shape[-1] // 2
    freq = THETA ** (-jnp.arange(half, dtype=jnp.float32) * 2.0 / value_rows.shape[-1])
    angle = position_index.astype(jnp.float32)[:, None] * freq[None, :]
    cosine = jnp.cos(angle)[:, None, :]
    sine = jnp.sin(angle)[:, None, :]
    front = value_rows[..., :half]
    behind = value_rows[..., half:]
    return jnp.concatenate(
        [front * cosine - behind * sine, behind * cosine + front * sine], axis=-1
    )


def head_prep(raw, gain, position_index, heads):
    shaped = raw.reshape(raw.shape[0], heads, -1)
    return rotary_embed(root_mean_square_scale(shaped, gain), position_index)


def segment_of(where, first, second):
    return (where >= first).astype(jnp.int32) + (where >= second).astype(jnp.int32)


def block_width(count):
    best = 1
    for candidate in range(1, min(count, 1024) + 1):
        if count % candidate == 0:
            best = candidate
    return best


def sweep(carry, count, visit):
    width = block_width(count)
    return lax.fori_loop(
        0, count // width, lambda index, inner: visit(inner, index * width, width), carry
    )


def inner_dot(left, right):
    return lax.dot_general(
        left, right, (((0,), (0,)), ((), ())), preferred_element_type=jnp.float32
    )


def outer_dot(left, right):
    return lax.dot_general(
        left, right, (((1,), (1,)), ((), ())), preferred_element_type=jnp.float32
    )


def scores_of(query_part, key_part, query_where, key_where, query_seg, key_seg, scale):
    raw = (
        jnp.einsum("tkgd,pkd->kgtp", query_part, key_part, preferred_element_type=jnp.float32)
        * scale
    )
    allowed = (query_seg[:, None] == key_seg[None, :]) & (
        query_where[:, None] >= key_where[None, :]
    )
    return (raw, allowed)


def grad_block(
    query_part,
    grad_part,
    logsum_part,
    delta_part,
    key_part,
    value_part,
    query_where,
    key_where,
    query_seg,
    key_seg,
    scale,
):
    raw, allowed = scores_of(
        query_part, key_part, query_where, key_where, query_seg, key_seg, scale
    )
    prob = jnp.where(allowed, jnp.exp(raw - logsum_part[..., None]), 0.0)
    prob_grad = jnp.einsum(
        "tkgd,pkd->kgtp", grad_part, value_part, preferred_element_type=jnp.float32
    )
    score_grad = (prob * (prob_grad - delta_part[..., None])).astype(jnp.bfloat16)
    query_grad = (
        jnp.einsum("kgtp,pkd->tkgd", score_grad, key_part, preferred_element_type=jnp.float32)
        * scale
    )
    key_grad = (
        jnp.einsum("kgtp,tkgd->pkd", score_grad, query_part, preferred_element_type=jnp.float32)
        * scale
    )
    value_grad = jnp.einsum(
        "kgtp,tkgd->pkd", prob.astype(jnp.bfloat16), grad_part, preferred_element_type=jnp.float32
    )
    return (query_grad, key_grad, value_grad)


def conv_local(extended, taps, fits_one, fits_two):
    rows = extended.shape[0] - 2
    return (
        taps[2] * extended[2:]
        + taps[1] * extended[1 : rows + 1] * fits_one
        + taps[0] * extended[:rows] * fits_two
    )


def feed_forward(hidden, gain, gate_weight, lift_weight, drop_weight):
    fnormed = root_mean_square_scale(hidden, gain).astype(jnp.bfloat16)
    gate_act = jnp.dot(fnormed, gate_weight, preferred_element_type=jnp.float32)
    lift_act = jnp.dot(fnormed, lift_weight, preferred_element_type=jnp.float32)
    inner = (jax.nn.silu(gate_act) * lift_act).astype(jnp.bfloat16)
    result = hidden + jnp.dot(inner, drop_weight, preferred_element_type=jnp.float32)
    return (result, (fnormed, gate_act, lift_act, inner))


def feed_back(grad, hidden, gain, kept, gate_weight, lift_weight, drop_weight):
    fnormed, gate_act, lift_act, inner = kept
    grad_low = grad.astype(jnp.bfloat16)
    drop_grad = inner_dot(inner, grad_low)
    inner_grad = outer_dot(grad_low, drop_weight)
    _, pull_gate = jax.vjp(
        lambda gate_in, lift_in: jax.nn.silu(gate_in) * lift_in, gate_act, lift_act
    )
    gate_grad, lift_grad = pull_gate(inner_grad)
    gate_low = gate_grad.astype(jnp.bfloat16)
    lift_low = lift_grad.astype(jnp.bfloat16)
    gate_wgrad = inner_dot(fnormed, gate_low)
    lift_wgrad = inner_dot(fnormed, lift_low)
    normed_grad = outer_dot(gate_low, gate_weight) + outer_dot(lift_low, lift_weight)
    _, pull_norm = jax.vjp(root_mean_square_scale, hidden, gain)
    hidden_grad, gain_grad = pull_norm(normed_grad)
    return (grad + hidden_grad, (gain_grad, gate_wgrad, lift_wgrad, drop_grad))


def per_device(
    tokens,
    lengths,
    cotangent,
    mixgain,
    mixentry,
    mixtaps,
    mixexit,
    lowgain,
    lowgate,
    lowlift,
    lowdrop,
    attgain,
    attquery,
    attkeys,
    attvalues,
    querygain,
    keysgain,
    attexit,
    topgain,
    topgate,
    toplift,
    topdrop,
):
    rows = tokens.shape[0]
    width_model = tokens.shape[1]
    head_size = querygain.shape[0]
    query_heads = attquery.shape[1] // head_size
    kv_heads = attkeys.shape[1] // head_size
    shared_gradient = query_heads // kv_heads
    scale = 1.0 / math.sqrt(head_size)
    place = lax.axis_index("ctx")
    first = lengths[0, 0]
    second = first + lengths[0, 1]
    mine = place * rows + jnp.arange(rows, dtype=jnp.int32)
    my_seg = segment_of(mine, first, second)
    begin = jnp.where(my_seg == 0, 0, jnp.where(my_seg == 1, first, second))
    position_index = mine - begin
    last_row = place * rows + rows - 1
    mixgain_f = mixgain.astype(jnp.float32)
    taps_f = mixtaps.astype(jnp.float32)
    lowgain_f = lowgain.astype(jnp.float32)
    attgain_f = attgain.astype(jnp.float32)
    querygain_f = querygain.astype(jnp.float32)
    keysgain_f = keysgain.astype(jnp.float32)
    topgain_f = topgain.astype(jnp.float32)
    hidden = tokens.astype(jnp.float32)
    normed_one = root_mean_square_scale(hidden, mixgain_f).astype(jnp.bfloat16)
    mixed = jnp.dot(normed_one, mixentry, preferred_element_type=jnp.float32)
    part_b = mixed[:, :width_model]
    part_c = mixed[:, width_model : 2 * width_model]
    part_x = mixed[:, 2 * width_model :]
    product = (part_b * part_x).astype(jnp.bfloat16)
    borrowed = passed_along(product[rows - 2 :], "ctx", 1)
    extended = jnp.concatenate([borrowed, product], axis=0).astype(jnp.float32)
    fits_one = ((mine >= 1) & (segment_of(mine - 1, first, second) == my_seg)).astype(jnp.float32)[
        :, None
    ]
    fits_two = ((mine >= 2) & (segment_of(mine - 2, first, second) == my_seg)).astype(jnp.float32)[
        :, None
    ]
    conved = conv_local(extended, taps_f, fits_one, fits_two)
    gated = (part_c * conved).astype(jnp.bfloat16)
    hidden_one = hidden + jnp.dot(gated, mixexit, preferred_element_type=jnp.float32)
    hidden_two, kept_low = feed_forward(hidden_one, lowgain_f, lowgate, lowlift, lowdrop)
    normed_two = root_mean_square_scale(hidden_two, attgain_f).astype(jnp.bfloat16)
    query_unrotated = jnp.dot(normed_two, attquery, preferred_element_type=jnp.float32)
    key_unrotated = jnp.dot(normed_two, attkeys, preferred_element_type=jnp.float32)
    value_projected = jnp.dot(normed_two, attvalues, preferred_element_type=jnp.float32)
    query_low = head_prep(query_unrotated, querygain_f, position_index, query_heads).astype(
        jnp.bfloat16
    )
    key_low = head_prep(key_unrotated, keysgain_f, position_index, kv_heads).astype(jnp.bfloat16)
    value_low = value_projected.astype(jnp.bfloat16).reshape(rows, kv_heads, head_size)
    query_grouped = query_low.reshape(rows, kv_heads, shared_gradient, head_size)

    def stat_visit(carry, keys_in, start, offset, width):
        top, total = carry
        key_part = lax.dynamic_slice_in_dim(keys_in, offset, width, 0)
        key_where = start + offset + jnp.arange(width, dtype=jnp.int32)
        raw, allowed = scores_of(
            query_grouped,
            key_part,
            mine,
            key_where,
            my_seg,
            segment_of(key_where, first, second),
            scale,
        )
        new_top = jnp.maximum(top, jnp.max(jnp.where(allowed, raw, NEGATIVE), axis=-1))
        weights = jnp.where(allowed, jnp.exp(raw - new_top[..., None]), 0.0)
        total = total * jnp.exp(top - new_top) + jnp.sum(weights, axis=-1)
        return (new_top, total)

    stat_state = (
        jnp.full((kv_heads, shared_gradient, rows), NEGATIVE, jnp.float32),
        jnp.zeros((kv_heads, shared_gradient, rows), jnp.float32),
    )
    piece = lax.all_gather(key_low, "ctx", axis=0, tiled=True)
    start = jnp.int32(0)
    count = piece.shape[0]

    def stat_running(inner):
        return sweep(
            inner, count, lambda acc, offset, width: stat_visit(acc, piece, start, offset, width)
        )

    top, total = lax.cond(start > last_row, lambda inner: inner, stat_running, stat_state)
    logsum = top + jnp.log(total)

    def forward_visit(accum, keys_in, values_in, start, offset, width):
        key_part = lax.dynamic_slice_in_dim(keys_in, offset, width, 0)
        value_part = lax.dynamic_slice_in_dim(values_in, offset, width, 0)
        key_where = start + offset + jnp.arange(width, dtype=jnp.int32)
        raw, allowed = scores_of(
            query_grouped,
            key_part,
            mine,
            key_where,
            my_seg,
            segment_of(key_where, first, second),
            scale,
        )
        prob_low = jnp.where(allowed, jnp.exp(raw - logsum[..., None]), 0.0).astype(jnp.bfloat16)
        return accum + jnp.einsum(
            "kgtp,pkd->kgtd", prob_low, value_part, preferred_element_type=jnp.float32
        )

    forward_start = jnp.int32(0)
    keys_in = lax.all_gather(key_low, "ctx", axis=0, tiled=True)
    values_in = lax.all_gather(value_low, "ctx", axis=0, tiled=True)
    forward_count = keys_in.shape[0]

    def forward_running(inner):
        return sweep(
            inner,
            forward_count,
            lambda acc, offset, width: forward_visit(
                acc, keys_in, values_in, forward_start, offset, width
            ),
        )

    accum = lax.cond(
        forward_start > last_row,
        lambda inner: inner,
        forward_running,
        jnp.zeros((kv_heads, shared_gradient, rows, head_size), jnp.float32),
    )
    attended = accum.transpose(2, 0, 1, 3).reshape(rows, -1)
    attended_low = attended.astype(jnp.bfloat16)
    hidden_three = hidden_two + jnp.dot(attended_low, attexit, preferred_element_type=jnp.float32)
    output, kept_top = feed_forward(hidden_three, topgain_f, topgate, toplift, topdrop)
    grad = cotangent.astype(jnp.float32)
    grad, top_grads = feed_back(grad, hidden_three, topgain_f, kept_top, topgate, toplift, topdrop)
    grad_low = grad.astype(jnp.bfloat16)
    attexit_grad = inner_dot(attended_low, grad_low)
    out_grads = (
        outer_dot(grad_low, attexit)
        .astype(jnp.bfloat16)
        .reshape(rows, kv_heads, shared_gradient, head_size)
    )
    delta = jnp.einsum(
        "tkgd,tkgd->kgt",
        out_grads.astype(jnp.float32),
        attended.reshape(rows, kv_heads, shared_gradient, head_size),
    )
    cycle_size = lax.axis_size("ctx")

    def cycle_visit(state, keys_in, values_in, start, offset, width):
        query_acc, key_acc, value_acc = state
        key_part = lax.dynamic_slice_in_dim(keys_in, offset, width, 0)
        value_part = lax.dynamic_slice_in_dim(values_in, offset, width, 0)
        key_where = start + offset + jnp.arange(width, dtype=jnp.int32)
        query_grad, key_grad, value_grad = grad_block(
            query_grouped,
            out_grads,
            logsum,
            delta,
            key_part,
            value_part,
            mine,
            key_where,
            my_seg,
            segment_of(key_where, first, second),
            scale,
        )
        key_acc = lax.dynamic_update_slice_in_dim(
            key_acc, lax.dynamic_slice_in_dim(key_acc, offset, width, 0) + key_grad, offset, 0
        )
        value_acc = lax.dynamic_update_slice_in_dim(
            value_acc, lax.dynamic_slice_in_dim(value_acc, offset, width, 0) + value_grad, offset, 0
        )
        return (query_acc + query_grad, key_acc, value_acc)

    def cycle_step(step, carry):
        keys_cur, values_cur, key_acc, value_acc, query_acc = carry
        anchor = (place - step + cycle_size) % cycle_size
        start = anchor * rows

        def cycle_running(state):
            return sweep(
                state,
                rows,
                lambda acc, offset, width: cycle_visit(
                    acc, keys_cur, values_cur, start, offset, width
                ),
            )

        query_acc, key_acc, value_acc = lax.cond(
            start > last_row, lambda state: state, cycle_running, (query_acc, key_acc, value_acc)
        )
        keys_cur, values_cur = passed_along((keys_cur, values_cur), "ctx", 1)
        key_acc, value_acc = (
            passed_along_2(key_acc.astype(jnp.bfloat16), "ctx", 1).astype(key_acc.dtype),
            passed_along_2(value_acc.astype(jnp.bfloat16), "ctx", 1).astype(value_acc.dtype),
        )
        return (keys_cur, values_cur, key_acc, value_acc, query_acc)

    cycle_state = (
        key_low,
        value_low,
        jnp.zeros((rows, kv_heads, head_size), jnp.float32),
        jnp.zeros((rows, kv_heads, head_size), jnp.float32),
        jnp.zeros((rows, kv_heads, shared_gradient, head_size), jnp.float32),
    )
    _, _, key_grads, value_grads, query_acc = lax.fori_loop(0, cycle_size, cycle_step, cycle_state)
    _, pull_query = jax.vjp(
        lambda raw, gain: head_prep(raw, gain, position_index, query_heads),
        query_unrotated,
        querygain_f,
    )
    query_raw_grad, querygain_grad = pull_query(query_acc.reshape(rows, query_heads, head_size))
    _, pull_key = jax.vjp(
        lambda raw, gain: head_prep(raw, gain, position_index, kv_heads), key_unrotated, keysgain_f
    )
    key_raw_grad, keysgain_grad = pull_key(key_grads)
    query_raw_low = query_raw_grad.astype(jnp.bfloat16)
    key_raw_low = key_raw_grad.astype(jnp.bfloat16)
    value_raw_low = value_grads.reshape(rows, -1).astype(jnp.bfloat16)
    attquery_grad = inner_dot(normed_two, query_raw_low)
    attkeys_grad = inner_dot(normed_two, key_raw_low)
    attvalues_grad = inner_dot(normed_two, value_raw_low)
    normed_two_grad = (
        outer_dot(query_raw_low, attquery)
        + outer_dot(key_raw_low, attkeys)
        + outer_dot(value_raw_low, attvalues)
    )
    _, pull_att = jax.vjp(root_mean_square_scale, hidden_two, attgain_f)
    hidden_two_grad, attgain_grad = pull_att(normed_two_grad)
    grad = grad + hidden_two_grad
    grad, low_grads = feed_back(grad, hidden_one, lowgain_f, kept_low, lowgate, lowlift, lowdrop)
    grad_low = grad.astype(jnp.bfloat16)
    mixexit_grad = inner_dot(gated, grad_low)
    gated_grad = outer_dot(grad_low, mixexit)
    part_c_grad = gated_grad * conved
    conved_grad = gated_grad * part_c
    _, pull_conv = jax.vjp(
        lambda ext, taps: conv_local(ext, taps, fits_one, fits_two), extended, taps_f
    )
    extended_grad, mixtaps_grad = pull_conv(conved_grad)
    returned_rim = passed_along(extended_grad[:2], "ctx", -1)
    product_grad = extended_grad[2:].at[rows - 2 :].add(returned_rim)
    mixed_grad = jnp.concatenate(
        [product_grad * part_x, part_c_grad, product_grad * part_b], axis=1
    ).astype(jnp.bfloat16)
    mixentry_grad = inner_dot(normed_one, mixed_grad)
    normed_one_grad = outer_dot(mixed_grad, mixentry)
    _, pull_mix = jax.vjp(root_mean_square_scale, hidden, mixgain_f)
    hidden_grad, mixgain_grad = pull_mix(normed_one_grad)
    tokens_grad = grad + hidden_grad
    lowgain_grad, lowgate_grad, lowlift_grad, lowdrop_grad = low_grads
    topgain_grad, topgate_grad, toplift_grad, topdrop_grad = top_grads
    shares = (
        lax.psum_scatter(mixentry_grad, "ctx", scatter_dimension=0, tiled=True),
        lax.psum_scatter(mixexit_grad, "ctx", scatter_dimension=0, tiled=True),
        lax.psum_scatter(lowgate_grad, "ctx", scatter_dimension=0, tiled=True),
        lax.psum_scatter(lowlift_grad, "ctx", scatter_dimension=0, tiled=True),
        lax.psum_scatter(lowdrop_grad, "ctx", scatter_dimension=0, tiled=True),
        lax.psum_scatter(attquery_grad, "ctx", scatter_dimension=0, tiled=True),
        lax.psum_scatter(attkeys_grad, "ctx", scatter_dimension=0, tiled=True),
        lax.psum_scatter(attvalues_grad, "ctx", scatter_dimension=0, tiled=True),
        lax.psum_scatter(attexit_grad, "ctx", scatter_dimension=0, tiled=True),
        lax.psum_scatter(topgate_grad, "ctx", scatter_dimension=0, tiled=True),
        lax.psum_scatter(toplift_grad, "ctx", scatter_dimension=0, tiled=True),
        lax.psum_scatter(topdrop_grad, "ctx", scatter_dimension=0, tiled=True),
    )
    smalls = lax.psum(
        (
            mixgain_grad,
            mixtaps_grad,
            lowgain_grad,
            attgain_grad,
            querygain_grad,
            keysgain_grad,
            topgain_grad,
        ),
        "ctx",
    )
    summed = (
        lax.psum(shares[0].astype(jnp.bfloat16), "dp").astype(jnp.float32),
        lax.psum(shares[1].astype(jnp.bfloat16), "dp").astype(jnp.float32),
        lax.psum(shares[2].astype(jnp.bfloat16), "dp").astype(jnp.float32),
        lax.psum(shares[3].astype(jnp.bfloat16), "dp").astype(jnp.float32),
        lax.psum(shares[4].astype(jnp.bfloat16), "dp").astype(jnp.float32),
        lax.psum(shares[5].astype(jnp.bfloat16), "dp").astype(jnp.float32),
        lax.psum(shares[6].astype(jnp.bfloat16), "dp").astype(jnp.float32),
        lax.psum(shares[7].astype(jnp.bfloat16), "dp").astype(jnp.float32),
        lax.psum(shares[8].astype(jnp.bfloat16), "dp").astype(jnp.float32),
        lax.psum(shares[9].astype(jnp.bfloat16), "dp").astype(jnp.float32),
        lax.psum(shares[10].astype(jnp.bfloat16), "dp").astype(jnp.float32),
        lax.psum(shares[11].astype(jnp.bfloat16), "dp").astype(jnp.float32),
        lax.psum(smalls[0].astype(jnp.bfloat16), "dp").astype(jnp.float32),
        lax.psum(smalls[1].astype(jnp.bfloat16), "dp").astype(jnp.float32),
        lax.psum(smalls[2].astype(jnp.bfloat16), "dp").astype(jnp.float32),
        lax.psum(smalls[3].astype(jnp.bfloat16), "dp").astype(jnp.float32),
        lax.psum(smalls[4].astype(jnp.bfloat16), "dp").astype(jnp.float32),
        lax.psum(smalls[5].astype(jnp.bfloat16), "dp").astype(jnp.float32),
        lax.psum(smalls[6].astype(jnp.bfloat16), "dp").astype(jnp.float32),
    )
    return (
        output,
        tokens_grad,
        summed[12],
        summed[0],
        summed[13],
        summed[1],
        summed[14],
        summed[2],
        summed[3],
        summed[4],
        summed[15],
        summed[5],
        summed[6],
        summed[7],
        summed[16],
        summed[17],
        summed[8],
        summed[18],
        summed[9],
        summed[10],
        summed[11],
    )


LANES = 128
BF = jnp.bfloat16
F32 = jnp.float32
ONES_NT = (((1,), (1,)), ((), ()))
ONES_TN = (((0,), (0,)), ((), ()))
VMEM_LIMIT = 60 * 1024 * 1024
PIECE = 16
SUB = 2 * PIECE
STRIP = 256
RING = 16
LAG = 3
AHEAD = 8


def vmem_specs(count):
    return [pl.BlockSpec(memory_space=pltpu.VMEM)] * count


def lane_of(shape):
    return lax.broadcasted_iota(jnp.int32, shape, len(shape) - 1)


def same_head(head):
    row = lax.broadcasted_iota(jnp.int32, (LANES, LANES), 0) // head
    column = lax.broadcasted_iota(jnp.int32, (LANES, LANES), 1) // head
    return jnp.where(row == column, 1.0 / head, 0.0).astype(F32)


def head_mean(value, blocks):
    return jnp.dot(value, blocks, precision=lax.Precision.HIGHEST, preferred_element_type=F32)


def other_half(value, head):
    lane = lane_of(value.shape)
    ahead = pltpu.roll(value, LANES - head // 2, 1)
    behind = pltpu.roll(value, head // 2, 1)
    return jnp.where(lane % head < head // 2, ahead, behind)


def swap_heads(value, head):
    return pltpu.roll(value, head, 1)


def three_parts(value):
    high = value.astype(BF)
    rest = value - high.astype(F32)
    middle = rest.astype(BF)
    low = (rest - middle.astype(F32)).astype(BF)
    return high.astype(F32), middle.astype(F32), low.astype(F32)


def project_kernel(head, hid_ref, gain_ref, wq_ref, wk_ref, wv_ref, cos_ref, sin_ref, qg_ref, kg_ref,
                   msg_ref, normt_ref, qraw_ref, kraw_ref):
    hid = hid_ref[...]
    scale = lax.rsqrt(jnp.mean(hid * hid, axis=-1, keepdims=True) + EPS)
    normed = hid * scale * gain_ref[...]
    normt_ref[...] = turned(normed)
    normed = normed.astype(BF)
    blocks = same_head(head)
    cosine, sine = cos_ref[...], sin_ref[...]
    half_rows = msg_ref.shape[1]
    lane = lane_of(cosine.shape)

    def prepared(raw, gain):
        unit = raw * lax.rsqrt(head_mean(raw * raw, blocks) + EPS) * gain
        return unit * cosine + other_half(unit, head) * sine

    def put(dest, start, tile):
        low = tile.astype(BF)
        for part in range(2):
            msg_ref[2 * dest + part, :, start:start + LANES] = low[part * half_rows:(part + 1) * half_rows]

    qraw = jnp.dot(normed, wq_ref[...], preferred_element_type=F32)
    qraw_ref[...] = qraw
    for tile in range(qraw.shape[1] // LANES):
        put(tile, 0, prepared(qraw[:, tile * LANES:(tile + 1) * LANES], qg_ref[...]))
    kraw = jnp.dot(normed, wk_ref[...], preferred_element_type=F32)
    kraw_ref[...] = kraw
    vraw = jnp.dot(normed, wv_ref[...], preferred_element_type=F32)
    for tile in range(kraw.shape[1] // LANES):
        keys = prepared(kraw[:, tile * LANES:(tile + 1) * LANES], kg_ref[...])
        values = vraw[:, tile * LANES:(tile + 1) * LANES]
        put(2 * tile, LANES, jnp.where(lane < head, keys, swap_heads(values, head)))
        put(2 * tile + 1, LANES, jnp.where(lane < head, swap_heads(keys, head), values))


def project_back_kernel(head, backq_ref, backk_ref, hid_ref, gain_ref, wq_ref, wk_ref, wv_ref, cos_ref, sin_ref, qg_ref,
                        kg_ref, qraw_ref, kraw_ref, grad_ref,
                        rawq_ref, keep_ref, send_ref, two_ref, again_ref, qgain_ref, kgain_ref):
    blocks = same_head(head)
    cosine, sine = cos_ref[...], sin_ref[...]
    lane = lane_of(cosine.shape)

    def fetch(source, dest):
        return jnp.concatenate([source[2 * dest], source[2 * dest + 1]], axis=0).astype(F32)

    def through(grad, raw, gain):
        scale = lax.rsqrt(head_mean(raw * raw, blocks) + EPS)
        unit = raw * scale
        turned = grad * cosine - other_half(grad, head) * sine
        gain_part = jnp.sum(turned * unit, axis=0, keepdims=True)
        inward = turned * gain
        return scale * (inward - unit * head_mean(inward * unit, blocks)), gain_part

    width_q = wq_ref.shape[1]
    width_k = wk_ref.shape[1]
    gain_total = jnp.zeros((1, LANES), F32)
    for tile in range(width_q // LANES):
        got, part = through(fetch(backq_ref, tile), qraw_ref[:, tile * LANES:(tile + 1) * LANES], qg_ref[...])
        gain_total = gain_total + part
        rawq_ref[:, tile * LANES:(tile + 1) * LANES] = got.astype(BF)
    qgain_ref[...] = gain_total
    gain_total = jnp.zeros((1, LANES), F32)
    key_tiles, value_tiles = [], []
    for tile in range(width_k // LANES):
        even, odd = fetch(backk_ref, 2 * tile), fetch(backk_ref, 2 * tile + 1)
        keys = jnp.where(lane < head, even, swap_heads(odd, head))
        values = jnp.where(lane < head, swap_heads(even, head), odd)
        got, part = through(keys, kraw_ref[:, tile * LANES:(tile + 1) * LANES], kg_ref[...])
        gain_total = gain_total + part
        key_tiles.append(got.astype(BF))
        value_tiles.append(values.astype(BF))
    kgain_ref[...] = gain_total
    keys, values = jnp.concatenate(key_tiles, axis=1), jnp.concatenate(value_tiles, axis=1)
    keep_ref[...], send_ref[...] = kept_first(keys, values)
    normed_grad = nt_dot(rawq_ref[...], wq_ref[...]) + nt_dot(keys, wk_ref[...]) + nt_dot(values, wv_ref[...])
    hid = hid_ref[...]
    scale = lax.rsqrt(jnp.mean(hid * hid, axis=-1, keepdims=True) + EPS)
    unit = hid * scale
    again_ref[...] = jnp.sum(normed_grad * unit, axis=0, keepdims=True)
    inward = normed_grad * gain_ref[...]
    two_ref[...] = grad_ref[...] + scale * (inward - unit * jnp.mean(inward * unit, axis=-1, keepdims=True))


def allowed_block(row_axis, key_axis, shape, first, second, part, base, start, rows, half_rows):
    row = lax.broadcasted_iota(jnp.int32, shape, row_axis)
    token = (base + row // (2 * half_rows)) * rows + part * half_rows + row % half_rows
    key = start + lax.broadcasted_iota(jnp.int32, shape, key_axis)
    begin = jnp.where(token >= second, second, jnp.where(token >= first, first, 0))
    return (key >= begin) & (key <= token)


MESH = pl.DeviceIdType.MESH


def turned(value):
    return value.astype(F32).T.astype(BF)


def norm_scale(hidden):
    return lax.rsqrt(jnp.mean(hidden * hidden, axis=-1, keepdims=True) + EPS)


def norm_pull(normed_grad, hidden, gain):
    scale = norm_scale(hidden)
    unit = hidden * scale
    inward = normed_grad * gain
    back = scale * (inward - unit * jnp.mean(inward * unit, axis=-1, keepdims=True))
    return back, jnp.sum(normed_grad * unit, axis=0, keepdims=True)


def kept_first(one, two):
    first = lax.axis_index("dp") == 0
    return jnp.where(first, one, two), jnp.where(first, two, one)


def nt_dot(left, right):
    return lax.dot_general(left, right, ONES_NT, preferred_element_type=F32)


def nn_dot(left, right):
    return jnp.dot(left, right, preferred_element_type=F32)


def activation_pull(gate_act, lift_act, sigma, inner_grad):
    gate_grad = inner_grad * lift_act * sigma * (1 + gate_act * (1 - sigma))
    return gate_grad.astype(BF), (inner_grad * gate_act * sigma).astype(BF)


def low_kernel(hid_ref, gain_ref, gate_ref, lift_ref, drop_ref,
               out_ref, normt_ref, gact_ref, lact_ref, innert_ref, norm_ref):
    step = pl.program_id(0)

    @pl.when(step == 0)
    def _():
        hid = hid_ref[...]
        normed = hid * norm_scale(hid) * gain_ref[...]
        norm_ref[...] = normed.astype(BF)
        normt_ref[...] = turned(normed)
        out_ref[...] = hid

    normed = norm_ref[...]
    gate_act = nn_dot(normed, gate_ref[...])
    lift_act = nn_dot(normed, lift_ref[...])
    inner = gate_act * jax.nn.sigmoid(gate_act) * lift_act
    gact_ref[...] = gate_act.astype(BF)
    lact_ref[...] = lift_act.astype(BF)
    innert_ref[...] = turned(inner)
    out_ref[...] += nn_dot(inner.astype(BF), drop_ref[...])


def low_back_kernel(grad_ref, hid_ref, gain_ref, gact_ref, lact_ref, gate_ref, lift_ref, drop_ref,
                    out_ref, again_ref, low_ref, outlow_ref, glow_ref, llow_ref, acc_ref):
    step = pl.program_id(0)

    @pl.when(step == 0)
    def _():
        low_ref[...] = grad_ref[...].astype(BF)
        acc_ref[...] = jnp.zeros_like(acc_ref)

    gate_act, lift_act = gact_ref[...].astype(F32), lact_ref[...].astype(F32)
    inner_grad = nt_dot(low_ref[...], drop_ref[...])
    gate_low, lift_low = activation_pull(gate_act, lift_act, jax.nn.sigmoid(gate_act), inner_grad)
    glow_ref[...], llow_ref[...] = kept_first(gate_low, lift_low)
    acc_ref[...] += nt_dot(gate_low, gate_ref[...]) + nt_dot(lift_low, lift_ref[...])

    @pl.when(step == pl.num_programs(0) - 1)
    def _():
        back, gain_part = norm_pull(acc_ref[...], hid_ref[...], gain_ref[...])
        again_ref[...] = gain_part
        out = grad_ref[...] + back
        out_ref[...] = out
        outlow_ref[...] = out.astype(BF)


def top_kernel(got_ref, two_ref, exit_ref, cot_ref, gain_ref, gate_ref, lift_ref, drop_ref,
               out_ref, grad_ref, gradlow_ref, send_ref, attt_ref, again_ref, normt_ref, innert_ref, glow_ref,
               llow_ref, hid_ref, norm_ref, acc_ref):
    step = pl.program_id(0)
    half_rows = got_ref.shape[1]

    @pl.when(step == 0)
    def _():
        tiles = []
        for tile in range(got_ref.shape[0] // 2):
            tiles.append(jnp.concatenate([got_ref[2 * tile], got_ref[2 * tile + 1]], axis=0))
        attended = jnp.concatenate(tiles, axis=1)
        attt_ref[...] = turned(attended)
        hid = two_ref[...] + nn_dot(attended, exit_ref[...])
        hid_ref[...] = hid
        normed = hid * norm_scale(hid) * gain_ref[...]
        norm_ref[...] = normed.astype(BF)
        normt_ref[...] = turned(normed)
        out_ref[...] = hid
        acc_ref[...] = jnp.zeros_like(acc_ref)

    normed = norm_ref[...]
    gate_act = nn_dot(normed, gate_ref[...])
    lift_act = nn_dot(normed, lift_ref[...])
    sigma = jax.nn.sigmoid(gate_act)
    inner = gate_act * sigma * lift_act
    innert_ref[...] = turned(inner)
    out_ref[...] += nn_dot(inner.astype(BF), drop_ref[...])
    inner_grad = nt_dot(cot_ref[...], drop_ref[...])
    gate_low, lift_low = activation_pull(gate_act, lift_act, sigma, inner_grad)
    glow_ref[...], llow_ref[...] = kept_first(gate_low, lift_low)
    acc_ref[...] += nt_dot(gate_low, gate_ref[...]) + nt_dot(lift_low, lift_ref[...])

    @pl.when(step == pl.num_programs(0) - 1)
    def _():
        back, gain_part = norm_pull(acc_ref[...], hid_ref[...], gain_ref[...])
        again_ref[...] = gain_part
        grad = cot_ref[...].astype(F32) + back
        grad_ref[...] = grad
        low = grad.astype(BF)
        gradlow_ref[...] = low
        sent = nt_dot(low, exit_ref[...]).astype(BF)
        for tile in range(send_ref.shape[0] // 2):
            for part in range(2):
                send_ref[2 * tile + part] = sent[part * half_rows:(part + 1) * half_rows,
                                                 tile * LANES:(tile + 1) * LANES]


TILE = 512
WIDE_TILE = 1152


def whole_block(shape):
    return pl.BlockSpec(shape, lambda step, rank=len(shape): (0,) * rank)


def column_block(rows, tile=TILE):
    return pl.BlockSpec((rows, tile), lambda step: (0, step))


def row_block(columns, tile=TILE):
    return pl.BlockSpec((tile, columns), lambda step: (step, 0))


def call_tiled(kernel, tiles, ins, outs, scratch, flops, moved, name):
    return pl.pallas_call(
        kernel,
        grid=(tiles,),
        in_specs=[spec for _, spec in ins],
        out_specs=tuple(spec for _, spec in outs),
        out_shape=tuple(shape for shape, _ in outs),
        scratch_shapes=scratch,
        compiler_params=pltpu.CompilerParams(vmem_limit_bytes=VMEM_LIMIT, dimension_semantics=("arbitrary",)),
        cost_estimate=pl.CostEstimate(flops=flops, bytes_accessed=moved, transcendentals=0),
        name=name,
    )(*[value for value, _ in ins])


def feed_low(hidden, gain, gate, lift, drop):
    rows, width = hidden.shape
    ff = gate.shape[1]
    S = jax.ShapeDtypeStruct
    return call_tiled(
        low_kernel, ff // WIDE_TILE,
        [(hidden, whole_block((rows, width))), (gain, whole_block((1, width))), (gate, column_block(width, WIDE_TILE)),
         (lift, column_block(width, WIDE_TILE)), (drop, row_block(width, WIDE_TILE))],
        [(S((rows, width), F32), whole_block((rows, width))), (S((width, rows), BF), whole_block((width, rows))),
         (S((rows, ff), BF), column_block(rows, WIDE_TILE)), (S((rows, ff), BF), column_block(rows, WIDE_TILE)),
         (S((ff, rows), BF), row_block(rows, WIDE_TILE))],
        [pltpu.VMEM((rows, width), BF)], 6 * rows * width * ff, 38 << 20, "feed_low")


def feed_low_back(grad, hidden, gain, gact, lact, gate, lift, drop):
    rows, width = hidden.shape
    ff = gate.shape[1]
    S = jax.ShapeDtypeStruct
    full = whole_block((rows, width))
    return call_tiled(
        low_back_kernel, ff // WIDE_TILE,
        [(grad, full), (hidden, full), (gain, whole_block((1, width))), (gact, column_block(rows, WIDE_TILE)),
         (lact, column_block(rows, WIDE_TILE)), (gate, column_block(width, WIDE_TILE)), (lift, column_block(width, WIDE_TILE)),
         (drop, row_block(width, WIDE_TILE))],
        [(S((rows, width), F32), full), (S((1, width), F32), whole_block((1, width))), (S((rows, width), BF), full),
         (S((rows, width), BF), full), (S((rows, ff), BF), column_block(rows, WIDE_TILE)), (S((rows, ff), BF), column_block(rows, WIDE_TILE))],
        [pltpu.VMEM((rows, width), F32)], 1 << 20, 1 << 10, "feed_low_back")


def feed_top(got, two, exit_weight, cotangent, gain, gate, lift, drop):
    rows, width = two.shape
    ff = gate.shape[1]
    S = jax.ShapeDtypeStruct
    full = whole_block((rows, width))
    flat = whole_block((1, width))
    standing = whole_block((width, rows))
    return call_tiled(
        top_kernel, ff // TILE,
        [(got, whole_block(got.shape)), (two, full), (exit_weight, whole_block(exit_weight.shape)), (cotangent, full),
         (gain, flat), (gate, column_block(width)), (lift, column_block(width)), (drop, row_block(width))],
        [(S((rows, width), F32), full), (S((rows, width), F32), full), (S((rows, width), BF), full),
         (S(got.shape, BF), whole_block(got.shape)), (S((width, rows), BF), standing), (S((1, width), F32), flat),
         (S((width, rows), BF), standing), (S((ff, rows), BF), row_block(rows)), (S((rows, ff), BF), column_block(rows)),
         (S((rows, ff), BF), column_block(rows))],
        [pltpu.VMEM((rows, width), F32), pltpu.VMEM((rows, width), BF), pltpu.VMEM((rows, width), F32)],
        12 * rows * width * ff, 45 << 20, "feed_top")


def sweep_keys(visit, index, tail, part, base, rows, half_rows, keys, sources):
    lowest = base * rows + part * half_rows
    end = (base + sources - 1) * rows + (part + 1) * half_rows
    count = (end + keys - 1) // keys
    free = jnp.where(end > tail, 0, jnp.maximum((lowest + 1) // keys - 1, 0))
    lax.fori_loop(0, free, lambda step, _: visit(step + 1, False), None)
    lax.fori_loop(0, count - free, lambda step, _: visit(jnp.where(step == 0, 0, free + step), True), None)


def greet(me, count):
    barrier = pltpu.get_barrier_semaphore()

    def hello(step, _):
        pl.semaphore_signal(barrier, inc=1, device_id={"ctx": lax.rem(me + step, count)}, device_id_type=MESH)

    lax.fori_loop(1, count, hello, None)
    pl.semaphore_signal(barrier, inc=1, device_id={"dp": 1 - lax.axis_index("dp")}, device_id_type=MESH)
    pl.semaphore_wait(barrier, count)


def hosted_copies(kinds, sources, landings, sends, recvs):
    y = lax.axis_index("dp")
    copies = []
    for number, (kind, source, landing) in enumerate(zip(kinds, sources, landings)):
        if kind == "rows":
            height = landing.shape[2]
            source = source.at[:, :, pl.ds(pl.multiple_of((1 - y) * height, PIECE), height), :]
        if kind == "columns":
            width = landing.shape[1]
            source = source.at[:, pl.ds(pl.multiple_of((1 - y) * width, STRIP), width)]
        copies.append(pltpu.make_async_remote_copy(
            src_ref=source, dst_ref=landing, send_sem=sends.at[number], recv_sem=recvs.at[number],
            device_id={"dp": 1 - y}, device_id_type=MESH))
    return copies


def hosted_shapes(hosted):
    shapes = []
    for kind, value in hosted:
        shape = list(value.shape)
        if kind == "rows":
            shape[2] //= 2
        if kind == "columns":
            shape[1] //= 2
        shapes.append(jax.ShapeDtypeStruct(tuple(shape), value.dtype))
    return shapes


def attend_kernel(head, rows, keys, sources, count, kinds, *refs):
    extra = len(kinds)
    (info_ref, msg_ref), guests, refs = refs[:2], refs[2:2 + extra], refs[2 + extra:]
    (got_ref, out_ref, aug_ref, all_ref), landings, refs = refs[:4], refs[4:4 + extra], refs[4 + extra:]
    (land, kv, tiles, arrive, ones_ref, acc_ref, msend, mrecv, fsend, frecv, gsend, grecv, hsend, hrecv) = refs
    first, second = info_ref[0], info_ref[1]
    me = lax.axis_index("ctx")
    part = me % 2
    twin = {"ctx": me + 1 - 2 * part}
    half_rows = msg_ref.shape[1]
    wide = sources * 2 * half_rows
    span = sources * rows
    factor = math.log2(math.e) / math.sqrt(head)
    lane = lane_of((half_rows, LANES))
    greet(me, count)

    def remote(src, dst, send, recv, where):
        return pltpu.make_async_remote_copy(src_ref=src, dst_ref=dst, send_sem=send, recv_sem=recv,
                                            device_id=where, device_id_type=MESH)

    def msg_copy(owner, dest):
        return remote(msg_ref.at[dest], land.at[owner], msend.at[dest], mrecv.at[owner], {"ctx": dest})

    def share_copy(source):
        return remote(kv.at[source, part], kv.at[source, part], fsend.at[source], frecv.at[source], twin)

    def tile_copy(owner, dest):
        return remote(tiles.at[dest], arrive.at[owner], gsend.at[dest], grecv.at[owner], {"ctx": dest})

    def start_msg(step, _):
        msg_copy(me, lax.rem(me + step, count)).start()

    lax.fori_loop(1, count, start_msg, None)
    hosted = hosted_copies(kinds, guests, landings, hsend, hrecv)
    for copy in hosted:
        copy.start()
    land[me] = msg_ref[me]

    def share(source):
        @pl.when(source != me)
        def _():
            msg_copy(source, me).wait_recv()

        kv[source, part] = land[source, :, LANES:]
        share_copy(source).start()

    def compute(index):
        base = index * sources
        stack = []
        for source in range(sources):
            share_copy(base + source).wait_recv()
            both = kv[base + source].reshape(rows, LANES)
            place = pl.ds(pl.multiple_of((base + source) * rows, rows), rows)
            all_ref[place] = both
            ones_ref[place] = jnp.where(lane_of(both.shape) < head, jnp.ones_like(both), both)
            tile = land[base + source, :, :LANES].astype(F32)
            stack.append(jnp.where(lane < head, tile, 0.0))
            stack.append(jnp.where(lane < head, swap_heads(tile, head), 0.0))
        queries = jnp.concatenate(stack, axis=0).astype(BF)
        acc_ref[...] = jnp.zeros_like(acc_ref)

        def visit(step, masked):
            start = pl.multiple_of(step * keys, keys)
            here = pl.ds(start, keys)
            raised = jnp.exp2(lax.dot_general(queries, all_ref[here], ONES_NT, preferred_element_type=F32) * factor)
            if masked:
                ok = allowed_block(0, 1, (wide, keys), first, second, part, base, start, rows, half_rows)
                raised = jnp.where(ok, raised, 0.0)
            acc_ref[...] += jnp.dot(raised.astype(BF), ones_ref[here], preferred_element_type=F32)

        sweep_keys(visit, index, count * rows - rows, part, base, rows, half_rows, keys, sources)
        for source in range(sources):
            tile = land[base + source, :, :LANES].astype(F32)
            outs = []
            for which in range(2):
                place = (2 * source + which) * half_rows
                acc = acc_ref[place:place + half_rows]
                turn = swap_heads(acc, head)
                outs.append(turn / acc if which == 0 else acc / turn)
                high, middle, low = three_parts(-math.sqrt(head) * jnp.log(turn))
                query = tile if which == 0 else swap_heads(tile, head)
                extra = jnp.where(lane == head, high, jnp.where(lane == head + 1, middle,
                                                                jnp.where(lane == head + 2, low, 0.0)))
                aug_ref[base + source, which] = jnp.where(lane < head, query, extra).astype(BF)
            out = jnp.where(lane < head, outs[0], outs[1])
            out_ref[base + source] = out
            tiles[base + source] = out.astype(BF)

            @pl.when(base + source != me)
            def _(source=source):
                tile_copy(me, base + source).start()

    def block(index, _):
        @pl.when(index < count // sources)
        def _():
            for source in range(sources):
                share(index * sources + source)

        @pl.when(index > 0)
        def _():
            compute(index - 1)

    lax.fori_loop(0, count // sources + 1, block, None)
    arrive[me] = tiles[me]

    def drain(other, _):
        share_copy(other).wait_send()

        @pl.when(other != me)
        def _():
            msg_copy(me, other).wait_send()
            tile_copy(me, other).wait_send()
            tile_copy(other, me).wait_recv()

    lax.fori_loop(0, count, drain, None)
    got_ref[...] = arrive[...]
    for copy in hosted:
        copy.wait()


def attend_back_kernel(head, rows, keys, sources, count, kinds, *refs):
    extra = len(kinds)
    (info_ref, aug_ref, out_ref, kv_ref, msg_ref), guests, refs = refs[:5], refs[5:5 + extra], refs[5 + extra:]
    (gotq_ref, gotk_ref), landings, refs = refs[:2], refs[2:2 + extra], refs[2 + extra:]
    (land, tiles, away, near, sums, arrive_q, arrive_k, kone_ref, vone_ref, kturn_ref, dk_ref, dv_ref, acc_ref,
     msend, mrecv, fsend, frecv, gsend, grecv, ksend, krecv, hsend, hrecv) = refs
    first, second = info_ref[0], info_ref[1]
    me = lax.axis_index("ctx")
    part = me % 2
    twin = {"ctx": me + 1 - 2 * part}
    half_rows = msg_ref.shape[1]
    wide = sources * 2 * half_rows
    factor = math.log2(math.e) / math.sqrt(head)
    shrink = 1.0 / math.sqrt(head)
    lane = lane_of((half_rows, LANES))
    greet(me, count)

    def remote(src, dst, send, recv, where):
        return pltpu.make_async_remote_copy(src_ref=src, dst_ref=dst, send_sem=send, recv_sem=recv,
                                            device_id=where, device_id_type=MESH)

    def msg_copy(owner, dest):
        return remote(msg_ref.at[dest], land.at[owner], msend.at[dest], mrecv.at[owner], {"ctx": dest})

    def share_copy(source):
        return remote(away.at[source], near.at[source], fsend.at[source], frecv.at[source], twin)

    def q_copy(owner, dest):
        return remote(tiles.at[dest], arrive_q.at[owner], gsend.at[dest], grecv.at[owner], {"ctx": dest})

    def k_copy(owner, dest):
        return remote(sums.at[dest], arrive_k.at[owner], ksend.at[dest], krecv.at[owner], {"ctx": dest})

    def start_msg(step, _):
        msg_copy(me, lax.rem(me + count - step, count)).start()

    lax.fori_loop(1, count, start_msg, None)
    hosted = hosted_copies(kinds, guests, landings, hsend, hrecv)
    for copy in hosted:
        copy.start()
    land[me] = msg_ref[me]
    whole = lane_of(kv_ref.shape)
    vone_ref[...] = jnp.where(whole < head, jnp.ones_like(kv_ref), kv_ref[...])
    kone_ref[...] = jnp.where(whole < head, kv_ref[...], jnp.ones_like(kv_ref))
    kturn_ref[...] = turned(kv_ref[...])
    dk_ref[...] = jnp.zeros_like(dk_ref)
    dv_ref[...] = jnp.zeros_like(dv_ref)

    def rows_of(source, which):
        return pl.ds(pl.multiple_of(source * rows + which * half_rows, half_rows), half_rows)

    def key_tile(source, which):
        here = rows_of(source, which)
        return jnp.where(lane < head, dk_ref[here] * shrink, dv_ref[here])

    def compute(index):
        base = index * sources
        stack_q, stack_d = [], []
        for source in range(sources):
            @pl.when(base + source != me)
            def _(source=source):
                msg_copy(base + source, me).wait_recv()

            grad = land[base + source].astype(F32)
            spread = grad * out_ref[base + source]
            for which in range(2):
                stack_q.append(aug_ref[base + source, which])
                mine = (lane < head) if which == 0 else (lane >= head)
                delta = jnp.sum(jnp.where(mine, spread, 0.0), axis=1, keepdims=True)
                high, middle, low = three_parts(-delta)
                extra = jnp.where(lane == 0, high, jnp.where(lane == 1, middle, jnp.where(lane == 2, low, 0.0)))
                moved = swap_heads(grad, head) if which == 0 else grad
                stack_d.append(jnp.where(lane < head, extra, moved).astype(BF))
        queries = jnp.concatenate(stack_q, axis=0)
        grads = jnp.concatenate(stack_d, axis=0)
        acc_ref[...] = jnp.zeros_like(acc_ref)

        def visit(step, masked):
            start = pl.multiple_of(step * keys, keys)
            here = pl.ds(start, keys)
            raw = lax.dot_general(kone_ref[here], queries, ONES_NT, preferred_element_type=F32)
            if masked:
                ok = allowed_block(1, 0, (keys, wide), first, second, part, base, start, rows, half_rows)
                prob = jnp.where(ok, jnp.exp2(jnp.where(ok, raw, 0.0) * factor), 0.0)
            else:
                prob = jnp.exp2(raw * factor)
            along = lax.dot_general(vone_ref[here], grads, ONES_NT, preferred_element_type=F32)
            score = (prob * along).astype(BF)
            dv_ref[here] += jnp.dot(prob.astype(BF), grads, preferred_element_type=F32)
            dk_ref[here] += jnp.dot(score, queries, preferred_element_type=F32)
            acc_ref[...] += jnp.dot(kturn_ref[:, here], score, preferred_element_type=F32)

        sweep_keys(visit, index, count * rows - rows, part, base, rows, half_rows, keys, sources)
        acc = acc_ref[...].T
        for source in range(sources):
            place = 2 * source * half_rows
            one = acc[place:place + half_rows]
            two = acc[place + half_rows:place + 2 * half_rows]
            tiles[base + source] = (jnp.where(lane < head, one, swap_heads(two, head)) * shrink).astype(BF)

            @pl.when(base + source != me)
            def _(source=source):
                q_copy(me, base + source).start()

            away[base + source] = key_tile(base + source, 1 - part).astype(BF)
            share_copy(base + source).start()

    def finish(index):
        for source in range(sources):
            block = index * sources + source
            share_copy(block).wait_recv()
            sums[block] = (key_tile(block, part) + near[block].astype(F32)).astype(BF)

            @pl.when(block != me)
            def _(block=block):
                k_copy(me, block).start()

    def sweep(step, _):
        index = count // sources - 1 - step

        @pl.when(index >= 0)
        def _():
            compute(jnp.maximum(index, 0))

        @pl.when(step > 0)
        def _():
            finish(index + 1)

    lax.fori_loop(0, count // sources + 1, sweep, None)
    arrive_q[me] = tiles[me]
    arrive_k[me] = sums[me]

    def drain(other, _):
        share_copy(other).wait_send()

        @pl.when(other != me)
        def _():
            msg_copy(me, other).wait_send()
            q_copy(me, other).wait_send()
            k_copy(me, other).wait_send()
            q_copy(other, me).wait_recv()
            k_copy(other, me).wait_recv()

    lax.fori_loop(0, count, drain, None)
    gotq_ref[...] = arrive_q[...]
    gotk_ref[...] = arrive_k[...]
    for copy in hosted:
        copy.wait()


def exchange_attend(msg, info, head, rows, hosted, collective_id):
    count, half_rows = msg.shape[0], msg.shape[1]
    keys, sources = 512, 2
    group = count * rows
    dma = pltpu.SemaphoreType.DMA((count,))
    S = jax.ShapeDtypeStruct
    tile = (count, half_rows, LANES)
    kinds = [kind for kind, _ in hosted]
    guests = [value for _, value in hosted]
    hdma = pltpu.SemaphoreType.DMA((len(hosted),))
    anywhere = [pl.BlockSpec(memory_space=pl.ANY)] * len(hosted)
    return pl.pallas_call(
        functools.partial(attend_kernel, head, rows, keys, sources, count, kinds),
        out_shape=(S(tile, BF), S(tile, F32), S((count, 2, half_rows, LANES), BF), S((group, LANES), BF),
                   *hosted_shapes(hosted)),
        in_specs=[pl.BlockSpec(memory_space=pltpu.SMEM)] + vmem_specs(1) + anywhere,
        out_specs=tuple(vmem_specs(4) + anywhere),
        scratch_shapes=[pltpu.VMEM((count, half_rows, 2 * LANES), BF), pltpu.VMEM((count, 2, half_rows, LANES), BF),
                        pltpu.VMEM(tile, BF), pltpu.VMEM(tile, BF), pltpu.VMEM((group, LANES), BF),
                        pltpu.VMEM((sources * rows, LANES), F32)] + [dma] * 6 + [hdma] * 2,
        compiler_params=pltpu.CompilerParams(collective_id=collective_id, has_side_effects=True,
                                             vmem_limit_bytes=VMEM_LIMIT),
        cost_estimate=pl.CostEstimate(flops=2 * group * group * LANES, bytes_accessed=6 << 20, transcendentals=0),
        name="attend",
    )(info, msg, *guests)


def exchange_attend_back(msg, info, augmented, attended, all_kv, head, rows, hosted, collective_id):
    count, half_rows = msg.shape[0], msg.shape[1]
    keys, sources = 512, 2
    group = count * rows
    dma = pltpu.SemaphoreType.DMA((count,))
    S = jax.ShapeDtypeStruct
    tile = (count, half_rows, LANES)
    kinds = [kind for kind, _ in hosted]
    guests = [value for _, value in hosted]
    hdma = pltpu.SemaphoreType.DMA((len(hosted),))
    anywhere = [pl.BlockSpec(memory_space=pl.ANY)] * len(hosted)
    long = (group, LANES)
    return pl.pallas_call(
        functools.partial(attend_back_kernel, head, rows, keys, sources, count, kinds),
        out_shape=(S(tile, BF), S(tile, BF), *hosted_shapes(hosted)),
        in_specs=[pl.BlockSpec(memory_space=pltpu.SMEM)] + vmem_specs(4) + anywhere,
        out_specs=tuple(vmem_specs(2) + anywhere),
        scratch_shapes=[pltpu.VMEM(tile, BF)] * 7 + [
            pltpu.VMEM(long, BF), pltpu.VMEM(long, BF), pltpu.VMEM((LANES, group), BF), pltpu.VMEM(long, F32),
            pltpu.VMEM(long, F32), pltpu.VMEM((LANES, sources * rows), F32)] + [dma] * 8 + [hdma] * 2,
        compiler_params=pltpu.CompilerParams(collective_id=collective_id, has_side_effects=True,
                                             vmem_limit_bytes=VMEM_LIMIT),
        cost_estimate=pl.CostEstimate(flops=5 * group * group * LANES, bytes_accessed=8 << 20, transcendentals=0),
        name="attend_back",
    )(info, augmented, attended, all_kv, msg, *guests)


def sum_kernel(jobs, sides, weights, lines, *refs):
    count = len(jobs)
    refs = list(refs)
    take = lambda number: [refs.pop(0) for _ in range(number)]
    lefts, lefts_y, rights = take(sides), take(sides), take(count)
    sent = [refs.pop(0) if job["late"] and job["kind"] == "pair" else None for job in jobs]
    early_y = [None if job["late"] else refs.pop(0) for job in jobs]
    (small_ref,) = take(1)
    outs, (small_out,) = take(weights), take(1)
    lefts_s, lefts_ys, rights_s, rights_ys = take(sides), take(sides), take(count), take(count)
    rights_y = [refs.pop(0) if job["late"] else early for job, early in zip(jobs, early_y)]
    (lbuf, rbuf, xp, xr, zp, us, ur, ds_, dr, fs, fr, cs, cr, stage, sm_s, sm_r,
     lsem, rsem, xs, xv, uss, urv, dss, drv, fss, frv, css, crv, osem, sms, smv, els, elv, ers, erv, yrs, yrv) = refs
    steps = sum(job["total"] for job in jobs)
    last = steps - 1
    tokens = lbuf.shape[-1] // 4
    me = lax.axis_index("ctx")
    y = lax.axis_index("dp")
    z = me // 4
    x = (me // 2) % 2
    c = me % 2
    top = lines - 1
    twin = {"ctx": me + 1 - 2 * c}
    across_x = {"ctx": me + 2 - 4 * x}
    across_y = {"dp": 1 - y}
    above = {"ctx": jnp.minimum(me + 4, 4 * top + me % 4)}
    below = {"ctx": jnp.maximum(me - 4, me % 4)}
    near = {"ctx": me + 4 - 8 * (z % 2)}
    far = {"ctx": me + 8 - 16 * (z // 2)}
    rounds = [twin, across_x, across_y, near, far]

    for buf in (ur, dr, zp):
        buf[...] = jnp.zeros_like(buf)
    sm_s[0] = small_ref[...]

    barrier = pltpu.get_barrier_semaphore()
    for where in (twin, across_x, across_y, far):
        pl.semaphore_signal(barrier, inc=1, device_id=where, device_id_type=MESH)

    @pl.when(z < top)
    def _():
        pl.semaphore_signal(barrier, inc=1, device_id=above, device_id_type=MESH)

    @pl.when(z > 0)
    def _():
        pl.semaphore_signal(barrier, inc=1, device_id=below, device_id_type=MESH)

    pl.semaphore_wait(barrier, 4 + (z < top).astype(jnp.int32) + (z > 0).astype(jnp.int32))

    def remote(src, dst, send, recv, where):
        return pltpu.make_async_remote_copy(src_ref=src, dst_ref=dst, send_sem=send, recv_sem=recv,
                                            device_id=where, device_id_type=MESH)

    def row_base(number):
        height = lefts_s[number].shape[2]
        return y * height if height < lefts[number].shape[2] else 0

    def column_base(number):
        width = 2 * rights_s[number].shape[1]
        return y * width if jobs[number]["kind"] == "quarter" else 0

    def left_copies(number):
        height = lefts_s[number].shape[2]
        rows = pl.ds(pl.multiple_of(row_base(number), PIECE), height)
        return [
            remote(lefts[number].at[:, :, rows, :], lefts_s[number], els.at[number, 0], elv.at[number, 0], twin),
            remote(lefts_y[number], lefts_ys[number], els.at[number, 1], elv.at[number, 1], twin),
        ]

    def right_own(number):
        width = rights_s[number].shape[1]
        start = pl.multiple_of(column_base(number) + (1 - c) * width, STRIP)
        return remote(rights[number].at[:, pl.ds(start, width)], rights_s[number], ers.at[number, 0],
                      erv.at[number, 0], twin)

    def right_forward(number):
        width = rights_s[number].shape[1]
        start = pl.multiple_of((1 - c) * width, STRIP)
        return remote(rights_y[number].at[:, pl.ds(start, width)], rights_ys[number], ers.at[number, 1],
                      erv.at[number, 1], twin)

    def right_cross(number, piece=None):
        width = 2 * rights_s[number].shape[1]
        kind = jobs[number]["kind"]
        source = sent[number] if kind == "pair" else rights[number]
        start = (1 - y) * width if kind == "quarter" else 0
        rows, inside = slice(None), 0
        size = width
        if piece is not None:
            rows = pl.ds(pl.multiple_of((piece & 1) * (tokens // 2), PIECE), tokens // 2)
            inside, size = (piece >> 1) * STRIP, STRIP
        place = pl.ds(pl.multiple_of(inside, STRIP), size)
        if piece is None:
            landing = rights_y[number]
        else:
            landing = rights_y[number].at[rows, place]
        return remote(source.at[rows, pl.ds(pl.multiple_of(start + inside, STRIP), size)], landing,
                      yrs.at[number], yrv.at[number], across_y)

    def x_copy(j):
        s = j & (RING - 1)
        return remote(xp.at[s, 1 - x], xr.at[s], xs.at[s], xv.at[s], across_x)

    def up_copy(j):
        s = j & (RING - 1)
        return remote(us.at[s], ur.at[s], uss.at[s], urv.at[s], above)

    def down_copy(j):
        s = j & (RING - 1)
        return remote(ds_.at[s], dr.at[s], dss.at[s], drv.at[s], below)

    def f_copy(j):
        s = j & (RING - 1)
        return remote(fs.at[s], fr.at[s], fss.at[s], frv.at[s], across_y)

    def c_copy(j):
        s = j & (RING - 1)
        return remote(cs.at[s], cr.at[s], css.at[s], crv.at[s], twin)

    def small_copy(k):
        return remote(sm_s.at[k], sm_r.at[k], sms.at[k], smv.at[k], rounds[k])

    def loads(number):
        job = jobs[number]
        left, s = job["left"], number % 2
        height, width = lefts_s[left].shape[2], rights_s[number].shape[1]
        own_rows = pl.ds(pl.multiple_of(row_base(left), PIECE), height)
        own_columns = pl.ds(pl.multiple_of(column_base(number) + c * width, STRIP), width)
        mine = pl.ds(pl.multiple_of(c * width, STRIP), width)
        copies = []
        for place, source in enumerate([lefts[left].at[:, :, own_rows, :], lefts_s[left], lefts_y[left],
                                        lefts_ys[left]]):
            copies.append(pltpu.make_async_copy(
                source, lbuf.at[s, :, :, pl.ds(0, height), pl.ds(place * tokens, tokens)], lsem.at[s, place]))
        for place, source in enumerate([rights[number].at[:, own_columns], rights_s[number],
                                        rights_y[number].at[:, mine], rights_ys[number]]):
            copies.append(pltpu.make_async_copy(
                source, rbuf.at[s, pl.ds(place * tokens, tokens), pl.ds(0, width)], rsem.at[s, place]))
        return copies

    def each_job(j, visit):
        begin = 0
        for number, job in enumerate(jobs):
            @pl.when((j >= begin) & (j < begin + job["total"]))
            def _(number=number, begin=begin):
                visit(number, j - begin)
            begin += job["total"]

    def begins():
        begin = 0
        for number, job in enumerate(jobs):
            yield number, job, begin
            begin += job["total"]

    def out_copies(number, k, j):
        job = jobs[number]
        o = j & (RING - 1)
        row = pl.multiple_of(lax.rem(k, job["subs"]) * PIECE, PIECE)
        column = pl.multiple_of(lax.div(k, job["subs"]) * STRIP, STRIP)
        width = rights_s[number].shape[1]
        copies = []
        for line in range(2):
            for core in range(2):
                out = outs[job["outs"][line if job["kind"] == "pair" else 0]]
                rows, columns = row, core * width + column
                if job["kind"] == "quarter":
                    columns = line * 2 * width + columns
                if job["kind"] == "drop":
                    rows = line * lefts_s[job["left"]].shape[2] + row
                copies.append(pltpu.make_async_copy(
                    stage.at[o, line, core],
                    out.at[pl.ds(pl.multiple_of(rows, PIECE), PIECE), pl.ds(pl.multiple_of(columns, STRIP), STRIP)],
                    osem.at[o, line, core]))
        return copies

    def out_wait(j):
        for copy in out_copies(0, 0, j):
            copy.wait()

    started = []
    for number, job, begin in begins():
        if job["left"] not in started:
            started.append(job["left"])
            for copy in left_copies(job["left"]):
                copy.start()
        right_own(number).start()
        if not job["late"]:
            right_forward(number).start()

    def step(t, _):
        slot = t & (RING - 1)

        for number, job, begin in begins():
            if job["late"]:
                ago = t - job["issue"]
                piece = ago - (ago >> 2)
                pieces = 4 * rights_s[number].shape[1] // STRIP

                @pl.when((ago >= 0) & (ago & 3 != 3) & (piece < pieces))
                def _(number=number, piece=piece):
                    right_cross(number, piece).start()

                @pl.when(t == begin - job["ahead"])
                def _(number=number):
                    right_cross(number).wait()
                    right_forward(number).start()

        done, before = [], 0
        for number, job, begin in begins():
            fresh = job["left"] not in done
            done.append(job["left"])

            @pl.when(t == max(before, begin - AHEAD))
            def _(number=number, job=job, fresh=fresh):
                if fresh:
                    for copy in left_copies(job["left"]):
                        copy.wait()
                right_own(number).wait()
                right_forward(number).wait()
                for copy in loads(number):
                    copy.start()

            before = begin

        for number, job, begin in begins():
            @pl.when(t == begin)
            def _(number=number):
                for copy in loads(number):
                    copy.wait()

        for k in range(len(rounds) + 1):
            @pl.when(t == LAG * k)
            def _(k=k):
                if k > 0:
                    small_copy(k - 1).wait()
                    total = sm_s[k - 1] + sm_r[k - 1]
                    if k == len(rounds):
                        small_out[...] = total
                    else:
                        sm_s[k] = total
                if k < len(rounds):
                    small_copy(k).start()

        @pl.when(t < steps)
        def _():
            which, begin_now, subs_now = 0, 0, jobs[0]["subs"]
            for number, job, begin in begins():
                here = t >= begin
                begin_now = jnp.where(here, begin, begin_now)
                subs_now = jnp.where(here, job["subs"], subs_now)
                which = jnp.where(here, number % 2, which)
            row = lax.rem(t - begin_now, subs_now) * PIECE
            column = lax.div(t - begin_now, subs_now) * STRIP
            rows = pl.ds(pl.multiple_of(row, PIECE), PIECE)
            left = lbuf[which, :, :, rows, :].reshape(2 * lines * SUB, 4 * tokens)
            right = rbuf[which, :, pl.ds(pl.multiple_of(column, STRIP), STRIP)]
            got = jnp.dot(left, right, preferred_element_type=F32).astype(BF)
            for line in range(lines):
                for side in range(2):
                    row = (2 * line + side) * SUB
                    xp[slot, side, line] = got[row:row + SUB]
            x_copy(t).start()

        @pl.when((t >= LAG) & (t - LAG <= last))
        def _():
            x_copy(t - LAG).wait()
            s = (t - LAG) & (RING - 1)
            zp[(t - LAG) & (2 * RING - 1)] = xp[s, x] + xr[s]

        ju = t - LAG * (1 + z)

        @pl.when((ju >= 0) & (ju <= last))
        def _():
            s = ju & (RING - 1)
            held = ju & (2 * RING - 1)

            @pl.when(z > 0)
            def _():
                up_copy(ju).wait_recv()
                zp[held, z] = zp[held, z] + ur[s, 0]

            @pl.when(z < top)
            def _():
                @pl.when(ju >= RING)
                def _():
                    up_copy(ju).wait_send()

                for m in range(top):
                    own = zp[held, jnp.minimum(z + 1 + m, top)]
                    if m + 1 < top:
                        own = own + ur[s, m + 1]
                    us[s, m] = own
                up_copy(ju).start()

        jd = t - LAG * (1 + top - z)

        @pl.when((jd >= 0) & (jd <= last))
        def _():
            s = jd & (RING - 1)
            held = jd & (2 * RING - 1)

            @pl.when(z < top)
            def _():
                down_copy(jd).wait_recv()
                zp[held, z] = zp[held, z] + dr[s, 0]

            @pl.when(z > 0)
            def _():
                @pl.when(jd >= RING)
                def _():
                    down_copy(jd).wait_send()

                for m in range(top):
                    own = zp[held, jnp.maximum(z - 1 - m, 0)]
                    if m + 1 < top:
                        own = own + dr[s, m + 1]
                    ds_[s, m] = own
                down_copy(jd).start()

        jf = t - LAG * (1 + top)

        @pl.when((jf >= 0) & (jf <= last))
        def _():
            fs[jf & (RING - 1)] = zp[jf & (2 * RING - 1), z]
            f_copy(jf).start()

        jo = jf - LAG

        @pl.when((jo >= 0) & (jo <= last))
        def _():
            f_copy(jo).wait()
            s = jo & (RING - 1)
            mine = pl.ds(pl.multiple_of(c * PIECE, PIECE), PIECE)
            away = pl.ds(pl.multiple_of((1 - c) * PIECE, PIECE), PIECE)
            cs[s, y] = fs[s, away]
            cs[s, 1 - y] = fr[s, away]
            c_copy(jo).start()
            stage[s, y, c] = fs[s, mine].astype(F32)
            stage[s, 1 - y, c] = fr[s, mine].astype(F32)

        jc = jo - LAG

        @pl.when((jc >= 0) & (jc <= last))
        def _():
            c_copy(jc).wait()
            s = jc & (RING - 1)
            stage[s, 0, 1 - c] = cr[s, 0].astype(F32)
            stage[s, 1, 1 - c] = cr[s, 1].astype(F32)

            def start(number, k):
                for copy in out_copies(number, k, jc):
                    copy.start()

            each_job(jc, start)

            @pl.when(jc >= LAG)
            def _():
                out_wait(jc - LAG)

    lax.fori_loop(0, last + LAG * (top + 3) + 1, step, None)
    for back in range(LAG):
        out_wait(last - back)
    for back in range(RING):
        j = last - back

        @pl.when(z < top)
        def _(j=j):
            up_copy(j).wait_send()

        @pl.when(z > 0)
        def _(j=j):
            down_copy(j).wait_send()


def sum_over_chips(lefts, works, small, lines, collective_id):
    S = jax.ShapeDtypeStruct
    jobs, landing_r, landing_y, outs, sent, early = [], [], [], [], [], []
    shaped = [own.reshape(2 * lines, 2, own.shape[0] // (4 * lines), own.shape[1]) for own, _ in lefts]
    crossed = [cross for _, cross in lefts]
    tokens = shaped[0].shape[-1]
    for work in works:
        job = {name: work[name] for name in ("left", "kind", "late", "issue", "ahead")}
        columns = work["own"].shape[1]
        width = columns // 4 if job["kind"] == "quarter" else columns // 2
        height = crossed[job["left"]].shape[2]
        job["subs"], job["strips"] = height // PIECE, width // STRIP
        job["total"] = job["subs"] * job["strips"]
        job["outs"] = []
        for _ in range(2 if job["kind"] == "pair" else 1):
            job["outs"].append(len(outs))
            outs.append(S((shaped[job["left"]].shape[2], columns), F32))
        landing_r.append(S((tokens, width), BF))
        if job["late"]:
            landing_y.append(S((tokens, 2 * width), BF))
            if job["kind"] == "pair":
                sent.append(work["cross"])
        else:
            early.append(work["cross"])
        jobs.append(job)
    steps = sum(job["total"] for job in jobs)
    top = lines - 1
    dma = pltpu.SemaphoreType.DMA
    ring = lambda *shape: pltpu.VMEM((RING,) + shape, BF)
    scratch = [
        pltpu.VMEM((2, 2 * lines, 2, max(value.shape[2] for value in crossed), 4 * tokens), BF),
        pltpu.VMEM((2, 4 * tokens, max(value.shape[1] for value in landing_r)), BF),
        ring(2, lines, SUB, STRIP), ring(lines, SUB, STRIP),
        pltpu.VMEM((2 * RING, lines, SUB, STRIP), BF),
        ring(top, SUB, STRIP), ring(top, SUB, STRIP), ring(top, SUB, STRIP), ring(top, SUB, STRIP),
        ring(SUB, STRIP), ring(SUB, STRIP), ring(2, PIECE, STRIP), ring(2, PIECE, STRIP),
        pltpu.VMEM((RING, 2, 2, PIECE, STRIP), F32),
        pltpu.VMEM((5,) + small.shape, F32),
        pltpu.VMEM((5,) + small.shape, F32),
        dma((2, 4)), dma((2, 4)),
    ] + [dma((RING,))] * 10 + [
        dma((RING, 2, 2)), dma((5,)), dma((5,)),
        dma((len(lefts), 2)), dma((len(lefts), 2)), dma((len(works), 2)), dma((len(works), 2)),
        dma((len(works),)), dma((len(works),)),
    ]
    anywhere = pl.BlockSpec(memory_space=pl.ANY)
    inside = pl.BlockSpec(memory_space=pltpu.VMEM)
    landings = [S(value.shape, BF) for value in crossed] * 2 + landing_r * 2 + landing_y
    operands = shaped + crossed + [work["own"] for work in works] + sent + early
    flops = 2 * steps * 2 * lines * SUB * STRIP * 4 * tokens
    got = pl.pallas_call(
        functools.partial(sum_kernel, jobs, len(lefts), len(outs), lines),
        out_shape=tuple(outs) + (S(small.shape, F32),) + tuple(landings),
        in_specs=[anywhere] * len(operands) + [inside],
        out_specs=tuple([anywhere] * len(outs) + [inside] + [anywhere] * len(landings)),
        scratch_shapes=scratch,
        compiler_params=pltpu.CompilerParams(collective_id=collective_id, has_side_effects=True,
                                             vmem_limit_bytes=VMEM_LIMIT),
        cost_estimate=pl.CostEstimate(flops=flops, bytes_accessed=steps * 1_100_000, transcendentals=0),
        name="sum_over_chips",
    )(*operands, small)
    return got[:len(outs)], got[len(outs)]


def call_plain(kernel, outs, args, smem=0, scratch=(), flops=0, moved=0, name=None):
    specs = [pl.BlockSpec(memory_space=pltpu.SMEM)] * smem + vmem_specs(len(args) - smem)
    many = isinstance(outs, (tuple, list))
    return pl.pallas_call(
        kernel,
        out_shape=tuple(outs) if many else outs,
        in_specs=specs,
        out_specs=tuple(vmem_specs(len(outs))) if many else vmem_specs(1)[0],
        scratch_shapes=list(scratch),
        compiler_params=pltpu.CompilerParams(vmem_limit_bytes=VMEM_LIMIT),
        cost_estimate=pl.CostEstimate(flops=flops, bytes_accessed=moved, transcendentals=0),
        name=name,
    )(*args)


def shape_of(shape, kind):
    return jax.ShapeDtypeStruct(shape, kind)


def sibling(value):
    count = lax.axis_size("ctx")
    return lax.ppermute(value, "ctx", [(i, i ^ 1) for i in range(count)])


def norm_back(grad, hidden, gain):
    scale = lax.rsqrt(jnp.mean(hidden * hidden, axis=-1, keepdims=True) + EPS)
    unit = hidden * scale
    inward = grad * gain
    gain_grad = jnp.sum(grad * unit, axis=0)
    return scale * (inward - unit * jnp.mean(inward * unit, axis=-1, keepdims=True)), gain_grad


def fast_device(tokens, lengths, cotangent, mixgain, mixentry, mixtaps, mixexit, lowgain, lowgate, lowlift,
                lowdrop, attgain, attquery, attkeys, attvalues, querygain, keysgain, attexit, topgain, topgate,
                toplift, topdrop):
    rows, width = tokens.shape
    head = querygain.shape[0]
    devices = lax.axis_size("ctx")
    lines = devices // 4
    half_rows = rows // 2
    place = lax.axis_index("ctx")
    core = place % 2
    first = lengths[0, 0]
    second = first + lengths[0, 1]
    mine = place * rows + jnp.arange(rows, dtype=jnp.int32)
    my_seg = segment_of(mine, first, second)
    begin = jnp.where(my_seg == 0, 0, jnp.where(my_seg == 1, first, second))
    position = (mine - begin).astype(F32)
    gains = [value.astype(F32) for value in (mixgain, lowgain, attgain, topgain)]
    mixgain_f, lowgain_f, attgain_f, topgain_f = gains
    taps_f = mixtaps.astype(F32)
    twice = lambda gain: jnp.tile(gain.astype(F32), LANES // head)[None, :]
    querygain_2, keysgain_2 = twice(querygain), twice(keysgain)
    spot = jnp.arange(LANES, dtype=jnp.int32) % (head // 2)
    angle = position[:, None] * (THETA ** (-spot.astype(F32) * 2.0 / head))[None, :]
    cosine = jnp.cos(angle)
    sine = jnp.sin(angle) * jnp.where(jnp.arange(LANES) % head < head // 2, -1.0, 1.0)[None, :]
    info = jnp.stack([first, second]).astype(jnp.int32)

    hidden = tokens.astype(F32)
    normed_one = root_mean_square_scale(hidden, mixgain_f).astype(BF)
    mixed = jnp.dot(normed_one, mixentry, preferred_element_type=F32)
    part_b, part_c, part_x = (mixed[:, i * width:(i + 1) * width] for i in range(3))
    product = (part_b * part_x).astype(BF)
    borrowed = passed_along(product[rows - 2:], "ctx", 1)
    extended = jnp.concatenate([borrowed, product], axis=0).astype(F32)
    fits_one = ((mine >= 1) & (segment_of(mine - 1, first, second) == my_seg)).astype(F32)[:, None]
    fits_two = ((mine >= 2) & (segment_of(mine - 2, first, second) == my_seg)).astype(F32)[:, None]
    conved = conv_local(extended, taps_f, fits_one, fits_two)
    gated = (part_c * conved).astype(BF)
    hidden_one = hidden + jnp.dot(gated, mixexit, preferred_element_type=F32)
    hidden_two, lownorm_t, gact_low, lact_low, lowinner_t = feed_low(
        hidden_one, lowgain_f[None, :], lowgate, lowlift, lowdrop)

    heads_q, heads_k = attquery.shape[1] // head, attkeys.shape[1] // head
    msg, normed_two_t, query_raw, key_raw = call_plain(
        functools.partial(project_kernel, head),
        (shape_of((devices, half_rows, 2 * LANES), BF), shape_of((width, rows), BF),
         shape_of((rows, attquery.shape[1]), F32), shape_of((rows, attkeys.shape[1]), F32)),
        (hidden_two, attgain_f[None, :], attquery, attkeys, attvalues, cosine, sine, querygain_2, keysgain_2),
        flops=2 * rows * width * 2 * width, moved=6 << 20, name="project")
    upright = lambda value: value.reshape(devices // 2, 2, value.shape[0] // devices, rows)
    over_dp = lambda value: lax.ppermute(value, "dp", [(0, 1), (1, 0)])
    gated_t, normed_one_t = gated.T, normed_one.T
    msg, gated_y, normed_one_y, cotangent_y = lax.optimization_barrier(
        (msg, over_dp(gated_t), over_dp(normed_one_t), over_dp(cotangent)))
    gated_y, normed_one_y = upright(gated_y), upright(normed_one_y)
    got, attended_f, augmented, all_kv, lowinner_y, lownorm_y = exchange_attend(
        msg, info, head, rows, [("rows", upright(lowinner_t)), ("whole", upright(lownorm_t))], 2)
    (output, grad, grad_low3, send, attended_t, topgain_grad, topnorm_t, topinner_t, keep_top, send_top) = feed_top(
        got, hidden_two, attexit, cotangent, topgain_f[None, :], topgate, toplift, topdrop)
    send, normed_two_y = lax.optimization_barrier((send, over_dp(normed_two_t)))
    normed_two_y = upright(normed_two_y)
    back_q, back_k, topinner_y, topnorm_y, attended_y, grad_low3_y = exchange_attend_back(
        send, info, augmented, attended_f, all_kv, head, rows,
        [("rows", upright(topinner_t)), ("whole", upright(topnorm_t)), ("whole", upright(attended_t)),
         ("columns", grad_low3)], 3)
    back_q, send_top = lax.optimization_barrier((back_q, send_top))
    top_y_one = over_dp(send_top[:half_rows])
    rawq_low, keep_kv, send_kv, grad_two, attgain_grad, querygain_grad, keysgain_grad = call_plain(
        functools.partial(project_back_kernel, head),
        (shape_of((rows, attquery.shape[1]), BF), shape_of((rows, attkeys.shape[1]), BF),
         shape_of((rows, attkeys.shape[1]), BF), shape_of((rows, width), F32), shape_of((1, width), F32),
         shape_of((1, LANES), F32), shape_of((1, LANES), F32)),
        (back_q, back_k, hidden_two, attgain_f[None, :], attquery, attkeys, attvalues, cosine, sine, querygain_2, keysgain_2,
         query_raw, key_raw, grad),
        flops=1 << 20, moved=1 << 10, name="project_back")
    fold = lambda value: value.reshape(LANES // head, head).sum(axis=0)
    querygain_grad, keysgain_grad = fold(querygain_grad), fold(keysgain_grad)
    grad, lowgain_grad, gb_low, grad_low1, keep_low, send_low = feed_low_back(
        grad_two, hidden_one, lowgain_f[None, :], gact_low, lact_low, lowgate, lowlift, lowdrop)
    grad, grad_low1, top_y_one = lax.optimization_barrier((grad, grad_low1, top_y_one))
    gated_grad = outer_dot(grad_low1, mixexit)
    part_c_grad = gated_grad * conved
    conved_grad = gated_grad * part_c
    _, pull_conv = jax.vjp(lambda ext, taps: conv_local(ext, taps, fits_one, fits_two), extended, taps_f)
    extended_grad, mixtaps_grad = pull_conv(conved_grad)
    returned_rim = passed_along(extended_grad[:2], "ctx", -1)
    product_grad = extended_grad[2:].at[rows - 2:].add(returned_rim)
    mixed_grad = jnp.concatenate(
        [product_grad * part_x, part_c_grad, product_grad * part_b], axis=1).astype(BF)
    hidden_grad, mixgain_grad = norm_back(outer_dot(mixed_grad, mixentry), hidden, mixgain_f)
    tokens_grad = grad + hidden_grad
    mixgain_grad, tokens_grad, top_y_two = lax.optimization_barrier(
        (mixgain_grad, tokens_grad, over_dp(send_top[half_rows:])))
    top_y = jnp.concatenate([top_y_one, top_y_two], axis=0)

    lefts = [(attended_t, attended_y), (topinner_t, topinner_y), (topnorm_t, topnorm_y), (normed_two_t, normed_two_y),
             (lowinner_t, lowinner_y), (lownorm_t, lownorm_y), (gated_t, gated_y), (normed_one_t, normed_one_y)]

    def work(left, kind, own, cross=None, issue=-1, ahead=12):
        return dict(left=left, kind=kind, own=own, cross=cross, late=issue >= 0, issue=issue, ahead=ahead)

    works = [work(0, "quarter", grad_low3, grad_low3_y), work(1, "drop", cotangent, cotangent_y),
             work(2, "pair", keep_top, top_y), work(3, "quarter", rawq_low, issue=0),
             work(3, "pair", keep_kv, send_kv, issue=5), work(4, "drop", gb_low, issue=10),
             work(5, "pair", keep_low, send_low, issue=20), work(6, "quarter", grad_low1, issue=68),
             work(7, "quarter", mixed_grad, issue=73)]
    heads = jnp.concatenate([querygain_grad, keysgain_grad, jnp.zeros((width - 2 * head,), F32)])
    small = jnp.concatenate([mixgain_grad[None, :], mixtaps_grad, lowgain_grad, attgain_grad, topgain_grad,
                             heads[None, :]], axis=0)
    grads, small = sum_over_chips(lefts, works, small, lines, 1)
    (attexit_grad, topdrop_grad, topgate_grad, toplift_grad, attquery_grad, attkeys_grad, attvalues_grad, lowdrop_grad,
     lowgate_grad, lowlift_grad, mixexit_grad, mixentry_grad) = grads
    return (output, tokens_grad, small[0], mixentry_grad, small[1:4], mixexit_grad, small[4], lowgate_grad,
            lowlift_grad, lowdrop_grad, small[5], attquery_grad, attkeys_grad, attvalues_grad, small[7, :head],
            small[7, head:2 * head], attexit_grad, small[6], topgate_grad, toplift_grad, topdrop_grad)


def solution(mesh):
    placed = (P(("dp", "ctx"), None), P("dp", None), P(("dp", "ctx"), None)) + (P(),) * 19
    split = {0: P(("dp", "ctx"), None), 1: P(("dp", "ctx"), None)}
    whole = (2, 4, 6, 10, 14, 15, 17)
    outs = tuple(split.get(i, P() if i in whole else P("ctx", None)) for i in range(21))
    small = mesh.shape["ctx"] == 16 and mesh.shape["dp"] == 2
    return jax.shard_map(fast_device if small else per_device, mesh=mesh, in_specs=placed, out_specs=outs,
                         check_vma=False)
```

```python
import functools
import math

import jax
import jax.numpy as jnp
from jax import lax
from jax.experimental import pallas as pl
from jax.experimental.pallas import tpu as pltpu
from jax.sharding import PartitionSpec as P

EPS = 1e-05
THETA = 1000000.0
NEGATIVE = -1e30


def passed_along(value, axis, steps):
    count = lax.axis_size(axis)
    first, last = (max(0, -steps), min(count, count - steps))
    return lax.ppermute(value, axis, [(source, source + steps) for source in range(first, last)])


def passed_along_2(block, axis, distance):
    devices = range(lax.axis_size(axis))
    route = [((i - distance) % len(devices), i) for i in devices]
    return lax.ppermute(block, axis, route)


def root_mean_square_scale(hidden, gain):
    return hidden * lax.rsqrt(jnp.mean(hidden * hidden, axis=-1, keepdims=True) + EPS) * gain


def rotary_embed(value_rows, position_index):
    half = value_rows.shape[-1] // 2
    freq = THETA ** (-jnp.arange(half, dtype=jnp.float32) * 2.0 / value_rows.shape[-1])
    angle = position_index.astype(jnp.float32)[:, None] * freq[None, :]
    cosine = jnp.cos(angle)[:, None, :]
    sine = jnp.sin(angle)[:, None, :]
    front = value_rows[..., :half]
    behind = value_rows[..., half:]
    return jnp.concatenate(
        [front * cosine - behind * sine, behind * cosine + front * sine], axis=-1
    )


def head_prep(raw, gain, position_index, heads):
    shaped = raw.reshape(raw.shape[0], heads, -1)
    return rotary_embed(root_mean_square_scale(shaped, gain), position_index)


def segment_of(where, first, second):
    return (where >= first).astype(jnp.int32) + (where >= second).astype(jnp.int32)


def block_width(count):
    best = 1
    for candidate in range(1, min(count, 1024) + 1):
        if count % candidate == 0:
            best = candidate
    return best


def sweep(carry, count, visit):
    width = block_width(count)
    return lax.fori_loop(
        0, count // width, lambda index, inner: visit(inner, index * width, width), carry
    )


def inner_dot(left, right):
    return lax.dot_general(
        left, right, (((0,), (0,)), ((), ())), preferred_element_type=jnp.float32
    )


def outer_dot(left, right):
    return lax.dot_general(
        left, right, (((1,), (1,)), ((), ())), preferred_element_type=jnp.float32
    )


def scores_of(query_part, key_part, query_where, key_where, query_seg, key_seg, scale):
    raw = (
        jnp.einsum("tkgd,pkd->kgtp", query_part, key_part, preferred_element_type=jnp.float32)
        * scale
    )
    allowed = (query_seg[:, None] == key_seg[None, :]) & (
        query_where[:, None] >= key_where[None, :]
    )
    return (raw, allowed)


def grad_block(
    query_part,
    grad_part,
    logsum_part,
    delta_part,
    key_part,
    value_part,
    query_where,
    key_where,
    query_seg,
    key_seg,
    scale,
):
    raw, allowed = scores_of(
        query_part, key_part, query_where, key_where, query_seg, key_seg, scale
    )
    prob = jnp.where(allowed, jnp.exp(raw - logsum_part[..., None]), 0.0)
    prob_grad = jnp.einsum(
        "tkgd,pkd->kgtp", grad_part, value_part, preferred_element_type=jnp.float32
    )
    score_grad = (prob * (prob_grad - delta_part[..., None])).astype(jnp.bfloat16)
    query_grad = (
        jnp.einsum("kgtp,pkd->tkgd", score_grad, key_part, preferred_element_type=jnp.float32)
        * scale
    )
    key_grad = (
        jnp.einsum("kgtp,tkgd->pkd", score_grad, query_part, preferred_element_type=jnp.float32)
        * scale
    )
    value_grad = jnp.einsum(
        "kgtp,tkgd->pkd", prob.astype(jnp.bfloat16), grad_part, preferred_element_type=jnp.float32
    )
    return (query_grad, key_grad, value_grad)


def conv_local(extended, taps, fits_one, fits_two):
    rows = extended.shape[0] - 2
    return (
        taps[2] * extended[2:]
        + taps[1] * extended[1 : rows + 1] * fits_one
        + taps[0] * extended[:rows] * fits_two
    )


def feed_forward(hidden, gain, gate_weight, lift_weight, drop_weight):
    fnormed = root_mean_square_scale(hidden, gain).astype(jnp.bfloat16)
    gate_act = jnp.dot(fnormed, gate_weight, preferred_element_type=jnp.float32)
    lift_act = jnp.dot(fnormed, lift_weight, preferred_element_type=jnp.float32)
    inner = (jax.nn.silu(gate_act) * lift_act).astype(jnp.bfloat16)
    result = hidden + jnp.dot(inner, drop_weight, preferred_element_type=jnp.float32)
    return (result, (fnormed, gate_act, lift_act, inner))


def feed_back(grad, hidden, gain, kept, gate_weight, lift_weight, drop_weight):
    fnormed, gate_act, lift_act, inner = kept
    grad_low = grad.astype(jnp.bfloat16)
    drop_grad = inner_dot(inner, grad_low)
    inner_grad = outer_dot(grad_low, drop_weight)
    _, pull_gate = jax.vjp(
        lambda gate_in, lift_in: jax.nn.silu(gate_in) * lift_in, gate_act, lift_act
    )
    gate_grad, lift_grad = pull_gate(inner_grad)
    gate_low = gate_grad.astype(jnp.bfloat16)
    lift_low = lift_grad.astype(jnp.bfloat16)
    gate_wgrad = inner_dot(fnormed, gate_low)
    lift_wgrad = inner_dot(fnormed, lift_low)
    normed_grad = outer_dot(gate_low, gate_weight) + outer_dot(lift_low, lift_weight)
    _, pull_norm = jax.vjp(root_mean_square_scale, hidden, gain)
    hidden_grad, gain_grad = pull_norm(normed_grad)
    return (grad + hidden_grad, (gain_grad, gate_wgrad, lift_wgrad, drop_grad))


def per_device(
    tokens,
    lengths,
    cotangent,
    mixgain,
    mixentry,
    mixtaps,
    mixexit,
    lowgain,
    lowgate,
    lowlift,
    lowdrop,
    attgain,
    attquery,
    attkeys,
    attvalues,
    querygain,
    keysgain,
    attexit,
    topgain,
    topgate,
    toplift,
    topdrop,
):
    rows = tokens.shape[0]
    width_model = tokens.shape[1]
    head_size = querygain.shape[0]
    query_heads = attquery.shape[1] // head_size
    kv_heads = attkeys.shape[1] // head_size
    shared_gradient = query_heads // kv_heads
    scale = 1.0 / math.sqrt(head_size)
    place = lax.axis_index("ctx")
    first = lengths[0, 0]
    second = first + lengths[0, 1]
    mine = place * rows + jnp.arange(rows, dtype=jnp.int32)
    my_seg = segment_of(mine, first, second)
    begin = jnp.where(my_seg == 0, 0, jnp.where(my_seg == 1, first, second))
    position_index = mine - begin
    last_row = place * rows + rows - 1
    mixgain_f = mixgain.astype(jnp.float32)
    taps_f = mixtaps.astype(jnp.float32)
    lowgain_f = lowgain.astype(jnp.float32)
    attgain_f = attgain.astype(jnp.float32)
    querygain_f = querygain.astype(jnp.float32)
    keysgain_f = keysgain.astype(jnp.float32)
    topgain_f = topgain.astype(jnp.float32)
    hidden = tokens.astype(jnp.float32)
    normed_one = root_mean_square_scale(hidden, mixgain_f).astype(jnp.bfloat16)
    mixed = jnp.dot(normed_one, mixentry, preferred_element_type=jnp.float32)
    part_b = mixed[:, :width_model]
    part_c = mixed[:, width_model : 2 * width_model]
    part_x = mixed[:, 2 * width_model :]
    product = (part_b * part_x).astype(jnp.bfloat16)
    borrowed = passed_along(product[rows - 2 :], "ctx", 1)
    extended = jnp.concatenate([borrowed, product], axis=0).astype(jnp.float32)
    fits_one = ((mine >= 1) & (segment_of(mine - 1, first, second) == my_seg)).astype(jnp.float32)[
        :, None
    ]
    fits_two = ((mine >= 2) & (segment_of(mine - 2, first, second) == my_seg)).astype(jnp.float32)[
        :, None
    ]
    conved = conv_local(extended, taps_f, fits_one, fits_two)
    gated = (part_c * conved).astype(jnp.bfloat16)
    hidden_one = hidden + jnp.dot(gated, mixexit, preferred_element_type=jnp.float32)
    hidden_two, kept_low = feed_forward(hidden_one, lowgain_f, lowgate, lowlift, lowdrop)
    normed_two = root_mean_square_scale(hidden_two, attgain_f).astype(jnp.bfloat16)
    query_unrotated = jnp.dot(normed_two, attquery, preferred_element_type=jnp.float32)
    key_unrotated = jnp.dot(normed_two, attkeys, preferred_element_type=jnp.float32)
    value_projected = jnp.dot(normed_two, attvalues, preferred_element_type=jnp.float32)
    query_low = head_prep(query_unrotated, querygain_f, position_index, query_heads).astype(
        jnp.bfloat16
    )
    key_low = head_prep(key_unrotated, keysgain_f, position_index, kv_heads).astype(jnp.bfloat16)
    value_low = value_projected.astype(jnp.bfloat16).reshape(rows, kv_heads, head_size)
    query_grouped = query_low.reshape(rows, kv_heads, shared_gradient, head_size)

    def stat_visit(carry, keys_in, start, offset, width):
        top, total = carry
        key_part = lax.dynamic_slice_in_dim(keys_in, offset, width, 0)
        key_where = start + offset + jnp.arange(width, dtype=jnp.int32)
        raw, allowed = scores_of(
            query_grouped,
            key_part,
            mine,
            key_where,
            my_seg,
            segment_of(key_where, first, second),
            scale,
        )
        new_top = jnp.maximum(top, jnp.max(jnp.where(allowed, raw, NEGATIVE), axis=-1))
        weights = jnp.where(allowed, jnp.exp(raw - new_top[..., None]), 0.0)
        total = total * jnp.exp(top - new_top) + jnp.sum(weights, axis=-1)
        return (new_top, total)

    stat_state = (
        jnp.full((kv_heads, shared_gradient, rows), NEGATIVE, jnp.float32),
        jnp.zeros((kv_heads, shared_gradient, rows), jnp.float32),
    )
    piece = lax.all_gather(key_low, "ctx", axis=0, tiled=True)
    start = jnp.int32(0)
    count = piece.shape[0]

    def stat_running(inner):
        return sweep(
            inner, count, lambda acc, offset, width: stat_visit(acc, piece, start, offset, width)
        )

    top, total = lax.cond(start > last_row, lambda inner: inner, stat_running, stat_state)
    logsum = top + jnp.log(total)

    def forward_visit(accum, keys_in, values_in, start, offset, width):
        key_part = lax.dynamic_slice_in_dim(keys_in, offset, width, 0)
        value_part = lax.dynamic_slice_in_dim(values_in, offset, width, 0)
        key_where = start + offset + jnp.arange(width, dtype=jnp.int32)
        raw, allowed = scores_of(
            query_grouped,
            key_part,
            mine,
            key_where,
            my_seg,
            segment_of(key_where, first, second),
            scale,
        )
        prob_low = jnp.where(allowed, jnp.exp(raw - logsum[..., None]), 0.0).astype(jnp.bfloat16)
        return accum + jnp.einsum(
            "kgtp,pkd->kgtd", prob_low, value_part, preferred_element_type=jnp.float32
        )

    forward_start = jnp.int32(0)
    keys_in = lax.all_gather(key_low, "ctx", axis=0, tiled=True)
    values_in = lax.all_gather(value_low, "ctx", axis=0, tiled=True)
    forward_count = keys_in.shape[0]

    def forward_running(inner):
        return sweep(
            inner,
            forward_count,
            lambda acc, offset, width: forward_visit(
                acc, keys_in, values_in, forward_start, offset, width
            ),
        )

    accum = lax.cond(
        forward_start > last_row,
        lambda inner: inner,
        forward_running,
        jnp.zeros((kv_heads, shared_gradient, rows, head_size), jnp.float32),
    )
    attended = accum.transpose(2, 0, 1, 3).reshape(rows, -1)
    attended_low = attended.astype(jnp.bfloat16)
    hidden_three = hidden_two + jnp.dot(attended_low, attexit, preferred_element_type=jnp.float32)
    output, kept_top = feed_forward(hidden_three, topgain_f, topgate, toplift, topdrop)
    grad = cotangent.astype(jnp.float32)
    grad, top_grads = feed_back(grad, hidden_three, topgain_f, kept_top, topgate, toplift, topdrop)
    grad_low = grad.astype(jnp.bfloat16)
    attexit_grad = inner_dot(attended_low, grad_low)
    out_grads = (
        outer_dot(grad_low, attexit)
        .astype(jnp.bfloat16)
        .reshape(rows, kv_heads, shared_gradient, head_size)
    )
    delta = jnp.einsum(
        "tkgd,tkgd->kgt",
        out_grads.astype(jnp.float32),
        attended.reshape(rows, kv_heads, shared_gradient, head_size),
    )
    cycle_size = lax.axis_size("ctx")

    def cycle_visit(state, keys_in, values_in, start, offset, width):
        query_acc, key_acc, value_acc = state
        key_part = lax.dynamic_slice_in_dim(keys_in, offset, width, 0)
        value_part = lax.dynamic_slice_in_dim(values_in, offset, width, 0)
        key_where = start + offset + jnp.arange(width, dtype=jnp.int32)
        query_grad, key_grad, value_grad = grad_block(
            query_grouped,
            out_grads,
            logsum,
            delta,
            key_part,
            value_part,
            mine,
            key_where,
            my_seg,
            segment_of(key_where, first, second),
            scale,
        )
        key_acc = lax.dynamic_update_slice_in_dim(
            key_acc, lax.dynamic_slice_in_dim(key_acc, offset, width, 0) + key_grad, offset, 0
        )
        value_acc = lax.dynamic_update_slice_in_dim(
            value_acc, lax.dynamic_slice_in_dim(value_acc, offset, width, 0) + value_grad, offset, 0
        )
        return (query_acc + query_grad, key_acc, value_acc)

    def cycle_step(step, carry):
        keys_cur, values_cur, key_acc, value_acc, query_acc = carry
        anchor = (place - step + cycle_size) % cycle_size
        start = anchor * rows

        def cycle_running(state):
            return sweep(
                state,
                rows,
                lambda acc, offset, width: cycle_visit(
                    acc, keys_cur, values_cur, start, offset, width
                ),
            )

        query_acc, key_acc, value_acc = lax.cond(
            start > last_row, lambda state: state, cycle_running, (query_acc, key_acc, value_acc)
        )
        keys_cur, values_cur = passed_along((keys_cur, values_cur), "ctx", 1)
        key_acc, value_acc = (
            passed_along_2(key_acc.astype(jnp.bfloat16), "ctx", 1).astype(key_acc.dtype),
            passed_along_2(value_acc.astype(jnp.bfloat16), "ctx", 1).astype(value_acc.dtype),
        )
        return (keys_cur, values_cur, key_acc, value_acc, query_acc)

    cycle_state = (
        key_low,
        value_low,
        jnp.zeros((rows, kv_heads, head_size), jnp.float32),
        jnp.zeros((rows, kv_heads, head_size), jnp.float32),
        jnp.zeros((rows, kv_heads, shared_gradient, head_size), jnp.float32),
    )
    _, _, key_grads, value_grads, query_acc = lax.fori_loop(0, cycle_size, cycle_step, cycle_state)
    _, pull_query = jax.vjp(
        lambda raw, gain: head_prep(raw, gain, position_index, query_heads),
        query_unrotated,
        querygain_f,
    )
    query_raw_grad, querygain_grad = pull_query(query_acc.reshape(rows, query_heads, head_size))
    _, pull_key = jax.vjp(
        lambda raw, gain: head_prep(raw, gain, position_index, kv_heads), key_unrotated, keysgain_f
    )
    key_raw_grad, keysgain_grad = pull_key(key_grads)
    query_raw_low = query_raw_grad.astype(jnp.bfloat16)
    key_raw_low = key_raw_grad.astype(jnp.bfloat16)
    value_raw_low = value_grads.reshape(rows, -1).astype(jnp.bfloat16)
    attquery_grad = inner_dot(normed_two, query_raw_low)
    attkeys_grad = inner_dot(normed_two, key_raw_low)
    attvalues_grad = inner_dot(normed_two, value_raw_low)
    normed_two_grad = (
        outer_dot(query_raw_low, attquery)
        + outer_dot(key_raw_low, attkeys)
        + outer_dot(value_raw_low, attvalues)
    )
    _, pull_att = jax.vjp(root_mean_square_scale, hidden_two, attgain_f)
    hidden_two_grad, attgain_grad = pull_att(normed_two_grad)
    grad = grad + hidden_two_grad
    grad, low_grads = feed_back(grad, hidden_one, lowgain_f, kept_low, lowgate, lowlift, lowdrop)
    grad_low = grad.astype(jnp.bfloat16)
    mixexit_grad = inner_dot(gated, grad_low)
    gated_grad = outer_dot(grad_low, mixexit)
    part_c_grad = gated_grad * conved
    conved_grad = gated_grad * part_c
    _, pull_conv = jax.vjp(
        lambda ext, taps: conv_local(ext, taps, fits_one, fits_two), extended, taps_f
    )
    extended_grad, mixtaps_grad = pull_conv(conved_grad)
    returned_rim = passed_along(extended_grad[:2], "ctx", -1)
    product_grad = extended_grad[2:].at[rows - 2 :].add(returned_rim)
    mixed_grad = jnp.concatenate(
        [product_grad * part_x, part_c_grad, product_grad * part_b], axis=1
    ).astype(jnp.bfloat16)
    mixentry_grad = inner_dot(normed_one, mixed_grad)
    normed_one_grad = outer_dot(mixed_grad, mixentry)
    _, pull_mix = jax.vjp(root_mean_square_scale, hidden, mixgain_f)
    hidden_grad, mixgain_grad = pull_mix(normed_one_grad)
    tokens_grad = grad + hidden_grad
    lowgain_grad, lowgate_grad, lowlift_grad, lowdrop_grad = low_grads
    topgain_grad, topgate_grad, toplift_grad, topdrop_grad = top_grads
    shares = (
        lax.psum_scatter(mixentry_grad, "ctx", scatter_dimension=0, tiled=True),
        lax.psum_scatter(mixexit_grad, "ctx", scatter_dimension=0, tiled=True),
        lax.psum_scatter(lowgate_grad, "ctx", scatter_dimension=0, tiled=True),
        lax.psum_scatter(lowlift_grad, "ctx", scatter_dimension=0, tiled=True),
        lax.psum_scatter(lowdrop_grad, "ctx", scatter_dimension=0, tiled=True),
        lax.psum_scatter(attquery_grad, "ctx", scatter_dimension=0, tiled=True),
        lax.psum_scatter(attkeys_grad, "ctx", scatter_dimension=0, tiled=True),
        lax.psum_scatter(attvalues_grad, "ctx", scatter_dimension=0, tiled=True),
        lax.psum_scatter(attexit_grad, "ctx", scatter_dimension=0, tiled=True),
        lax.psum_scatter(topgate_grad, "ctx", scatter_dimension=0, tiled=True),
        lax.psum_scatter(toplift_grad, "ctx", scatter_dimension=0, tiled=True),
        lax.psum_scatter(topdrop_grad, "ctx", scatter_dimension=0, tiled=True),
    )
    smalls = lax.psum(
        (
            mixgain_grad,
            mixtaps_grad,
            lowgain_grad,
            attgain_grad,
            querygain_grad,
            keysgain_grad,
            topgain_grad,
        ),
        "ctx",
    )
    summed = (
        lax.psum(shares[0].astype(jnp.bfloat16), "dp").astype(jnp.float32),
        lax.psum(shares[1].astype(jnp.bfloat16), "dp").astype(jnp.float32),
        lax.psum(shares[2].astype(jnp.bfloat16), "dp").astype(jnp.float32),
        lax.psum(shares[3].astype(jnp.bfloat16), "dp").astype(jnp.float32),
        lax.psum(shares[4].astype(jnp.bfloat16), "dp").astype(jnp.float32),
        lax.psum(shares[5].astype(jnp.bfloat16), "dp").astype(jnp.float32),
        lax.psum(shares[6].astype(jnp.bfloat16), "dp").astype(jnp.float32),
        lax.psum(shares[7].astype(jnp.bfloat16), "dp").astype(jnp.float32),
        lax.psum(shares[8].astype(jnp.bfloat16), "dp").astype(jnp.float32),
        lax.psum(shares[9].astype(jnp.bfloat16), "dp").astype(jnp.float32),
        lax.psum(shares[10].astype(jnp.bfloat16), "dp").astype(jnp.float32),
        lax.psum(shares[11].astype(jnp.bfloat16), "dp").astype(jnp.float32),
        lax.psum(smalls[0].astype(jnp.bfloat16), "dp").astype(jnp.float32),
        lax.psum(smalls[1].astype(jnp.bfloat16), "dp").astype(jnp.float32),
        lax.psum(smalls[2].astype(jnp.bfloat16), "dp").astype(jnp.float32),
        lax.psum(smalls[3].astype(jnp.bfloat16), "dp").astype(jnp.float32),
        lax.psum(smalls[4].astype(jnp.bfloat16), "dp").astype(jnp.float32),
        lax.psum(smalls[5].astype(jnp.bfloat16), "dp").astype(jnp.float32),
        lax.psum(smalls[6].astype(jnp.bfloat16), "dp").astype(jnp.float32),
    )
    return (
        output,
        tokens_grad,
        summed[12],
        summed[0],
        summed[13],
        summed[1],
        summed[14],
        summed[2],
        summed[3],
        summed[4],
        summed[15],
        summed[5],
        summed[6],
        summed[7],
        summed[16],
        summed[17],
        summed[8],
        summed[18],
        summed[9],
        summed[10],
        summed[11],
    )


LANES = 128
BF = jnp.bfloat16
F32 = jnp.float32
ONES_NT = (((1,), (1,)), ((), ()))
ONES_TN = (((0,), (0,)), ((), ()))
VMEM_LIMIT = 60 * 1024 * 1024
PIECE = 16
SUB = 2 * PIECE
STRIP = 256
RING = 16
LAG = 3
AHEAD = 8


def vmem_specs(count):
    return [pl.BlockSpec(memory_space=pltpu.VMEM)] * count


def lane_of(shape):
    return lax.broadcasted_iota(jnp.int32, shape, len(shape) - 1)


def row_of(ref):
    return ref[...].astype(F32).reshape(1, ref.shape[0])


def same_head(head):
    row = lax.broadcasted_iota(jnp.int32, (LANES, LANES), 0) // head
    column = lax.broadcasted_iota(jnp.int32, (LANES, LANES), 1) // head
    return jnp.where(row == column, 1.0 / head, 0.0).astype(F32)


def head_mean(value, blocks):
    return jnp.dot(value, blocks, precision=lax.Precision.HIGHEST, preferred_element_type=F32)


def other_half(value, head):
    lane = lane_of(value.shape)
    ahead = pltpu.roll(value, LANES - head // 2, 1)
    behind = pltpu.roll(value, head // 2, 1)
    return jnp.where(lane % head < head // 2, ahead, behind)


def swap_heads(value, head):
    return pltpu.roll(value, head, 1)


def three_parts(value):
    high = value.astype(BF)
    rest = value - high.astype(F32)
    middle = rest.astype(BF)
    low = (rest - middle.astype(F32)).astype(BF)
    return high.astype(F32), middle.astype(F32), low.astype(F32)


def project_kernel(head, hid_ref, gain_ref, wq_ref, wk_ref, wv_ref, cos_ref, sin_ref, qg_ref, kg_ref,
                   msg_ref, normt_ref, qraw_ref, kraw_ref):
    hid = hid_ref[...]
    scale = lax.rsqrt(jnp.mean(hid * hid, axis=-1, keepdims=True) + EPS)
    normed = hid * scale * row_of(gain_ref)
    normt_ref[...] = turned(normed)
    normed = normed.astype(BF)
    blocks = same_head(head)
    cosine, sine = cos_ref[...], sin_ref[...]
    half_rows = msg_ref.shape[1]
    lane = lane_of(cosine.shape)

    def prepared(raw, gain):
        unit = raw * lax.rsqrt(head_mean(raw * raw, blocks) + EPS) * gain
        return unit * cosine + other_half(unit, head) * sine

    def put(dest, start, tile):
        low = tile.astype(BF)
        for part in range(2):
            msg_ref[2 * dest + part, :, start:start + LANES] = low[part * half_rows:(part + 1) * half_rows]

    qraw = jnp.dot(normed, wq_ref[...], preferred_element_type=F32)
    qraw_ref[...] = qraw
    for tile in range(qraw.shape[1] // LANES):
        put(tile, 0, prepared(qraw[:, tile * LANES:(tile + 1) * LANES], qg_ref[...]))
    kraw = jnp.dot(normed, wk_ref[...], preferred_element_type=F32)
    kraw_ref[...] = kraw
    vraw = jnp.dot(normed, wv_ref[...], preferred_element_type=F32)
    for tile in range(kraw.shape[1] // LANES):
        keys = prepared(kraw[:, tile * LANES:(tile + 1) * LANES], kg_ref[...])
        values = vraw[:, tile * LANES:(tile + 1) * LANES]
        put(2 * tile, LANES, jnp.where(lane < head, keys, swap_heads(values, head)))
        put(2 * tile + 1, LANES, jnp.where(lane < head, swap_heads(keys, head), values))


def project_back_kernel(head, backq_ref, backk_ref, hid_ref, gain_ref, wq_ref, wk_ref, wv_ref, cos_ref, sin_ref, qg_ref,
                        kg_ref, qraw_ref, kraw_ref, grad_ref,
                        rawq_ref, keep_ref, send_ref, two_ref, again_ref, qgain_ref, kgain_ref):
    blocks = same_head(head)
    cosine, sine = cos_ref[...], sin_ref[...]
    lane = lane_of(cosine.shape)

    def fetch(source, dest):
        return jnp.concatenate([source[2 * dest], source[2 * dest + 1]], axis=0).astype(F32)

    def through(grad, raw, gain):
        scale = lax.rsqrt(head_mean(raw * raw, blocks) + EPS)
        unit = raw * scale
        turned = grad * cosine - other_half(grad, head) * sine
        gain_part = jnp.sum(turned * unit, axis=0, keepdims=True)
        inward = turned * gain
        return scale * (inward - unit * head_mean(inward * unit, blocks)), gain_part

    width_q = wq_ref.shape[1]
    width_k = wk_ref.shape[1]
    gain_total = jnp.zeros((1, LANES), F32)
    for tile in range(width_q // LANES):
        got, part = through(fetch(backq_ref, tile), qraw_ref[:, tile * LANES:(tile + 1) * LANES], qg_ref[...])
        gain_total = gain_total + part
        rawq_ref[:, tile * LANES:(tile + 1) * LANES] = got.astype(BF)
    qgain_ref[...] = gain_total
    gain_total = jnp.zeros((1, LANES), F32)
    key_tiles, value_tiles = [], []
    for tile in range(width_k // LANES):
        even, odd = fetch(backk_ref, 2 * tile), fetch(backk_ref, 2 * tile + 1)
        keys = jnp.where(lane < head, even, swap_heads(odd, head))
        values = jnp.where(lane < head, swap_heads(even, head), odd)
        got, part = through(keys, kraw_ref[:, tile * LANES:(tile + 1) * LANES], kg_ref[...])
        gain_total = gain_total + part
        key_tiles.append(got.astype(BF))
        value_tiles.append(values.astype(BF))
    kgain_ref[...] = gain_total
    keys, values = jnp.concatenate(key_tiles, axis=1), jnp.concatenate(value_tiles, axis=1)
    keep_ref[...], send_ref[...] = kept_first(keys, values)
    normed_grad = nt_dot(rawq_ref[...], wq_ref[...]) + nt_dot(keys, wk_ref[...]) + nt_dot(values, wv_ref[...])
    hid = hid_ref[...]
    scale = lax.rsqrt(jnp.mean(hid * hid, axis=-1, keepdims=True) + EPS)
    unit = hid * scale
    again_ref[...] = jnp.sum(normed_grad * unit, axis=0, keepdims=True)
    inward = normed_grad * row_of(gain_ref)
    two_ref[...] = grad_ref[...] + scale * (inward - unit * jnp.mean(inward * unit, axis=-1, keepdims=True))


def allowed_block(row_axis, key_axis, shape, first, second, part, base, start, rows, half_rows):
    row = lax.broadcasted_iota(jnp.int32, shape, row_axis)
    token = (base + row // (2 * half_rows)) * rows + part * half_rows + row % half_rows
    key = start + lax.broadcasted_iota(jnp.int32, shape, key_axis)
    begin = jnp.where(token >= second, second, jnp.where(token >= first, first, 0))
    return (key >= begin) & (key <= token)


MESH = pl.DeviceIdType.MESH


def turned(value):
    return value.astype(F32).T.astype(BF)


def norm_scale(hidden):
    return lax.rsqrt(jnp.mean(hidden * hidden, axis=-1, keepdims=True) + EPS)


def norm_pull(normed_grad, hidden, gain):
    scale = norm_scale(hidden)
    unit = hidden * scale
    inward = normed_grad * gain
    back = scale * (inward - unit * jnp.mean(inward * unit, axis=-1, keepdims=True))
    return back, jnp.sum(normed_grad * unit, axis=0, keepdims=True)


def kept_first(one, two):
    first = lax.axis_index("dp") == 0
    return jnp.where(first, one, two), jnp.where(first, two, one)


def nt_dot(left, right):
    return lax.dot_general(left, right, ONES_NT, preferred_element_type=F32)


def nn_dot(left, right):
    return jnp.dot(left, right, preferred_element_type=F32)


def activation_pull(gate_act, lift_act, sigma, inner_grad):
    gate_grad = inner_grad * lift_act * sigma * (1 + gate_act * (1 - sigma))
    return gate_grad.astype(BF), (inner_grad * gate_act * sigma).astype(BF)


def low_kernel(hid_ref, gain_ref, gate_ref, lift_ref, drop_ref,
               out_ref, normt_ref, gact_ref, lact_ref, innert_ref, norm_ref):
    step = pl.program_id(0)

    @pl.when(step == 0)
    def _():
        hid = hid_ref[...]
        normed = hid * norm_scale(hid) * row_of(gain_ref)
        norm_ref[...] = normed.astype(BF)
        normt_ref[...] = turned(normed)
        out_ref[...] = hid

    normed = norm_ref[...]
    gate_act = nn_dot(normed, gate_ref[...])
    lift_act = nn_dot(normed, lift_ref[...])
    inner = gate_act * jax.nn.sigmoid(gate_act) * lift_act
    gact_ref[...] = gate_act.astype(BF)
    lact_ref[...] = lift_act.astype(BF)
    innert_ref[...] = turned(inner)
    out_ref[...] += nn_dot(inner.astype(BF), drop_ref[...])


def low_back_kernel(grad_ref, hid_ref, gain_ref, gact_ref, lact_ref, gate_ref, lift_ref, drop_ref,
                    out_ref, again_ref, low_ref, outlow_ref, glow_ref, llow_ref, acc_ref):
    step = pl.program_id(0)

    @pl.when(step == 0)
    def _():
        low_ref[...] = grad_ref[...].astype(BF)
        acc_ref[...] = jnp.zeros_like(acc_ref)

    gate_act, lift_act = gact_ref[...].astype(F32), lact_ref[...].astype(F32)
    inner_grad = nt_dot(low_ref[...], drop_ref[...])
    gate_low, lift_low = activation_pull(gate_act, lift_act, jax.nn.sigmoid(gate_act), inner_grad)
    glow_ref[...], llow_ref[...] = kept_first(gate_low, lift_low)
    acc_ref[...] += nt_dot(gate_low, gate_ref[...]) + nt_dot(lift_low, lift_ref[...])

    @pl.when(step == pl.num_programs(0) - 1)
    def _():
        back, gain_part = norm_pull(acc_ref[...], hid_ref[...], row_of(gain_ref))
        again_ref[...] = gain_part
        out = grad_ref[...] + back
        out_ref[...] = out
        outlow_ref[...] = out.astype(BF)


def top_kernel(got_ref, two_ref, exit_ref, cot_ref, gain_ref, gate_ref, lift_ref, drop_ref,
               out_ref, grad_ref, gradlow_ref, send_ref, attt_ref, again_ref, normt_ref, innert_ref, keep_ref,
               senda_ref, sendb_ref, hid_ref, norm_ref, acc_ref):
    step = pl.program_id(0)
    half_rows = got_ref.shape[1]

    @pl.when(step == 0)
    def _():
        tiles = []
        for tile in range(got_ref.shape[0] // 2):
            tiles.append(jnp.concatenate([got_ref[2 * tile], got_ref[2 * tile + 1]], axis=0))
        attended = jnp.concatenate(tiles, axis=1)
        attt_ref[...] = turned(attended)
        hid = two_ref[...] + nn_dot(attended, exit_ref[...])
        hid_ref[...] = hid
        normed = hid * norm_scale(hid) * row_of(gain_ref)
        norm_ref[...] = normed.astype(BF)
        normt_ref[...] = turned(normed)
        out_ref[...] = hid
        acc_ref[...] = jnp.zeros_like(acc_ref)

    normed = norm_ref[...]
    gate_act = nn_dot(normed, gate_ref[...])
    lift_act = nn_dot(normed, lift_ref[...])
    sigma = jax.nn.sigmoid(gate_act)
    inner = gate_act * sigma * lift_act
    innert_ref[...] = turned(inner)
    out_ref[...] += nn_dot(inner.astype(BF), drop_ref[...])
    inner_grad = nt_dot(cot_ref[...], drop_ref[...])
    gate_low, lift_low = activation_pull(gate_act, lift_act, sigma, inner_grad)
    keep_ref[...], sent_part = kept_first(gate_low, lift_low)
    senda_ref[...], sendb_ref[...] = sent_part[:half_rows], sent_part[half_rows:]
    acc_ref[...] += nt_dot(gate_low, gate_ref[...]) + nt_dot(lift_low, lift_ref[...])

    @pl.when(step == pl.num_programs(0) - 1)
    def _():
        back, gain_part = norm_pull(acc_ref[...], hid_ref[...], row_of(gain_ref))
        again_ref[...] = gain_part
        grad = cot_ref[...].astype(F32) + back
        grad_ref[...] = grad
        low = grad.astype(BF)
        gradlow_ref[...] = low
        sent = nt_dot(low, exit_ref[...]).astype(BF)
        for tile in range(send_ref.shape[0] // 2):
            for part in range(2):
                send_ref[2 * tile + part] = sent[part * half_rows:(part + 1) * half_rows,
                                                 tile * LANES:(tile + 1) * LANES]


TILE = 512
WIDE_TILE = 1152


def whole_block(shape):
    return pl.BlockSpec(shape, lambda step, rank=len(shape): (0,) * rank)


def column_block(rows, tile=TILE):
    return pl.BlockSpec((rows, tile), lambda step: (0, step))


def row_block(columns, tile=TILE):
    return pl.BlockSpec((tile, columns), lambda step: (step, 0))


def call_tiled(kernel, tiles, ins, outs, scratch, flops, moved, name):
    return pl.pallas_call(
        kernel,
        grid=(tiles,),
        in_specs=[spec for _, spec in ins],
        out_specs=tuple(spec for _, spec in outs),
        out_shape=tuple(shape for shape, _ in outs),
        scratch_shapes=scratch,
        compiler_params=pltpu.CompilerParams(vmem_limit_bytes=VMEM_LIMIT, dimension_semantics=("arbitrary",)),
        cost_estimate=pl.CostEstimate(flops=flops, bytes_accessed=moved, transcendentals=0),
        name=name,
    )(*[value for value, _ in ins])


def feed_low(hidden, gain, gate, lift, drop):
    rows, width = hidden.shape
    ff = gate.shape[1]
    S = jax.ShapeDtypeStruct
    return call_tiled(
        low_kernel, ff // WIDE_TILE,
        [(hidden, whole_block((rows, width))), (gain, whole_block((width,))), (gate, column_block(width, WIDE_TILE)),
         (lift, column_block(width, WIDE_TILE)), (drop, row_block(width, WIDE_TILE))],
        [(S((rows, width), F32), whole_block((rows, width))), (S((width, rows), BF), whole_block((width, rows))),
         (S((rows, ff), BF), column_block(rows, WIDE_TILE)), (S((rows, ff), BF), column_block(rows, WIDE_TILE)),
         (S((ff, rows), BF), row_block(rows, WIDE_TILE))],
        [pltpu.VMEM((rows, width), BF)], 6 * rows * width * ff, 38 << 20, "feed_low")


def feed_low_back(grad, hidden, gain, gact, lact, gate, lift, drop):
    rows, width = hidden.shape
    ff = gate.shape[1]
    S = jax.ShapeDtypeStruct
    full = whole_block((rows, width))
    return call_tiled(
        low_back_kernel, ff // WIDE_TILE,
        [(grad, full), (hidden, full), (gain, whole_block((width,))), (gact, column_block(rows, WIDE_TILE)),
         (lact, column_block(rows, WIDE_TILE)), (gate, column_block(width, WIDE_TILE)), (lift, column_block(width, WIDE_TILE)),
         (drop, row_block(width, WIDE_TILE))],
        [(S((rows, width), F32), full), (S((1, width), F32), whole_block((1, width))), (S((rows, width), BF), full),
         (S((rows, width), BF), full), (S((rows, ff), BF), column_block(rows, WIDE_TILE)), (S((rows, ff), BF), column_block(rows, WIDE_TILE))],
        [pltpu.VMEM((rows, width), F32)], 1 << 20, 1 << 10, "feed_low_back")


def feed_top(got, two, exit_weight, cotangent, gain, gate, lift, drop):
    rows, width = two.shape
    ff = gate.shape[1]
    S = jax.ShapeDtypeStruct
    full = whole_block((rows, width))
    flat = whole_block((1, width))
    standing = whole_block((width, rows))
    return call_tiled(
        top_kernel, ff // TILE,
        [(got, whole_block(got.shape)), (two, full), (exit_weight, whole_block(exit_weight.shape)), (cotangent, full),
         (gain, whole_block((width,))), (gate, column_block(width)), (lift, column_block(width)), (drop, row_block(width))],
        [(S((rows, width), F32), full), (S((rows, width), F32), full), (S((rows, width), BF), full),
         (S(got.shape, BF), whole_block(got.shape)), (S((width, rows), BF), standing), (S((1, width), F32), flat),
         (S((width, rows), BF), standing), (S((ff, rows), BF), row_block(rows)), (S((rows, ff), BF), column_block(rows)),
         (S((rows // 2, ff), BF), column_block(rows // 2)), (S((rows // 2, ff), BF), column_block(rows // 2))],
        [pltpu.VMEM((rows, width), F32), pltpu.VMEM((rows, width), BF), pltpu.VMEM((rows, width), F32)],
        12 * rows * width * ff, 45 << 20, "feed_top")


MIX_TILE = 256
HALO = 16


def shifted(value, steps):
    return pltpu.roll(value, steps, 0)


def mix_kernel(tok_ref, prev_ref, pos_ref, gain_ref, taps_ref, entb_ref, entc_ref, entx_ref, exit_ref,
               out_ref, normt_ref, gatedt_ref, b_ref, c_ref, x_ref, conv_ref, prod_ref, norm_ref):
    step = pl.program_id(0)

    @pl.when(step == 0)
    def _():
        hid = tok_ref[...].astype(F32)
        normed = hid * norm_scale(hid) * row_of(gain_ref)
        norm_ref[HALO:] = normed.astype(BF)
        normt_ref[...] = turned(normed)
        before = prev_ref[...].astype(F32)
        norm_ref[:HALO] = (before * norm_scale(before) * row_of(gain_ref)).astype(BF)
        out_ref[...] = hid

    taps = taps_ref[...].astype(F32)
    part_b = nn_dot(norm_ref[...], entb_ref[...])
    part_x = nn_dot(norm_ref[...], entx_ref[...])
    part_c = nn_dot(norm_ref[HALO:], entc_ref[...])
    product = (part_b * part_x).astype(BF)
    prod_ref[...] = product
    product = product.astype(F32)
    one = jnp.where(pos_ref[...] >= 1.0, shifted(product, 1)[HALO:], 0.0)
    two = jnp.where(pos_ref[...] >= 2.0, shifted(product, 2)[HALO:], 0.0)
    conved = taps[2:3] * product[HALO:] + taps[1:2] * one + taps[0:1] * two
    gated = part_c * conved
    b_ref[...] = part_b[HALO:].astype(BF)
    c_ref[...] = part_c.astype(BF)
    x_ref[...] = part_x[HALO:].astype(BF)
    conv_ref[...] = conved.astype(BF)
    gatedt_ref[...] = turned(gated)
    out_ref[...] += nn_dot(gated.astype(BF), exit_ref[...])


def mix_back_kernel(grad_ref, low_ref, next_ref, cnext_ref, pos_ref, tok_ref, gain_ref, taps_ref, b_ref, c_ref, x_ref,
                    conv_ref, prod_ref, entb_ref, entc_ref, entx_ref, exit_ref,
                    out_ref, again_ref, taps_out_ref, mixed_ref, acc_ref):
    step = pl.program_id(0)
    rows, width = grad_ref.shape
    tile = b_ref.shape[1]

    @pl.when(step == 0)
    def _():
        acc_ref[...] = jnp.zeros_like(acc_ref)

    taps = taps_ref[...].astype(F32)
    lows = jnp.concatenate([low_ref[...], next_ref[...]], axis=0)
    gated_grad = nt_dot(lows, exit_ref[...])
    gate = jnp.concatenate([c_ref[...], cnext_ref[...]], axis=0).astype(F32)
    conved_grad = gated_grad * gate
    first = jnp.where(pos_ref[...] >= 1.0, conved_grad, 0.0)
    second = jnp.where(pos_ref[...] >= 2.0, conved_grad, 0.0)
    ahead_one = shifted(first, rows + HALO - 1)[:rows]
    ahead_two = shifted(second, rows + HALO - 2)[:rows]
    own = conved_grad[:rows]
    product_grad = taps[2:3] * own + taps[1:2] * ahead_one + taps[0:1] * ahead_two
    product = prod_ref[...].astype(F32)
    total = lambda value: jnp.sum(value, axis=0, keepdims=True)
    taps_out_ref[0:1] = total(shifted(product, 2)[HALO:] * second[:rows])
    taps_out_ref[1:2] = total(shifted(product, 1)[HALO:] * first[:rows])
    taps_out_ref[2:3] = total(product[HALO:] * own)
    b_low = (product_grad * x_ref[...].astype(F32)).astype(BF)
    c_low = (gated_grad[:rows] * conv_ref[...].astype(F32)).astype(BF)
    x_low = (product_grad * b_ref[...].astype(F32)).astype(BF)
    for place, value in enumerate((b_low, c_low, x_low)):
        mixed_ref[:, pl.ds(pl.multiple_of(place * width + step * tile, tile), tile)] = value
    acc_ref[...] += nt_dot(b_low, entb_ref[...]) + nt_dot(c_low, entc_ref[...]) + nt_dot(x_low, entx_ref[...])

    @pl.when(step == pl.num_programs(0) - 1)
    def _():
        back, gain_part = norm_pull(acc_ref[...], tok_ref[...].astype(F32), row_of(gain_ref))
        again_ref[...] = gain_part
        out_ref[...] = grad_ref[...] + back


def mix_specs(width):
    tiles = width // MIX_TILE
    entry = [pl.BlockSpec((width, MIX_TILE), lambda step, part=part: (0, part * tiles + step)) for part in range(3)]
    return tiles, entry, row_block(width, MIX_TILE)


def mix_forward(tokens, before, position, gain, taps, entry, exit_weight):
    rows, width = tokens.shape
    tiles, entry_specs, exit_spec = mix_specs(width)
    S = jax.ShapeDtypeStruct
    full = whole_block((rows, width))
    columns = column_block(rows, MIX_TILE)
    return call_tiled(
        mix_kernel, tiles,
        [(tokens, full), (before, whole_block(before.shape)), (position, whole_block(position.shape)),
         (gain, whole_block((width,))), (taps, column_block(3, MIX_TILE)), *[(entry, spec) for spec in entry_specs],
         (exit_weight, exit_spec)],
        [(S((rows, width), F32), full), (S((width, rows), BF), whole_block((width, rows))),
         (S((width, rows), BF), row_block(rows, MIX_TILE))] + [(S((rows, width), BF), columns)] * 4
        + [(S((rows + HALO, width), BF), column_block(rows + HALO, MIX_TILE))],
        [pltpu.VMEM((rows + HALO, width), BF)], 8 * rows * width * width, 12 << 20, "mix")


def mix_backward(grad, low, after, gate_after, position, tokens, gain, taps, kept, entry, exit_weight):
    rows, width = grad.shape
    tiles, entry_specs, exit_spec = mix_specs(width)
    S = jax.ShapeDtypeStruct
    full = whole_block((rows, width))
    flat = whole_block((1, width))
    columns = column_block(rows, MIX_TILE)
    part_b, part_c, part_x, conved, product = kept
    return call_tiled(
        mix_back_kernel, tiles,
        [(grad, full), (low, full), (after, whole_block(after.shape)), (gate_after, column_block(HALO, MIX_TILE)),
         (position, whole_block(position.shape)), (tokens, full), (gain, whole_block((width,))), (taps, column_block(3, MIX_TILE)),
         (part_b, columns), (part_c, columns), (part_x, columns), (conved, columns),
         (product, column_block(rows + HALO, MIX_TILE)), *[(entry, spec) for spec in entry_specs],
         (exit_weight, exit_spec)],
        [(S((rows, width), F32), full), (S((1, width), F32), flat), (S((3, width), F32), column_block(3, MIX_TILE)),
         (S((rows, 3 * width), BF), whole_block((rows, 3 * width)))],
        [pltpu.VMEM((rows, width), F32)], 8 * rows * width * width, 16 << 20, "mix_back")


def sweep_keys(visit, index, tail, part, base, rows, half_rows, keys, sources):
    lowest = base * rows + part * half_rows
    end = (base + sources - 1) * rows + (part + 1) * half_rows
    count = (end + keys - 1) // keys
    free = jnp.where(end > tail, 0, jnp.maximum((lowest + 1) // keys - 1, 0))
    lax.fori_loop(0, free, lambda step, _: visit(step + 1, False), None)
    lax.fori_loop(0, count - free, lambda step, _: visit(jnp.where(step == 0, 0, free + step), True), None)


def greet(me, count):
    barrier = pltpu.get_barrier_semaphore()

    def hello(step, _):
        pl.semaphore_signal(barrier, inc=1, device_id={"ctx": lax.rem(me + step, count)}, device_id_type=MESH)

    lax.fori_loop(1, count, hello, None)
    pl.semaphore_signal(barrier, inc=1, device_id={"dp": 1 - lax.axis_index("dp")}, device_id_type=MESH)
    pl.semaphore_wait(barrier, count)


def hosted_copies(kinds, sources, landings, sends, recvs):
    y = lax.axis_index("dp")
    copies = []
    for number, (kind, source, landing) in enumerate(zip(kinds, sources, landings)):
        if kind == "rows":
            height = landing.shape[2]
            source = source.at[:, :, pl.ds(pl.multiple_of((1 - y) * height, PIECE), height), :]
        if kind == "columns":
            width = landing.shape[1]
            source = source.at[:, pl.ds(pl.multiple_of((1 - y) * width, STRIP), width)]
        copies.append(pltpu.make_async_remote_copy(
            src_ref=source, dst_ref=landing, send_sem=sends.at[number], recv_sem=recvs.at[number],
            device_id={"dp": 1 - y}, device_id_type=MESH))
    return copies


def hosted_shapes(hosted):
    shapes = []
    for kind, value in hosted:
        shape = list(value.shape)
        if kind == "rows":
            shape[2] //= 2
        if kind == "columns":
            shape[1] //= 2
        shapes.append(jax.ShapeDtypeStruct(tuple(shape), value.dtype))
    return shapes


def attend_kernel(head, rows, keys, sources, count, kinds, *refs):
    extra = len(kinds)
    (info_ref, msg_ref), guests, refs = refs[:2], refs[2:2 + extra], refs[2 + extra:]
    (got_ref, out_ref, aug_ref, all_ref), landings, refs = refs[:4], refs[4:4 + extra], refs[4 + extra:]
    (land, kv, tiles, arrive, ones_ref, acc_ref, msend, mrecv, fsend, frecv, gsend, grecv, hsend, hrecv) = refs
    first, second = info_ref[0], info_ref[1]
    me = lax.axis_index("ctx")
    part = me % 2
    twin = {"ctx": me + 1 - 2 * part}
    half_rows = msg_ref.shape[1]
    wide = sources * 2 * half_rows
    span = sources * rows
    factor = math.log2(math.e) / math.sqrt(head)
    lane = lane_of((half_rows, LANES))
    greet(me, count)

    def remote(src, dst, send, recv, where):
        return pltpu.make_async_remote_copy(src_ref=src, dst_ref=dst, send_sem=send, recv_sem=recv,
                                            device_id=where, device_id_type=MESH)

    def msg_copy(owner, dest):
        return remote(msg_ref.at[dest], land.at[owner], msend.at[dest], mrecv.at[owner], {"ctx": dest})

    def share_copy(source):
        return remote(kv.at[source, part], kv.at[source, part], fsend.at[source], frecv.at[source], twin)

    def tile_copy(owner, dest):
        return remote(tiles.at[dest], arrive.at[owner], gsend.at[dest], grecv.at[owner], {"ctx": dest})

    def start_msg(step, _):
        msg_copy(me, lax.rem(me + step, count)).start()

    lax.fori_loop(1, count, start_msg, None)
    hosted = hosted_copies(kinds, guests, landings, hsend, hrecv)
    for copy in hosted:
        copy.start()
    land[me] = msg_ref[me]

    def share(source):
        @pl.when(source != me)
        def _():
            msg_copy(source, me).wait_recv()

        kv[source, part] = land[source, :, LANES:]
        share_copy(source).start()

    def compute(index):
        base = index * sources
        stack = []
        for source in range(sources):
            share_copy(base + source).wait_recv()
            both = kv[base + source].reshape(rows, LANES)
            place = pl.ds(pl.multiple_of((base + source) * rows, rows), rows)
            all_ref[place] = both
            ones_ref[place] = jnp.where(lane_of(both.shape) < head, jnp.ones_like(both), both)
            tile = land[base + source, :, :LANES].astype(F32)
            stack.append(jnp.where(lane < head, tile, 0.0))
            stack.append(jnp.where(lane < head, swap_heads(tile, head), 0.0))
        queries = jnp.concatenate(stack, axis=0).astype(BF)
        acc_ref[...] = jnp.zeros_like(acc_ref)

        def visit(step, masked):
            start = pl.multiple_of(step * keys, keys)
            here = pl.ds(start, keys)
            raised = jnp.exp2(lax.dot_general(queries, all_ref[here], ONES_NT, preferred_element_type=F32) * factor)
            if masked:
                ok = allowed_block(0, 1, (wide, keys), first, second, part, base, start, rows, half_rows)
                raised = jnp.where(ok, raised, 0.0)
            acc_ref[...] += jnp.dot(raised.astype(BF), ones_ref[here], preferred_element_type=F32)

        sweep_keys(visit, index, count * rows - rows, part, base, rows, half_rows, keys, sources)
        for source in range(sources):
            tile = land[base + source, :, :LANES].astype(F32)
            outs = []
            for which in range(2):
                place = (2 * source + which) * half_rows
                acc = acc_ref[place:place + half_rows]
                turn = swap_heads(acc, head)
                outs.append(turn / acc if which == 0 else acc / turn)
                high, middle, low = three_parts(-math.sqrt(head) * jnp.log(turn))
                query = tile if which == 0 else swap_heads(tile, head)
                extra = jnp.where(lane == head, high, jnp.where(lane == head + 1, middle,
                                                                jnp.where(lane == head + 2, low, 0.0)))
                aug_ref[base + source, which] = jnp.where(lane < head, query, extra).astype(BF)
            out = jnp.where(lane < head, outs[0], outs[1])
            out_ref[base + source] = out
            tiles[base + source] = out.astype(BF)

            @pl.when(base + source != me)
            def _(source=source):
                tile_copy(me, base + source).start()

    def block(index, _):
        @pl.when(index < count // sources)
        def _():
            for source in range(sources):
                share(index * sources + source)

        @pl.when(index > 0)
        def _():
            compute(index - 1)

    lax.fori_loop(0, count // sources + 1, block, None)
    arrive[me] = tiles[me]

    def drain(other, _):
        share_copy(other).wait_send()

        @pl.when(other != me)
        def _():
            msg_copy(me, other).wait_send()
            tile_copy(me, other).wait_send()
            tile_copy(other, me).wait_recv()

    lax.fori_loop(0, count, drain, None)
    got_ref[...] = arrive[...]
    for copy in hosted:
        copy.wait()


def attend_back_kernel(head, rows, keys, sources, count, kinds, *refs):
    extra = len(kinds)
    (info_ref, aug_ref, out_ref, kv_ref, msg_ref), guests, refs = refs[:5], refs[5:5 + extra], refs[5 + extra:]
    (gotq_ref, gotk_ref), landings, refs = refs[:2], refs[2:2 + extra], refs[2 + extra:]
    (land, tiles, away, near, sums, arrive_q, arrive_k, kone_ref, vone_ref, kturn_ref, dk_ref, dv_ref, acc_ref,
     msend, mrecv, fsend, frecv, gsend, grecv, ksend, krecv, hsend, hrecv) = refs
    first, second = info_ref[0], info_ref[1]
    me = lax.axis_index("ctx")
    part = me % 2
    twin = {"ctx": me + 1 - 2 * part}
    half_rows = msg_ref.shape[1]
    wide = sources * 2 * half_rows
    factor = math.log2(math.e) / math.sqrt(head)
    shrink = 1.0 / math.sqrt(head)
    lane = lane_of((half_rows, LANES))
    greet(me, count)

    def remote(src, dst, send, recv, where):
        return pltpu.make_async_remote_copy(src_ref=src, dst_ref=dst, send_sem=send, recv_sem=recv,
                                            device_id=where, device_id_type=MESH)

    def msg_copy(owner, dest):
        return remote(msg_ref.at[dest], land.at[owner], msend.at[dest], mrecv.at[owner], {"ctx": dest})

    def share_copy(source):
        return remote(away.at[source], near.at[source], fsend.at[source], frecv.at[source], twin)

    def q_copy(owner, dest):
        return remote(tiles.at[dest], arrive_q.at[owner], gsend.at[dest], grecv.at[owner], {"ctx": dest})

    def k_copy(owner, dest):
        return remote(sums.at[dest], arrive_k.at[owner], ksend.at[dest], krecv.at[owner], {"ctx": dest})

    def start_msg(step, _):
        msg_copy(me, lax.rem(me + count - step, count)).start()

    lax.fori_loop(1, count, start_msg, None)
    hosted = hosted_copies(kinds, guests, landings, hsend, hrecv)
    for copy in hosted:
        copy.start()
    land[me] = msg_ref[me]
    whole = lane_of(kv_ref.shape)
    vone_ref[...] = jnp.where(whole < head, jnp.ones_like(kv_ref), kv_ref[...])
    kone_ref[...] = jnp.where(whole < head, kv_ref[...], jnp.ones_like(kv_ref))
    kturn_ref[...] = turned(kv_ref[...])
    dk_ref[...] = jnp.zeros_like(dk_ref)
    dv_ref[...] = jnp.zeros_like(dv_ref)

    def rows_of(source, which):
        return pl.ds(pl.multiple_of(source * rows + which * half_rows, half_rows), half_rows)

    def key_tile(source, which):
        here = rows_of(source, which)
        return jnp.where(lane < head, dk_ref[here] * shrink, dv_ref[here])

    def compute(index):
        base = index * sources
        stack_q, stack_d = [], []
        for source in range(sources):
            @pl.when(base + source != me)
            def _(source=source):
                msg_copy(base + source, me).wait_recv()

            grad = land[base + source].astype(F32)
            spread = grad * out_ref[base + source]
            for which in range(2):
                stack_q.append(aug_ref[base + source, which])
                mine = (lane < head) if which == 0 else (lane >= head)
                delta = jnp.sum(jnp.where(mine, spread, 0.0), axis=1, keepdims=True)
                high, middle, low = three_parts(-delta)
                extra = jnp.where(lane == 0, high, jnp.where(lane == 1, middle, jnp.where(lane == 2, low, 0.0)))
                moved = swap_heads(grad, head) if which == 0 else grad
                stack_d.append(jnp.where(lane < head, extra, moved).astype(BF))
        queries = jnp.concatenate(stack_q, axis=0)
        grads = jnp.concatenate(stack_d, axis=0)
        acc_ref[...] = jnp.zeros_like(acc_ref)

        def visit(step, masked):
            start = pl.multiple_of(step * keys, keys)
            here = pl.ds(start, keys)
            raw = lax.dot_general(kone_ref[here], queries, ONES_NT, preferred_element_type=F32)
            if masked:
                ok = allowed_block(1, 0, (keys, wide), first, second, part, base, start, rows, half_rows)
                prob = jnp.where(ok, jnp.exp2(jnp.where(ok, raw, 0.0) * factor), 0.0)
            else:
                prob = jnp.exp2(raw * factor)
            along = lax.dot_general(vone_ref[here], grads, ONES_NT, preferred_element_type=F32)
            score = (prob * along).astype(BF)
            dv_ref[here] += jnp.dot(prob.astype(BF), grads, preferred_element_type=F32)
            dk_ref[here] += jnp.dot(score, queries, preferred_element_type=F32)
            acc_ref[...] += jnp.dot(kturn_ref[:, here], score, preferred_element_type=F32)

        sweep_keys(visit, index, count * rows - rows, part, base, rows, half_rows, keys, sources)
        acc = acc_ref[...].T
        for source in range(sources):
            place = 2 * source * half_rows
            one = acc[place:place + half_rows]
            two = acc[place + half_rows:place + 2 * half_rows]
            tiles[base + source] = (jnp.where(lane < head, one, swap_heads(two, head)) * shrink).astype(BF)

            @pl.when(base + source != me)
            def _(source=source):
                q_copy(me, base + source).start()

            away[base + source] = key_tile(base + source, 1 - part).astype(BF)
            share_copy(base + source).start()

    def finish(index):
        for source in range(sources):
            block = index * sources + source
            share_copy(block).wait_recv()
            sums[block] = (key_tile(block, part) + near[block].astype(F32)).astype(BF)

            @pl.when(block != me)
            def _(block=block):
                k_copy(me, block).start()

    def sweep(step, _):
        index = count // sources - 1 - step

        @pl.when(index >= 0)
        def _():
            compute(jnp.maximum(index, 0))

        @pl.when(step > 0)
        def _():
            finish(index + 1)

    lax.fori_loop(0, count // sources + 1, sweep, None)
    arrive_q[me] = tiles[me]
    arrive_k[me] = sums[me]

    def drain(other, _):
        share_copy(other).wait_send()

        @pl.when(other != me)
        def _():
            msg_copy(me, other).wait_send()
            q_copy(me, other).wait_send()
            k_copy(me, other).wait_send()
            q_copy(other, me).wait_recv()
            k_copy(other, me).wait_recv()

    lax.fori_loop(0, count, drain, None)
    gotq_ref[...] = arrive_q[...]
    gotk_ref[...] = arrive_k[...]
    for copy in hosted:
        copy.wait()


def exchange_attend(msg, info, head, rows, hosted, collective_id):
    count, half_rows = msg.shape[0], msg.shape[1]
    keys, sources = 512, 2
    group = count * rows
    dma = pltpu.SemaphoreType.DMA((count,))
    S = jax.ShapeDtypeStruct
    tile = (count, half_rows, LANES)
    kinds = [kind for kind, _ in hosted]
    guests = [value for _, value in hosted]
    hdma = pltpu.SemaphoreType.DMA((len(hosted),))
    anywhere = [pl.BlockSpec(memory_space=pl.ANY)] * len(hosted)
    return pl.pallas_call(
        functools.partial(attend_kernel, head, rows, keys, sources, count, kinds),
        out_shape=(S(tile, BF), S(tile, F32), S((count, 2, half_rows, LANES), BF), S((group, LANES), BF),
                   *hosted_shapes(hosted)),
        in_specs=[pl.BlockSpec(memory_space=pltpu.SMEM)] + vmem_specs(1) + anywhere,
        out_specs=tuple(vmem_specs(4) + anywhere),
        scratch_shapes=[pltpu.VMEM((count, half_rows, 2 * LANES), BF), pltpu.VMEM((count, 2, half_rows, LANES), BF),
                        pltpu.VMEM(tile, BF), pltpu.VMEM(tile, BF), pltpu.VMEM((group, LANES), BF),
                        pltpu.VMEM((sources * rows, LANES), F32)] + [dma] * 6 + [hdma] * 2,
        compiler_params=pltpu.CompilerParams(collective_id=collective_id, has_side_effects=True,
                                             vmem_limit_bytes=VMEM_LIMIT),
        cost_estimate=pl.CostEstimate(flops=2 * group * group * LANES, bytes_accessed=6 << 20, transcendentals=0),
        name="attend",
    )(info, msg, *guests)


def exchange_attend_back(msg, info, augmented, attended, all_kv, head, rows, hosted, collective_id):
    count, half_rows = msg.shape[0], msg.shape[1]
    keys, sources = 512, 2
    group = count * rows
    dma = pltpu.SemaphoreType.DMA((count,))
    S = jax.ShapeDtypeStruct
    tile = (count, half_rows, LANES)
    kinds = [kind for kind, _ in hosted]
    guests = [value for _, value in hosted]
    hdma = pltpu.SemaphoreType.DMA((len(hosted),))
    anywhere = [pl.BlockSpec(memory_space=pl.ANY)] * len(hosted)
    long = (group, LANES)
    return pl.pallas_call(
        functools.partial(attend_back_kernel, head, rows, keys, sources, count, kinds),
        out_shape=(S(tile, BF), S(tile, BF), *hosted_shapes(hosted)),
        in_specs=[pl.BlockSpec(memory_space=pltpu.SMEM)] + vmem_specs(4) + anywhere,
        out_specs=tuple(vmem_specs(2) + anywhere),
        scratch_shapes=[pltpu.VMEM(tile, BF)] * 7 + [
            pltpu.VMEM(long, BF), pltpu.VMEM(long, BF), pltpu.VMEM((LANES, group), BF), pltpu.VMEM(long, F32),
            pltpu.VMEM(long, F32), pltpu.VMEM((LANES, sources * rows), F32)] + [dma] * 8 + [hdma] * 2,
        compiler_params=pltpu.CompilerParams(collective_id=collective_id, has_side_effects=True,
                                             vmem_limit_bytes=VMEM_LIMIT),
        cost_estimate=pl.CostEstimate(flops=5 * group * group * LANES, bytes_accessed=8 << 20, transcendentals=0),
        name="attend_back",
    )(info, augmented, attended, all_kv, msg, *guests)


def sum_kernel(jobs, sides, weights, lines, *refs):
    count = len(jobs)
    refs = list(refs)
    take = lambda number: [refs.pop(0) for _ in range(number)]
    lefts, lefts_y, rights = take(sides), take(sides), take(count)
    sent = [refs.pop(0) if job["late"] and job["kind"] == "pair" else None for job in jobs]
    early_y = [None if job["late"] else take(job["parts"]) for job in jobs]
    (small_ref,) = take(1)
    outs, (small_out,) = take(weights), take(1)
    lefts_s, lefts_ys, rights_s, rights_ys = take(sides), take(sides), take(count), take(count)
    rights_y = [take(1) if job["late"] else early for job, early in zip(jobs, early_y)]
    (lbuf, rbuf, xp, xr, zp, us, ur, ds_, dr, fs, fr, cs, cr, stage, sm_s, sm_r,
     lsem, rsem, xs, xv, uss, urv, dss, drv, fss, frv, css, crv, osem, sms, smv, els, elv, ers, erv, yrs, yrv) = refs
    steps = sum(job["total"] for job in jobs)
    last = steps - 1
    tokens = lbuf.shape[-1] // 4
    me = lax.axis_index("ctx")
    y = lax.axis_index("dp")
    z = me // 4
    x = (me // 2) % 2
    c = me % 2
    top = lines - 1
    twin = {"ctx": me + 1 - 2 * c}
    across_x = {"ctx": me + 2 - 4 * x}
    across_y = {"dp": 1 - y}
    above = {"ctx": jnp.minimum(me + 4, 4 * top + me % 4)}
    below = {"ctx": jnp.maximum(me - 4, me % 4)}
    near = {"ctx": me + 4 - 8 * (z % 2)}
    far = {"ctx": me + 8 - 16 * (z // 2)}
    rounds = [twin, across_x, across_y, near, far]

    for buf in (ur, dr, zp):
        buf[...] = jnp.zeros_like(buf)
    sm_s[0] = small_ref[...]

    barrier = pltpu.get_barrier_semaphore()
    for where in (twin, across_x, across_y, far):
        pl.semaphore_signal(barrier, inc=1, device_id=where, device_id_type=MESH)

    @pl.when(z < top)
    def _():
        pl.semaphore_signal(barrier, inc=1, device_id=above, device_id_type=MESH)

    @pl.when(z > 0)
    def _():
        pl.semaphore_signal(barrier, inc=1, device_id=below, device_id_type=MESH)

    pl.semaphore_wait(barrier, 4 + (z < top).astype(jnp.int32) + (z > 0).astype(jnp.int32))

    def remote(src, dst, send, recv, where):
        return pltpu.make_async_remote_copy(src_ref=src, dst_ref=dst, send_sem=send, recv_sem=recv,
                                            device_id=where, device_id_type=MESH)

    def row_base(number):
        height = lefts_s[number].shape[2]
        return y * height if height < lefts[number].shape[2] else 0

    def column_base(number):
        width = 2 * rights_s[number].shape[1]
        return y * width if jobs[number]["kind"] == "quarter" else 0

    def left_copies(number):
        height = lefts_s[number].shape[2]
        rows = pl.ds(pl.multiple_of(row_base(number), PIECE), height)
        return [
            remote(lefts[number].at[:, :, rows, :], lefts_s[number], els.at[number, 0], elv.at[number, 0], twin),
            remote(lefts_y[number], lefts_ys[number], els.at[number, 1], elv.at[number, 1], twin),
        ]

    def right_own(number):
        width = rights_s[number].shape[1]
        start = pl.multiple_of(column_base(number) + (1 - c) * width, STRIP)
        return remote(rights[number].at[:, pl.ds(start, width)], rights_s[number], ers.at[number, 0],
                      erv.at[number, 0], twin)

    def right_forward(number):
        width = rights_s[number].shape[1]
        columns = pl.ds(pl.multiple_of((1 - c) * width, STRIP), width)
        tall = tokens // len(rights_y[number])
        return [remote(source.at[:, columns], rights_ys[number].at[pl.ds(part * tall, tall)],
                       ers.at[number, 1 + part], erv.at[number, 1 + part], twin)
                for part, source in enumerate(rights_y[number])]

    def right_cross(number, piece=None):
        width = 2 * rights_s[number].shape[1]
        kind = jobs[number]["kind"]
        source = sent[number] if kind == "pair" else rights[number]
        start = (1 - y) * width if kind == "quarter" else 0
        rows, inside = slice(None), 0
        size = width
        if piece is not None:
            rows = pl.ds(pl.multiple_of((piece & 1) * (tokens // 2), PIECE), tokens // 2)
            inside, size = (piece >> 1) * STRIP, STRIP
        place = pl.ds(pl.multiple_of(inside, STRIP), size)
        if piece is None:
            landing = rights_y[number][0]
        else:
            landing = rights_y[number][0].at[rows, place]
        return remote(source.at[rows, pl.ds(pl.multiple_of(start + inside, STRIP), size)], landing,
                      yrs.at[number], yrv.at[number], across_y)

    def x_copy(j):
        s = j & (RING - 1)
        return remote(xp.at[s, 1 - x], xr.at[s], xs.at[s], xv.at[s], across_x)

    def up_copy(j):
        s = j & (RING - 1)
        return remote(us.at[s], ur.at[s], uss.at[s], urv.at[s], above)

    def down_copy(j):
        s = j & (RING - 1)
        return remote(ds_.at[s], dr.at[s], dss.at[s], drv.at[s], below)

    def f_copy(j):
        s = j & (RING - 1)
        return remote(fs.at[s], fr.at[s], fss.at[s], frv.at[s], across_y)

    def c_copy(j):
        s = j & (RING - 1)
        return remote(cs.at[s], cr.at[s], css.at[s], crv.at[s], twin)

    def small_copy(k):
        return remote(sm_s.at[k], sm_r.at[k], sms.at[k], smv.at[k], rounds[k])

    def loads(number):
        job = jobs[number]
        left, s = job["left"], number % 2
        height, width = lefts_s[left].shape[2], rights_s[number].shape[1]
        own_rows = pl.ds(pl.multiple_of(row_base(left), PIECE), height)
        own_columns = pl.ds(pl.multiple_of(column_base(number) + c * width, STRIP), width)
        mine = pl.ds(pl.multiple_of(c * width, STRIP), width)
        copies = []
        for place, source in enumerate([lefts[left].at[:, :, own_rows, :], lefts_s[left], lefts_y[left],
                                        lefts_ys[left]]):
            copies.append(pltpu.make_async_copy(
                source, lbuf.at[s, :, :, pl.ds(0, height), pl.ds(place * tokens, tokens)], lsem.at[s, place]))
        tall = tokens // len(rights_y[number])
        pieces = [(0, rights[number].at[:, own_columns]), (tokens, rights_s[number]), (3 * tokens, rights_ys[number])]
        pieces += [(2 * tokens + part * tall, source.at[:, mine]) for part, source in enumerate(rights_y[number])]
        for place, (start, source) in enumerate(pieces):
            copies.append(pltpu.make_async_copy(
                source, rbuf.at[s, pl.ds(start, source.shape[0]), pl.ds(0, width)], rsem.at[s, place]))
        return copies

    def each_job(j, visit):
        begin = 0
        for number, job in enumerate(jobs):
            @pl.when((j >= begin) & (j < begin + job["total"]))
            def _(number=number, begin=begin):
                visit(number, j - begin)
            begin += job["total"]

    def begins():
        begin = 0
        for number, job in enumerate(jobs):
            yield number, job, begin
            begin += job["total"]

    def out_copies(number, k, j):
        job = jobs[number]
        o = j & (RING - 1)
        row = pl.multiple_of(lax.rem(k, job["subs"]) * PIECE, PIECE)
        column = pl.multiple_of(lax.div(k, job["subs"]) * STRIP, STRIP)
        width = rights_s[number].shape[1]
        copies = []
        for line in range(2):
            for core in range(2):
                out = outs[job["outs"][line if job["kind"] == "pair" else 0]]
                rows, columns = row, core * width + column
                if job["kind"] == "quarter":
                    columns = line * 2 * width + columns
                if job["kind"] == "drop":
                    rows = line * lefts_s[job["left"]].shape[2] + row
                copies.append(pltpu.make_async_copy(
                    stage.at[o, line, core],
                    out.at[pl.ds(pl.multiple_of(rows, PIECE), PIECE), pl.ds(pl.multiple_of(columns, STRIP), STRIP)],
                    osem.at[o, line, core]))
        return copies

    def out_wait(j):
        for copy in out_copies(0, 0, j):
            copy.wait()

    started = []
    for number, job, begin in begins():
        if job["left"] not in started:
            started.append(job["left"])
            for copy in left_copies(job["left"]):
                copy.start()
        right_own(number).start()
        if not job["late"]:
            for copy in right_forward(number):
                copy.start()

    def step(t, _):
        slot = t & (RING - 1)

        for number, job, begin in begins():
            if job["late"]:
                ago = t - job["issue"]
                piece = ago - (ago >> 2)
                pieces = 4 * rights_s[number].shape[1] // STRIP

                @pl.when((ago >= 0) & (ago & 3 != 3) & (piece < pieces))
                def _(number=number, piece=piece):
                    right_cross(number, piece).start()

                @pl.when(t == begin - job["ahead"])
                def _(number=number):
                    right_cross(number).wait()
                    for copy in right_forward(number):
                        copy.start()

        done, before = [], 0
        for number, job, begin in begins():
            fresh = job["left"] not in done
            done.append(job["left"])

            @pl.when(t == max(before, begin - AHEAD))
            def _(number=number, job=job, fresh=fresh):
                if fresh:
                    for copy in left_copies(job["left"]):
                        copy.wait()
                right_own(number).wait()
                for copy in right_forward(number):
                    copy.wait()
                for copy in loads(number):
                    copy.start()

            before = begin

        for number, job, begin in begins():
            @pl.when(t == begin)
            def _(number=number):
                for copy in loads(number):
                    copy.wait()

        for k in range(len(rounds) + 1):
            @pl.when(t == LAG * k)
            def _(k=k):
                if k > 0:
                    small_copy(k - 1).wait()
                    total = sm_s[k - 1] + sm_r[k - 1]
                    if k == len(rounds):
                        small_out[...] = total
                    else:
                        sm_s[k] = total
                if k < len(rounds):
                    small_copy(k).start()

        @pl.when(t < steps)
        def _():
            which, begin_now, subs_now = 0, 0, jobs[0]["subs"]
            for number, job, begin in begins():
                here = t >= begin
                begin_now = jnp.where(here, begin, begin_now)
                subs_now = jnp.where(here, job["subs"], subs_now)
                which = jnp.where(here, number % 2, which)
            row = lax.rem(t - begin_now, subs_now) * PIECE
            column = lax.div(t - begin_now, subs_now) * STRIP
            rows = pl.ds(pl.multiple_of(row, PIECE), PIECE)
            left = lbuf[which, :, :, rows, :].reshape(2 * lines * SUB, 4 * tokens)
            right = rbuf[which, :, pl.ds(pl.multiple_of(column, STRIP), STRIP)]
            got = jnp.dot(left, right, preferred_element_type=F32).astype(BF)
            for line in range(lines):
                for side in range(2):
                    row = (2 * line + side) * SUB
                    xp[slot, side, line] = got[row:row + SUB]
            x_copy(t).start()

        @pl.when((t >= LAG) & (t - LAG <= last))
        def _():
            x_copy(t - LAG).wait()
            s = (t - LAG) & (RING - 1)
            zp[(t - LAG) & (2 * RING - 1)] = xp[s, x] + xr[s]

        ju = t - LAG * (1 + z)

        @pl.when((ju >= 0) & (ju <= last))
        def _():
            s = ju & (RING - 1)
            held = ju & (2 * RING - 1)

            @pl.when(z > 0)
            def _():
                up_copy(ju).wait_recv()
                zp[held, z] = zp[held, z] + ur[s, 0]

            @pl.when(z < top)
            def _():
                @pl.when(ju >= RING)
                def _():
                    up_copy(ju).wait_send()

                for m in range(top):
                    own = zp[held, jnp.minimum(z + 1 + m, top)]
                    if m + 1 < top:
                        own = own + ur[s, m + 1]
                    us[s, m] = own
                up_copy(ju).start()

        jd = t - LAG * (1 + top - z)

        @pl.when((jd >= 0) & (jd <= last))
        def _():
            s = jd & (RING - 1)
            held = jd & (2 * RING - 1)

            @pl.when(z < top)
            def _():
                down_copy(jd).wait_recv()
                zp[held, z] = zp[held, z] + dr[s, 0]

            @pl.when(z > 0)
            def _():
                @pl.when(jd >= RING)
                def _():
                    down_copy(jd).wait_send()

                for m in range(top):
                    own = zp[held, jnp.maximum(z - 1 - m, 0)]
                    if m + 1 < top:
                        own = own + dr[s, m + 1]
                    ds_[s, m] = own
                down_copy(jd).start()

        jf = t - LAG * (1 + top)

        @pl.when((jf >= 0) & (jf <= last))
        def _():
            fs[jf & (RING - 1)] = zp[jf & (2 * RING - 1), z]
            f_copy(jf).start()

        jo = jf - LAG

        @pl.when((jo >= 0) & (jo <= last))
        def _():
            f_copy(jo).wait()
            s = jo & (RING - 1)
            mine = pl.ds(pl.multiple_of(c * PIECE, PIECE), PIECE)
            away = pl.ds(pl.multiple_of((1 - c) * PIECE, PIECE), PIECE)
            cs[s, y] = fs[s, away]
            cs[s, 1 - y] = fr[s, away]
            c_copy(jo).start()
            stage[s, y, c] = fs[s, mine].astype(F32)
            stage[s, 1 - y, c] = fr[s, mine].astype(F32)

        jc = jo - LAG

        @pl.when((jc >= 0) & (jc <= last))
        def _():
            c_copy(jc).wait()
            s = jc & (RING - 1)
            stage[s, 0, 1 - c] = cr[s, 0].astype(F32)
            stage[s, 1, 1 - c] = cr[s, 1].astype(F32)

            def start(number, k):
                for copy in out_copies(number, k, jc):
                    copy.start()

            each_job(jc, start)

            @pl.when(jc >= LAG)
            def _():
                out_wait(jc - LAG)

    lax.fori_loop(0, last + LAG * (top + 3) + 1, step, None)
    for back in range(LAG):
        out_wait(last - back)
    for back in range(RING):
        j = last - back

        @pl.when(z < top)
        def _(j=j):
            up_copy(j).wait_send()

        @pl.when(z > 0)
        def _(j=j):
            down_copy(j).wait_send()


def sum_over_chips(lefts, works, small, lines, collective_id):
    S = jax.ShapeDtypeStruct
    jobs, landing_r, landing_y, outs, sent, early = [], [], [], [], [], []
    shaped = [own.reshape(2 * lines, 2, own.shape[0] // (4 * lines), own.shape[1]) for own, _ in lefts]
    crossed = [cross for _, cross in lefts]
    tokens = shaped[0].shape[-1]
    for work in works:
        job = {name: work[name] for name in ("left", "kind", "late", "issue", "ahead")}
        columns = work["own"].shape[1]
        width = columns // 4 if job["kind"] == "quarter" else columns // 2
        height = crossed[job["left"]].shape[2]
        job["subs"], job["strips"] = height // PIECE, width // STRIP
        job["total"] = job["subs"] * job["strips"]
        job["outs"] = []
        for _ in range(2 if job["kind"] == "pair" else 1):
            job["outs"].append(len(outs))
            outs.append(S((shaped[job["left"]].shape[2], columns), F32))
        landing_r.append(S((tokens, width), BF))
        if job["late"]:
            landing_y.append(S((tokens, 2 * width), BF))
            if job["kind"] == "pair":
                sent.append(work["cross"])
        else:
            job["parts"] = len(work["cross"])
            early.extend(work["cross"])
        jobs.append(job)
    steps = sum(job["total"] for job in jobs)
    top = lines - 1
    dma = pltpu.SemaphoreType.DMA
    ring = lambda *shape: pltpu.VMEM((RING,) + shape, BF)
    scratch = [
        pltpu.VMEM((2, 2 * lines, 2, max(value.shape[2] for value in crossed), 4 * tokens), BF),
        pltpu.VMEM((2, 4 * tokens, max(value.shape[1] for value in landing_r)), BF),
        ring(2, lines, SUB, STRIP), ring(lines, SUB, STRIP),
        pltpu.VMEM((2 * RING, lines, SUB, STRIP), BF),
        ring(top, SUB, STRIP), ring(top, SUB, STRIP), ring(top, SUB, STRIP), ring(top, SUB, STRIP),
        ring(SUB, STRIP), ring(SUB, STRIP), ring(2, PIECE, STRIP), ring(2, PIECE, STRIP),
        pltpu.VMEM((RING, 2, 2, PIECE, STRIP), F32),
        pltpu.VMEM((5,) + small.shape, F32),
        pltpu.VMEM((5,) + small.shape, F32),
        dma((2, 4)), dma((2, 5)),
    ] + [dma((RING,))] * 10 + [
        dma((RING, 2, 2)), dma((5,)), dma((5,)),
        dma((len(lefts), 2)), dma((len(lefts), 2)), dma((len(works), 3)), dma((len(works), 3)),
        dma((len(works),)), dma((len(works),)),
    ]
    anywhere = pl.BlockSpec(memory_space=pl.ANY)
    inside = pl.BlockSpec(memory_space=pltpu.VMEM)
    landings = [S(value.shape, BF) for value in crossed] * 2 + landing_r * 2 + landing_y
    operands = shaped + crossed + [work["own"] for work in works] + sent + early
    flops = 2 * steps * 2 * lines * SUB * STRIP * 4 * tokens
    got = pl.pallas_call(
        functools.partial(sum_kernel, jobs, len(lefts), len(outs), lines),
        out_shape=tuple(outs) + (S(small.shape, F32),) + tuple(landings),
        in_specs=[anywhere] * len(operands) + [inside],
        out_specs=tuple([anywhere] * len(outs) + [inside] + [anywhere] * len(landings)),
        scratch_shapes=scratch,
        compiler_params=pltpu.CompilerParams(collective_id=collective_id, has_side_effects=True,
                                             vmem_limit_bytes=VMEM_LIMIT),
        cost_estimate=pl.CostEstimate(flops=flops, bytes_accessed=steps * 1_100_000, transcendentals=0),
        name="sum_over_chips",
    )(*operands, small)
    return got[:len(outs)], got[len(outs)]


def hand_over_kernel(count, head, *refs):
    sources, small_ref, results = refs[:count], refs[count], refs[count + 1:2 * count + 1]
    mix_ref, taps_ref, low_ref, att_ref, top_ref, query_ref, keys_ref = refs[2 * count + 1:2 * count + 8]
    holds, (ins, outs) = refs[2 * count + 8:3 * count + 8], refs[3 * count + 8:]
    arrive = [pltpu.make_async_copy(source, hold, ins.at[number])
              for number, (source, hold) in enumerate(zip(sources, holds))]
    leave = [pltpu.make_async_copy(hold, result, outs.at[number])
             for number, (hold, result) in enumerate(zip(holds, results))]
    for copy in arrive:
        copy.start()
    mix_ref[...] = small_ref[0]
    taps_ref[...] = small_ref[1:4]
    low_ref[...] = small_ref[4]
    att_ref[...] = small_ref[5]
    top_ref[...] = small_ref[6]
    query_ref[...] = small_ref[7, :head]
    keys_ref[...] = small_ref[7, LANES:LANES + head]
    for first, then in zip(arrive, leave):
        first.wait()
        then.start()
    for copy in leave:
        copy.wait()


def hand_over(grads, small, head):
    count, width = len(grads), small.shape[1]
    S = jax.ShapeDtypeStruct
    anywhere = [pl.BlockSpec(memory_space=pl.ANY)] * count
    smalls = (S((width,), F32), S((3, width), F32), S((width,), F32), S((width,), F32), S((width,), F32),
              S((head,), F32), S((head,), F32))
    got = pl.pallas_call(
        functools.partial(hand_over_kernel, count, head),
        out_shape=tuple(S(value.shape, F32) for value in grads) + smalls,
        in_specs=anywhere + vmem_specs(1),
        out_specs=tuple(anywhere + vmem_specs(len(smalls))),
        scratch_shapes=[pltpu.VMEM(value.shape, F32) for value in grads] + [pltpu.SemaphoreType.DMA((count,))] * 2,
        compiler_params=pltpu.CompilerParams(vmem_limit_bytes=VMEM_LIMIT),
        name="hand_over",
    )(*grads, small)
    return got[:count], got[count:]


def call_plain(kernel, outs, args, smem=0, scratch=(), flops=0, moved=0, name=None):
    specs = [pl.BlockSpec(memory_space=pltpu.SMEM)] * smem + vmem_specs(len(args) - smem)
    many = isinstance(outs, (tuple, list))
    return pl.pallas_call(
        kernel,
        out_shape=tuple(outs) if many else outs,
        in_specs=specs,
        out_specs=tuple(vmem_specs(len(outs))) if many else vmem_specs(1)[0],
        scratch_shapes=list(scratch),
        compiler_params=pltpu.CompilerParams(vmem_limit_bytes=VMEM_LIMIT),
        cost_estimate=pl.CostEstimate(flops=flops, bytes_accessed=moved, transcendentals=0),
        name=name,
    )(*args)


def shape_of(shape, kind):
    return jax.ShapeDtypeStruct(shape, kind)


def sibling(value):
    count = lax.axis_size("ctx")
    return lax.ppermute(value, "ctx", [(i, i ^ 1) for i in range(count)])


def fast_device(tokens, lengths, cotangent, mixgain, mixentry, mixtaps, mixexit, lowgain, lowgate, lowlift,
                lowdrop, attgain, attquery, attkeys, attvalues, querygain, keysgain, attexit, topgain, topgate,
                toplift, topdrop):
    rows, width = tokens.shape
    head = querygain.shape[0]
    devices = lax.axis_size("ctx")
    lines = devices // 4
    half_rows = rows // 2
    place = lax.axis_index("ctx")
    core = place % 2
    first = lengths[0, 0]
    second = first + lengths[0, 1]
    mine = place * rows + jnp.arange(rows, dtype=jnp.int32)
    my_seg = segment_of(mine, first, second)
    begin = jnp.where(my_seg == 0, 0, jnp.where(my_seg == 1, first, second))
    position = (mine - begin).astype(F32)
    twice = lambda gain: jnp.tile(gain.astype(F32), LANES // head)[None, :]
    querygain_2, keysgain_2 = twice(querygain), twice(keysgain)
    spot = jnp.arange(LANES, dtype=jnp.int32) % (head // 2)
    angle = position[:, None] * (THETA ** (-spot.astype(F32) * 2.0 / head))[None, :]
    cosine = jnp.cos(angle)
    sine = jnp.sin(angle) * jnp.where(jnp.arange(LANES) % head < head // 2, -1.0, 1.0)[None, :]
    info = jnp.stack([first, second]).astype(jnp.int32)

    before = passed_along(tokens[rows - HALO:], "ctx", 1)
    spot_of = lambda where: (where - jnp.where(where >= second, second, jnp.where(where >= first, first, 0))).astype(F32)
    (hidden_one, normed_one_t, gated_t, part_b, part_c, part_x, conved, product) = mix_forward(
        tokens, before, position[:, None], mixgain, mixtaps, mixentry, mixexit)
    gate_after = passed_along(part_c[:HALO], "ctx", -1)
    hidden_two, lownorm_t, gact_low, lact_low, lowinner_t = feed_low(
        hidden_one, lowgain, lowgate, lowlift, lowdrop)

    heads_q, heads_k = attquery.shape[1] // head, attkeys.shape[1] // head
    msg, normed_two_t, query_raw, key_raw = call_plain(
        functools.partial(project_kernel, head),
        (shape_of((devices, half_rows, 2 * LANES), BF), shape_of((width, rows), BF),
         shape_of((rows, attquery.shape[1]), F32), shape_of((rows, attkeys.shape[1]), F32)),
        (hidden_two, attgain, attquery, attkeys, attvalues, cosine, sine, querygain_2, keysgain_2),
        flops=2 * rows * width * 2 * width, moved=6 << 20, name="project")
    upright = lambda value: value.reshape(devices // 2, 2, value.shape[0] // devices, rows)
    over_dp = lambda value: lax.ppermute(value, "dp", [(0, 1), (1, 0)])
    msg, gated_y, normed_one_y, cotangent_y, gate_after = lax.optimization_barrier(
        (msg, over_dp(gated_t), over_dp(normed_one_t), over_dp(cotangent), gate_after))
    gated_y, normed_one_y = upright(gated_y), upright(normed_one_y)
    got, attended_f, augmented, all_kv, lowinner_y, lownorm_y = exchange_attend(
        msg, info, head, rows, [("rows", upright(lowinner_t)), ("whole", upright(lownorm_t))], 2)
    (output, grad, grad_low3, send, attended_t, topgain_grad, topnorm_t, topinner_t, keep_top, send_top_a,
     send_top_b) = feed_top(
        got, hidden_two, attexit, cotangent, topgain, topgate, toplift, topdrop)
    send, normed_two_y = lax.optimization_barrier((send, over_dp(normed_two_t)))
    normed_two_y = upright(normed_two_y)
    back_q, back_k, topinner_y, topnorm_y, attended_y, grad_low3_y = exchange_attend_back(
        send, info, augmented, attended_f, all_kv, head, rows,
        [("rows", upright(topinner_t)), ("whole", upright(topnorm_t)), ("whole", upright(attended_t)),
         ("columns", grad_low3)], 3)
    back_q, send_top_a, send_top_b = lax.optimization_barrier((back_q, send_top_a, send_top_b))
    top_y_one = over_dp(send_top_a)
    rawq_low, keep_kv, send_kv, grad_two, attgain_grad, querygain_grad, keysgain_grad = call_plain(
        functools.partial(project_back_kernel, head),
        (shape_of((rows, attquery.shape[1]), BF), shape_of((rows, attkeys.shape[1]), BF),
         shape_of((rows, attkeys.shape[1]), BF), shape_of((rows, width), F32), shape_of((1, width), F32),
         shape_of((1, LANES), F32), shape_of((1, LANES), F32)),
        (back_q, back_k, hidden_two, attgain, attquery, attkeys, attvalues, cosine, sine, querygain_2, keysgain_2,
         query_raw, key_raw, grad),
        flops=1 << 20, moved=1 << 10, name="project_back")
    fold = lambda value: value.reshape(LANES // head, head).sum(axis=0)
    querygain_grad, keysgain_grad = fold(querygain_grad), fold(keysgain_grad)
    grad, lowgain_grad, gb_low, grad_low1, keep_low, send_low = feed_low_back(
        grad_two, hidden_one, lowgain, gact_low, lact_low, lowgate, lowlift, lowdrop)
    grad, grad_low1, top_y_one = lax.optimization_barrier((grad, grad_low1, top_y_one))
    ext = place * rows + jnp.arange(rows + HALO, dtype=jnp.int32)
    after = passed_along(grad_low1[:HALO], "ctx", -1)
    tokens_grad, mixgain_grad, mixtaps_grad, mixed_grad = mix_backward(
        grad, grad_low1, after, gate_after, spot_of(ext)[:, None], tokens, mixgain, mixtaps,
        (part_b, part_c, part_x, conved, product), mixentry, mixexit)
    mixgain_grad, tokens_grad, top_y_two = lax.optimization_barrier(
        (mixgain_grad, tokens_grad, over_dp(send_top_b)))

    lefts = [(attended_t, attended_y), (topinner_t, topinner_y), (topnorm_t, topnorm_y), (normed_two_t, normed_two_y),
             (lowinner_t, lowinner_y), (lownorm_t, lownorm_y), (gated_t, gated_y), (normed_one_t, normed_one_y)]

    def work(left, kind, own, cross=None, issue=-1, ahead=12):
        return dict(left=left, kind=kind, own=own, cross=cross, late=issue >= 0, issue=issue, ahead=ahead)

    works = [work(0, "quarter", grad_low3, (grad_low3_y,)), work(1, "drop", cotangent, (cotangent_y,)),
             work(2, "pair", keep_top, (top_y_one, top_y_two)), work(3, "quarter", rawq_low, issue=0),
             work(3, "pair", keep_kv, send_kv, issue=5), work(4, "drop", gb_low, issue=10),
             work(5, "pair", keep_low, send_low, issue=20), work(6, "quarter", grad_low1, issue=68),
             work(7, "quarter", mixed_grad, issue=73)]
    heads = jnp.concatenate([querygain_grad, jnp.zeros((LANES - head,), F32), keysgain_grad, jnp.zeros((width - LANES - head,), F32)])
    small = jnp.concatenate([mixgain_grad, mixtaps_grad, lowgain_grad, attgain_grad, topgain_grad,
                             heads[None, :]], axis=0)
    grads, small = sum_over_chips(lefts, works, small, lines, 1)
    grads, smalls = hand_over(grads, small, head)
    (attexit_grad, topdrop_grad, topgate_grad, toplift_grad, attquery_grad, attkeys_grad, attvalues_grad, lowdrop_grad,
     lowgate_grad, lowlift_grad, mixexit_grad, mixentry_grad) = grads
    (mixgain_grad, mixtaps_grad, lowgain_grad, attgain_grad, topgain_grad, querygain_grad, keysgain_grad) = smalls
    return (output, tokens_grad, mixgain_grad, mixentry_grad, mixtaps_grad, mixexit_grad, lowgain_grad, lowgate_grad,
            lowlift_grad, lowdrop_grad, attgain_grad, attquery_grad, attkeys_grad, attvalues_grad, querygain_grad,
            keysgain_grad, attexit_grad, topgain_grad, topgate_grad, toplift_grad, topdrop_grad)


def solution(mesh):
    placed = (P(("dp", "ctx"), None), P("dp", None), P(("dp", "ctx"), None)) + (P(),) * 19
    split = {0: P(("dp", "ctx"), None), 1: P(("dp", "ctx"), None)}
    whole = (2, 4, 6, 10, 14, 15, 17)
    outs = tuple(split.get(i, P() if i in whole else P("ctx", None)) for i in range(21))
    small = mesh.shape["ctx"] == 16 and mesh.shape["dp"] == 2
    return jax.shard_map(fast_device if small else per_device, mesh=mesh, in_specs=placed, out_specs=outs,
                         check_vma=False)
```

```python
import functools
import math

import jax
import jax.numpy as jnp
from jax import lax
from jax.experimental import pallas as pl
from jax.experimental.pallas import tpu as pltpu
from jax.sharding import PartitionSpec as P

EPS = 1e-05
THETA = 1000000.0
NEGATIVE = -1e30


def passed_along(value, axis, steps):
    count = lax.axis_size(axis)
    first, last = (max(0, -steps), min(count, count - steps))
    return lax.ppermute(value, axis, [(source, source + steps) for source in range(first, last)])


def passed_along_2(block, axis, distance):
    devices = range(lax.axis_size(axis))
    route = [((i - distance) % len(devices), i) for i in devices]
    return lax.ppermute(block, axis, route)


def root_mean_square_scale(hidden, gain):
    return hidden * lax.rsqrt(jnp.mean(hidden * hidden, axis=-1, keepdims=True) + EPS) * gain


def rotary_embed(value_rows, position_index):
    half = value_rows.shape[-1] // 2
    freq = THETA ** (-jnp.arange(half, dtype=jnp.float32) * 2.0 / value_rows.shape[-1])
    angle = position_index.astype(jnp.float32)[:, None] * freq[None, :]
    cosine = jnp.cos(angle)[:, None, :]
    sine = jnp.sin(angle)[:, None, :]
    front = value_rows[..., :half]
    behind = value_rows[..., half:]
    return jnp.concatenate(
        [front * cosine - behind * sine, behind * cosine + front * sine], axis=-1
    )


def head_prep(raw, gain, position_index, heads):
    shaped = raw.reshape(raw.shape[0], heads, -1)
    return rotary_embed(root_mean_square_scale(shaped, gain), position_index)


def segment_of(where, first, second):
    return (where >= first).astype(jnp.int32) + (where >= second).astype(jnp.int32)


def block_width(count):
    best = 1
    for candidate in range(1, min(count, 1024) + 1):
        if count % candidate == 0:
            best = candidate
    return best


def sweep(carry, count, visit):
    width = block_width(count)
    return lax.fori_loop(
        0, count // width, lambda index, inner: visit(inner, index * width, width), carry
    )


def inner_dot(left, right):
    return lax.dot_general(
        left, right, (((0,), (0,)), ((), ())), preferred_element_type=jnp.float32
    )


def outer_dot(left, right):
    return lax.dot_general(
        left, right, (((1,), (1,)), ((), ())), preferred_element_type=jnp.float32
    )


def scores_of(query_part, key_part, query_where, key_where, query_seg, key_seg, scale):
    raw = (
        jnp.einsum("tkgd,pkd->kgtp", query_part, key_part, preferred_element_type=jnp.float32)
        * scale
    )
    allowed = (query_seg[:, None] == key_seg[None, :]) & (
        query_where[:, None] >= key_where[None, :]
    )
    return (raw, allowed)


def grad_block(
    query_part,
    grad_part,
    logsum_part,
    delta_part,
    key_part,
    value_part,
    query_where,
    key_where,
    query_seg,
    key_seg,
    scale,
):
    raw, allowed = scores_of(
        query_part, key_part, query_where, key_where, query_seg, key_seg, scale
    )
    prob = jnp.where(allowed, jnp.exp(raw - logsum_part[..., None]), 0.0)
    prob_grad = jnp.einsum(
        "tkgd,pkd->kgtp", grad_part, value_part, preferred_element_type=jnp.float32
    )
    score_grad = (prob * (prob_grad - delta_part[..., None])).astype(jnp.bfloat16)
    query_grad = (
        jnp.einsum("kgtp,pkd->tkgd", score_grad, key_part, preferred_element_type=jnp.float32)
        * scale
    )
    key_grad = (
        jnp.einsum("kgtp,tkgd->pkd", score_grad, query_part, preferred_element_type=jnp.float32)
        * scale
    )
    value_grad = jnp.einsum(
        "kgtp,tkgd->pkd", prob.astype(jnp.bfloat16), grad_part, preferred_element_type=jnp.float32
    )
    return (query_grad, key_grad, value_grad)


def conv_local(extended, taps, fits_one, fits_two):
    rows = extended.shape[0] - 2
    return (
        taps[2] * extended[2:]
        + taps[1] * extended[1 : rows + 1] * fits_one
        + taps[0] * extended[:rows] * fits_two
    )


def feed_forward(hidden, gain, gate_weight, lift_weight, drop_weight):
    fnormed = root_mean_square_scale(hidden, gain).astype(jnp.bfloat16)
    gate_act = jnp.dot(fnormed, gate_weight, preferred_element_type=jnp.float32)
    lift_act = jnp.dot(fnormed, lift_weight, preferred_element_type=jnp.float32)
    inner = (jax.nn.silu(gate_act) * lift_act).astype(jnp.bfloat16)
    result = hidden + jnp.dot(inner, drop_weight, preferred_element_type=jnp.float32)
    return (result, (fnormed, gate_act, lift_act, inner))


def feed_back(grad, hidden, gain, kept, gate_weight, lift_weight, drop_weight):
    fnormed, gate_act, lift_act, inner = kept
    grad_low = grad.astype(jnp.bfloat16)
    drop_grad = inner_dot(inner, grad_low)
    inner_grad = outer_dot(grad_low, drop_weight)
    _, pull_gate = jax.vjp(
        lambda gate_in, lift_in: jax.nn.silu(gate_in) * lift_in, gate_act, lift_act
    )
    gate_grad, lift_grad = pull_gate(inner_grad)
    gate_low = gate_grad.astype(jnp.bfloat16)
    lift_low = lift_grad.astype(jnp.bfloat16)
    gate_wgrad = inner_dot(fnormed, gate_low)
    lift_wgrad = inner_dot(fnormed, lift_low)
    normed_grad = outer_dot(gate_low, gate_weight) + outer_dot(lift_low, lift_weight)
    _, pull_norm = jax.vjp(root_mean_square_scale, hidden, gain)
    hidden_grad, gain_grad = pull_norm(normed_grad)
    return (grad + hidden_grad, (gain_grad, gate_wgrad, lift_wgrad, drop_grad))


def per_device(
    tokens,
    lengths,
    cotangent,
    mixgain,
    mixentry,
    mixtaps,
    mixexit,
    lowgain,
    lowgate,
    lowlift,
    lowdrop,
    attgain,
    attquery,
    attkeys,
    attvalues,
    querygain,
    keysgain,
    attexit,
    topgain,
    topgate,
    toplift,
    topdrop,
):
    rows = tokens.shape[0]
    width_model = tokens.shape[1]
    head_size = querygain.shape[0]
    query_heads = attquery.shape[1] // head_size
    kv_heads = attkeys.shape[1] // head_size
    shared_gradient = query_heads // kv_heads
    scale = 1.0 / math.sqrt(head_size)
    place = lax.axis_index("ctx")
    first = lengths[0, 0]
    second = first + lengths[0, 1]
    mine = place * rows + jnp.arange(rows, dtype=jnp.int32)
    my_seg = segment_of(mine, first, second)
    begin = jnp.where(my_seg == 0, 0, jnp.where(my_seg == 1, first, second))
    position_index = mine - begin
    last_row = place * rows + rows - 1
    mixgain_f = mixgain.astype(jnp.float32)
    taps_f = mixtaps.astype(jnp.float32)
    lowgain_f = lowgain.astype(jnp.float32)
    attgain_f = attgain.astype(jnp.float32)
    querygain_f = querygain.astype(jnp.float32)
    keysgain_f = keysgain.astype(jnp.float32)
    topgain_f = topgain.astype(jnp.float32)
    hidden = tokens.astype(jnp.float32)
    normed_one = root_mean_square_scale(hidden, mixgain_f).astype(jnp.bfloat16)
    mixed = jnp.dot(normed_one, mixentry, preferred_element_type=jnp.float32)
    part_b = mixed[:, :width_model]
    part_c = mixed[:, width_model : 2 * width_model]
    part_x = mixed[:, 2 * width_model :]
    product = (part_b * part_x).astype(jnp.bfloat16)
    borrowed = passed_along(product[rows - 2 :], "ctx", 1)
    extended = jnp.concatenate([borrowed, product], axis=0).astype(jnp.float32)
    fits_one = ((mine >= 1) & (segment_of(mine - 1, first, second) == my_seg)).astype(jnp.float32)[
        :, None
    ]
    fits_two = ((mine >= 2) & (segment_of(mine - 2, first, second) == my_seg)).astype(jnp.float32)[
        :, None
    ]
    conved = conv_local(extended, taps_f, fits_one, fits_two)
    gated = (part_c * conved).astype(jnp.bfloat16)
    hidden_one = hidden + jnp.dot(gated, mixexit, preferred_element_type=jnp.float32)
    hidden_two, kept_low = feed_forward(hidden_one, lowgain_f, lowgate, lowlift, lowdrop)
    normed_two = root_mean_square_scale(hidden_two, attgain_f).astype(jnp.bfloat16)
    query_unrotated = jnp.dot(normed_two, attquery, preferred_element_type=jnp.float32)
    key_unrotated = jnp.dot(normed_two, attkeys, preferred_element_type=jnp.float32)
    value_projected = jnp.dot(normed_two, attvalues, preferred_element_type=jnp.float32)
    query_low = head_prep(query_unrotated, querygain_f, position_index, query_heads).astype(
        jnp.bfloat16
    )
    key_low = head_prep(key_unrotated, keysgain_f, position_index, kv_heads).astype(jnp.bfloat16)
    value_low = value_projected.astype(jnp.bfloat16).reshape(rows, kv_heads, head_size)
    query_grouped = query_low.reshape(rows, kv_heads, shared_gradient, head_size)

    def stat_visit(carry, keys_in, start, offset, width):
        top, total = carry
        key_part = lax.dynamic_slice_in_dim(keys_in, offset, width, 0)
        key_where = start + offset + jnp.arange(width, dtype=jnp.int32)
        raw, allowed = scores_of(
            query_grouped,
            key_part,
            mine,
            key_where,
            my_seg,
            segment_of(key_where, first, second),
            scale,
        )
        new_top = jnp.maximum(top, jnp.max(jnp.where(allowed, raw, NEGATIVE), axis=-1))
        weights = jnp.where(allowed, jnp.exp(raw - new_top[..., None]), 0.0)
        total = total * jnp.exp(top - new_top) + jnp.sum(weights, axis=-1)
        return (new_top, total)

    stat_state = (
        jnp.full((kv_heads, shared_gradient, rows), NEGATIVE, jnp.float32),
        jnp.zeros((kv_heads, shared_gradient, rows), jnp.float32),
    )
    piece = lax.all_gather(key_low, "ctx", axis=0, tiled=True)
    start = jnp.int32(0)
    count = piece.shape[0]

    def stat_running(inner):
        return sweep(
            inner, count, lambda acc, offset, width: stat_visit(acc, piece, start, offset, width)
        )

    top, total = lax.cond(start > last_row, lambda inner: inner, stat_running, stat_state)
    logsum = top + jnp.log(total)

    def forward_visit(accum, keys_in, values_in, start, offset, width):
        key_part = lax.dynamic_slice_in_dim(keys_in, offset, width, 0)
        value_part = lax.dynamic_slice_in_dim(values_in, offset, width, 0)
        key_where = start + offset + jnp.arange(width, dtype=jnp.int32)
        raw, allowed = scores_of(
            query_grouped,
            key_part,
            mine,
            key_where,
            my_seg,
            segment_of(key_where, first, second),
            scale,
        )
        prob_low = jnp.where(allowed, jnp.exp(raw - logsum[..., None]), 0.0).astype(jnp.bfloat16)
        return accum + jnp.einsum(
            "kgtp,pkd->kgtd", prob_low, value_part, preferred_element_type=jnp.float32
        )

    forward_start = jnp.int32(0)
    keys_in = lax.all_gather(key_low, "ctx", axis=0, tiled=True)
    values_in = lax.all_gather(value_low, "ctx", axis=0, tiled=True)
    forward_count = keys_in.shape[0]

    def forward_running(inner):
        return sweep(
            inner,
            forward_count,
            lambda acc, offset, width: forward_visit(
                acc, keys_in, values_in, forward_start, offset, width
            ),
        )

    accum = lax.cond(
        forward_start > last_row,
        lambda inner: inner,
        forward_running,
        jnp.zeros((kv_heads, shared_gradient, rows, head_size), jnp.float32),
    )
    attended = accum.transpose(2, 0, 1, 3).reshape(rows, -1)
    attended_low = attended.astype(jnp.bfloat16)
    hidden_three = hidden_two + jnp.dot(attended_low, attexit, preferred_element_type=jnp.float32)
    output, kept_top = feed_forward(hidden_three, topgain_f, topgate, toplift, topdrop)
    grad = cotangent.astype(jnp.float32)
    grad, top_grads = feed_back(grad, hidden_three, topgain_f, kept_top, topgate, toplift, topdrop)
    grad_low = grad.astype(jnp.bfloat16)
    attexit_grad = inner_dot(attended_low, grad_low)
    out_grads = (
        outer_dot(grad_low, attexit)
        .astype(jnp.bfloat16)
        .reshape(rows, kv_heads, shared_gradient, head_size)
    )
    delta = jnp.einsum(
        "tkgd,tkgd->kgt",
        out_grads.astype(jnp.float32),
        attended.reshape(rows, kv_heads, shared_gradient, head_size),
    )
    cycle_size = lax.axis_size("ctx")

    def cycle_visit(state, keys_in, values_in, start, offset, width):
        query_acc, key_acc, value_acc = state
        key_part = lax.dynamic_slice_in_dim(keys_in, offset, width, 0)
        value_part = lax.dynamic_slice_in_dim(values_in, offset, width, 0)
        key_where = start + offset + jnp.arange(width, dtype=jnp.int32)
        query_grad, key_grad, value_grad = grad_block(
            query_grouped,
            out_grads,
            logsum,
            delta,
            key_part,
            value_part,
            mine,
            key_where,
            my_seg,
            segment_of(key_where, first, second),
            scale,
        )
        key_acc = lax.dynamic_update_slice_in_dim(
            key_acc, lax.dynamic_slice_in_dim(key_acc, offset, width, 0) + key_grad, offset, 0
        )
        value_acc = lax.dynamic_update_slice_in_dim(
            value_acc, lax.dynamic_slice_in_dim(value_acc, offset, width, 0) + value_grad, offset, 0
        )
        return (query_acc + query_grad, key_acc, value_acc)

    def cycle_step(step, carry):
        keys_cur, values_cur, key_acc, value_acc, query_acc = carry
        anchor = (place - step + cycle_size) % cycle_size
        start = anchor * rows

        def cycle_running(state):
            return sweep(
                state,
                rows,
                lambda acc, offset, width: cycle_visit(
                    acc, keys_cur, values_cur, start, offset, width
                ),
            )

        query_acc, key_acc, value_acc = lax.cond(
            start > last_row, lambda state: state, cycle_running, (query_acc, key_acc, value_acc)
        )
        keys_cur, values_cur = passed_along((keys_cur, values_cur), "ctx", 1)
        key_acc, value_acc = (
            passed_along_2(key_acc.astype(jnp.bfloat16), "ctx", 1).astype(key_acc.dtype),
            passed_along_2(value_acc.astype(jnp.bfloat16), "ctx", 1).astype(value_acc.dtype),
        )
        return (keys_cur, values_cur, key_acc, value_acc, query_acc)

    cycle_state = (
        key_low,
        value_low,
        jnp.zeros((rows, kv_heads, head_size), jnp.float32),
        jnp.zeros((rows, kv_heads, head_size), jnp.float32),
        jnp.zeros((rows, kv_heads, shared_gradient, head_size), jnp.float32),
    )
    _, _, key_grads, value_grads, query_acc = lax.fori_loop(0, cycle_size, cycle_step, cycle_state)
    _, pull_query = jax.vjp(
        lambda raw, gain: head_prep(raw, gain, position_index, query_heads),
        query_unrotated,
        querygain_f,
    )
    query_raw_grad, querygain_grad = pull_query(query_acc.reshape(rows, query_heads, head_size))
    _, pull_key = jax.vjp(
        lambda raw, gain: head_prep(raw, gain, position_index, kv_heads), key_unrotated, keysgain_f
    )
    key_raw_grad, keysgain_grad = pull_key(key_grads)
    query_raw_low = query_raw_grad.astype(jnp.bfloat16)
    key_raw_low = key_raw_grad.astype(jnp.bfloat16)
    value_raw_low = value_grads.reshape(rows, -1).astype(jnp.bfloat16)
    attquery_grad = inner_dot(normed_two, query_raw_low)
    attkeys_grad = inner_dot(normed_two, key_raw_low)
    attvalues_grad = inner_dot(normed_two, value_raw_low)
    normed_two_grad = (
        outer_dot(query_raw_low, attquery)
        + outer_dot(key_raw_low, attkeys)
        + outer_dot(value_raw_low, attvalues)
    )
    _, pull_att = jax.vjp(root_mean_square_scale, hidden_two, attgain_f)
    hidden_two_grad, attgain_grad = pull_att(normed_two_grad)
    grad = grad + hidden_two_grad
    grad, low_grads = feed_back(grad, hidden_one, lowgain_f, kept_low, lowgate, lowlift, lowdrop)
    grad_low = grad.astype(jnp.bfloat16)
    mixexit_grad = inner_dot(gated, grad_low)
    gated_grad = outer_dot(grad_low, mixexit)
    part_c_grad = gated_grad * conved
    conved_grad = gated_grad * part_c
    _, pull_conv = jax.vjp(
        lambda ext, taps: conv_local(ext, taps, fits_one, fits_two), extended, taps_f
    )
    extended_grad, mixtaps_grad = pull_conv(conved_grad)
    returned_rim = passed_along(extended_grad[:2], "ctx", -1)
    product_grad = extended_grad[2:].at[rows - 2 :].add(returned_rim)
    mixed_grad = jnp.concatenate(
        [product_grad * part_x, part_c_grad, product_grad * part_b], axis=1
    ).astype(jnp.bfloat16)
    mixentry_grad = inner_dot(normed_one, mixed_grad)
    normed_one_grad = outer_dot(mixed_grad, mixentry)
    _, pull_mix = jax.vjp(root_mean_square_scale, hidden, mixgain_f)
    hidden_grad, mixgain_grad = pull_mix(normed_one_grad)
    tokens_grad = grad + hidden_grad
    lowgain_grad, lowgate_grad, lowlift_grad, lowdrop_grad = low_grads
    topgain_grad, topgate_grad, toplift_grad, topdrop_grad = top_grads
    shares = (
        lax.psum_scatter(mixentry_grad, "ctx", scatter_dimension=0, tiled=True),
        lax.psum_scatter(mixexit_grad, "ctx", scatter_dimension=0, tiled=True),
        lax.psum_scatter(lowgate_grad, "ctx", scatter_dimension=0, tiled=True),
        lax.psum_scatter(lowlift_grad, "ctx", scatter_dimension=0, tiled=True),
        lax.psum_scatter(lowdrop_grad, "ctx", scatter_dimension=0, tiled=True),
        lax.psum_scatter(attquery_grad, "ctx", scatter_dimension=0, tiled=True),
        lax.psum_scatter(attkeys_grad, "ctx", scatter_dimension=0, tiled=True),
        lax.psum_scatter(attvalues_grad, "ctx", scatter_dimension=0, tiled=True),
        lax.psum_scatter(attexit_grad, "ctx", scatter_dimension=0, tiled=True),
        lax.psum_scatter(topgate_grad, "ctx", scatter_dimension=0, tiled=True),
        lax.psum_scatter(toplift_grad, "ctx", scatter_dimension=0, tiled=True),
        lax.psum_scatter(topdrop_grad, "ctx", scatter_dimension=0, tiled=True),
    )
    smalls = lax.psum(
        (
            mixgain_grad,
            mixtaps_grad,
            lowgain_grad,
            attgain_grad,
            querygain_grad,
            keysgain_grad,
            topgain_grad,
        ),
        "ctx",
    )
    summed = (
        lax.psum(shares[0].astype(jnp.bfloat16), "dp").astype(jnp.float32),
        lax.psum(shares[1].astype(jnp.bfloat16), "dp").astype(jnp.float32),
        lax.psum(shares[2].astype(jnp.bfloat16), "dp").astype(jnp.float32),
        lax.psum(shares[3].astype(jnp.bfloat16), "dp").astype(jnp.float32),
        lax.psum(shares[4].astype(jnp.bfloat16), "dp").astype(jnp.float32),
        lax.psum(shares[5].astype(jnp.bfloat16), "dp").astype(jnp.float32),
        lax.psum(shares[6].astype(jnp.bfloat16), "dp").astype(jnp.float32),
        lax.psum(shares[7].astype(jnp.bfloat16), "dp").astype(jnp.float32),
        lax.psum(shares[8].astype(jnp.bfloat16), "dp").astype(jnp.float32),
        lax.psum(shares[9].astype(jnp.bfloat16), "dp").astype(jnp.float32),
        lax.psum(shares[10].astype(jnp.bfloat16), "dp").astype(jnp.float32),
        lax.psum(shares[11].astype(jnp.bfloat16), "dp").astype(jnp.float32),
        lax.psum(smalls[0].astype(jnp.bfloat16), "dp").astype(jnp.float32),
        lax.psum(smalls[1].astype(jnp.bfloat16), "dp").astype(jnp.float32),
        lax.psum(smalls[2].astype(jnp.bfloat16), "dp").astype(jnp.float32),
        lax.psum(smalls[3].astype(jnp.bfloat16), "dp").astype(jnp.float32),
        lax.psum(smalls[4].astype(jnp.bfloat16), "dp").astype(jnp.float32),
        lax.psum(smalls[5].astype(jnp.bfloat16), "dp").astype(jnp.float32),
        lax.psum(smalls[6].astype(jnp.bfloat16), "dp").astype(jnp.float32),
    )
    return (
        output,
        tokens_grad,
        summed[12],
        summed[0],
        summed[13],
        summed[1],
        summed[14],
        summed[2],
        summed[3],
        summed[4],
        summed[15],
        summed[5],
        summed[6],
        summed[7],
        summed[16],
        summed[17],
        summed[8],
        summed[18],
        summed[9],
        summed[10],
        summed[11],
    )


LANES = 128
BF = jnp.bfloat16
F32 = jnp.float32
ONES_NT = (((1,), (1,)), ((), ()))
ONES_TN = (((0,), (0,)), ((), ()))
VMEM_LIMIT = 60 * 1024 * 1024
PIECE = 16
SUB = 2 * PIECE
STRIP = 256
RING = 16
LAG = 3
AHEAD = 8
SMALL_ROWS = ((0, 0), (1, 0), (4, 0), (5, 0), (6, 0), (7, 0), (7, LANES))


def vmem_specs(count):
    return [pl.BlockSpec(memory_space=pltpu.VMEM)] * count


def lane_of(shape):
    return lax.broadcasted_iota(jnp.int32, shape, len(shape) - 1)


def row_of(ref):
    return ref[...].astype(F32).reshape(1, ref.shape[0])


def same_head(head):
    row = lax.broadcasted_iota(jnp.int32, (LANES, LANES), 0) // head
    column = lax.broadcasted_iota(jnp.int32, (LANES, LANES), 1) // head
    return jnp.where(row == column, 1.0 / head, 0.0).astype(BF)


def head_mean(value, blocks):
    high = value.astype(BF)
    low = (value - high.astype(F32)).astype(BF)
    return (jnp.dot(high, blocks, preferred_element_type=F32) + jnp.dot(low, blocks, preferred_element_type=F32))


def twice(ref):
    row = row_of(ref)
    return jnp.concatenate([row, row], axis=1)


def other_half(value, head):
    lane = lane_of(value.shape)
    ahead = pltpu.roll(value, LANES - head // 2, 1)
    behind = pltpu.roll(value, head // 2, 1)
    return jnp.where(lane % head < head // 2, ahead, behind)


def swap_heads(value, head):
    return pltpu.roll(value, head, 1)


def three_parts(value):
    high = value.astype(BF)
    rest = value - high.astype(F32)
    middle = rest.astype(BF)
    low = (rest - middle.astype(F32)).astype(BF)
    return high.astype(F32), middle.astype(F32), low.astype(F32)


def project_kernel(head, hid_ref, gain_ref, wq_ref, wk_ref, wv_ref, cos_ref, sin_ref, qg_ref, kg_ref,
                   msg_ref, normt_ref, qraw_ref, kraw_ref):
    hid = hid_ref[...]
    scale = lax.rsqrt(jnp.mean(hid * hid, axis=-1, keepdims=True) + EPS)
    normed = hid * scale * row_of(gain_ref)
    normt_ref[...] = turned(normed)
    normed = normed.astype(BF)
    blocks = same_head(head)
    query_gain, keys_gain = twice(qg_ref), twice(kg_ref)
    cosine, sine = cos_ref[...], sin_ref[...]
    half_rows = msg_ref.shape[1]
    lane = lane_of(cosine.shape)

    def prepared(raw, gain):
        unit = raw * lax.rsqrt(head_mean(raw * raw, blocks) + EPS) * gain
        return unit * cosine + other_half(unit, head) * sine

    def put(dest, start, tile):
        low = tile.astype(BF)
        for part in range(2):
            msg_ref[2 * dest + part, :, start:start + LANES] = low[part * half_rows:(part + 1) * half_rows]

    qraw = jnp.dot(normed, wq_ref[...], preferred_element_type=F32)
    qraw_ref[...] = qraw
    for tile in range(qraw.shape[1] // LANES):
        put(tile, 0, prepared(qraw[:, tile * LANES:(tile + 1) * LANES], query_gain))
    kraw = jnp.dot(normed, wk_ref[...], preferred_element_type=F32)
    kraw_ref[...] = kraw
    vraw = jnp.dot(normed, wv_ref[...], preferred_element_type=F32)
    for tile in range(kraw.shape[1] // LANES):
        keys = prepared(kraw[:, tile * LANES:(tile + 1) * LANES], keys_gain)
        values = vraw[:, tile * LANES:(tile + 1) * LANES]
        put(2 * tile, LANES, jnp.where(lane < head, keys, swap_heads(values, head)))
        put(2 * tile + 1, LANES, jnp.where(lane < head, swap_heads(keys, head), values))


def project_back_kernel(head, backq_ref, backk_ref, hid_ref, gain_ref, wq_ref, wk_ref, wv_ref, cos_ref, sin_ref, qg_ref,
                        kg_ref, qraw_ref, kraw_ref, grad_ref,
                        rawq_ref, keep_ref, send_ref, two_ref, again_ref, qgain_ref, kgain_ref):
    query_gain, keys_gain = twice(qg_ref), twice(kg_ref)
    blocks = same_head(head)
    cosine, sine = cos_ref[...], sin_ref[...]
    lane = lane_of(cosine.shape)

    def fetch(source, dest):
        return jnp.concatenate([source[2 * dest], source[2 * dest + 1]], axis=0).astype(F32)

    def through(grad, raw, gain):
        scale = lax.rsqrt(head_mean(raw * raw, blocks) + EPS)
        unit = raw * scale
        turned = grad * cosine - other_half(grad, head) * sine
        gain_part = jnp.sum(turned * unit, axis=0, keepdims=True)
        inward = turned * gain
        return scale * (inward - unit * head_mean(inward * unit, blocks)), gain_part

    width_q = wq_ref.shape[1]
    width_k = wk_ref.shape[1]
    gain_total = jnp.zeros((1, LANES), F32)
    for tile in range(width_q // LANES):
        got, part = through(fetch(backq_ref, tile), qraw_ref[:, tile * LANES:(tile + 1) * LANES], query_gain)
        gain_total = gain_total + part
        rawq_ref[:, tile * LANES:(tile + 1) * LANES] = got.astype(BF)
    qgain_ref[...] = gain_total
    gain_total = jnp.zeros((1, LANES), F32)
    key_tiles, value_tiles = [], []
    for tile in range(width_k // LANES):
        even, odd = fetch(backk_ref, 2 * tile), fetch(backk_ref, 2 * tile + 1)
        keys = jnp.where(lane < head, even, swap_heads(odd, head))
        values = jnp.where(lane < head, swap_heads(even, head), odd)
        got, part = through(keys, kraw_ref[:, tile * LANES:(tile + 1) * LANES], keys_gain)
        gain_total = gain_total + part
        key_tiles.append(got.astype(BF))
        value_tiles.append(values.astype(BF))
    kgain_ref[...] = gain_total
    keys, values = jnp.concatenate(key_tiles, axis=1), jnp.concatenate(value_tiles, axis=1)
    keep_ref[...], send_ref[...] = kept_first(keys, values)
    normed_grad = nt_dot(rawq_ref[...], wq_ref[...]) + nt_dot(keys, wk_ref[...]) + nt_dot(values, wv_ref[...])
    hid = hid_ref[...]
    scale = lax.rsqrt(jnp.mean(hid * hid, axis=-1, keepdims=True) + EPS)
    unit = hid * scale
    again_ref[...] = jnp.sum(normed_grad * unit, axis=0, keepdims=True)
    inward = normed_grad * row_of(gain_ref)
    two_ref[...] = grad_ref[...] + scale * (inward - unit * jnp.mean(inward * unit, axis=-1, keepdims=True))


def allowed_block(row_axis, key_axis, shape, first, second, part, base, start, rows, half_rows):
    row = lax.broadcasted_iota(jnp.int32, shape, row_axis)
    token = (base + row // (2 * half_rows)) * rows + part * half_rows + row % half_rows
    key = start + lax.broadcasted_iota(jnp.int32, shape, key_axis)
    begin = jnp.where(token >= second, second, jnp.where(token >= first, first, 0))
    return (key >= begin) & (key <= token)


MESH = pl.DeviceIdType.MESH


def turned(value):
    return value.astype(F32).T.astype(BF)


def norm_scale(hidden):
    return lax.rsqrt(jnp.mean(hidden * hidden, axis=-1, keepdims=True) + EPS)


def norm_pull(normed_grad, hidden, gain):
    scale = norm_scale(hidden)
    unit = hidden * scale
    inward = normed_grad * gain
    back = scale * (inward - unit * jnp.mean(inward * unit, axis=-1, keepdims=True))
    return back, jnp.sum(normed_grad * unit, axis=0, keepdims=True)


def kept_first(one, two):
    first = lax.axis_index("dp") == 0
    return jnp.where(first, one, two), jnp.where(first, two, one)


def nt_dot(left, right):
    return lax.dot_general(left, right, ONES_NT, preferred_element_type=F32)


def nn_dot(left, right):
    return jnp.dot(left, right, preferred_element_type=F32)


def activation_pull(gate_act, lift_act, sigma, inner_grad):
    gate_grad = inner_grad * lift_act * sigma * (1 + gate_act * (1 - sigma))
    return gate_grad.astype(BF), (inner_grad * gate_act * sigma).astype(BF)


def low_kernel(hid_ref, gain_ref, gate_ref, lift_ref, drop_ref,
               out_ref, normt_ref, gact_ref, lact_ref, innert_ref, norm_ref):
    step = pl.program_id(0)

    @pl.when(step == 0)
    def _():
        hid = hid_ref[...]
        normed = hid * norm_scale(hid) * row_of(gain_ref)
        norm_ref[...] = normed.astype(BF)
        normt_ref[...] = turned(normed)
        out_ref[...] = hid

    normed = norm_ref[...]
    gate_act = nn_dot(normed, gate_ref[...])
    lift_act = nn_dot(normed, lift_ref[...])
    inner = gate_act * jax.nn.sigmoid(gate_act) * lift_act
    gact_ref[...] = gate_act.astype(BF)
    lact_ref[...] = lift_act.astype(BF)
    innert_ref[...] = turned(inner)
    out_ref[...] += nn_dot(inner.astype(BF), drop_ref[...])


def low_back_kernel(grad_ref, hid_ref, gain_ref, gact_ref, lact_ref, gate_ref, lift_ref, drop_ref,
                    out_ref, again_ref, low_ref, outlow_ref, glow_ref, llow_ref, acc_ref):
    step = pl.program_id(0)

    @pl.when(step == 0)
    def _():
        low_ref[...] = grad_ref[...].astype(BF)
        acc_ref[...] = jnp.zeros_like(acc_ref)

    gate_act, lift_act = gact_ref[...].astype(F32), lact_ref[...].astype(F32)
    inner_grad = nt_dot(low_ref[...], drop_ref[...])
    gate_low, lift_low = activation_pull(gate_act, lift_act, jax.nn.sigmoid(gate_act), inner_grad)
    glow_ref[...], llow_ref[...] = kept_first(gate_low, lift_low)
    acc_ref[...] += nt_dot(gate_low, gate_ref[...]) + nt_dot(lift_low, lift_ref[...])

    @pl.when(step == pl.num_programs(0) - 1)
    def _():
        back, gain_part = norm_pull(acc_ref[...], hid_ref[...], row_of(gain_ref))
        again_ref[...] = gain_part
        out = grad_ref[...] + back
        out_ref[...] = out
        outlow_ref[...] = out.astype(BF)


def top_kernel(got_ref, two_ref, exit_ref, cot_ref, gain_ref, gate_ref, lift_ref, drop_ref,
               out_ref, grad_ref, gradlow_ref, send_ref, attt_ref, again_ref, normt_ref, innert_ref, keep_ref,
               senda_ref, sendb_ref, hid_ref, norm_ref, acc_ref):
    step = pl.program_id(0)
    half_rows = got_ref.shape[1]

    @pl.when(step == 0)
    def _():
        tiles = []
        for tile in range(got_ref.shape[0] // 2):
            tiles.append(jnp.concatenate([got_ref[2 * tile], got_ref[2 * tile + 1]], axis=0))
        attended = jnp.concatenate(tiles, axis=1)
        attt_ref[...] = turned(attended)
        hid = two_ref[...] + nn_dot(attended, exit_ref[...])
        hid_ref[...] = hid
        normed = hid * norm_scale(hid) * row_of(gain_ref)
        norm_ref[...] = normed.astype(BF)
        normt_ref[...] = turned(normed)
        out_ref[...] = hid
        acc_ref[...] = jnp.zeros_like(acc_ref)

    normed = norm_ref[...]
    gate_act = nn_dot(normed, gate_ref[...])
    lift_act = nn_dot(normed, lift_ref[...])
    sigma = jax.nn.sigmoid(gate_act)
    inner = gate_act * sigma * lift_act
    innert_ref[...] = turned(inner)
    out_ref[...] += nn_dot(inner.astype(BF), drop_ref[...])
    inner_grad = nt_dot(cot_ref[...], drop_ref[...])
    gate_low, lift_low = activation_pull(gate_act, lift_act, sigma, inner_grad)
    keep_ref[...], sent_part = kept_first(gate_low, lift_low)
    senda_ref[...], sendb_ref[...] = sent_part[:half_rows], sent_part[half_rows:]
    acc_ref[...] += nt_dot(gate_low, gate_ref[...]) + nt_dot(lift_low, lift_ref[...])

    @pl.when(step == pl.num_programs(0) - 1)
    def _():
        back, gain_part = norm_pull(acc_ref[...], hid_ref[...], row_of(gain_ref))
        again_ref[...] = gain_part
        grad = cot_ref[...].astype(F32) + back
        grad_ref[...] = grad
        low = grad.astype(BF)
        gradlow_ref[...] = low
        sent = nt_dot(low, exit_ref[...]).astype(BF)
        for tile in range(send_ref.shape[0] // 2):
            for part in range(2):
                send_ref[2 * tile + part] = sent[part * half_rows:(part + 1) * half_rows,
                                                 tile * LANES:(tile + 1) * LANES]


TILE = 512
WIDE_TILE = 1152


def whole_block(shape):
    return pl.BlockSpec(shape, lambda step, rank=len(shape): (0,) * rank)


def column_block(rows, tile=TILE):
    return pl.BlockSpec((rows, tile), lambda step: (0, step))


def row_block(columns, tile=TILE):
    return pl.BlockSpec((tile, columns), lambda step: (step, 0))


def call_tiled(kernel, tiles, ins, outs, scratch, flops, moved, name):
    return pl.pallas_call(
        kernel,
        grid=(tiles,),
        in_specs=[spec for _, spec in ins],
        out_specs=tuple(spec for _, spec in outs),
        out_shape=tuple(shape for shape, _ in outs),
        scratch_shapes=scratch,
        compiler_params=pltpu.CompilerParams(vmem_limit_bytes=VMEM_LIMIT, dimension_semantics=("arbitrary",)),
        cost_estimate=pl.CostEstimate(flops=flops, bytes_accessed=moved, transcendentals=0),
        name=name,
    )(*[value for value, _ in ins])


def feed_low(hidden, gain, gate, lift, drop):
    rows, width = hidden.shape
    ff = gate.shape[1]
    S = jax.ShapeDtypeStruct
    return call_tiled(
        low_kernel, ff // WIDE_TILE,
        [(hidden, whole_block((rows, width))), (gain, whole_block((width,))), (gate, column_block(width, WIDE_TILE)),
         (lift, column_block(width, WIDE_TILE)), (drop, row_block(width, WIDE_TILE))],
        [(S((rows, width), F32), whole_block((rows, width))), (S((width, rows), BF), whole_block((width, rows))),
         (S((rows, ff), BF), column_block(rows, WIDE_TILE)), (S((rows, ff), BF), column_block(rows, WIDE_TILE)),
         (S((ff, rows), BF), row_block(rows, WIDE_TILE))],
        [pltpu.VMEM((rows, width), BF)], 6 * rows * width * ff, 38 << 20, "feed_low")


def feed_low_back(grad, hidden, gain, gact, lact, gate, lift, drop):
    rows, width = hidden.shape
    ff = gate.shape[1]
    S = jax.ShapeDtypeStruct
    full = whole_block((rows, width))
    return call_tiled(
        low_back_kernel, ff // WIDE_TILE,
        [(grad, full), (hidden, full), (gain, whole_block((width,))), (gact, column_block(rows, WIDE_TILE)),
         (lact, column_block(rows, WIDE_TILE)), (gate, column_block(width, WIDE_TILE)), (lift, column_block(width, WIDE_TILE)),
         (drop, row_block(width, WIDE_TILE))],
        [(S((rows, width), F32), full), (S((1, width), F32), whole_block((1, width))), (S((rows, width), BF), full),
         (S((rows, width), BF), full), (S((rows, ff), BF), column_block(rows, WIDE_TILE)), (S((rows, ff), BF), column_block(rows, WIDE_TILE))],
        [pltpu.VMEM((rows, width), F32)], 1 << 20, 1 << 10, "feed_low_back")


def feed_top(got, two, exit_weight, cotangent, gain, gate, lift, drop):
    rows, width = two.shape
    ff = gate.shape[1]
    S = jax.ShapeDtypeStruct
    full = whole_block((rows, width))
    flat = whole_block((1, width))
    standing = whole_block((width, rows))
    return call_tiled(
        top_kernel, ff // TILE,
        [(got, whole_block(got.shape)), (two, full), (exit_weight, whole_block(exit_weight.shape)), (cotangent, full),
         (gain, whole_block((width,))), (gate, column_block(width)), (lift, column_block(width)), (drop, row_block(width))],
        [(S((rows, width), F32), full), (S((rows, width), F32), full), (S((rows, width), BF), full),
         (S(got.shape, BF), whole_block(got.shape)), (S((width, rows), BF), standing), (S((1, width), F32), flat),
         (S((width, rows), BF), standing), (S((ff, rows), BF), row_block(rows)), (S((rows, ff), BF), column_block(rows)),
         (S((rows // 2, ff), BF), column_block(rows // 2)), (S((rows // 2, ff), BF), column_block(rows // 2))],
        [pltpu.VMEM((rows, width), F32), pltpu.VMEM((rows, width), BF), pltpu.VMEM((rows, width), F32)],
        12 * rows * width * ff, 45 << 20, "feed_top")


MIX_TILE = 256
HALO = 16


def shifted(value, steps):
    return pltpu.roll(value, steps, 0)


def mix_kernel(tok_ref, prev_ref, pos_ref, gain_ref, taps_ref, entb_ref, entc_ref, entx_ref, exit_ref,
               out_ref, normt_ref, gatedt_ref, b_ref, c_ref, x_ref, conv_ref, prod_ref, norm_ref):
    step = pl.program_id(0)

    @pl.when(step == 0)
    def _():
        hid = tok_ref[...].astype(F32)
        normed = hid * norm_scale(hid) * row_of(gain_ref)
        norm_ref[HALO:] = normed.astype(BF)
        normt_ref[...] = turned(normed)
        before = prev_ref[...].astype(F32)
        norm_ref[:HALO] = (before * norm_scale(before) * row_of(gain_ref)).astype(BF)
        out_ref[...] = hid

    taps = taps_ref[...].astype(F32)
    part_b = nn_dot(norm_ref[...], entb_ref[...])
    part_x = nn_dot(norm_ref[...], entx_ref[...])
    part_c = nn_dot(norm_ref[HALO:], entc_ref[...])
    product = (part_b * part_x).astype(BF)
    prod_ref[...] = product
    product = product.astype(F32)
    one = jnp.where(pos_ref[:-HALO] >= 1.0, shifted(product, 1)[HALO:], 0.0)
    two = jnp.where(pos_ref[:-HALO] >= 2.0, shifted(product, 2)[HALO:], 0.0)
    conved = taps[2:3] * product[HALO:] + taps[1:2] * one + taps[0:1] * two
    gated = part_c * conved
    b_ref[...] = part_b[HALO:].astype(BF)
    c_ref[...] = part_c.astype(BF)
    x_ref[...] = part_x[HALO:].astype(BF)
    conv_ref[...] = conved.astype(BF)
    gatedt_ref[...] = turned(gated)
    out_ref[...] += nn_dot(gated.astype(BF), exit_ref[...])


def mix_back_kernel(grad_ref, low_ref, next_ref, cnext_ref, pos_ref, tok_ref, gain_ref, taps_ref, b_ref, c_ref, x_ref,
                    conv_ref, prod_ref, entb_ref, entc_ref, entx_ref, exit_ref,
                    out_ref, again_ref, taps_out_ref, mixed_ref, acc_ref):
    step = pl.program_id(0)
    rows, width = grad_ref.shape
    tile = b_ref.shape[1]

    @pl.when(step == 0)
    def _():
        acc_ref[...] = jnp.zeros_like(acc_ref)

    taps = taps_ref[...].astype(F32)
    lows = jnp.concatenate([low_ref[...], next_ref[...]], axis=0)
    gated_grad = nt_dot(lows, exit_ref[...])
    gate = jnp.concatenate([c_ref[...], cnext_ref[...]], axis=0).astype(F32)
    conved_grad = gated_grad * gate
    first = jnp.where(pos_ref[...] >= 1.0, conved_grad, 0.0)
    second = jnp.where(pos_ref[...] >= 2.0, conved_grad, 0.0)
    ahead_one = shifted(first, rows + HALO - 1)[:rows]
    ahead_two = shifted(second, rows + HALO - 2)[:rows]
    own = conved_grad[:rows]
    product_grad = taps[2:3] * own + taps[1:2] * ahead_one + taps[0:1] * ahead_two
    product = prod_ref[...].astype(F32)
    total = lambda value: jnp.sum(value, axis=0, keepdims=True)
    taps_out_ref[0:1] = total(shifted(product, 2)[HALO:] * second[:rows])
    taps_out_ref[1:2] = total(shifted(product, 1)[HALO:] * first[:rows])
    taps_out_ref[2:3] = total(product[HALO:] * own)
    b_low = (product_grad * x_ref[...].astype(F32)).astype(BF)
    c_low = (gated_grad[:rows] * conv_ref[...].astype(F32)).astype(BF)
    x_low = (product_grad * b_ref[...].astype(F32)).astype(BF)
    for place, value in enumerate((b_low, c_low, x_low)):
        mixed_ref[:, pl.ds(pl.multiple_of(place * width + step * tile, tile), tile)] = value
    acc_ref[...] += nt_dot(b_low, entb_ref[...]) + nt_dot(c_low, entc_ref[...]) + nt_dot(x_low, entx_ref[...])

    @pl.when(step == pl.num_programs(0) - 1)
    def _():
        back, gain_part = norm_pull(acc_ref[...], tok_ref[...].astype(F32), row_of(gain_ref))
        again_ref[...] = gain_part
        out_ref[...] = grad_ref[...] + back


def mix_specs(width):
    tiles = width // MIX_TILE
    entry = [pl.BlockSpec((width, MIX_TILE), lambda step, part=part: (0, part * tiles + step)) for part in range(3)]
    return tiles, entry, row_block(width, MIX_TILE)


def mix_forward(tokens, before, position, gain, taps, entry, exit_weight):
    rows, width = tokens.shape
    tiles, entry_specs, exit_spec = mix_specs(width)
    S = jax.ShapeDtypeStruct
    full = whole_block((rows, width))
    columns = column_block(rows, MIX_TILE)
    return call_tiled(
        mix_kernel, tiles,
        [(tokens, full), (before, whole_block(before.shape)), (position, whole_block(position.shape)),
         (gain, whole_block((width,))), (taps, column_block(3, MIX_TILE)), *[(entry, spec) for spec in entry_specs],
         (exit_weight, exit_spec)],
        [(S((rows, width), F32), full), (S((width, rows), BF), whole_block((width, rows))),
         (S((width, rows), BF), row_block(rows, MIX_TILE))] + [(S((rows, width), BF), columns)] * 4
        + [(S((rows + HALO, width), BF), column_block(rows + HALO, MIX_TILE))],
        [pltpu.VMEM((rows + HALO, width), BF)], 8 * rows * width * width, 12 << 20, "mix")


def mix_backward(grad, low, after, gate_after, position, tokens, gain, taps, kept, entry, exit_weight):
    rows, width = grad.shape
    tiles, entry_specs, exit_spec = mix_specs(width)
    S = jax.ShapeDtypeStruct
    full = whole_block((rows, width))
    flat = whole_block((1, width))
    columns = column_block(rows, MIX_TILE)
    part_b, part_c, part_x, conved, product = kept
    return call_tiled(
        mix_back_kernel, tiles,
        [(grad, full), (low, full), (after, whole_block(after.shape)), (gate_after, column_block(HALO, MIX_TILE)),
         (position, whole_block(position.shape)), (tokens, full), (gain, whole_block((width,))), (taps, column_block(3, MIX_TILE)),
         (part_b, columns), (part_c, columns), (part_x, columns), (conved, columns),
         (product, column_block(rows + HALO, MIX_TILE)), *[(entry, spec) for spec in entry_specs],
         (exit_weight, exit_spec)],
        [(S((rows, width), F32), full), (S((1, width), F32), flat), (S((3, width), F32), column_block(3, MIX_TILE)),
         (S((rows, 3 * width), BF), whole_block((rows, 3 * width)))],
        [pltpu.VMEM((rows, width), F32)], 8 * rows * width * width, 16 << 20, "mix_back")


def sweep_keys(visit, index, tail, part, base, rows, half_rows, keys, sources):
    lowest = base * rows + part * half_rows
    end = (base + sources - 1) * rows + (part + 1) * half_rows
    count = (end + keys - 1) // keys
    free = jnp.where(end > tail, 0, jnp.maximum((lowest + 1) // keys - 1, 0))
    lax.fori_loop(0, free, lambda step, _: visit(step + 1, False), None)
    lax.fori_loop(0, count - free, lambda step, _: visit(jnp.where(step == 0, 0, free + step), True), None)


def greet(me, count):
    barrier = pltpu.get_barrier_semaphore()

    def hello(step, _):
        pl.semaphore_signal(barrier, inc=1, device_id={"ctx": lax.rem(me + step, count)}, device_id_type=MESH)

    lax.fori_loop(1, count, hello, None)
    pl.semaphore_signal(barrier, inc=1, device_id={"dp": 1 - lax.axis_index("dp")}, device_id_type=MESH)
    pl.semaphore_wait(barrier, count)


def hosted_copies(kinds, sources, landings, sends, recvs):
    y = lax.axis_index("dp")
    copies = []
    for number, (kind, source, landing) in enumerate(zip(kinds, sources, landings)):
        if kind == "rows":
            height = landing.shape[2]
            source = source.at[:, :, pl.ds(pl.multiple_of((1 - y) * height, PIECE), height), :]
        if kind == "columns":
            width = landing.shape[1]
            source = source.at[:, pl.ds(pl.multiple_of((1 - y) * width, STRIP), width)]
        copies.append(pltpu.make_async_remote_copy(
            src_ref=source, dst_ref=landing, send_sem=sends.at[number], recv_sem=recvs.at[number],
            device_id={"dp": 1 - y}, device_id_type=MESH))
    return copies


def hosted_shapes(hosted):
    shapes = []
    for kind, value in hosted:
        shape = list(value.shape)
        if kind == "rows":
            shape[2] //= 2
        if kind == "columns":
            shape[1] //= 2
        shapes.append(jax.ShapeDtypeStruct(tuple(shape), value.dtype))
    return shapes


def attend_kernel(head, rows, keys, sources, count, kinds, *refs):
    extra = len(kinds)
    (info_ref, msg_ref), guests, refs = refs[:2], refs[2:2 + extra], refs[2 + extra:]
    (got_ref, out_ref, aug_ref, all_ref), landings, refs = refs[:4], refs[4:4 + extra], refs[4 + extra:]
    (land, kv, tiles, arrive, ones_ref, acc_ref, msend, mrecv, fsend, frecv, gsend, grecv, hsend, hrecv) = refs
    first = info_ref[0, 0]
    second = first + info_ref[0, 1]
    me = lax.axis_index("ctx")
    part = me % 2
    twin = {"ctx": me + 1 - 2 * part}
    half_rows = msg_ref.shape[1]
    wide = sources * 2 * half_rows
    span = sources * rows
    factor = math.log2(math.e) / math.sqrt(head)
    lane = lane_of((half_rows, LANES))
    greet(me, count)

    def remote(src, dst, send, recv, where):
        return pltpu.make_async_remote_copy(src_ref=src, dst_ref=dst, send_sem=send, recv_sem=recv,
                                            device_id=where, device_id_type=MESH)

    def msg_copy(owner, dest):
        return remote(msg_ref.at[dest], land.at[owner], msend.at[dest], mrecv.at[owner], {"ctx": dest})

    def share_copy(source):
        return remote(kv.at[source, part], kv.at[source, part], fsend.at[source], frecv.at[source], twin)

    def tile_copy(owner, dest):
        return remote(tiles.at[dest], arrive.at[owner], gsend.at[dest], grecv.at[owner], {"ctx": dest})

    def start_msg(step, _):
        msg_copy(me, lax.rem(me + step, count)).start()

    lax.fori_loop(1, count, start_msg, None)
    hosted = hosted_copies(kinds, guests, landings, hsend, hrecv)
    for copy in hosted:
        copy.start()
    land[me] = msg_ref[me]

    def share(source):
        @pl.when(source != me)
        def _():
            msg_copy(source, me).wait_recv()

        kv[source, part] = land[source, :, LANES:]
        share_copy(source).start()

    def compute(index):
        base = index * sources
        stack = []
        for source in range(sources):
            share_copy(base + source).wait_recv()
            both = kv[base + source].reshape(rows, LANES)
            place = pl.ds(pl.multiple_of((base + source) * rows, rows), rows)
            all_ref[place] = both
            ones_ref[place] = jnp.where(lane_of(both.shape) < head, jnp.ones_like(both), both)
            tile = land[base + source, :, :LANES].astype(F32)
            stack.append(jnp.where(lane < head, tile, 0.0))
            stack.append(jnp.where(lane < head, swap_heads(tile, head), 0.0))
        queries = jnp.concatenate(stack, axis=0).astype(BF)
        acc_ref[...] = jnp.zeros_like(acc_ref)

        def visit(step, masked):
            start = pl.multiple_of(step * keys, keys)
            here = pl.ds(start, keys)
            raised = jnp.exp2(lax.dot_general(queries, all_ref[here], ONES_NT, preferred_element_type=F32) * factor)
            if masked:
                ok = allowed_block(0, 1, (wide, keys), first, second, part, base, start, rows, half_rows)
                raised = jnp.where(ok, raised, 0.0)
            acc_ref[...] += jnp.dot(raised.astype(BF), ones_ref[here], preferred_element_type=F32)

        sweep_keys(visit, index, count * rows - rows, part, base, rows, half_rows, keys, sources)
        for source in range(sources):
            tile = land[base + source, :, :LANES].astype(F32)
            outs = []
            for which in range(2):
                place = (2 * source + which) * half_rows
                acc = acc_ref[place:place + half_rows]
                turn = swap_heads(acc, head)
                outs.append(turn / acc if which == 0 else acc / turn)
                high, middle, low = three_parts(-math.sqrt(head) * jnp.log(turn))
                query = tile if which == 0 else swap_heads(tile, head)
                extra = jnp.where(lane == head, high, jnp.where(lane == head + 1, middle,
                                                                jnp.where(lane == head + 2, low, 0.0)))
                aug_ref[base + source, which] = jnp.where(lane < head, query, extra).astype(BF)
            out = jnp.where(lane < head, outs[0], outs[1])
            out_ref[base + source] = out
            tiles[base + source] = out.astype(BF)

            @pl.when(base + source != me)
            def _(source=source):
                tile_copy(me, base + source).start()

    def block(index, _):
        @pl.when(index < count // sources)
        def _():
            for source in range(sources):
                share(index * sources + source)

        @pl.when(index > 0)
        def _():
            compute(index - 1)

    lax.fori_loop(0, count // sources + 1, block, None)
    arrive[me] = tiles[me]

    def drain(other, _):
        share_copy(other).wait_send()

        @pl.when(other != me)
        def _():
            msg_copy(me, other).wait_send()
            tile_copy(me, other).wait_send()
            tile_copy(other, me).wait_recv()

    lax.fori_loop(0, count, drain, None)
    got_ref[...] = arrive[...]
    for copy in hosted:
        copy.wait()


def attend_back_kernel(head, rows, keys, sources, count, kinds, *refs):
    extra = len(kinds)
    (info_ref, aug_ref, out_ref, kv_ref, msg_ref), guests, refs = refs[:5], refs[5:5 + extra], refs[5 + extra:]
    (gotq_ref, gotk_ref), landings, refs = refs[:2], refs[2:2 + extra], refs[2 + extra:]
    (land, tiles, away, near, sums, arrive_q, arrive_k, kone_ref, vone_ref, kturn_ref, dk_ref, dv_ref, acc_ref,
     msend, mrecv, fsend, frecv, gsend, grecv, ksend, krecv, hsend, hrecv) = refs
    first = info_ref[0, 0]
    second = first + info_ref[0, 1]
    me = lax.axis_index("ctx")
    part = me % 2
    twin = {"ctx": me + 1 - 2 * part}
    half_rows = msg_ref.shape[1]
    wide = sources * 2 * half_rows
    factor = math.log2(math.e) / math.sqrt(head)
    shrink = 1.0 / math.sqrt(head)
    lane = lane_of((half_rows, LANES))
    greet(me, count)

    def remote(src, dst, send, recv, where):
        return pltpu.make_async_remote_copy(src_ref=src, dst_ref=dst, send_sem=send, recv_sem=recv,
                                            device_id=where, device_id_type=MESH)

    def msg_copy(owner, dest):
        return remote(msg_ref.at[dest], land.at[owner], msend.at[dest], mrecv.at[owner], {"ctx": dest})

    def share_copy(source):
        return remote(away.at[source], near.at[source], fsend.at[source], frecv.at[source], twin)

    def q_copy(owner, dest):
        return remote(tiles.at[dest], arrive_q.at[owner], gsend.at[dest], grecv.at[owner], {"ctx": dest})

    def k_copy(owner, dest):
        return remote(sums.at[dest], arrive_k.at[owner], ksend.at[dest], krecv.at[owner], {"ctx": dest})

    def start_msg(step, _):
        msg_copy(me, lax.rem(me + count - step, count)).start()

    lax.fori_loop(1, count, start_msg, None)
    hosted = hosted_copies(kinds, guests, landings, hsend, hrecv)
    for copy in hosted:
        copy.start()
    land[me] = msg_ref[me]
    whole = lane_of(kv_ref.shape)
    vone_ref[...] = jnp.where(whole < head, jnp.ones_like(kv_ref), kv_ref[...])
    kone_ref[...] = jnp.where(whole < head, kv_ref[...], jnp.ones_like(kv_ref))
    kturn_ref[...] = turned(kv_ref[...])
    dk_ref[...] = jnp.zeros_like(dk_ref)
    dv_ref[...] = jnp.zeros_like(dv_ref)

    def rows_of(source, which):
        return pl.ds(pl.multiple_of(source * rows + which * half_rows, half_rows), half_rows)

    def key_tile(source, which):
        here = rows_of(source, which)
        return jnp.where(lane < head, dk_ref[here] * shrink, dv_ref[here])

    def compute(index):
        base = index * sources
        stack_q, stack_d = [], []
        for source in range(sources):
            @pl.when(base + source != me)
            def _(source=source):
                msg_copy(base + source, me).wait_recv()

            grad = land[base + source].astype(F32)
            spread = grad * out_ref[base + source]
            for which in range(2):
                stack_q.append(aug_ref[base + source, which])
                mine = (lane < head) if which == 0 else (lane >= head)
                delta = jnp.sum(jnp.where(mine, spread, 0.0), axis=1, keepdims=True)
                high, middle, low = three_parts(-delta)
                extra = jnp.where(lane == 0, high, jnp.where(lane == 1, middle, jnp.where(lane == 2, low, 0.0)))
                moved = swap_heads(grad, head) if which == 0 else grad
                stack_d.append(jnp.where(lane < head, extra, moved).astype(BF))
        queries = jnp.concatenate(stack_q, axis=0)
        grads = jnp.concatenate(stack_d, axis=0)
        acc_ref[...] = jnp.zeros_like(acc_ref)

        def visit(step, masked):
            start = pl.multiple_of(step * keys, keys)
            here = pl.ds(start, keys)
            raw = lax.dot_general(kone_ref[here], queries, ONES_NT, preferred_element_type=F32)
            if masked:
                ok = allowed_block(1, 0, (keys, wide), first, second, part, base, start, rows, half_rows)
                prob = jnp.where(ok, jnp.exp2(jnp.where(ok, raw, 0.0) * factor), 0.0)
            else:
                prob = jnp.exp2(raw * factor)
            along = lax.dot_general(vone_ref[here], grads, ONES_NT, preferred_element_type=F32)
            score = (prob * along).astype(BF)
            dv_ref[here] += jnp.dot(prob.astype(BF), grads, preferred_element_type=F32)
            dk_ref[here] += jnp.dot(score, queries, preferred_element_type=F32)
            acc_ref[...] += jnp.dot(kturn_ref[:, here], score, preferred_element_type=F32)

        sweep_keys(visit, index, count * rows - rows, part, base, rows, half_rows, keys, sources)
        acc = acc_ref[...].T
        for source in range(sources):
            place = 2 * source * half_rows
            one = acc[place:place + half_rows]
            two = acc[place + half_rows:place + 2 * half_rows]
            tiles[base + source] = (jnp.where(lane < head, one, swap_heads(two, head)) * shrink).astype(BF)

            @pl.when(base + source != me)
            def _(source=source):
                q_copy(me, base + source).start()

            away[base + source] = key_tile(base + source, 1 - part).astype(BF)
            share_copy(base + source).start()

    def finish(index):
        for source in range(sources):
            block = index * sources + source
            share_copy(block).wait_recv()
            sums[block] = (key_tile(block, part) + near[block].astype(F32)).astype(BF)

            @pl.when(block != me)
            def _(block=block):
                k_copy(me, block).start()

    def sweep(step, _):
        index = count // sources - 1 - step

        @pl.when(index >= 0)
        def _():
            compute(jnp.maximum(index, 0))

        @pl.when(step > 0)
        def _():
            finish(index + 1)

    lax.fori_loop(0, count // sources + 1, sweep, None)
    arrive_q[me] = tiles[me]
    arrive_k[me] = sums[me]

    def drain(other, _):
        share_copy(other).wait_send()

        @pl.when(other != me)
        def _():
            msg_copy(me, other).wait_send()
            q_copy(me, other).wait_send()
            k_copy(me, other).wait_send()
            q_copy(other, me).wait_recv()
            k_copy(other, me).wait_recv()

    lax.fori_loop(0, count, drain, None)
    gotq_ref[...] = arrive_q[...]
    gotk_ref[...] = arrive_k[...]
    for copy in hosted:
        copy.wait()


def exchange_attend(msg, info, head, rows, hosted, collective_id):
    count, half_rows = msg.shape[0], msg.shape[1]
    keys, sources = 512, 2
    group = count * rows
    dma = pltpu.SemaphoreType.DMA((count,))
    S = jax.ShapeDtypeStruct
    tile = (count, half_rows, LANES)
    kinds = [kind for kind, _ in hosted]
    guests = [value for _, value in hosted]
    hdma = pltpu.SemaphoreType.DMA((len(hosted),))
    anywhere = [pl.BlockSpec(memory_space=pl.ANY)] * len(hosted)
    return pl.pallas_call(
        functools.partial(attend_kernel, head, rows, keys, sources, count, kinds),
        out_shape=(S(tile, BF), S(tile, F32), S((count, 2, half_rows, LANES), BF), S((group, LANES), BF),
                   *hosted_shapes(hosted)),
        in_specs=[pl.BlockSpec(memory_space=pltpu.SMEM)] + vmem_specs(1) + anywhere,
        out_specs=tuple(vmem_specs(4) + anywhere),
        scratch_shapes=[pltpu.VMEM((count, half_rows, 2 * LANES), BF), pltpu.VMEM((count, 2, half_rows, LANES), BF),
                        pltpu.VMEM(tile, BF), pltpu.VMEM(tile, BF), pltpu.VMEM((group, LANES), BF),
                        pltpu.VMEM((sources * rows, LANES), F32)] + [dma] * 6 + [hdma] * 2,
        compiler_params=pltpu.CompilerParams(collective_id=collective_id, has_side_effects=True,
                                             vmem_limit_bytes=VMEM_LIMIT),
        cost_estimate=pl.CostEstimate(flops=2 * group * group * LANES, bytes_accessed=6 << 20, transcendentals=0),
        name="attend",
    )(info, msg, *guests)


def exchange_attend_back(msg, info, augmented, attended, all_kv, head, rows, hosted, collective_id):
    count, half_rows = msg.shape[0], msg.shape[1]
    keys, sources = 512, 2
    group = count * rows
    dma = pltpu.SemaphoreType.DMA((count,))
    S = jax.ShapeDtypeStruct
    tile = (count, half_rows, LANES)
    kinds = [kind for kind, _ in hosted]
    guests = [value for _, value in hosted]
    hdma = pltpu.SemaphoreType.DMA((len(hosted),))
    anywhere = [pl.BlockSpec(memory_space=pl.ANY)] * len(hosted)
    long = (group, LANES)
    return pl.pallas_call(
        functools.partial(attend_back_kernel, head, rows, keys, sources, count, kinds),
        out_shape=(S(tile, BF), S(tile, BF), *hosted_shapes(hosted)),
        in_specs=[pl.BlockSpec(memory_space=pltpu.SMEM)] + vmem_specs(4) + anywhere,
        out_specs=tuple(vmem_specs(2) + anywhere),
        scratch_shapes=[pltpu.VMEM(tile, BF)] * 7 + [
            pltpu.VMEM(long, BF), pltpu.VMEM(long, BF), pltpu.VMEM((LANES, group), BF), pltpu.VMEM(long, F32),
            pltpu.VMEM(long, F32), pltpu.VMEM((LANES, sources * rows), F32)] + [dma] * 8 + [hdma] * 2,
        compiler_params=pltpu.CompilerParams(collective_id=collective_id, has_side_effects=True,
                                             vmem_limit_bytes=VMEM_LIMIT),
        cost_estimate=pl.CostEstimate(flops=5 * group * group * LANES, bytes_accessed=8 << 20, transcendentals=0),
        name="attend_back",
    )(info, augmented, attended, all_kv, msg, *guests)


def sum_kernel(jobs, sides, weights, lines, *refs):
    count = len(jobs)
    refs = list(refs)
    take = lambda number: [refs.pop(0) for _ in range(number)]
    lefts, lefts_y, rights = take(sides), take(sides), take(count)
    sent = [refs.pop(0) if job["late"] and job["kind"] == "pair" else None for job in jobs]
    early_y = [None if job["late"] else take(job["parts"]) for job in jobs]
    small_refs = take(len(SMALL_ROWS))
    outs, (small_out,) = take(weights), take(1)
    lefts_s, lefts_ys, rights_s, rights_ys = take(sides), take(sides), take(count), take(count)
    rights_y = [take(1) if job["late"] else early for job, early in zip(jobs, early_y)]
    (lbuf, rbuf, xp, xr, zp, us, ur, ds_, dr, fs, fr, cs, cr, stage, sm_s, sm_r,
     lsem, rsem, xs, xv, uss, urv, dss, drv, fss, frv, css, crv, osem, sms, smv, els, elv, ers, erv, yrs, yrv) = refs
    steps = sum(job["total"] for job in jobs)
    last = steps - 1
    tokens = lbuf.shape[-1] // 4
    me = lax.axis_index("ctx")
    y = lax.axis_index("dp")
    z = me // 4
    x = (me // 2) % 2
    c = me % 2
    top = lines - 1
    twin = {"ctx": me + 1 - 2 * c}
    across_x = {"ctx": me + 2 - 4 * x}
    across_y = {"dp": 1 - y}
    above = {"ctx": jnp.minimum(me + 4, 4 * top + me % 4)}
    below = {"ctx": jnp.maximum(me - 4, me % 4)}
    near = {"ctx": me + 4 - 8 * (z % 2)}
    far = {"ctx": me + 8 - 16 * (z // 2)}
    rounds = [twin, across_x, across_y, near, far]

    for buf in (ur, dr, zp):
        buf[...] = jnp.zeros_like(buf)
    sm_s[0] = jnp.zeros(sm_s.shape[1:], F32)
    for (row, column), ref in zip(SMALL_ROWS, small_refs):
        sm_s[0, row:row + ref.shape[0], column:column + ref.shape[1]] = ref[...]

    barrier = pltpu.get_barrier_semaphore()
    for where in (twin, across_x, across_y, far):
        pl.semaphore_signal(barrier, inc=1, device_id=where, device_id_type=MESH)

    @pl.when(z < top)
    def _():
        pl.semaphore_signal(barrier, inc=1, device_id=above, device_id_type=MESH)

    @pl.when(z > 0)
    def _():
        pl.semaphore_signal(barrier, inc=1, device_id=below, device_id_type=MESH)

    pl.semaphore_wait(barrier, 4 + (z < top).astype(jnp.int32) + (z > 0).astype(jnp.int32))

    def remote(src, dst, send, recv, where):
        return pltpu.make_async_remote_copy(src_ref=src, dst_ref=dst, send_sem=send, recv_sem=recv,
                                            device_id=where, device_id_type=MESH)

    def row_base(number):
        height = lefts_s[number].shape[2]
        return y * height if height < lefts[number].shape[2] else 0

    def column_base(number):
        width = 2 * rights_s[number].shape[1]
        return y * width if jobs[number]["kind"] == "quarter" else 0

    def left_copies(number):
        height = lefts_s[number].shape[2]
        rows = pl.ds(pl.multiple_of(row_base(number), PIECE), height)
        return [
            remote(lefts[number].at[:, :, rows, :], lefts_s[number], els.at[number, 0], elv.at[number, 0], twin),
            remote(lefts_y[number], lefts_ys[number], els.at[number, 1], elv.at[number, 1], twin),
        ]

    def right_own(number):
        width = rights_s[number].shape[1]
        start = pl.multiple_of(column_base(number) + (1 - c) * width, STRIP)
        return remote(rights[number].at[:, pl.ds(start, width)], rights_s[number], ers.at[number, 0],
                      erv.at[number, 0], twin)

    def right_forward(number):
        width = rights_s[number].shape[1]
        columns = pl.ds(pl.multiple_of((1 - c) * width, STRIP), width)
        tall = tokens // len(rights_y[number])
        return [remote(source.at[:, columns], rights_ys[number].at[pl.ds(part * tall, tall)],
                       ers.at[number, 1 + part], erv.at[number, 1 + part], twin)
                for part, source in enumerate(rights_y[number])]

    def right_cross(number, piece=None):
        width = 2 * rights_s[number].shape[1]
        kind = jobs[number]["kind"]
        source = sent[number] if kind == "pair" else rights[number]
        start = (1 - y) * width if kind == "quarter" else 0
        rows, inside = slice(None), 0
        size = width
        if piece is not None:
            rows = pl.ds(pl.multiple_of((piece & 1) * (tokens // 2), PIECE), tokens // 2)
            inside, size = (piece >> 1) * STRIP, STRIP
        place = pl.ds(pl.multiple_of(inside, STRIP), size)
        if piece is None:
            landing = rights_y[number][0]
        else:
            landing = rights_y[number][0].at[rows, place]
        return remote(source.at[rows, pl.ds(pl.multiple_of(start + inside, STRIP), size)], landing,
                      yrs.at[number], yrv.at[number], across_y)

    def x_copy(j):
        s = j & (RING - 1)
        return remote(xp.at[s, 1 - x], xr.at[s], xs.at[s], xv.at[s], across_x)

    def up_copy(j):
        s = j & (RING - 1)
        return remote(us.at[s], ur.at[s], uss.at[s], urv.at[s], above)

    def down_copy(j):
        s = j & (RING - 1)
        return remote(ds_.at[s], dr.at[s], dss.at[s], drv.at[s], below)

    def f_copy(j):
        s = j & (RING - 1)
        return remote(fs.at[s], fr.at[s], fss.at[s], frv.at[s], across_y)

    def c_copy(j):
        s = j & (RING - 1)
        return remote(cs.at[s], cr.at[s], css.at[s], crv.at[s], twin)

    def small_copy(k):
        return remote(sm_s.at[k], sm_r.at[k], sms.at[k], smv.at[k], rounds[k])

    def loads(number):
        job = jobs[number]
        left, s = job["left"], number % 2
        height, width = lefts_s[left].shape[2], rights_s[number].shape[1]
        own_rows = pl.ds(pl.multiple_of(row_base(left), PIECE), height)
        own_columns = pl.ds(pl.multiple_of(column_base(number) + c * width, STRIP), width)
        mine = pl.ds(pl.multiple_of(c * width, STRIP), width)
        copies = []
        for place, source in enumerate([lefts[left].at[:, :, own_rows, :], lefts_s[left], lefts_y[left],
                                        lefts_ys[left]]):
            copies.append(pltpu.make_async_copy(
                source, lbuf.at[s, :, :, pl.ds(0, height), pl.ds(place * tokens, tokens)], lsem.at[s, place]))
        tall = tokens // len(rights_y[number])
        pieces = [(0, rights[number].at[:, own_columns]), (tokens, rights_s[number]), (3 * tokens, rights_ys[number])]
        pieces += [(2 * tokens + part * tall, source.at[:, mine]) for part, source in enumerate(rights_y[number])]
        for place, (start, source) in enumerate(pieces):
            copies.append(pltpu.make_async_copy(
                source, rbuf.at[s, pl.ds(start, source.shape[0]), pl.ds(0, width)], rsem.at[s, place]))
        return copies

    def each_job(j, visit):
        begin = 0
        for number, job in enumerate(jobs):
            @pl.when((j >= begin) & (j < begin + job["total"]))
            def _(number=number, begin=begin):
                visit(number, j - begin)
            begin += job["total"]

    def begins():
        begin = 0
        for number, job in enumerate(jobs):
            yield number, job, begin
            begin += job["total"]

    def out_copies(number, k, j):
        job = jobs[number]
        o = j & (RING - 1)
        row = pl.multiple_of(lax.rem(k, job["subs"]) * PIECE, PIECE)
        column = pl.multiple_of(lax.div(k, job["subs"]) * STRIP, STRIP)
        width = rights_s[number].shape[1]
        copies = []
        for line in range(2):
            for core in range(2):
                out = outs[job["outs"][line if job["kind"] == "pair" else 0]]
                rows, columns = row, core * width + column
                if job["kind"] == "quarter":
                    columns = line * 2 * width + columns
                if job["kind"] == "drop":
                    rows = line * lefts_s[job["left"]].shape[2] + row
                copies.append(pltpu.make_async_copy(
                    stage.at[o, line, core],
                    out.at[pl.ds(pl.multiple_of(rows, PIECE), PIECE), pl.ds(pl.multiple_of(columns, STRIP), STRIP)],
                    osem.at[o, line, core]))
        return copies

    def out_wait(j):
        for copy in out_copies(0, 0, j):
            copy.wait()

    started = []
    for number, job, begin in begins():
        if job["left"] not in started:
            started.append(job["left"])
            for copy in left_copies(job["left"]):
                copy.start()
        right_own(number).start()
        if not job["late"]:
            for copy in right_forward(number):
                copy.start()

    def step(t, _):
        slot = t & (RING - 1)

        for number, job, begin in begins():
            if job["late"]:
                ago = t - job["issue"]
                piece = ago - (ago >> 2)
                pieces = 4 * rights_s[number].shape[1] // STRIP

                @pl.when((ago >= 0) & (ago & 3 != 3) & (piece < pieces))
                def _(number=number, piece=piece):
                    right_cross(number, piece).start()

                @pl.when(t == begin - job["ahead"])
                def _(number=number):
                    right_cross(number).wait()
                    for copy in right_forward(number):
                        copy.start()

        done, before = [], 0
        for number, job, begin in begins():
            fresh = job["left"] not in done
            done.append(job["left"])

            @pl.when(t == max(before, begin - AHEAD))
            def _(number=number, job=job, fresh=fresh):
                if fresh:
                    for copy in left_copies(job["left"]):
                        copy.wait()
                right_own(number).wait()
                for copy in right_forward(number):
                    copy.wait()
                for copy in loads(number):
                    copy.start()

            before = begin

        for number, job, begin in begins():
            @pl.when(t == begin)
            def _(number=number):
                for copy in loads(number):
                    copy.wait()

        for k in range(len(rounds) + 1):
            @pl.when(t == LAG * k)
            def _(k=k):
                if k > 0:
                    small_copy(k - 1).wait()
                    total = sm_s[k - 1] + sm_r[k - 1]
                    if k == len(rounds):
                        small_out[...] = total
                    else:
                        sm_s[k] = total
                if k < len(rounds):
                    small_copy(k).start()

        @pl.when(t < steps)
        def _():
            which, begin_now, subs_now = 0, 0, jobs[0]["subs"]
            for number, job, begin in begins():
                here = t >= begin
                begin_now = jnp.where(here, begin, begin_now)
                subs_now = jnp.where(here, job["subs"], subs_now)
                which = jnp.where(here, number % 2, which)
            row = lax.rem(t - begin_now, subs_now) * PIECE
            column = lax.div(t - begin_now, subs_now) * STRIP
            rows = pl.ds(pl.multiple_of(row, PIECE), PIECE)
            left = lbuf[which, :, :, rows, :].reshape(2 * lines * SUB, 4 * tokens)
            right = rbuf[which, :, pl.ds(pl.multiple_of(column, STRIP), STRIP)]
            got = jnp.dot(left, right, preferred_element_type=F32).astype(BF)
            for line in range(lines):
                for side in range(2):
                    row = (2 * line + side) * SUB
                    xp[slot, side, line] = got[row:row + SUB]
            x_copy(t).start()

        @pl.when((t >= LAG) & (t - LAG <= last))
        def _():
            x_copy(t - LAG).wait()
            s = (t - LAG) & (RING - 1)
            zp[(t - LAG) & (2 * RING - 1)] = xp[s, x] + xr[s]

        ju = t - LAG * (1 + z)

        @pl.when((ju >= 0) & (ju <= last))
        def _():
            s = ju & (RING - 1)
            held = ju & (2 * RING - 1)

            @pl.when(z > 0)
            def _():
                up_copy(ju).wait_recv()
                zp[held, z] = zp[held, z] + ur[s, 0]

            @pl.when(z < top)
            def _():
                @pl.when(ju >= RING)
                def _():
                    up_copy(ju).wait_send()

                for m in range(top):
                    own = zp[held, jnp.minimum(z + 1 + m, top)]
                    if m + 1 < top:
                        own = own + ur[s, m + 1]
                    us[s, m] = own
                up_copy(ju).start()

        jd = t - LAG * (1 + top - z)

        @pl.when((jd >= 0) & (jd <= last))
        def _():
            s = jd & (RING - 1)
            held = jd & (2 * RING - 1)

            @pl.when(z < top)
            def _():
                down_copy(jd).wait_recv()
                zp[held, z] = zp[held, z] + dr[s, 0]

            @pl.when(z > 0)
            def _():
                @pl.when(jd >= RING)
                def _():
                    down_copy(jd).wait_send()

                for m in range(top):
                    own = zp[held, jnp.maximum(z - 1 - m, 0)]
                    if m + 1 < top:
                        own = own + dr[s, m + 1]
                    ds_[s, m] = own
                down_copy(jd).start()

        jf = t - LAG * (1 + top)

        @pl.when((jf >= 0) & (jf <= last))
        def _():
            fs[jf & (RING - 1)] = zp[jf & (2 * RING - 1), z]
            f_copy(jf).start()

        jo = jf - LAG

        @pl.when((jo >= 0) & (jo <= last))
        def _():
            f_copy(jo).wait()
            s = jo & (RING - 1)
            mine = pl.ds(pl.multiple_of(c * PIECE, PIECE), PIECE)
            away = pl.ds(pl.multiple_of((1 - c) * PIECE, PIECE), PIECE)
            cs[s, y] = fs[s, away]
            cs[s, 1 - y] = fr[s, away]
            c_copy(jo).start()
            stage[s, y, c] = fs[s, mine].astype(F32)
            stage[s, 1 - y, c] = fr[s, mine].astype(F32)

        jc = jo - LAG

        @pl.when((jc >= 0) & (jc <= last))
        def _():
            c_copy(jc).wait()
            s = jc & (RING - 1)
            stage[s, 0, 1 - c] = cr[s, 0].astype(F32)
            stage[s, 1, 1 - c] = cr[s, 1].astype(F32)

            def start(number, k):
                for copy in out_copies(number, k, jc):
                    copy.start()

            each_job(jc, start)

            @pl.when(jc >= LAG)
            def _():
                out_wait(jc - LAG)

    lax.fori_loop(0, last + LAG * (top + 3) + 1, step, None)
    for back in range(LAG):
        out_wait(last - back)
    for back in range(RING):
        j = last - back

        @pl.when(z < top)
        def _(j=j):
            up_copy(j).wait_send()

        @pl.when(z > 0)
        def _(j=j):
            down_copy(j).wait_send()


def sum_over_chips(lefts, works, small, lines, collective_id):
    S = jax.ShapeDtypeStruct
    jobs, landing_r, landing_y, outs, sent, early = [], [], [], [], [], []
    shaped = [own.reshape(2 * lines, 2, own.shape[0] // (4 * lines), own.shape[1]) for own, _ in lefts]
    crossed = [cross for _, cross in lefts]
    tokens = shaped[0].shape[-1]
    for work in works:
        job = {name: work[name] for name in ("left", "kind", "late", "issue", "ahead")}
        columns = work["own"].shape[1]
        width = columns // 4 if job["kind"] == "quarter" else columns // 2
        height = crossed[job["left"]].shape[2]
        job["subs"], job["strips"] = height // PIECE, width // STRIP
        job["total"] = job["subs"] * job["strips"]
        job["outs"] = []
        for _ in range(2 if job["kind"] == "pair" else 1):
            job["outs"].append(len(outs))
            outs.append(S((shaped[job["left"]].shape[2], columns), F32))
        landing_r.append(S((tokens, width), BF))
        if job["late"]:
            landing_y.append(S((tokens, 2 * width), BF))
            if job["kind"] == "pair":
                sent.append(work["cross"])
        else:
            job["parts"] = len(work["cross"])
            early.extend(work["cross"])
        jobs.append(job)
    steps = sum(job["total"] for job in jobs)
    flat = (8, small[0].shape[1])
    top = lines - 1
    dma = pltpu.SemaphoreType.DMA
    ring = lambda *shape: pltpu.VMEM((RING,) + shape, BF)
    scratch = [
        pltpu.VMEM((2, 2 * lines, 2, max(value.shape[2] for value in crossed), 4 * tokens), BF),
        pltpu.VMEM((2, 4 * tokens, max(value.shape[1] for value in landing_r)), BF),
        ring(2, lines, SUB, STRIP), ring(lines, SUB, STRIP),
        pltpu.VMEM((2 * RING, lines, SUB, STRIP), BF),
        ring(top, SUB, STRIP), ring(top, SUB, STRIP), ring(top, SUB, STRIP), ring(top, SUB, STRIP),
        ring(SUB, STRIP), ring(SUB, STRIP), ring(2, PIECE, STRIP), ring(2, PIECE, STRIP),
        pltpu.VMEM((RING, 2, 2, PIECE, STRIP), F32),
        pltpu.VMEM((5,) + flat, F32),
        pltpu.VMEM((5,) + flat, F32),
        dma((2, 4)), dma((2, 5)),
    ] + [dma((RING,))] * 10 + [
        dma((RING, 2, 2)), dma((5,)), dma((5,)),
        dma((len(lefts), 2)), dma((len(lefts), 2)), dma((len(works), 3)), dma((len(works), 3)),
        dma((len(works),)), dma((len(works),)),
    ]
    anywhere = pl.BlockSpec(memory_space=pl.ANY)
    inside = pl.BlockSpec(memory_space=pltpu.VMEM)
    landings = [S(value.shape, BF) for value in crossed] * 2 + landing_r * 2 + landing_y
    operands = shaped + crossed + [work["own"] for work in works] + sent + early
    flops = 2 * steps * 2 * lines * SUB * STRIP * 4 * tokens
    got = pl.pallas_call(
        functools.partial(sum_kernel, jobs, len(lefts), len(outs), lines),
        out_shape=tuple(outs) + (S(flat, F32),) + tuple(landings),
        in_specs=[anywhere] * len(operands) + [inside] * len(small),
        out_specs=tuple([anywhere] * len(outs) + [inside] + [anywhere] * len(landings)),
        scratch_shapes=scratch,
        compiler_params=pltpu.CompilerParams(collective_id=collective_id, has_side_effects=True,
                                             vmem_limit_bytes=VMEM_LIMIT),
        cost_estimate=pl.CostEstimate(flops=flops, bytes_accessed=steps * 1_100_000, transcendentals=0),
        name="sum_over_chips",
    )(*operands, *small)
    return got[:len(outs)], got[len(outs)]


def hand_over_kernel(count, head, *refs):
    sources, small_ref, results = refs[:count], refs[count], refs[count + 1:2 * count + 1]
    mix_ref, taps_ref, low_ref, att_ref, top_ref, query_ref, keys_ref = refs[2 * count + 1:2 * count + 8]
    holds, (ins, outs) = refs[2 * count + 8:3 * count + 8], refs[3 * count + 8:]
    arrive = [pltpu.make_async_copy(source, hold, ins.at[number])
              for number, (source, hold) in enumerate(zip(sources, holds))]
    leave = [pltpu.make_async_copy(hold, result, outs.at[number])
             for number, (hold, result) in enumerate(zip(holds, results))]
    for copy in arrive:
        copy.start()
    mix_ref[...] = small_ref[0]
    taps_ref[...] = small_ref[1:4]
    low_ref[...] = small_ref[4]
    att_ref[...] = small_ref[5]
    top_ref[...] = small_ref[6]
    query_ref[...] = small_ref[7, :head] + small_ref[7, head:LANES]
    keys_ref[...] = small_ref[7, LANES:LANES + head] + small_ref[7, LANES + head:2 * LANES]
    for first, then in zip(arrive, leave):
        first.wait()
        then.start()
    for copy in leave:
        copy.wait()


def hand_over(grads, small, head):
    count, width = len(grads), small.shape[1]
    S = jax.ShapeDtypeStruct
    anywhere = [pl.BlockSpec(memory_space=pl.ANY)] * count
    smalls = (S((width,), F32), S((3, width), F32), S((width,), F32), S((width,), F32), S((width,), F32),
              S((head,), F32), S((head,), F32))
    got = pl.pallas_call(
        functools.partial(hand_over_kernel, count, head),
        out_shape=tuple(S(value.shape, F32) for value in grads) + smalls,
        in_specs=anywhere + vmem_specs(1),
        out_specs=tuple(anywhere + vmem_specs(len(smalls))),
        scratch_shapes=[pltpu.VMEM(value.shape, F32) for value in grads] + [pltpu.SemaphoreType.DMA((count,))] * 2,
        compiler_params=pltpu.CompilerParams(vmem_limit_bytes=VMEM_LIMIT),
        name="hand_over",
    )(*grads, small)
    return got[:count], got[count:]


def call_plain(kernel, outs, args, smem=0, scratch=(), flops=0, moved=0, name=None):
    specs = [pl.BlockSpec(memory_space=pltpu.SMEM)] * smem + vmem_specs(len(args) - smem)
    many = isinstance(outs, (tuple, list))
    return pl.pallas_call(
        kernel,
        out_shape=tuple(outs) if many else outs,
        in_specs=specs,
        out_specs=tuple(vmem_specs(len(outs))) if many else vmem_specs(1)[0],
        scratch_shapes=list(scratch),
        compiler_params=pltpu.CompilerParams(vmem_limit_bytes=VMEM_LIMIT),
        cost_estimate=pl.CostEstimate(flops=flops, bytes_accessed=moved, transcendentals=0),
        name=name,
    )(*args)


def shape_of(shape, kind):
    return jax.ShapeDtypeStruct(shape, kind)


def sibling(value):
    count = lax.axis_size("ctx")
    return lax.ppermute(value, "ctx", [(i, i ^ 1) for i in range(count)])


def fast_device(tokens, lengths, cotangent, mixgain, mixentry, mixtaps, mixexit, lowgain, lowgate, lowlift,
                lowdrop, attgain, attquery, attkeys, attvalues, querygain, keysgain, attexit, topgain, topgate,
                toplift, topdrop):
    rows, width = tokens.shape
    head = querygain.shape[0]
    devices = lax.axis_size("ctx")
    lines = devices // 4
    half_rows = rows // 2
    place = lax.axis_index("ctx")
    core = place % 2
    first = lengths[0, 0]
    second = first + lengths[0, 1]
    where = place * rows + jnp.arange(rows + HALO, dtype=jnp.int32)
    begin = jnp.where(where >= second, second, jnp.where(where >= first, first, 0))
    spots = (where - begin).astype(F32)[:, None]
    spot = jnp.arange(LANES, dtype=jnp.int32) % (head // 2)
    angle = spots[:rows] * (THETA ** (-spot.astype(F32) * 2.0 / head))[None, :]
    cosine = jnp.cos(angle)
    sine = jnp.sin(angle) * jnp.where(jnp.arange(LANES) % head < head // 2, -1.0, 1.0)[None, :]

    before = passed_along(tokens[rows - HALO:], "ctx", 1)
    (hidden_one, normed_one_t, gated_t, part_b, part_c, part_x, conved, product) = mix_forward(
        tokens, before, spots, mixgain, mixtaps, mixentry, mixexit)
    gate_after = passed_along(part_c[:HALO], "ctx", -1)
    hidden_two, lownorm_t, gact_low, lact_low, lowinner_t = feed_low(
        hidden_one, lowgain, lowgate, lowlift, lowdrop)

    heads_q, heads_k = attquery.shape[1] // head, attkeys.shape[1] // head
    msg, normed_two_t, query_raw, key_raw = call_plain(
        functools.partial(project_kernel, head),
        (shape_of((devices, half_rows, 2 * LANES), BF), shape_of((width, rows), BF),
         shape_of((rows, attquery.shape[1]), F32), shape_of((rows, attkeys.shape[1]), F32)),
        (hidden_two, attgain, attquery, attkeys, attvalues, cosine, sine, querygain, keysgain),
        flops=2 * rows * width * 2 * width, moved=6 << 20, name="project")
    upright = lambda value: value.reshape(devices // 2, 2, value.shape[0] // devices, rows)
    over_dp = lambda value: lax.ppermute(value, "dp", [(0, 1), (1, 0)])
    msg, gated_y, normed_one_y, cotangent_y, gate_after = lax.optimization_barrier(
        (msg, over_dp(gated_t), over_dp(normed_one_t), over_dp(cotangent), gate_after))
    gated_y, normed_one_y = upright(gated_y), upright(normed_one_y)
    got, attended_f, augmented, all_kv, lowinner_y, lownorm_y = exchange_attend(
        msg, lengths, head, rows, [("rows", upright(lowinner_t)), ("whole", upright(lownorm_t))], 2)
    (output, grad, grad_low3, send, attended_t, topgain_grad, topnorm_t, topinner_t, keep_top, send_top_a,
     send_top_b) = feed_top(
        got, hidden_two, attexit, cotangent, topgain, topgate, toplift, topdrop)
    send, normed_two_y = lax.optimization_barrier((send, over_dp(normed_two_t)))
    normed_two_y = upright(normed_two_y)
    back_q, back_k, topinner_y, topnorm_y, attended_y, grad_low3_y = exchange_attend_back(
        send, lengths, augmented, attended_f, all_kv, head, rows,
        [("rows", upright(topinner_t)), ("whole", upright(topnorm_t)), ("whole", upright(attended_t)),
         ("columns", grad_low3)], 3)
    back_q, send_top_a, send_top_b = lax.optimization_barrier((back_q, send_top_a, send_top_b))
    top_y_one = over_dp(send_top_a)
    rawq_low, keep_kv, send_kv, grad_two, attgain_grad, querygain_grad, keysgain_grad = call_plain(
        functools.partial(project_back_kernel, head),
        (shape_of((rows, attquery.shape[1]), BF), shape_of((rows, attkeys.shape[1]), BF),
         shape_of((rows, attkeys.shape[1]), BF), shape_of((rows, width), F32), shape_of((1, width), F32),
         shape_of((1, LANES), F32), shape_of((1, LANES), F32)),
        (back_q, back_k, hidden_two, attgain, attquery, attkeys, attvalues, cosine, sine, querygain, keysgain,
         query_raw, key_raw, grad),
        flops=1 << 20, moved=1 << 10, name="project_back")
    grad, lowgain_grad, gb_low, grad_low1, keep_low, send_low = feed_low_back(
        grad_two, hidden_one, lowgain, gact_low, lact_low, lowgate, lowlift, lowdrop)
    grad, grad_low1, top_y_one = lax.optimization_barrier((grad, grad_low1, top_y_one))
    after = passed_along(grad_low1[:HALO], "ctx", -1)
    tokens_grad, mixgain_grad, mixtaps_grad, mixed_grad = mix_backward(
        grad, grad_low1, after, gate_after, spots, tokens, mixgain, mixtaps,
        (part_b, part_c, part_x, conved, product), mixentry, mixexit)
    mixgain_grad, tokens_grad, top_y_two = lax.optimization_barrier(
        (mixgain_grad, tokens_grad, over_dp(send_top_b)))

    lefts = [(attended_t, attended_y), (topinner_t, topinner_y), (topnorm_t, topnorm_y), (normed_two_t, normed_two_y),
             (lowinner_t, lowinner_y), (lownorm_t, lownorm_y), (gated_t, gated_y), (normed_one_t, normed_one_y)]

    def work(left, kind, own, cross=None, issue=-1, ahead=12):
        return dict(left=left, kind=kind, own=own, cross=cross, late=issue >= 0, issue=issue, ahead=ahead)

    works = [work(0, "quarter", grad_low3, (grad_low3_y,)), work(1, "drop", cotangent, (cotangent_y,)),
             work(2, "pair", keep_top, (top_y_one, top_y_two)), work(3, "quarter", rawq_low, issue=0),
             work(3, "pair", keep_kv, send_kv, issue=5), work(4, "drop", gb_low, issue=10),
             work(5, "pair", keep_low, send_low, issue=20), work(6, "quarter", grad_low1, issue=68),
             work(7, "quarter", mixed_grad, issue=73)]
    small = (mixgain_grad, mixtaps_grad, lowgain_grad, attgain_grad, topgain_grad, querygain_grad, keysgain_grad)
    grads, small = sum_over_chips(lefts, works, small, lines, 1)
    grads, smalls = hand_over(grads, small, head)
    (attexit_grad, topdrop_grad, topgate_grad, toplift_grad, attquery_grad, attkeys_grad, attvalues_grad, lowdrop_grad,
     lowgate_grad, lowlift_grad, mixexit_grad, mixentry_grad) = grads
    (mixgain_grad, mixtaps_grad, lowgain_grad, attgain_grad, topgain_grad, querygain_grad, keysgain_grad) = smalls
    return (output, tokens_grad, mixgain_grad, mixentry_grad, mixtaps_grad, mixexit_grad, lowgain_grad, lowgate_grad,
            lowlift_grad, lowdrop_grad, attgain_grad, attquery_grad, attkeys_grad, attvalues_grad, querygain_grad,
            keysgain_grad, attexit_grad, topgain_grad, topgate_grad, toplift_grad, topdrop_grad)


def solution(mesh):
    placed = (P(("dp", "ctx"), None), P("dp", None), P(("dp", "ctx"), None)) + (P(),) * 19
    split = {0: P(("dp", "ctx"), None), 1: P(("dp", "ctx"), None)}
    whole = (2, 4, 6, 10, 14, 15, 17)
    outs = tuple(split.get(i, P() if i in whole else P("ctx", None)) for i in range(21))
    small = mesh.shape["ctx"] == 16 and mesh.shape["dp"] == 2
    return jax.shard_map(fast_device if small else per_device, mesh=mesh, in_specs=placed, out_specs=outs,
                         check_vma=False)
```

```python
import functools
import math

import jax
import jax.numpy as jnp
from jax import lax
from jax.experimental import pallas as pl
from jax.experimental.pallas import tpu as pltpu
from jax.sharding import PartitionSpec as P

EPS = 1e-05
THETA = 1000000.0
NEGATIVE = -1e30


def passed_along(value, axis, steps):
    count = lax.axis_size(axis)
    first, last = (max(0, -steps), min(count, count - steps))
    return lax.ppermute(value, axis, [(source, source + steps) for source in range(first, last)])


def passed_along_2(block, axis, distance):
    devices = range(lax.axis_size(axis))
    route = [((i - distance) % len(devices), i) for i in devices]
    return lax.ppermute(block, axis, route)


def root_mean_square_scale(hidden, gain):
    return hidden * lax.rsqrt(jnp.mean(hidden * hidden, axis=-1, keepdims=True) + EPS) * gain


def rotary_embed(value_rows, position_index):
    half = value_rows.shape[-1] // 2
    freq = THETA ** (-jnp.arange(half, dtype=jnp.float32) * 2.0 / value_rows.shape[-1])
    angle = position_index.astype(jnp.float32)[:, None] * freq[None, :]
    cosine = jnp.cos(angle)[:, None, :]
    sine = jnp.sin(angle)[:, None, :]
    front = value_rows[..., :half]
    behind = value_rows[..., half:]
    return jnp.concatenate(
        [front * cosine - behind * sine, behind * cosine + front * sine], axis=-1
    )


def head_prep(raw, gain, position_index, heads):
    shaped = raw.reshape(raw.shape[0], heads, -1)
    return rotary_embed(root_mean_square_scale(shaped, gain), position_index)


def segment_of(where, first, second):
    return (where >= first).astype(jnp.int32) + (where >= second).astype(jnp.int32)


def block_width(count):
    best = 1
    for candidate in range(1, min(count, 1024) + 1):
        if count % candidate == 0:
            best = candidate
    return best


def sweep(carry, count, visit):
    width = block_width(count)
    return lax.fori_loop(
        0, count // width, lambda index, inner: visit(inner, index * width, width), carry
    )


def inner_dot(left, right):
    return lax.dot_general(
        left, right, (((0,), (0,)), ((), ())), preferred_element_type=jnp.float32
    )


def outer_dot(left, right):
    return lax.dot_general(
        left, right, (((1,), (1,)), ((), ())), preferred_element_type=jnp.float32
    )


def scores_of(query_part, key_part, query_where, key_where, query_seg, key_seg, scale):
    raw = (
        jnp.einsum("tkgd,pkd->kgtp", query_part, key_part, preferred_element_type=jnp.float32)
        * scale
    )
    allowed = (query_seg[:, None] == key_seg[None, :]) & (
        query_where[:, None] >= key_where[None, :]
    )
    return (raw, allowed)


def grad_block(
    query_part,
    grad_part,
    logsum_part,
    delta_part,
    key_part,
    value_part,
    query_where,
    key_where,
    query_seg,
    key_seg,
    scale,
):
    raw, allowed = scores_of(
        query_part, key_part, query_where, key_where, query_seg, key_seg, scale
    )
    prob = jnp.where(allowed, jnp.exp(raw - logsum_part[..., None]), 0.0)
    prob_grad = jnp.einsum(
        "tkgd,pkd->kgtp", grad_part, value_part, preferred_element_type=jnp.float32
    )
    score_grad = (prob * (prob_grad - delta_part[..., None])).astype(jnp.bfloat16)
    query_grad = (
        jnp.einsum("kgtp,pkd->tkgd", score_grad, key_part, preferred_element_type=jnp.float32)
        * scale
    )
    key_grad = (
        jnp.einsum("kgtp,tkgd->pkd", score_grad, query_part, preferred_element_type=jnp.float32)
        * scale
    )
    value_grad = jnp.einsum(
        "kgtp,tkgd->pkd", prob.astype(jnp.bfloat16), grad_part, preferred_element_type=jnp.float32
    )
    return (query_grad, key_grad, value_grad)


def conv_local(extended, taps, fits_one, fits_two):
    rows = extended.shape[0] - 2
    return (
        taps[2] * extended[2:]
        + taps[1] * extended[1 : rows + 1] * fits_one
        + taps[0] * extended[:rows] * fits_two
    )


def feed_forward(hidden, gain, gate_weight, lift_weight, drop_weight):
    fnormed = root_mean_square_scale(hidden, gain).astype(jnp.bfloat16)
    gate_act = jnp.dot(fnormed, gate_weight, preferred_element_type=jnp.float32)
    lift_act = jnp.dot(fnormed, lift_weight, preferred_element_type=jnp.float32)
    inner = (jax.nn.silu(gate_act) * lift_act).astype(jnp.bfloat16)
    result = hidden + jnp.dot(inner, drop_weight, preferred_element_type=jnp.float32)
    return (result, (fnormed, gate_act, lift_act, inner))


def feed_back(grad, hidden, gain, kept, gate_weight, lift_weight, drop_weight):
    fnormed, gate_act, lift_act, inner = kept
    grad_low = grad.astype(jnp.bfloat16)
    drop_grad = inner_dot(inner, grad_low)
    inner_grad = outer_dot(grad_low, drop_weight)
    _, pull_gate = jax.vjp(
        lambda gate_in, lift_in: jax.nn.silu(gate_in) * lift_in, gate_act, lift_act
    )
    gate_grad, lift_grad = pull_gate(inner_grad)
    gate_low = gate_grad.astype(jnp.bfloat16)
    lift_low = lift_grad.astype(jnp.bfloat16)
    gate_wgrad = inner_dot(fnormed, gate_low)
    lift_wgrad = inner_dot(fnormed, lift_low)
    normed_grad = outer_dot(gate_low, gate_weight) + outer_dot(lift_low, lift_weight)
    _, pull_norm = jax.vjp(root_mean_square_scale, hidden, gain)
    hidden_grad, gain_grad = pull_norm(normed_grad)
    return (grad + hidden_grad, (gain_grad, gate_wgrad, lift_wgrad, drop_grad))


def per_device(
    tokens,
    lengths,
    cotangent,
    mixgain,
    mixentry,
    mixtaps,
    mixexit,
    lowgain,
    lowgate,
    lowlift,
    lowdrop,
    attgain,
    attquery,
    attkeys,
    attvalues,
    querygain,
    keysgain,
    attexit,
    topgain,
    topgate,
    toplift,
    topdrop,
):
    rows = tokens.shape[0]
    width_model = tokens.shape[1]
    head_size = querygain.shape[0]
    query_heads = attquery.shape[1] // head_size
    kv_heads = attkeys.shape[1] // head_size
    shared_gradient = query_heads // kv_heads
    scale = 1.0 / math.sqrt(head_size)
    place = lax.axis_index("ctx")
    first = lengths[0, 0]
    second = first + lengths[0, 1]
    mine = place * rows + jnp.arange(rows, dtype=jnp.int32)
    my_seg = segment_of(mine, first, second)
    begin = jnp.where(my_seg == 0, 0, jnp.where(my_seg == 1, first, second))
    position_index = mine - begin
    last_row = place * rows + rows - 1
    mixgain_f = mixgain.astype(jnp.float32)
    taps_f = mixtaps.astype(jnp.float32)
    lowgain_f = lowgain.astype(jnp.float32)
    attgain_f = attgain.astype(jnp.float32)
    querygain_f = querygain.astype(jnp.float32)
    keysgain_f = keysgain.astype(jnp.float32)
    topgain_f = topgain.astype(jnp.float32)
    hidden = tokens.astype(jnp.float32)
    normed_one = root_mean_square_scale(hidden, mixgain_f).astype(jnp.bfloat16)
    mixed = jnp.dot(normed_one, mixentry, preferred_element_type=jnp.float32)
    part_b = mixed[:, :width_model]
    part_c = mixed[:, width_model : 2 * width_model]
    part_x = mixed[:, 2 * width_model :]
    product = (part_b * part_x).astype(jnp.bfloat16)
    borrowed = passed_along(product[rows - 2 :], "ctx", 1)
    extended = jnp.concatenate([borrowed, product], axis=0).astype(jnp.float32)
    fits_one = ((mine >= 1) & (segment_of(mine - 1, first, second) == my_seg)).astype(jnp.float32)[
        :, None
    ]
    fits_two = ((mine >= 2) & (segment_of(mine - 2, first, second) == my_seg)).astype(jnp.float32)[
        :, None
    ]
    conved = conv_local(extended, taps_f, fits_one, fits_two)
    gated = (part_c * conved).astype(jnp.bfloat16)
    hidden_one = hidden + jnp.dot(gated, mixexit, preferred_element_type=jnp.float32)
    hidden_two, kept_low = feed_forward(hidden_one, lowgain_f, lowgate, lowlift, lowdrop)
    normed_two = root_mean_square_scale(hidden_two, attgain_f).astype(jnp.bfloat16)
    query_unrotated = jnp.dot(normed_two, attquery, preferred_element_type=jnp.float32)
    key_unrotated = jnp.dot(normed_two, attkeys, preferred_element_type=jnp.float32)
    value_projected = jnp.dot(normed_two, attvalues, preferred_element_type=jnp.float32)
    query_low = head_prep(query_unrotated, querygain_f, position_index, query_heads).astype(
        jnp.bfloat16
    )
    key_low = head_prep(key_unrotated, keysgain_f, position_index, kv_heads).astype(jnp.bfloat16)
    value_low = value_projected.astype(jnp.bfloat16).reshape(rows, kv_heads, head_size)
    query_grouped = query_low.reshape(rows, kv_heads, shared_gradient, head_size)

    def stat_visit(carry, keys_in, start, offset, width):
        top, total = carry
        key_part = lax.dynamic_slice_in_dim(keys_in, offset, width, 0)
        key_where = start + offset + jnp.arange(width, dtype=jnp.int32)
        raw, allowed = scores_of(
            query_grouped,
            key_part,
            mine,
            key_where,
            my_seg,
            segment_of(key_where, first, second),
            scale,
        )
        new_top = jnp.maximum(top, jnp.max(jnp.where(allowed, raw, NEGATIVE), axis=-1))
        weights = jnp.where(allowed, jnp.exp(raw - new_top[..., None]), 0.0)
        total = total * jnp.exp(top - new_top) + jnp.sum(weights, axis=-1)
        return (new_top, total)

    stat_state = (
        jnp.full((kv_heads, shared_gradient, rows), NEGATIVE, jnp.float32),
        jnp.zeros((kv_heads, shared_gradient, rows), jnp.float32),
    )
    piece = lax.all_gather(key_low, "ctx", axis=0, tiled=True)
    start = jnp.int32(0)
    count = piece.shape[0]

    def stat_running(inner):
        return sweep(
            inner, count, lambda acc, offset, width: stat_visit(acc, piece, start, offset, width)
        )

    top, total = lax.cond(start > last_row, lambda inner: inner, stat_running, stat_state)
    logsum = top + jnp.log(total)

    def forward_visit(accum, keys_in, values_in, start, offset, width):
        key_part = lax.dynamic_slice_in_dim(keys_in, offset, width, 0)
        value_part = lax.dynamic_slice_in_dim(values_in, offset, width, 0)
        key_where = start + offset + jnp.arange(width, dtype=jnp.int32)
        raw, allowed = scores_of(
            query_grouped,
            key_part,
            mine,
            key_where,
            my_seg,
            segment_of(key_where, first, second),
            scale,
        )
        prob_low = jnp.where(allowed, jnp.exp(raw - logsum[..., None]), 0.0).astype(jnp.bfloat16)
        return accum + jnp.einsum(
            "kgtp,pkd->kgtd", prob_low, value_part, preferred_element_type=jnp.float32
        )

    forward_start = jnp.int32(0)
    keys_in = lax.all_gather(key_low, "ctx", axis=0, tiled=True)
    values_in = lax.all_gather(value_low, "ctx", axis=0, tiled=True)
    forward_count = keys_in.shape[0]

    def forward_running(inner):
        return sweep(
            inner,
            forward_count,
            lambda acc, offset, width: forward_visit(
                acc, keys_in, values_in, forward_start, offset, width
            ),
        )

    accum = lax.cond(
        forward_start > last_row,
        lambda inner: inner,
        forward_running,
        jnp.zeros((kv_heads, shared_gradient, rows, head_size), jnp.float32),
    )
    attended = accum.transpose(2, 0, 1, 3).reshape(rows, -1)
    attended_low = attended.astype(jnp.bfloat16)
    hidden_three = hidden_two + jnp.dot(attended_low, attexit, preferred_element_type=jnp.float32)
    output, kept_top = feed_forward(hidden_three, topgain_f, topgate, toplift, topdrop)
    grad = cotangent.astype(jnp.float32)
    grad, top_grads = feed_back(grad, hidden_three, topgain_f, kept_top, topgate, toplift, topdrop)
    grad_low = grad.astype(jnp.bfloat16)
    attexit_grad = inner_dot(attended_low, grad_low)
    out_grads = (
        outer_dot(grad_low, attexit)
        .astype(jnp.bfloat16)
        .reshape(rows, kv_heads, shared_gradient, head_size)
    )
    delta = jnp.einsum(
        "tkgd,tkgd->kgt",
        out_grads.astype(jnp.float32),
        attended.reshape(rows, kv_heads, shared_gradient, head_size),
    )
    cycle_size = lax.axis_size("ctx")

    def cycle_visit(state, keys_in, values_in, start, offset, width):
        query_acc, key_acc, value_acc = state
        key_part = lax.dynamic_slice_in_dim(keys_in, offset, width, 0)
        value_part = lax.dynamic_slice_in_dim(values_in, offset, width, 0)
        key_where = start + offset + jnp.arange(width, dtype=jnp.int32)
        query_grad, key_grad, value_grad = grad_block(
            query_grouped,
            out_grads,
            logsum,
            delta,
            key_part,
            value_part,
            mine,
            key_where,
            my_seg,
            segment_of(key_where, first, second),
            scale,
        )
        key_acc = lax.dynamic_update_slice_in_dim(
            key_acc, lax.dynamic_slice_in_dim(key_acc, offset, width, 0) + key_grad, offset, 0
        )
        value_acc = lax.dynamic_update_slice_in_dim(
            value_acc, lax.dynamic_slice_in_dim(value_acc, offset, width, 0) + value_grad, offset, 0
        )
        return (query_acc + query_grad, key_acc, value_acc)

    def cycle_step(step, carry):
        keys_cur, values_cur, key_acc, value_acc, query_acc = carry
        anchor = (place - step + cycle_size) % cycle_size
        start = anchor * rows

        def cycle_running(state):
            return sweep(
                state,
                rows,
                lambda acc, offset, width: cycle_visit(
                    acc, keys_cur, values_cur, start, offset, width
                ),
            )

        query_acc, key_acc, value_acc = lax.cond(
            start > last_row, lambda state: state, cycle_running, (query_acc, key_acc, value_acc)
        )
        keys_cur, values_cur = passed_along((keys_cur, values_cur), "ctx", 1)
        key_acc, value_acc = (
            passed_along_2(key_acc.astype(jnp.bfloat16), "ctx", 1).astype(key_acc.dtype),
            passed_along_2(value_acc.astype(jnp.bfloat16), "ctx", 1).astype(value_acc.dtype),
        )
        return (keys_cur, values_cur, key_acc, value_acc, query_acc)

    cycle_state = (
        key_low,
        value_low,
        jnp.zeros((rows, kv_heads, head_size), jnp.float32),
        jnp.zeros((rows, kv_heads, head_size), jnp.float32),
        jnp.zeros((rows, kv_heads, shared_gradient, head_size), jnp.float32),
    )
    _, _, key_grads, value_grads, query_acc = lax.fori_loop(0, cycle_size, cycle_step, cycle_state)
    _, pull_query = jax.vjp(
        lambda raw, gain: head_prep(raw, gain, position_index, query_heads),
        query_unrotated,
        querygain_f,
    )
    query_raw_grad, querygain_grad = pull_query(query_acc.reshape(rows, query_heads, head_size))
    _, pull_key = jax.vjp(
        lambda raw, gain: head_prep(raw, gain, position_index, kv_heads), key_unrotated, keysgain_f
    )
    key_raw_grad, keysgain_grad = pull_key(key_grads)
    query_raw_low = query_raw_grad.astype(jnp.bfloat16)
    key_raw_low = key_raw_grad.astype(jnp.bfloat16)
    value_raw_low = value_grads.reshape(rows, -1).astype(jnp.bfloat16)
    attquery_grad = inner_dot(normed_two, query_raw_low)
    attkeys_grad = inner_dot(normed_two, key_raw_low)
    attvalues_grad = inner_dot(normed_two, value_raw_low)
    normed_two_grad = (
        outer_dot(query_raw_low, attquery)
        + outer_dot(key_raw_low, attkeys)
        + outer_dot(value_raw_low, attvalues)
    )
    _, pull_att = jax.vjp(root_mean_square_scale, hidden_two, attgain_f)
    hidden_two_grad, attgain_grad = pull_att(normed_two_grad)
    grad = grad + hidden_two_grad
    grad, low_grads = feed_back(grad, hidden_one, lowgain_f, kept_low, lowgate, lowlift, lowdrop)
    grad_low = grad.astype(jnp.bfloat16)
    mixexit_grad = inner_dot(gated, grad_low)
    gated_grad = outer_dot(grad_low, mixexit)
    part_c_grad = gated_grad * conved
    conved_grad = gated_grad * part_c
    _, pull_conv = jax.vjp(
        lambda ext, taps: conv_local(ext, taps, fits_one, fits_two), extended, taps_f
    )
    extended_grad, mixtaps_grad = pull_conv(conved_grad)
    returned_rim = passed_along(extended_grad[:2], "ctx", -1)
    product_grad = extended_grad[2:].at[rows - 2 :].add(returned_rim)
    mixed_grad = jnp.concatenate(
        [product_grad * part_x, part_c_grad, product_grad * part_b], axis=1
    ).astype(jnp.bfloat16)
    mixentry_grad = inner_dot(normed_one, mixed_grad)
    normed_one_grad = outer_dot(mixed_grad, mixentry)
    _, pull_mix = jax.vjp(root_mean_square_scale, hidden, mixgain_f)
    hidden_grad, mixgain_grad = pull_mix(normed_one_grad)
    tokens_grad = grad + hidden_grad
    lowgain_grad, lowgate_grad, lowlift_grad, lowdrop_grad = low_grads
    topgain_grad, topgate_grad, toplift_grad, topdrop_grad = top_grads
    shares = (
        lax.psum_scatter(mixentry_grad, "ctx", scatter_dimension=0, tiled=True),
        lax.psum_scatter(mixexit_grad, "ctx", scatter_dimension=0, tiled=True),
        lax.psum_scatter(lowgate_grad, "ctx", scatter_dimension=0, tiled=True),
        lax.psum_scatter(lowlift_grad, "ctx", scatter_dimension=0, tiled=True),
        lax.psum_scatter(lowdrop_grad, "ctx", scatter_dimension=0, tiled=True),
        lax.psum_scatter(attquery_grad, "ctx", scatter_dimension=0, tiled=True),
        lax.psum_scatter(attkeys_grad, "ctx", scatter_dimension=0, tiled=True),
        lax.psum_scatter(attvalues_grad, "ctx", scatter_dimension=0, tiled=True),
        lax.psum_scatter(attexit_grad, "ctx", scatter_dimension=0, tiled=True),
        lax.psum_scatter(topgate_grad, "ctx", scatter_dimension=0, tiled=True),
        lax.psum_scatter(toplift_grad, "ctx", scatter_dimension=0, tiled=True),
        lax.psum_scatter(topdrop_grad, "ctx", scatter_dimension=0, tiled=True),
    )
    smalls = lax.psum(
        (
            mixgain_grad,
            mixtaps_grad,
            lowgain_grad,
            attgain_grad,
            querygain_grad,
            keysgain_grad,
            topgain_grad,
        ),
        "ctx",
    )
    summed = (
        lax.psum(shares[0].astype(jnp.bfloat16), "dp").astype(jnp.float32),
        lax.psum(shares[1].astype(jnp.bfloat16), "dp").astype(jnp.float32),
        lax.psum(shares[2].astype(jnp.bfloat16), "dp").astype(jnp.float32),
        lax.psum(shares[3].astype(jnp.bfloat16), "dp").astype(jnp.float32),
        lax.psum(shares[4].astype(jnp.bfloat16), "dp").astype(jnp.float32),
        lax.psum(shares[5].astype(jnp.bfloat16), "dp").astype(jnp.float32),
        lax.psum(shares[6].astype(jnp.bfloat16), "dp").astype(jnp.float32),
        lax.psum(shares[7].astype(jnp.bfloat16), "dp").astype(jnp.float32),
        lax.psum(shares[8].astype(jnp.bfloat16), "dp").astype(jnp.float32),
        lax.psum(shares[9].astype(jnp.bfloat16), "dp").astype(jnp.float32),
        lax.psum(shares[10].astype(jnp.bfloat16), "dp").astype(jnp.float32),
        lax.psum(shares[11].astype(jnp.bfloat16), "dp").astype(jnp.float32),
        lax.psum(smalls[0].astype(jnp.bfloat16), "dp").astype(jnp.float32),
        lax.psum(smalls[1].astype(jnp.bfloat16), "dp").astype(jnp.float32),
        lax.psum(smalls[2].astype(jnp.bfloat16), "dp").astype(jnp.float32),
        lax.psum(smalls[3].astype(jnp.bfloat16), "dp").astype(jnp.float32),
        lax.psum(smalls[4].astype(jnp.bfloat16), "dp").astype(jnp.float32),
        lax.psum(smalls[5].astype(jnp.bfloat16), "dp").astype(jnp.float32),
        lax.psum(smalls[6].astype(jnp.bfloat16), "dp").astype(jnp.float32),
    )
    return (
        output,
        tokens_grad,
        summed[12],
        summed[0],
        summed[13],
        summed[1],
        summed[14],
        summed[2],
        summed[3],
        summed[4],
        summed[15],
        summed[5],
        summed[6],
        summed[7],
        summed[16],
        summed[17],
        summed[8],
        summed[18],
        summed[9],
        summed[10],
        summed[11],
    )


LANES = 128
BF = jnp.bfloat16
F32 = jnp.float32
ONES_NT = (((1,), (1,)), ((), ()))
ONES_TN = (((0,), (0,)), ((), ()))
VMEM_LIMIT = 60 * 1024 * 1024
PIECE = 16
SUB = 2 * PIECE
STRIP = 256
RING = 16
LAG = 4
LINE_LAG = 4
CORE_LAG = 1
AHEAD = 8
LINE_FIRST = 6
SMALL_ROWS = ((0, 0), (1, 0), (4, 0), (5, 0), (6, 0), (7, 0), (7, LANES))


def vmem_specs(count):
    return [pl.BlockSpec(memory_space=pltpu.VMEM)] * count


def lane_of(shape):
    return lax.broadcasted_iota(jnp.int32, shape, len(shape) - 1)


def row_of(ref):
    return ref[...].astype(F32).reshape(1, ref.shape[0])


def same_head(head):
    row = lax.broadcasted_iota(jnp.int32, (LANES, LANES), 0) // head
    column = lax.broadcasted_iota(jnp.int32, (LANES, LANES), 1) // head
    return jnp.where(row == column, 1.0 / head, 0.0).astype(BF)


def head_mean(value, blocks):
    high = value.astype(BF)
    low = (value - high.astype(F32)).astype(BF)
    return (jnp.dot(high, blocks, preferred_element_type=F32) + jnp.dot(low, blocks, preferred_element_type=F32))


def twice(ref):
    row = row_of(ref)
    return jnp.concatenate([row, row], axis=1)


def other_half(value, head):
    lane = lane_of(value.shape)
    ahead = pltpu.roll(value, LANES - head // 2, 1)
    behind = pltpu.roll(value, head // 2, 1)
    return jnp.where(lane % head < head // 2, ahead, behind)


def swap_heads(value, head):
    return pltpu.roll(value, head, 1)


def three_parts(value):
    high = value.astype(BF)
    rest = value - high.astype(F32)
    middle = rest.astype(BF)
    low = (rest - middle.astype(F32)).astype(BF)
    return high.astype(F32), middle.astype(F32), low.astype(F32)


def project_kernel(head, hid_ref, gain_ref, wq_ref, wk_ref, wv_ref, cos_ref, sin_ref, qg_ref, kg_ref,
                   msg_ref, normt_ref, qraw_ref, kraw_ref):
    hid = hid_ref[...]
    scale = lax.rsqrt(jnp.mean(hid * hid, axis=-1, keepdims=True) + EPS)
    normed = hid * scale * row_of(gain_ref)
    normt_ref[...] = turned(normed)
    normed = normed.astype(BF)
    blocks = same_head(head)
    query_gain, keys_gain = twice(qg_ref), twice(kg_ref)
    cosine, sine = cos_ref[...], sin_ref[...]
    half_rows = msg_ref.shape[1]
    lane = lane_of(cosine.shape)

    def prepared(raw, gain):
        unit = raw * lax.rsqrt(head_mean(raw * raw, blocks) + EPS) * gain
        return unit * cosine + other_half(unit, head) * sine

    def put(dest, start, tile):
        low = tile.astype(BF)
        for part in range(2):
            msg_ref[2 * dest + part, :, start:start + LANES] = low[part * half_rows:(part + 1) * half_rows]

    qraw = jnp.dot(normed, wq_ref[...], preferred_element_type=F32)
    qraw_ref[...] = qraw
    for tile in range(qraw.shape[1] // LANES):
        put(tile, 0, prepared(qraw[:, tile * LANES:(tile + 1) * LANES], query_gain))
    kraw = jnp.dot(normed, wk_ref[...], preferred_element_type=F32)
    kraw_ref[...] = kraw
    vraw = jnp.dot(normed, wv_ref[...], preferred_element_type=F32)
    for tile in range(kraw.shape[1] // LANES):
        keys = prepared(kraw[:, tile * LANES:(tile + 1) * LANES], keys_gain)
        values = vraw[:, tile * LANES:(tile + 1) * LANES]
        put(2 * tile, LANES, jnp.where(lane < head, keys, swap_heads(values, head)))
        put(2 * tile + 1, LANES, jnp.where(lane < head, swap_heads(keys, head), values))


def project_back_kernel(head, backq_ref, backk_ref, hid_ref, gain_ref, wq_ref, wk_ref, wv_ref, cos_ref, sin_ref, qg_ref,
                        kg_ref, qraw_ref, kraw_ref, grad_ref,
                        rawq_ref, keep_ref, send_ref, two_ref, again_ref, qgain_ref, kgain_ref):
    query_gain, keys_gain = twice(qg_ref), twice(kg_ref)
    blocks = same_head(head)
    cosine, sine = cos_ref[...], sin_ref[...]
    lane = lane_of(cosine.shape)

    def fetch(source, dest):
        return jnp.concatenate([source[2 * dest], source[2 * dest + 1]], axis=0).astype(F32)

    def through(grad, raw, gain):
        scale = lax.rsqrt(head_mean(raw * raw, blocks) + EPS)
        unit = raw * scale
        turned = grad * cosine - other_half(grad, head) * sine
        gain_part = jnp.sum(turned * unit, axis=0, keepdims=True)
        inward = turned * gain
        return scale * (inward - unit * head_mean(inward * unit, blocks)), gain_part

    width_q = wq_ref.shape[1]
    width_k = wk_ref.shape[1]
    gain_total = jnp.zeros((1, LANES), F32)
    for tile in range(width_q // LANES):
        got, part = through(fetch(backq_ref, tile), qraw_ref[:, tile * LANES:(tile + 1) * LANES], query_gain)
        gain_total = gain_total + part
        rawq_ref[:, tile * LANES:(tile + 1) * LANES] = got.astype(BF)
    qgain_ref[...] = gain_total
    gain_total = jnp.zeros((1, LANES), F32)
    key_tiles, value_tiles = [], []
    for tile in range(width_k // LANES):
        even, odd = fetch(backk_ref, 2 * tile), fetch(backk_ref, 2 * tile + 1)
        keys = jnp.where(lane < head, even, swap_heads(odd, head))
        values = jnp.where(lane < head, swap_heads(even, head), odd)
        got, part = through(keys, kraw_ref[:, tile * LANES:(tile + 1) * LANES], keys_gain)
        gain_total = gain_total + part
        key_tiles.append(got.astype(BF))
        value_tiles.append(values.astype(BF))
    kgain_ref[...] = gain_total
    keys, values = jnp.concatenate(key_tiles, axis=1), jnp.concatenate(value_tiles, axis=1)
    keep_ref[...], send_ref[...] = kept_first(keys, values)
    normed_grad = nt_dot(rawq_ref[...], wq_ref[...]) + nt_dot(keys, wk_ref[...]) + nt_dot(values, wv_ref[...])
    hid = hid_ref[...]
    scale = lax.rsqrt(jnp.mean(hid * hid, axis=-1, keepdims=True) + EPS)
    unit = hid * scale
    again_ref[...] = jnp.sum(normed_grad * unit, axis=0, keepdims=True)
    inward = normed_grad * row_of(gain_ref)
    two_ref[...] = grad_ref[...] + scale * (inward - unit * jnp.mean(inward * unit, axis=-1, keepdims=True))


def allowed_block(row_axis, key_axis, shape, first, second, part, base, start, rows, half_rows):
    row = lax.broadcasted_iota(jnp.int32, shape, row_axis)
    token = (base + row // (2 * half_rows)) * rows + part * half_rows + row % half_rows
    key = start + lax.broadcasted_iota(jnp.int32, shape, key_axis)
    begin = jnp.where(token >= second, second, jnp.where(token >= first, first, 0))
    return (key >= begin) & (key <= token)


MESH = pl.DeviceIdType.MESH


def turned(value):
    return value.astype(F32).T.astype(BF)


def norm_scale(hidden):
    return lax.rsqrt(jnp.mean(hidden * hidden, axis=-1, keepdims=True) + EPS)


def norm_pull(normed_grad, hidden, gain):
    scale = norm_scale(hidden)
    unit = hidden * scale
    inward = normed_grad * gain
    back = scale * (inward - unit * jnp.mean(inward * unit, axis=-1, keepdims=True))
    return back, jnp.sum(normed_grad * unit, axis=0, keepdims=True)


def kept_first(one, two):
    first = lax.axis_index("dp") == 0
    return jnp.where(first, one, two), jnp.where(first, two, one)


def nt_dot(left, right):
    return lax.dot_general(left, right, ONES_NT, preferred_element_type=F32)


def nn_dot(left, right):
    return jnp.dot(left, right, preferred_element_type=F32)


def activation_pull(gate_act, lift_act, sigma, inner_grad):
    gate_grad = inner_grad * lift_act * sigma * (1 + gate_act * (1 - sigma))
    return gate_grad.astype(BF), (inner_grad * gate_act * sigma).astype(BF)


def low_kernel(hid_ref, gain_ref, gate_ref, lift_ref, drop_ref,
               out_ref, normt_ref, gact_ref, lact_ref, innert_ref, norm_ref):
    step = pl.program_id(0)

    @pl.when(step == 0)
    def _():
        hid = hid_ref[...]
        normed = hid * norm_scale(hid) * row_of(gain_ref)
        norm_ref[...] = normed.astype(BF)
        normt_ref[...] = turned(normed)
        out_ref[...] = hid

    normed = norm_ref[...]
    gate_act = nn_dot(normed, gate_ref[...])
    lift_act = nn_dot(normed, lift_ref[...])
    inner = gate_act * jax.nn.sigmoid(gate_act) * lift_act
    gact_ref[...] = gate_act.astype(BF)
    lact_ref[...] = lift_act.astype(BF)
    innert_ref[...] = turned(inner)
    out_ref[...] += nn_dot(inner.astype(BF), drop_ref[...])


def low_back_kernel(grad_ref, hid_ref, gain_ref, gact_ref, lact_ref, gate_ref, lift_ref, drop_ref,
                    out_ref, again_ref, low_ref, outlow_ref, glow_ref, llow_ref, acc_ref):
    step = pl.program_id(0)

    @pl.when(step == 0)
    def _():
        low_ref[...] = grad_ref[...].astype(BF)
        acc_ref[...] = jnp.zeros_like(acc_ref)

    gate_act, lift_act = gact_ref[...].astype(F32), lact_ref[...].astype(F32)
    inner_grad = nt_dot(low_ref[...], drop_ref[...])
    gate_low, lift_low = activation_pull(gate_act, lift_act, jax.nn.sigmoid(gate_act), inner_grad)
    glow_ref[...], llow_ref[...] = kept_first(gate_low, lift_low)
    acc_ref[...] += nt_dot(gate_low, gate_ref[...]) + nt_dot(lift_low, lift_ref[...])

    @pl.when(step == pl.num_programs(0) - 1)
    def _():
        back, gain_part = norm_pull(acc_ref[...], hid_ref[...], row_of(gain_ref))
        again_ref[...] = gain_part
        out = grad_ref[...] + back
        out_ref[...] = out
        outlow_ref[...] = out.astype(BF)


def top_kernel(got_ref, two_ref, exit_ref, cot_ref, gain_ref, gate_ref, lift_ref, drop_ref,
               out_ref, grad_ref, gradlow_ref, send_ref, attt_ref, again_ref, normt_ref, innert_ref, keep_ref,
               senda_ref, sendb_ref, hid_ref, norm_ref, acc_ref):
    step = pl.program_id(0)
    half_rows = got_ref.shape[1]

    @pl.when(step == 0)
    def _():
        tiles = []
        for tile in range(got_ref.shape[0] // 2):
            tiles.append(jnp.concatenate([got_ref[2 * tile], got_ref[2 * tile + 1]], axis=0))
        attended = jnp.concatenate(tiles, axis=1)
        attt_ref[...] = turned(attended)
        hid = two_ref[...] + nn_dot(attended, exit_ref[...])
        hid_ref[...] = hid
        normed = hid * norm_scale(hid) * row_of(gain_ref)
        norm_ref[...] = normed.astype(BF)
        normt_ref[...] = turned(normed)
        out_ref[...] = hid
        acc_ref[...] = jnp.zeros_like(acc_ref)

    normed = norm_ref[...]
    gate_act = nn_dot(normed, gate_ref[...])
    lift_act = nn_dot(normed, lift_ref[...])
    sigma = jax.nn.sigmoid(gate_act)
    inner = gate_act * sigma * lift_act
    innert_ref[...] = turned(inner)
    out_ref[...] += nn_dot(inner.astype(BF), drop_ref[...])
    inner_grad = nt_dot(cot_ref[...], drop_ref[...])
    gate_low, lift_low = activation_pull(gate_act, lift_act, sigma, inner_grad)
    keep_ref[...], sent_part = kept_first(gate_low, lift_low)
    senda_ref[...], sendb_ref[...] = sent_part[:half_rows], sent_part[half_rows:]
    acc_ref[...] += nt_dot(gate_low, gate_ref[...]) + nt_dot(lift_low, lift_ref[...])

    @pl.when(step == pl.num_programs(0) - 1)
    def _():
        back, gain_part = norm_pull(acc_ref[...], hid_ref[...], row_of(gain_ref))
        again_ref[...] = gain_part
        grad = cot_ref[...].astype(F32) + back
        grad_ref[...] = grad
        low = grad.astype(BF)
        gradlow_ref[...] = low
        sent = nt_dot(low, exit_ref[...]).astype(BF)
        for tile in range(send_ref.shape[0] // 2):
            for part in range(2):
                send_ref[2 * tile + part] = sent[part * half_rows:(part + 1) * half_rows,
                                                 tile * LANES:(tile + 1) * LANES]


TILE = 512
WIDE_TILE = 1152


def whole_block(shape):
    return pl.BlockSpec(shape, lambda step, rank=len(shape): (0,) * rank)


def column_block(rows, tile=TILE):
    return pl.BlockSpec((rows, tile), lambda step: (0, step))


def row_block(columns, tile=TILE):
    return pl.BlockSpec((tile, columns), lambda step: (step, 0))


def call_tiled(kernel, tiles, ins, outs, scratch, flops, moved, name):
    return pl.pallas_call(
        kernel,
        grid=(tiles,),
        in_specs=[spec for _, spec in ins],
        out_specs=tuple(spec for _, spec in outs),
        out_shape=tuple(shape for shape, _ in outs),
        scratch_shapes=scratch,
        compiler_params=pltpu.CompilerParams(vmem_limit_bytes=VMEM_LIMIT, dimension_semantics=("arbitrary",)),
        cost_estimate=pl.CostEstimate(flops=flops, bytes_accessed=moved, transcendentals=0),
        name=name,
    )(*[value for value, _ in ins])


def feed_low(hidden, gain, gate, lift, drop):
    rows, width = hidden.shape
    ff = gate.shape[1]
    S = jax.ShapeDtypeStruct
    return call_tiled(
        low_kernel, ff // WIDE_TILE,
        [(hidden, whole_block((rows, width))), (gain, whole_block((width,))), (gate, column_block(width, WIDE_TILE)),
         (lift, column_block(width, WIDE_TILE)), (drop, row_block(width, WIDE_TILE))],
        [(S((rows, width), F32), whole_block((rows, width))), (S((width, rows), BF), whole_block((width, rows))),
         (S((rows, ff), BF), column_block(rows, WIDE_TILE)), (S((rows, ff), BF), column_block(rows, WIDE_TILE)),
         (S((ff, rows), BF), row_block(rows, WIDE_TILE))],
        [pltpu.VMEM((rows, width), BF)], 6 * rows * width * ff, 38 << 20, "feed_low")


def feed_low_back(grad, hidden, gain, gact, lact, gate, lift, drop):
    rows, width = hidden.shape
    ff = gate.shape[1]
    S = jax.ShapeDtypeStruct
    full = whole_block((rows, width))
    return call_tiled(
        low_back_kernel, ff // WIDE_TILE,
        [(grad, full), (hidden, full), (gain, whole_block((width,))), (gact, column_block(rows, WIDE_TILE)),
         (lact, column_block(rows, WIDE_TILE)), (gate, column_block(width, WIDE_TILE)), (lift, column_block(width, WIDE_TILE)),
         (drop, row_block(width, WIDE_TILE))],
        [(S((rows, width), F32), full), (S((1, width), F32), whole_block((1, width))), (S((rows, width), BF), full),
         (S((rows, width), BF), full), (S((rows, ff), BF), column_block(rows, WIDE_TILE)), (S((rows, ff), BF), column_block(rows, WIDE_TILE))],
        [pltpu.VMEM((rows, width), F32)], 1 << 20, 1 << 10, "feed_low_back")


def feed_top(got, two, exit_weight, cotangent, gain, gate, lift, drop):
    rows, width = two.shape
    ff = gate.shape[1]
    S = jax.ShapeDtypeStruct
    full = whole_block((rows, width))
    flat = whole_block((1, width))
    standing = whole_block((width, rows))
    return call_tiled(
        top_kernel, ff // TILE,
        [(got, whole_block(got.shape)), (two, full), (exit_weight, whole_block(exit_weight.shape)), (cotangent, full),
         (gain, whole_block((width,))), (gate, column_block(width)), (lift, column_block(width)), (drop, row_block(width))],
        [(S((rows, width), F32), full), (S((rows, width), F32), full), (S((rows, width), BF), full),
         (S(got.shape, BF), whole_block(got.shape)), (S((width, rows), BF), standing), (S((1, width), F32), flat),
         (S((width, rows), BF), standing), (S((ff, rows), BF), row_block(rows)), (S((rows, ff), BF), column_block(rows)),
         (S((rows // 2, ff), BF), column_block(rows // 2)), (S((rows // 2, ff), BF), column_block(rows // 2))],
        [pltpu.VMEM((rows, width), F32), pltpu.VMEM((rows, width), BF), pltpu.VMEM((rows, width), F32)],
        12 * rows * width * ff, 45 << 20, "feed_top")


MIX_TILE = 256
HALO = 16


def shifted(value, steps):
    return pltpu.roll(value, steps, 0)


def mix_kernel(tok_ref, prev_ref, pos_ref, gain_ref, taps_ref, entb_ref, entc_ref, entx_ref, exit_ref,
               out_ref, normt_ref, gatedt_ref, b_ref, c_ref, x_ref, conv_ref, prod_ref, norm_ref):
    step = pl.program_id(0)

    @pl.when(step == 0)
    def _():
        hid = tok_ref[...].astype(F32)
        normed = hid * norm_scale(hid) * row_of(gain_ref)
        norm_ref[HALO:] = normed.astype(BF)
        normt_ref[...] = turned(normed)
        before = prev_ref[...].astype(F32)
        norm_ref[:HALO] = (before * norm_scale(before) * row_of(gain_ref)).astype(BF)
        out_ref[...] = hid

    taps = taps_ref[...].astype(F32)
    part_b = nn_dot(norm_ref[...], entb_ref[...])
    part_x = nn_dot(norm_ref[...], entx_ref[...])
    part_c = nn_dot(norm_ref[HALO:], entc_ref[...])
    product = (part_b * part_x).astype(BF)
    prod_ref[...] = product
    product = product.astype(F32)
    one = jnp.where(pos_ref[:-HALO] >= 1.0, shifted(product, 1)[HALO:], 0.0)
    two = jnp.where(pos_ref[:-HALO] >= 2.0, shifted(product, 2)[HALO:], 0.0)
    conved = taps[2:3] * product[HALO:] + taps[1:2] * one + taps[0:1] * two
    gated = part_c * conved
    b_ref[...] = part_b[HALO:].astype(BF)
    c_ref[...] = part_c.astype(BF)
    x_ref[...] = part_x[HALO:].astype(BF)
    conv_ref[...] = conved.astype(BF)
    gatedt_ref[...] = turned(gated)
    out_ref[...] += nn_dot(gated.astype(BF), exit_ref[...])


def mix_back_kernel(grad_ref, low_ref, next_ref, cnext_ref, pos_ref, tok_ref, gain_ref, taps_ref, b_ref, c_ref, x_ref,
                    conv_ref, prod_ref, entb_ref, entc_ref, entx_ref, exit_ref,
                    out_ref, again_ref, taps_out_ref, mixed_ref, acc_ref):
    step = pl.program_id(0)
    rows, width = grad_ref.shape
    tile = b_ref.shape[1]

    @pl.when(step == 0)
    def _():
        acc_ref[...] = jnp.zeros_like(acc_ref)

    taps = taps_ref[...].astype(F32)
    lows = jnp.concatenate([low_ref[...], next_ref[...]], axis=0)
    gated_grad = nt_dot(lows, exit_ref[...])
    gate = jnp.concatenate([c_ref[...], cnext_ref[...]], axis=0).astype(F32)
    conved_grad = gated_grad * gate
    first = jnp.where(pos_ref[...] >= 1.0, conved_grad, 0.0)
    second = jnp.where(pos_ref[...] >= 2.0, conved_grad, 0.0)
    ahead_one = shifted(first, rows + HALO - 1)[:rows]
    ahead_two = shifted(second, rows + HALO - 2)[:rows]
    own = conved_grad[:rows]
    product_grad = taps[2:3] * own + taps[1:2] * ahead_one + taps[0:1] * ahead_two
    product = prod_ref[...].astype(F32)
    total = lambda value: jnp.sum(value, axis=0, keepdims=True)
    taps_out_ref[0:1] = total(shifted(product, 2)[HALO:] * second[:rows])
    taps_out_ref[1:2] = total(shifted(product, 1)[HALO:] * first[:rows])
    taps_out_ref[2:3] = total(product[HALO:] * own)
    b_low = (product_grad * x_ref[...].astype(F32)).astype(BF)
    c_low = (gated_grad[:rows] * conv_ref[...].astype(F32)).astype(BF)
    x_low = (product_grad * b_ref[...].astype(F32)).astype(BF)
    for place, value in enumerate((b_low, c_low, x_low)):
        mixed_ref[:, pl.ds(pl.multiple_of(place * width + step * tile, tile), tile)] = value
    acc_ref[...] += nt_dot(b_low, entb_ref[...]) + nt_dot(c_low, entc_ref[...]) + nt_dot(x_low, entx_ref[...])

    @pl.when(step == pl.num_programs(0) - 1)
    def _():
        back, gain_part = norm_pull(acc_ref[...], tok_ref[...].astype(F32), row_of(gain_ref))
        again_ref[...] = gain_part
        out_ref[...] = grad_ref[...] + back


def mix_specs(width):
    tiles = width // MIX_TILE
    entry = [pl.BlockSpec((width, MIX_TILE), lambda step, part=part: (0, part * tiles + step)) for part in range(3)]
    return tiles, entry, row_block(width, MIX_TILE)


def mix_forward(tokens, before, position, gain, taps, entry, exit_weight):
    rows, width = tokens.shape
    tiles, entry_specs, exit_spec = mix_specs(width)
    S = jax.ShapeDtypeStruct
    full = whole_block((rows, width))
    columns = column_block(rows, MIX_TILE)
    return call_tiled(
        mix_kernel, tiles,
        [(tokens, full), (before, whole_block(before.shape)), (position, whole_block(position.shape)),
         (gain, whole_block((width,))), (taps, column_block(3, MIX_TILE)), *[(entry, spec) for spec in entry_specs],
         (exit_weight, exit_spec)],
        [(S((rows, width), F32), full), (S((width, rows), BF), whole_block((width, rows))),
         (S((width, rows), BF), row_block(rows, MIX_TILE))] + [(S((rows, width), BF), columns)] * 4
        + [(S((rows + HALO, width), BF), column_block(rows + HALO, MIX_TILE))],
        [pltpu.VMEM((rows + HALO, width), BF)], 8 * rows * width * width, 12 << 20, "mix")


def mix_backward(grad, low, after, gate_after, position, tokens, gain, taps, kept, entry, exit_weight):
    rows, width = grad.shape
    tiles, entry_specs, exit_spec = mix_specs(width)
    S = jax.ShapeDtypeStruct
    full = whole_block((rows, width))
    flat = whole_block((1, width))
    columns = column_block(rows, MIX_TILE)
    part_b, part_c, part_x, conved, product = kept
    return call_tiled(
        mix_back_kernel, tiles,
        [(grad, full), (low, full), (after, whole_block(after.shape)), (gate_after, column_block(HALO, MIX_TILE)),
         (position, whole_block(position.shape)), (tokens, full), (gain, whole_block((width,))), (taps, column_block(3, MIX_TILE)),
         (part_b, columns), (part_c, columns), (part_x, columns), (conved, columns),
         (product, column_block(rows + HALO, MIX_TILE)), *[(entry, spec) for spec in entry_specs],
         (exit_weight, exit_spec)],
        [(S((rows, width), F32), full), (S((1, width), F32), flat), (S((3, width), F32), column_block(3, MIX_TILE)),
         (S((rows, 3 * width), BF), whole_block((rows, 3 * width)))],
        [pltpu.VMEM((rows, width), F32)], 8 * rows * width * width, 16 << 20, "mix_back")


def sweep_keys(visit, index, tail, part, base, rows, half_rows, keys, sources):
    lowest = base * rows + part * half_rows
    end = (base + sources - 1) * rows + (part + 1) * half_rows
    count = (end + keys - 1) // keys
    free = jnp.where(end > tail, 0, jnp.maximum((lowest + 1) // keys - 1, 0))
    lax.fori_loop(0, free, lambda step, _: visit(step + 1, False), None)
    lax.fori_loop(0, count - free, lambda step, _: visit(jnp.where(step == 0, 0, free + step), True), None)


def greet(me, count):
    barrier = pltpu.get_barrier_semaphore()

    def hello(step, _):
        pl.semaphore_signal(barrier, inc=1, device_id={"ctx": lax.rem(me + step, count)}, device_id_type=MESH)

    lax.fori_loop(1, count, hello, None)
    pl.semaphore_signal(barrier, inc=1, device_id={"dp": 1 - lax.axis_index("dp")}, device_id_type=MESH)
    pl.semaphore_wait(barrier, count)


def hosted_copies(kinds, sources, landings, sends, recvs):
    y = lax.axis_index("dp")
    copies = []
    for number, (kind, source, landing) in enumerate(zip(kinds, sources, landings)):
        if kind == "rows":
            height = landing.shape[2]
            source = source.at[:, :, pl.ds(pl.multiple_of((1 - y) * height, PIECE), height), :]
        if kind == "columns":
            width = landing.shape[1]
            source = source.at[:, pl.ds(pl.multiple_of((1 - y) * width, STRIP), width)]
        copies.append(pltpu.make_async_remote_copy(
            src_ref=source, dst_ref=landing, send_sem=sends.at[number], recv_sem=recvs.at[number],
            device_id={"dp": 1 - y}, device_id_type=MESH))
    return copies


def hosted_shapes(hosted):
    shapes = []
    for kind, value in hosted:
        shape = list(value.shape)
        if kind == "rows":
            shape[2] //= 2
        if kind == "columns":
            shape[1] //= 2
        shapes.append(jax.ShapeDtypeStruct(tuple(shape), value.dtype))
    return shapes


def attend_kernel(head, rows, keys, sources, count, kinds, *refs):
    extra = len(kinds)
    (info_ref, msg_ref), guests, refs = refs[:2], refs[2:2 + extra], refs[2 + extra:]
    (got_ref, out_ref, aug_ref, all_ref), landings, refs = refs[:4], refs[4:4 + extra], refs[4 + extra:]
    (land, kv, tiles, arrive, ones_ref, acc_ref, msend, mrecv, fsend, frecv, gsend, grecv, hsend, hrecv) = refs
    first = info_ref[0, 0]
    second = first + info_ref[0, 1]
    me = lax.axis_index("ctx")
    part = me % 2
    twin = {"ctx": me + 1 - 2 * part}
    half_rows = msg_ref.shape[1]
    wide = sources * 2 * half_rows
    span = sources * rows
    factor = math.log2(math.e) / math.sqrt(head)
    lane = lane_of((half_rows, LANES))
    greet(me, count)

    def remote(src, dst, send, recv, where):
        return pltpu.make_async_remote_copy(src_ref=src, dst_ref=dst, send_sem=send, recv_sem=recv,
                                            device_id=where, device_id_type=MESH)

    def msg_copy(owner, dest):
        return remote(msg_ref.at[dest], land.at[owner], msend.at[dest], mrecv.at[owner], {"ctx": dest})

    def share_copy(source):
        return remote(kv.at[source, part], kv.at[source, part], fsend.at[source], frecv.at[source], twin)

    def tile_copy(owner, dest):
        return remote(tiles.at[dest], arrive.at[owner], gsend.at[dest], grecv.at[owner], {"ctx": dest})

    def start_msg(step, _):
        msg_copy(me, lax.rem(me + step, count)).start()

    lax.fori_loop(1, count, start_msg, None)
    hosted = hosted_copies(kinds, guests, landings, hsend, hrecv)
    for copy in hosted:
        copy.start()
    land[me] = msg_ref[me]

    def share(source):
        @pl.when(source != me)
        def _():
            msg_copy(source, me).wait_recv()

        kv[source, part] = land[source, :, LANES:]
        share_copy(source).start()

    def compute(index):
        base = index * sources
        stack = []
        for source in range(sources):
            share_copy(base + source).wait_recv()
            both = kv[base + source].reshape(rows, LANES)
            place = pl.ds(pl.multiple_of((base + source) * rows, rows), rows)
            all_ref[place] = both
            ones_ref[place] = jnp.where(lane_of(both.shape) < head, jnp.ones_like(both), both)
            tile = land[base + source, :, :LANES].astype(F32)
            stack.append(jnp.where(lane < head, tile, 0.0))
            stack.append(jnp.where(lane < head, swap_heads(tile, head), 0.0))
        queries = jnp.concatenate(stack, axis=0).astype(BF)
        acc_ref[...] = jnp.zeros_like(acc_ref)

        def visit(step, masked):
            start = pl.multiple_of(step * keys, keys)
            here = pl.ds(start, keys)
            raised = jnp.exp2(lax.dot_general(queries, all_ref[here], ONES_NT, preferred_element_type=F32) * factor)
            if masked:
                ok = allowed_block(0, 1, (wide, keys), first, second, part, base, start, rows, half_rows)
                raised = jnp.where(ok, raised, 0.0)
            acc_ref[...] += jnp.dot(raised.astype(BF), ones_ref[here], preferred_element_type=F32)

        sweep_keys(visit, index, count * rows - rows, part, base, rows, half_rows, keys, sources)
        for source in range(sources):
            tile = land[base + source, :, :LANES].astype(F32)
            outs = []
            for which in range(2):
                place = (2 * source + which) * half_rows
                acc = acc_ref[place:place + half_rows]
                turn = swap_heads(acc, head)
                outs.append(turn / acc if which == 0 else acc / turn)
                high, middle, low = three_parts(-math.sqrt(head) * jnp.log(turn))
                query = tile if which == 0 else swap_heads(tile, head)
                extra = jnp.where(lane == head, high, jnp.where(lane == head + 1, middle,
                                                                jnp.where(lane == head + 2, low, 0.0)))
                aug_ref[base + source, which] = jnp.where(lane < head, query, extra).astype(BF)
            out = jnp.where(lane < head, outs[0], outs[1])
            out_ref[base + source] = out
            tiles[base + source] = out.astype(BF)

            @pl.when(base + source != me)
            def _(source=source):
                tile_copy(me, base + source).start()

    def block(index, _):
        @pl.when(index < count // sources)
        def _():
            for source in range(sources):
                share(index * sources + source)

        @pl.when(index > 0)
        def _():
            compute(index - 1)

    lax.fori_loop(0, count // sources + 1, block, None)
    arrive[me] = tiles[me]

    def drain(other, _):
        share_copy(other).wait_send()

        @pl.when(other != me)
        def _():
            msg_copy(me, other).wait_send()
            tile_copy(me, other).wait_send()
            tile_copy(other, me).wait_recv()

    lax.fori_loop(0, count, drain, None)
    got_ref[...] = arrive[...]
    for copy in hosted:
        copy.wait()


def attend_back_kernel(head, rows, keys, sources, count, kinds, *refs):
    extra = len(kinds)
    (info_ref, aug_ref, out_ref, kv_ref, msg_ref), guests, refs = refs[:5], refs[5:5 + extra], refs[5 + extra:]
    (gotq_ref, gotk_ref), landings, refs = refs[:2], refs[2:2 + extra], refs[2 + extra:]
    (land, tiles, away, near, sums, arrive_q, arrive_k, kone_ref, vone_ref, kturn_ref, dk_ref, dv_ref, acc_ref,
     msend, mrecv, fsend, frecv, gsend, grecv, ksend, krecv, hsend, hrecv) = refs
    first = info_ref[0, 0]
    second = first + info_ref[0, 1]
    me = lax.axis_index("ctx")
    part = me % 2
    twin = {"ctx": me + 1 - 2 * part}
    half_rows = msg_ref.shape[1]
    wide = sources * 2 * half_rows
    factor = math.log2(math.e) / math.sqrt(head)
    shrink = 1.0 / math.sqrt(head)
    lane = lane_of((half_rows, LANES))
    greet(me, count)

    def remote(src, dst, send, recv, where):
        return pltpu.make_async_remote_copy(src_ref=src, dst_ref=dst, send_sem=send, recv_sem=recv,
                                            device_id=where, device_id_type=MESH)

    def msg_copy(owner, dest):
        return remote(msg_ref.at[dest], land.at[owner], msend.at[dest], mrecv.at[owner], {"ctx": dest})

    def share_copy(source):
        return remote(away.at[source], near.at[source], fsend.at[source], frecv.at[source], twin)

    def q_copy(owner, dest):
        return remote(tiles.at[dest], arrive_q.at[owner], gsend.at[dest], grecv.at[owner], {"ctx": dest})

    def k_copy(owner, dest):
        return remote(sums.at[dest], arrive_k.at[owner], ksend.at[dest], krecv.at[owner], {"ctx": dest})

    def start_msg(step, _):
        msg_copy(me, lax.rem(me + count - step, count)).start()

    lax.fori_loop(1, count, start_msg, None)
    hosted = hosted_copies(kinds, guests, landings, hsend, hrecv)
    for copy in hosted:
        copy.start()
    land[me] = msg_ref[me]
    whole = lane_of(kv_ref.shape)
    vone_ref[...] = jnp.where(whole < head, jnp.ones_like(kv_ref), kv_ref[...])
    kone_ref[...] = jnp.where(whole < head, kv_ref[...], jnp.ones_like(kv_ref))
    kturn_ref[...] = turned(kv_ref[...])
    dk_ref[...] = jnp.zeros_like(dk_ref)
    dv_ref[...] = jnp.zeros_like(dv_ref)

    def rows_of(source, which):
        return pl.ds(pl.multiple_of(source * rows + which * half_rows, half_rows), half_rows)

    def key_tile(source, which):
        here = rows_of(source, which)
        return jnp.where(lane < head, dk_ref[here] * shrink, dv_ref[here])

    def compute(index):
        base = index * sources
        stack_q, stack_d = [], []
        for source in range(sources):
            @pl.when(base + source != me)
            def _(source=source):
                msg_copy(base + source, me).wait_recv()

            grad = land[base + source].astype(F32)
            spread = grad * out_ref[base + source]
            for which in range(2):
                stack_q.append(aug_ref[base + source, which])
                mine = (lane < head) if which == 0 else (lane >= head)
                delta = jnp.sum(jnp.where(mine, spread, 0.0), axis=1, keepdims=True)
                high, middle, low = three_parts(-delta)
                extra = jnp.where(lane == 0, high, jnp.where(lane == 1, middle, jnp.where(lane == 2, low, 0.0)))
                moved = swap_heads(grad, head) if which == 0 else grad
                stack_d.append(jnp.where(lane < head, extra, moved).astype(BF))
        queries = jnp.concatenate(stack_q, axis=0)
        grads = jnp.concatenate(stack_d, axis=0)
        acc_ref[...] = jnp.zeros_like(acc_ref)

        def visit(step, masked):
            start = pl.multiple_of(step * keys, keys)
            here = pl.ds(start, keys)
            raw = lax.dot_general(kone_ref[here], queries, ONES_NT, preferred_element_type=F32)
            if masked:
                ok = allowed_block(1, 0, (keys, wide), first, second, part, base, start, rows, half_rows)
                prob = jnp.where(ok, jnp.exp2(jnp.where(ok, raw, 0.0) * factor), 0.0)
            else:
                prob = jnp.exp2(raw * factor)
            along = lax.dot_general(vone_ref[here], grads, ONES_NT, preferred_element_type=F32)
            score = (prob * along).astype(BF)
            dv_ref[here] += jnp.dot(prob.astype(BF), grads, preferred_element_type=F32)
            dk_ref[here] += jnp.dot(score, queries, preferred_element_type=F32)
            acc_ref[...] += jnp.dot(kturn_ref[:, here], score, preferred_element_type=F32)

        sweep_keys(visit, index, count * rows - rows, part, base, rows, half_rows, keys, sources)
        acc = acc_ref[...].T
        for source in range(sources):
            place = 2 * source * half_rows
            one = acc[place:place + half_rows]
            two = acc[place + half_rows:place + 2 * half_rows]
            tiles[base + source] = (jnp.where(lane < head, one, swap_heads(two, head)) * shrink).astype(BF)

            @pl.when(base + source != me)
            def _(source=source):
                q_copy(me, base + source).start()

            away[base + source] = key_tile(base + source, 1 - part).astype(BF)
            share_copy(base + source).start()

    def finish(index):
        for source in range(sources):
            block = index * sources + source
            share_copy(block).wait_recv()
            sums[block] = (key_tile(block, part) + near[block].astype(F32)).astype(BF)

            @pl.when(block != me)
            def _(block=block):
                k_copy(me, block).start()

    def sweep(step, _):
        index = count // sources - 1 - step

        @pl.when(index >= 0)
        def _():
            compute(jnp.maximum(index, 0))

        @pl.when(step > 0)
        def _():
            finish(index + 1)

    lax.fori_loop(0, count // sources + 1, sweep, None)
    arrive_q[me] = tiles[me]
    arrive_k[me] = sums[me]

    def drain(other, _):
        share_copy(other).wait_send()

        @pl.when(other != me)
        def _():
            msg_copy(me, other).wait_send()
            q_copy(me, other).wait_send()
            k_copy(me, other).wait_send()
            q_copy(other, me).wait_recv()
            k_copy(other, me).wait_recv()

    lax.fori_loop(0, count, drain, None)
    gotq_ref[...] = arrive_q[...]
    gotk_ref[...] = arrive_k[...]
    for copy in hosted:
        copy.wait()


def exchange_attend(msg, info, head, rows, hosted, collective_id):
    count, half_rows = msg.shape[0], msg.shape[1]
    keys, sources = 512, 2
    group = count * rows
    dma = pltpu.SemaphoreType.DMA((count,))
    S = jax.ShapeDtypeStruct
    tile = (count, half_rows, LANES)
    kinds = [kind for kind, _ in hosted]
    guests = [value for _, value in hosted]
    hdma = pltpu.SemaphoreType.DMA((len(hosted),))
    anywhere = [pl.BlockSpec(memory_space=pl.ANY)] * len(hosted)
    return pl.pallas_call(
        functools.partial(attend_kernel, head, rows, keys, sources, count, kinds),
        out_shape=(S(tile, BF), S(tile, F32), S((count, 2, half_rows, LANES), BF), S((group, LANES), BF),
                   *hosted_shapes(hosted)),
        in_specs=[pl.BlockSpec(memory_space=pltpu.SMEM)] + vmem_specs(1) + anywhere,
        out_specs=tuple(vmem_specs(4) + anywhere),
        scratch_shapes=[pltpu.VMEM((count, half_rows, 2 * LANES), BF), pltpu.VMEM((count, 2, half_rows, LANES), BF),
                        pltpu.VMEM(tile, BF), pltpu.VMEM(tile, BF), pltpu.VMEM((group, LANES), BF),
                        pltpu.VMEM((sources * rows, LANES), F32)] + [dma] * 6 + [hdma] * 2,
        compiler_params=pltpu.CompilerParams(collective_id=collective_id, has_side_effects=True,
                                             vmem_limit_bytes=VMEM_LIMIT),
        cost_estimate=pl.CostEstimate(flops=2 * group * group * LANES, bytes_accessed=6 << 20, transcendentals=0),
        name="attend",
    )(info, msg, *guests)


def exchange_attend_back(msg, info, augmented, attended, all_kv, head, rows, hosted, collective_id):
    count, half_rows = msg.shape[0], msg.shape[1]
    keys, sources = 512, 2
    group = count * rows
    dma = pltpu.SemaphoreType.DMA((count,))
    S = jax.ShapeDtypeStruct
    tile = (count, half_rows, LANES)
    kinds = [kind for kind, _ in hosted]
    guests = [value for _, value in hosted]
    hdma = pltpu.SemaphoreType.DMA((len(hosted),))
    anywhere = [pl.BlockSpec(memory_space=pl.ANY)] * len(hosted)
    long = (group, LANES)
    return pl.pallas_call(
        functools.partial(attend_back_kernel, head, rows, keys, sources, count, kinds),
        out_shape=(S(tile, BF), S(tile, BF), *hosted_shapes(hosted)),
        in_specs=[pl.BlockSpec(memory_space=pltpu.SMEM)] + vmem_specs(4) + anywhere,
        out_specs=tuple(vmem_specs(2) + anywhere),
        scratch_shapes=[pltpu.VMEM(tile, BF)] * 7 + [
            pltpu.VMEM(long, BF), pltpu.VMEM(long, BF), pltpu.VMEM((LANES, group), BF), pltpu.VMEM(long, F32),
            pltpu.VMEM(long, F32), pltpu.VMEM((LANES, sources * rows), F32)] + [dma] * 8 + [hdma] * 2,
        compiler_params=pltpu.CompilerParams(collective_id=collective_id, has_side_effects=True,
                                             vmem_limit_bytes=VMEM_LIMIT),
        cost_estimate=pl.CostEstimate(flops=5 * group * group * LANES, bytes_accessed=8 << 20, transcendentals=0),
        name="attend_back",
    )(info, augmented, attended, all_kv, msg, *guests)


def sum_kernel(jobs, sides, weights, lines, *refs):
    count = len(jobs)
    refs = list(refs)
    take = lambda number: [refs.pop(0) for _ in range(number)]
    lefts, lefts_y, rights = take(sides), take(sides), take(count)
    sent = [refs.pop(0) if job["late"] and job["kind"] == "pair" else None for job in jobs]
    early_y = [None if job["late"] else take(job["parts"]) for job in jobs]
    small_refs = take(len(SMALL_ROWS))
    outs, (small_out,) = take(weights), take(1)
    lefts_s, lefts_ys, rights_s, rights_ys = take(sides), take(sides), take(count), take(count)
    rights_y = [take(1) if job["late"] else early for job, early in zip(jobs, early_y)]
    (lbuf, rbuf, xp, xr, x2r, zp, us, ur, ds_, dr, fs, fr, cs, cr, stage, sm_s, sm_r,
     lsem, rsem, xs, xv, x2s, x2v, uss, urv, dss, drv, fss, frv, css, crv, osem, sms, smv, els, elv, ers, erv, yrs, yrv) = refs
    steps = sum(job["total"] for job in jobs)
    last = steps - 1
    tokens = lbuf.shape[-1] // 4
    me = lax.axis_index("ctx")
    y = lax.axis_index("dp")
    z = me // 4
    x = (me // 2) % 2
    c = me % 2
    top = lines - 1
    twin = {"ctx": me + 1 - 2 * c}
    across_x = {"ctx": me + 2 - 4 * x}
    across_y = {"dp": 1 - y}
    above = {"ctx": jnp.minimum(me + 4, 4 * top + me % 4)}
    below = {"ctx": jnp.maximum(me - 4, me % 4)}
    near = {"ctx": me + 4 - 8 * (z % 2)}
    far = {"ctx": me + 8 - 16 * (z // 2)}
    rounds = [twin, across_x, across_y, near, far]

    for buf in (ur, dr, zp):
        buf[...] = jnp.zeros_like(buf)
    sm_s[0] = jnp.zeros(sm_s.shape[1:], F32)
    for (row, column), ref in zip(SMALL_ROWS, small_refs):
        sm_s[0, row:row + ref.shape[0], column:column + ref.shape[1]] = ref[...]

    barrier = pltpu.get_barrier_semaphore()
    for where in (twin, across_x, across_y, far):
        pl.semaphore_signal(barrier, inc=1, device_id=where, device_id_type=MESH)

    @pl.when(z < top)
    def _():
        pl.semaphore_signal(barrier, inc=1, device_id=above, device_id_type=MESH)

    @pl.when(z > 0)
    def _():
        pl.semaphore_signal(barrier, inc=1, device_id=below, device_id_type=MESH)

    pl.semaphore_wait(barrier, 4 + (z < top).astype(jnp.int32) + (z > 0).astype(jnp.int32))

    def remote(src, dst, send, recv, where):
        return pltpu.make_async_remote_copy(src_ref=src, dst_ref=dst, send_sem=send, recv_sem=recv,
                                            device_id=where, device_id_type=MESH)

    def row_base(number):
        height = lefts_s[number].shape[2]
        return y * height if height < lefts[number].shape[2] else 0

    def column_base(number):
        width = 2 * rights_s[number].shape[1]
        return y * width if jobs[number]["kind"] == "quarter" else 0

    def left_copies(number):
        height = lefts_s[number].shape[2]
        rows = pl.ds(pl.multiple_of(row_base(number), PIECE), height)
        return [
            remote(lefts[number].at[:, :, rows, :], lefts_s[number], els.at[number, 0], elv.at[number, 0], twin),
            remote(lefts_y[number], lefts_ys[number], els.at[number, 1], elv.at[number, 1], twin),
        ]

    def right_own(number):
        width = rights_s[number].shape[1]
        start = pl.multiple_of(column_base(number) + (1 - c) * width, STRIP)
        return remote(rights[number].at[:, pl.ds(start, width)], rights_s[number], ers.at[number, 0],
                      erv.at[number, 0], twin)

    def right_forward(number):
        width = rights_s[number].shape[1]
        columns = pl.ds(pl.multiple_of((1 - c) * width, STRIP), width)
        tall = tokens // len(rights_y[number])
        return [remote(source.at[:, columns], rights_ys[number].at[pl.ds(part * tall, tall)],
                       ers.at[number, 1 + part], erv.at[number, 1 + part], twin)
                for part, source in enumerate(rights_y[number])]

    def right_cross(number, piece=None):
        width = 2 * rights_s[number].shape[1]
        kind = jobs[number]["kind"]
        source = sent[number] if kind == "pair" else rights[number]
        start = (1 - y) * width if kind == "quarter" else 0
        rows, inside = slice(None), 0
        size = width
        if piece is not None:
            rows = pl.ds(pl.multiple_of((piece & 1) * (tokens // 2), PIECE), tokens // 2)
            inside, size = (piece >> 1) * STRIP, STRIP
        place = pl.ds(pl.multiple_of(inside, STRIP), size)
        if piece is None:
            landing = rights_y[number][0]
        else:
            landing = rights_y[number][0].at[rows, place]
        return remote(source.at[rows, pl.ds(pl.multiple_of(start + inside, STRIP), size)], landing,
                      yrs.at[number], yrv.at[number], across_y)

    def x_copy(j):
        s = j & (RING - 1)
        return remote(xp.at[s, 1 - x], xr.at[s], xs.at[s], xv.at[s], across_x)

    def x2_copy(j):
        s = j & (RING - 1)
        return remote(zp.at[j & (2 * RING - 1), z, 1 - x], x2r.at[s], x2s.at[s], x2v.at[s], across_x)

    def line_first(j):
        return lax.rem(j, LINE_FIRST) == LINE_FIRST - 1

    def either(j, act):
        both = line_first(j)
        pl.when(both)(lambda: act(True))
        pl.when(jnp.logical_not(both))(lambda: act(False))

    def up_copy(j, both):
        s = j & (RING - 1)
        src, dst = (us.at[s], ur.at[s]) if both else (us.at[s, :, 0], ur.at[s, :, 0])
        return remote(src, dst, uss.at[s], urv.at[s], above)

    def down_copy(j, both):
        s = j & (RING - 1)
        src, dst = (ds_.at[s], dr.at[s]) if both else (ds_.at[s, :, 0], dr.at[s, :, 0])
        return remote(src, dst, dss.at[s], drv.at[s], below)

    def f_copy(j):
        s = j & (RING - 1)
        return remote(fs.at[s], fr.at[s], fss.at[s], frv.at[s], across_y)

    def c_copy(j):
        s = j & (RING - 1)
        return remote(cs.at[s], cr.at[s], css.at[s], crv.at[s], twin)

    def small_copy(k):
        return remote(sm_s.at[k], sm_r.at[k], sms.at[k], smv.at[k], rounds[k])

    def loads(number):
        job = jobs[number]
        left, s = job["left"], number % 2
        height, width = lefts_s[left].shape[2], rights_s[number].shape[1]
        own_rows = pl.ds(pl.multiple_of(row_base(left), PIECE), height)
        own_columns = pl.ds(pl.multiple_of(column_base(number) + c * width, STRIP), width)
        mine = pl.ds(pl.multiple_of(c * width, STRIP), width)
        copies = []
        for place, source in enumerate([lefts[left].at[:, :, own_rows, :], lefts_s[left], lefts_y[left],
                                        lefts_ys[left]]):
            copies.append(pltpu.make_async_copy(
                source, lbuf.at[s, :, :, pl.ds(0, height), pl.ds(place * tokens, tokens)], lsem.at[s, place]))
        tall = tokens // len(rights_y[number])
        pieces = [(0, rights[number].at[:, own_columns]), (tokens, rights_s[number]), (3 * tokens, rights_ys[number])]
        pieces += [(2 * tokens + part * tall, source.at[:, mine]) for part, source in enumerate(rights_y[number])]
        for place, (start, source) in enumerate(pieces):
            copies.append(pltpu.make_async_copy(
                source, rbuf.at[s, pl.ds(start, source.shape[0]), pl.ds(0, width)], rsem.at[s, place]))
        return copies

    def each_job(j, visit):
        begin = 0
        for number, job in enumerate(jobs):
            @pl.when((j >= begin) & (j < begin + job["total"]))
            def _(number=number, begin=begin):
                visit(number, j - begin)
            begin += job["total"]

    def begins():
        begin = 0
        for number, job in enumerate(jobs):
            yield number, job, begin
            begin += job["total"]

    def out_copies(number, k, j):
        job = jobs[number]
        o = j & (RING - 1)
        row = pl.multiple_of(lax.rem(k, job["subs"]) * PIECE, PIECE)
        column = pl.multiple_of(lax.div(k, job["subs"]) * STRIP, STRIP)
        width = rights_s[number].shape[1]
        copies = []
        for line in range(2):
            for core in range(2):
                out = outs[job["outs"][line if job["kind"] == "pair" else 0]]
                rows, columns = row, core * width + column
                if job["kind"] == "quarter":
                    columns = line * 2 * width + columns
                if job["kind"] == "drop":
                    rows = line * lefts_s[job["left"]].shape[2] + row
                copies.append(pltpu.make_async_copy(
                    stage.at[o, line, core],
                    out.at[pl.ds(pl.multiple_of(rows, PIECE), PIECE), pl.ds(pl.multiple_of(columns, STRIP), STRIP)],
                    osem.at[o, line, core]))
        return copies

    def out_wait(j):
        for copy in out_copies(0, 0, j):
            copy.wait()

    started = []
    for number, job, begin in begins():
        if job["left"] not in started:
            started.append(job["left"])
            for copy in left_copies(job["left"]):
                copy.start()
        right_own(number).start()
        if not job["late"]:
            for copy in right_forward(number):
                copy.start()

    def step(t, _):
        slot = t & (RING - 1)

        for number, job, begin in begins():
            if job["late"]:
                ago = t - job["issue"]
                piece = ago - (ago >> 2)
                pieces = 4 * rights_s[number].shape[1] // STRIP

                @pl.when((ago >= 0) & (ago & 3 != 3) & (piece < pieces))
                def _(number=number, piece=piece):
                    right_cross(number, piece).start()

                @pl.when(t == begin - job["ahead"])
                def _(number=number):
                    right_cross(number).wait()
                    for copy in right_forward(number):
                        copy.start()

        done, before = [], 0
        for number, job, begin in begins():
            fresh = job["left"] not in done
            done.append(job["left"])

            @pl.when(t == max(before, begin - AHEAD))
            def _(number=number, job=job, fresh=fresh):
                if fresh:
                    for copy in left_copies(job["left"]):
                        copy.wait()
                right_own(number).wait()
                for copy in right_forward(number):
                    copy.wait()
                for copy in loads(number):
                    copy.start()

            before = begin

        for number, job, begin in begins():
            @pl.when(t == begin)
            def _(number=number):
                for copy in loads(number):
                    copy.wait()

        for k in range(len(rounds) + 1):
            @pl.when(t == LAG * k)
            def _(k=k):
                if k > 0:
                    small_copy(k - 1).wait()
                    total = sm_s[k - 1] + sm_r[k - 1]
                    if k == len(rounds):
                        small_out[...] = total
                    else:
                        sm_s[k] = total
                if k < len(rounds):
                    small_copy(k).start()

        @pl.when(t < steps)
        def _():
            which, begin_now, subs_now = 0, 0, jobs[0]["subs"]
            for number, job, begin in begins():
                here = t >= begin
                begin_now = jnp.where(here, begin, begin_now)
                subs_now = jnp.where(here, job["subs"], subs_now)
                which = jnp.where(here, number % 2, which)
            row = lax.rem(t - begin_now, subs_now) * PIECE
            column = lax.div(t - begin_now, subs_now) * STRIP
            rows = pl.ds(pl.multiple_of(row, PIECE), PIECE)
            left = lbuf[which, :, :, rows, :].reshape(2 * lines * SUB, 4 * tokens)
            right = rbuf[which, :, pl.ds(pl.multiple_of(column, STRIP), STRIP)]
            got = jnp.dot(left, right, preferred_element_type=F32).astype(BF)
            @pl.when(line_first(t))
            def _():
                for line in range(lines):
                    for side in range(2):
                        row = (2 * line + side) * SUB
                        zp[t & (2 * RING - 1), line, side] = got[row:row + SUB]

            @pl.when(jnp.logical_not(line_first(t)))
            def _():
                for line in range(lines):
                    for side in range(2):
                        row = (2 * line + side) * SUB
                        xp[slot, side, line] = got[row:row + SUB]
                x_copy(t).start()

        @pl.when((t >= LAG) & (t - LAG <= last) & jnp.logical_not(line_first(jnp.maximum(t - LAG, 0))))
        def _():
            x_copy(t - LAG).wait()
            s = (t - LAG) & (RING - 1)
            zp[(t - LAG) & (2 * RING - 1), :, 0] = xp[s, x] + xr[s]

        ju = t - LAG - LINE_LAG * z

        @pl.when((ju >= 0) & (ju <= last))
        def _():
            s = ju & (RING - 1)
            held = ju & (2 * RING - 1)

            @pl.when(z > 0)
            def _():
                either(ju, lambda both: up_copy(ju, both).wait_recv())
                zp[held, z] = zp[held, z] + ur[s, 0]

            @pl.when(z < top)
            def _():
                @pl.when(ju >= RING)
                def _():
                    either(ju - RING, lambda both: up_copy(ju - RING, both).wait_send())

                for m in range(top):
                    own = zp[held, jnp.minimum(z + 1 + m, top)]
                    if m + 1 < top:
                        own = own + ur[s, m + 1]
                    us[s, m] = own
                either(ju, lambda both: up_copy(ju, both).start())

        jd = t - LAG - LINE_LAG * (top - z)

        @pl.when((jd >= 0) & (jd <= last))
        def _():
            s = jd & (RING - 1)
            held = jd & (2 * RING - 1)

            @pl.when(z < top)
            def _():
                either(jd, lambda both: down_copy(jd, both).wait_recv())
                zp[held, z] = zp[held, z] + dr[s, 0]

            @pl.when(z > 0)
            def _():
                @pl.when(jd >= RING)
                def _():
                    either(jd - RING, lambda both: down_copy(jd - RING, both).wait_send())

                for m in range(top):
                    own = zp[held, jnp.maximum(z - 1 - m, 0)]
                    if m + 1 < top:
                        own = own + dr[s, m + 1]
                    ds_[s, m] = own
                either(jd, lambda both: down_copy(jd, both).start())

        jx = t - LAG - LINE_LAG * top

        @pl.when((jx >= 0) & (jx <= last) & line_first(jnp.maximum(jx, 0)))
        def _():
            x2_copy(jx).start()

        jf = jx - LAG

        @pl.when((jf >= 0) & (jf <= last))
        def _():
            s = jf & (RING - 1)
            held = jf & (2 * RING - 1)

            def gather(both):
                if both:
                    x2_copy(jf).wait()
                    fs[s] = zp[held, z, x] + x2r[s]
                else:
                    fs[s] = zp[held, z, 0]

            either(jf, gather)
            f_copy(jf).start()

        jo = jf - LAG

        @pl.when((jo >= 0) & (jo <= last))
        def _():
            f_copy(jo).wait()
            s = jo & (RING - 1)
            mine = pl.ds(pl.multiple_of(c * PIECE, PIECE), PIECE)
            away = pl.ds(pl.multiple_of((1 - c) * PIECE, PIECE), PIECE)
            cs[s, y] = fs[s, away]
            cs[s, 1 - y] = fr[s, away]
            c_copy(jo).start()
            stage[s, y, c] = fs[s, mine].astype(F32)
            stage[s, 1 - y, c] = fr[s, mine].astype(F32)

        jc = jo - CORE_LAG

        @pl.when((jc >= 0) & (jc <= last))
        def _():
            c_copy(jc).wait()
            s = jc & (RING - 1)
            stage[s, 0, 1 - c] = cr[s, 0].astype(F32)
            stage[s, 1, 1 - c] = cr[s, 1].astype(F32)

            def start(number, k):
                for copy in out_copies(number, k, jc):
                    copy.start()

            each_job(jc, start)

            @pl.when(jc >= LAG)
            def _():
                out_wait(jc - LAG)

    lax.fori_loop(0, last + 3 * LAG + LINE_LAG * top + CORE_LAG + 1, step, None)
    for back in range(LAG):
        out_wait(last - back)
    for back in range(RING):
        j = last - back

        @pl.when(z < top)
        def _(j=j):
            up_copy(j, j % LINE_FIRST == LINE_FIRST - 1).wait_send()

        @pl.when(z > 0)
        def _(j=j):
            down_copy(j, j % LINE_FIRST == LINE_FIRST - 1).wait_send()


def sum_over_chips(lefts, works, small, lines, collective_id):
    S = jax.ShapeDtypeStruct
    jobs, landing_r, landing_y, outs, sent, early = [], [], [], [], [], []
    shaped = [own.reshape(2 * lines, 2, own.shape[0] // (4 * lines), own.shape[1]) for own, _ in lefts]
    crossed = [cross for _, cross in lefts]
    tokens = shaped[0].shape[-1]
    for work in works:
        job = {name: work[name] for name in ("left", "kind", "late", "issue", "ahead")}
        columns = work["own"].shape[1]
        width = columns // 4 if job["kind"] == "quarter" else columns // 2
        height = crossed[job["left"]].shape[2]
        job["subs"], job["strips"] = height // PIECE, width // STRIP
        job["total"] = job["subs"] * job["strips"]
        job["outs"] = []
        for _ in range(2 if job["kind"] == "pair" else 1):
            job["outs"].append(len(outs))
            outs.append(S((shaped[job["left"]].shape[2], columns), F32))
        landing_r.append(S((tokens, width), BF))
        if job["late"]:
            landing_y.append(S((tokens, 2 * width), BF))
            if job["kind"] == "pair":
                sent.append(work["cross"])
        else:
            job["parts"] = len(work["cross"])
            early.extend(work["cross"])
        jobs.append(job)
    steps = sum(job["total"] for job in jobs)
    flat = (8, small[0].shape[1])
    top = lines - 1
    dma = pltpu.SemaphoreType.DMA
    ring = lambda *shape: pltpu.VMEM((RING,) + shape, BF)
    scratch = [
        pltpu.VMEM((2, 2 * lines, 2, max(value.shape[2] for value in crossed), 4 * tokens), BF),
        pltpu.VMEM((2, 4 * tokens, max(value.shape[1] for value in landing_r)), BF),
        ring(2, lines, SUB, STRIP), ring(lines, SUB, STRIP), ring(SUB, STRIP),
        pltpu.VMEM((2 * RING, lines, 2, SUB, STRIP), BF),
        ring(top, 2, SUB, STRIP), ring(top, 2, SUB, STRIP), ring(top, 2, SUB, STRIP), ring(top, 2, SUB, STRIP),
        ring(SUB, STRIP), ring(SUB, STRIP), ring(2, PIECE, STRIP), ring(2, PIECE, STRIP),
        pltpu.VMEM((RING, 2, 2, PIECE, STRIP), F32),
        pltpu.VMEM((5,) + flat, F32),
        pltpu.VMEM((5,) + flat, F32),
        dma((2, 4)), dma((2, 5)),
    ] + [dma((RING,))] * 12 + [
        dma((RING, 2, 2)), dma((5,)), dma((5,)),
        dma((len(lefts), 2)), dma((len(lefts), 2)), dma((len(works), 3)), dma((len(works), 3)),
        dma((len(works),)), dma((len(works),)),
    ]
    anywhere = pl.BlockSpec(memory_space=pl.ANY)
    inside = pl.BlockSpec(memory_space=pltpu.VMEM)
    landings = [S(value.shape, BF) for value in crossed] * 2 + landing_r * 2 + landing_y
    operands = shaped + crossed + [work["own"] for work in works] + sent + early
    flops = 2 * steps * 2 * lines * SUB * STRIP * 4 * tokens
    got = pl.pallas_call(
        functools.partial(sum_kernel, jobs, len(lefts), len(outs), lines),
        out_shape=tuple(outs) + (S(flat, F32),) + tuple(landings),
        in_specs=[anywhere] * len(operands) + [inside] * len(small),
        out_specs=tuple([anywhere] * len(outs) + [inside] + [anywhere] * len(landings)),
        scratch_shapes=scratch,
        compiler_params=pltpu.CompilerParams(collective_id=collective_id, has_side_effects=True,
                                             vmem_limit_bytes=VMEM_LIMIT),
        cost_estimate=pl.CostEstimate(flops=flops, bytes_accessed=steps * 1_100_000, transcendentals=0),
        name="sum_over_chips",
    )(*operands, *small)
    return got[:len(outs)], got[len(outs)]


def hand_over_kernel(count, head, *refs):
    sources, small_ref, results = refs[:count], refs[count], refs[count + 1:2 * count + 1]
    mix_ref, taps_ref, low_ref, att_ref, top_ref, query_ref, keys_ref = refs[2 * count + 1:2 * count + 8]
    holds, (ins, outs) = refs[2 * count + 8:3 * count + 8], refs[3 * count + 8:]
    arrive = [pltpu.make_async_copy(source, hold, ins.at[number])
              for number, (source, hold) in enumerate(zip(sources, holds))]
    leave = [pltpu.make_async_copy(hold, result, outs.at[number])
             for number, (hold, result) in enumerate(zip(holds, results))]
    for copy in arrive:
        copy.start()
    mix_ref[...] = small_ref[0]
    taps_ref[...] = small_ref[1:4]
    low_ref[...] = small_ref[4]
    att_ref[...] = small_ref[5]
    top_ref[...] = small_ref[6]
    query_ref[...] = small_ref[7, :head] + small_ref[7, head:LANES]
    keys_ref[...] = small_ref[7, LANES:LANES + head] + small_ref[7, LANES + head:2 * LANES]
    for first, then in zip(arrive, leave):
        first.wait()
        then.start()
    for copy in leave:
        copy.wait()


def hand_over(grads, small, head):
    count, width = len(grads), small.shape[1]
    S = jax.ShapeDtypeStruct
    anywhere = [pl.BlockSpec(memory_space=pl.ANY)] * count
    smalls = (S((width,), F32), S((3, width), F32), S((width,), F32), S((width,), F32), S((width,), F32),
              S((head,), F32), S((head,), F32))
    got = pl.pallas_call(
        functools.partial(hand_over_kernel, count, head),
        out_shape=tuple(S(value.shape, F32) for value in grads) + smalls,
        in_specs=anywhere + vmem_specs(1),
        out_specs=tuple(anywhere + vmem_specs(len(smalls))),
        scratch_shapes=[pltpu.VMEM(value.shape, F32) for value in grads] + [pltpu.SemaphoreType.DMA((count,))] * 2,
        compiler_params=pltpu.CompilerParams(vmem_limit_bytes=VMEM_LIMIT),
        name="hand_over",
    )(*grads, small)
    return got[:count], got[count:]


def call_plain(kernel, outs, args, smem=0, scratch=(), flops=0, moved=0, name=None):
    specs = [pl.BlockSpec(memory_space=pltpu.SMEM)] * smem + vmem_specs(len(args) - smem)
    many = isinstance(outs, (tuple, list))
    return pl.pallas_call(
        kernel,
        out_shape=tuple(outs) if many else outs,
        in_specs=specs,
        out_specs=tuple(vmem_specs(len(outs))) if many else vmem_specs(1)[0],
        scratch_shapes=list(scratch),
        compiler_params=pltpu.CompilerParams(vmem_limit_bytes=VMEM_LIMIT),
        cost_estimate=pl.CostEstimate(flops=flops, bytes_accessed=moved, transcendentals=0),
        name=name,
    )(*args)


def shape_of(shape, kind):
    return jax.ShapeDtypeStruct(shape, kind)


def sibling(value):
    count = lax.axis_size("ctx")
    return lax.ppermute(value, "ctx", [(i, i ^ 1) for i in range(count)])


def fast_device(tokens, lengths, cotangent, mixgain, mixentry, mixtaps, mixexit, lowgain, lowgate, lowlift,
                lowdrop, attgain, attquery, attkeys, attvalues, querygain, keysgain, attexit, topgain, topgate,
                toplift, topdrop):
    rows, width = tokens.shape
    head = querygain.shape[0]
    devices = lax.axis_size("ctx")
    lines = devices // 4
    half_rows = rows // 2
    place = lax.axis_index("ctx")
    core = place % 2
    first = lengths[0, 0]
    second = first + lengths[0, 1]
    where = place * rows + jnp.arange(rows + HALO, dtype=jnp.int32)
    begin = jnp.where(where >= second, second, jnp.where(where >= first, first, 0))
    spots = (where - begin).astype(F32)[:, None]
    spot = jnp.arange(LANES, dtype=jnp.int32) % (head // 2)
    angle = spots[:rows] * (THETA ** (-spot.astype(F32) * 2.0 / head))[None, :]
    cosine = jnp.cos(angle)
    sine = jnp.sin(angle) * jnp.where(jnp.arange(LANES) % head < head // 2, -1.0, 1.0)[None, :]

    before = passed_along(tokens[rows - HALO:], "ctx", 1)
    (hidden_one, normed_one_t, gated_t, part_b, part_c, part_x, conved, product) = mix_forward(
        tokens, before, spots, mixgain, mixtaps, mixentry, mixexit)
    gate_after = passed_along(part_c[:HALO], "ctx", -1)
    hidden_two, lownorm_t, gact_low, lact_low, lowinner_t = feed_low(
        hidden_one, lowgain, lowgate, lowlift, lowdrop)

    heads_q, heads_k = attquery.shape[1] // head, attkeys.shape[1] // head
    msg, normed_two_t, query_raw, key_raw = call_plain(
        functools.partial(project_kernel, head),
        (shape_of((devices, half_rows, 2 * LANES), BF), shape_of((width, rows), BF),
         shape_of((rows, attquery.shape[1]), F32), shape_of((rows, attkeys.shape[1]), F32)),
        (hidden_two, attgain, attquery, attkeys, attvalues, cosine, sine, querygain, keysgain),
        flops=2 * rows * width * 2 * width, moved=6 << 20, name="project")
    upright = lambda value: value.reshape(devices // 2, 2, value.shape[0] // devices, rows)
    over_dp = lambda value: lax.ppermute(value, "dp", [(0, 1), (1, 0)])
    msg, gated_y, normed_one_y, cotangent_y, gate_after = lax.optimization_barrier(
        (msg, over_dp(gated_t), over_dp(normed_one_t), over_dp(cotangent), gate_after))
    gated_y, normed_one_y = upright(gated_y), upright(normed_one_y)
    got, attended_f, augmented, all_kv, lowinner_y, lownorm_y = exchange_attend(
        msg, lengths, head, rows, [("rows", upright(lowinner_t)), ("whole", upright(lownorm_t))], 2)
    (output, grad, grad_low3, send, attended_t, topgain_grad, topnorm_t, topinner_t, keep_top, send_top_a,
     send_top_b) = feed_top(
        got, hidden_two, attexit, cotangent, topgain, topgate, toplift, topdrop)
    send, normed_two_y = lax.optimization_barrier((send, over_dp(normed_two_t)))
    normed_two_y = upright(normed_two_y)
    back_q, back_k, topinner_y, topnorm_y, attended_y, grad_low3_y = exchange_attend_back(
        send, lengths, augmented, attended_f, all_kv, head, rows,
        [("rows", upright(topinner_t)), ("whole", upright(topnorm_t)), ("whole", upright(attended_t)),
         ("columns", grad_low3)], 3)
    back_q, send_top_a, send_top_b = lax.optimization_barrier((back_q, send_top_a, send_top_b))
    top_y_one = over_dp(send_top_a)
    rawq_low, keep_kv, send_kv, grad_two, attgain_grad, querygain_grad, keysgain_grad = call_plain(
        functools.partial(project_back_kernel, head),
        (shape_of((rows, attquery.shape[1]), BF), shape_of((rows, attkeys.shape[1]), BF),
         shape_of((rows, attkeys.shape[1]), BF), shape_of((rows, width), F32), shape_of((1, width), F32),
         shape_of((1, LANES), F32), shape_of((1, LANES), F32)),
        (back_q, back_k, hidden_two, attgain, attquery, attkeys, attvalues, cosine, sine, querygain, keysgain,
         query_raw, key_raw, grad),
        flops=1 << 20, moved=1 << 10, name="project_back")
    grad, lowgain_grad, gb_low, grad_low1, keep_low, send_low = feed_low_back(
        grad_two, hidden_one, lowgain, gact_low, lact_low, lowgate, lowlift, lowdrop)
    grad, grad_low1, top_y_one = lax.optimization_barrier((grad, grad_low1, top_y_one))
    after = passed_along(grad_low1[:HALO], "ctx", -1)
    tokens_grad, mixgain_grad, mixtaps_grad, mixed_grad = mix_backward(
        grad, grad_low1, after, gate_after, spots, tokens, mixgain, mixtaps,
        (part_b, part_c, part_x, conved, product), mixentry, mixexit)
    mixgain_grad, tokens_grad, top_y_two = lax.optimization_barrier(
        (mixgain_grad, tokens_grad, over_dp(send_top_b)))

    lefts = [(attended_t, attended_y), (topinner_t, topinner_y), (topnorm_t, topnorm_y), (normed_two_t, normed_two_y),
             (lowinner_t, lowinner_y), (lownorm_t, lownorm_y), (gated_t, gated_y), (normed_one_t, normed_one_y)]

    def work(left, kind, own, cross=None, issue=-1, ahead=12):
        return dict(left=left, kind=kind, own=own, cross=cross, late=issue >= 0, issue=issue, ahead=ahead)

    works = [work(0, "quarter", grad_low3, (grad_low3_y,)), work(1, "drop", cotangent, (cotangent_y,)),
             work(2, "pair", keep_top, (top_y_one, top_y_two)), work(3, "quarter", rawq_low, issue=0),
             work(3, "pair", keep_kv, send_kv, issue=5), work(4, "drop", gb_low, issue=10),
             work(5, "pair", keep_low, send_low, issue=20), work(6, "quarter", grad_low1, issue=68),
             work(7, "quarter", mixed_grad, issue=73)]
    small = (mixgain_grad, mixtaps_grad, lowgain_grad, attgain_grad, topgain_grad, querygain_grad, keysgain_grad)
    grads, small = sum_over_chips(lefts, works, small, lines, 1)
    grads, smalls = hand_over(grads, small, head)
    (attexit_grad, topdrop_grad, topgate_grad, toplift_grad, attquery_grad, attkeys_grad, attvalues_grad, lowdrop_grad,
     lowgate_grad, lowlift_grad, mixexit_grad, mixentry_grad) = grads
    (mixgain_grad, mixtaps_grad, lowgain_grad, attgain_grad, topgain_grad, querygain_grad, keysgain_grad) = smalls
    return (output, tokens_grad, mixgain_grad, mixentry_grad, mixtaps_grad, mixexit_grad, lowgain_grad, lowgate_grad,
            lowlift_grad, lowdrop_grad, attgain_grad, attquery_grad, attkeys_grad, attvalues_grad, querygain_grad,
            keysgain_grad, attexit_grad, topgain_grad, topgate_grad, toplift_grad, topdrop_grad)


def solution(mesh):
    placed = (P(("dp", "ctx"), None), P("dp", None), P(("dp", "ctx"), None)) + (P(),) * 19
    split = {0: P(("dp", "ctx"), None), 1: P(("dp", "ctx"), None)}
    whole = (2, 4, 6, 10, 14, 15, 17)
    outs = tuple(split.get(i, P() if i in whole else P("ctx", None)) for i in range(21))
    small = mesh.shape["ctx"] == 16 and mesh.shape["dp"] == 2
    return jax.shard_map(fast_device if small else per_device, mesh=mesh, in_specs=placed, out_specs=outs,
                         check_vma=False)
```

```python
import functools
import math

import jax
import jax.numpy as jnp
from jax import lax
from jax.experimental import pallas as pl
from jax.experimental.pallas import tpu as pltpu
from jax.sharding import PartitionSpec as P

EPS = 1e-05
THETA = 1000000.0
NEGATIVE = -1e30


def passed_along(value, axis, steps):
    count = lax.axis_size(axis)
    first, last = (max(0, -steps), min(count, count - steps))
    return lax.ppermute(value, axis, [(source, source + steps) for source in range(first, last)])


def passed_along_2(block, axis, distance):
    devices = range(lax.axis_size(axis))
    route = [((i - distance) % len(devices), i) for i in devices]
    return lax.ppermute(block, axis, route)


def root_mean_square_scale(hidden, gain):
    return hidden * lax.rsqrt(jnp.mean(hidden * hidden, axis=-1, keepdims=True) + EPS) * gain


def rotary_embed(value_rows, position_index):
    half = value_rows.shape[-1] // 2
    freq = THETA ** (-jnp.arange(half, dtype=jnp.float32) * 2.0 / value_rows.shape[-1])
    angle = position_index.astype(jnp.float32)[:, None] * freq[None, :]
    cosine = jnp.cos(angle)[:, None, :]
    sine = jnp.sin(angle)[:, None, :]
    front = value_rows[..., :half]
    behind = value_rows[..., half:]
    return jnp.concatenate(
        [front * cosine - behind * sine, behind * cosine + front * sine], axis=-1
    )


def head_prep(raw, gain, position_index, heads):
    shaped = raw.reshape(raw.shape[0], heads, -1)
    return rotary_embed(root_mean_square_scale(shaped, gain), position_index)


def segment_of(where, first, second):
    return (where >= first).astype(jnp.int32) + (where >= second).astype(jnp.int32)


def block_width(count):
    best = 1
    for candidate in range(1, min(count, 1024) + 1):
        if count % candidate == 0:
            best = candidate
    return best


def sweep(carry, count, visit):
    width = block_width(count)
    return lax.fori_loop(
        0, count // width, lambda index, inner: visit(inner, index * width, width), carry
    )


def inner_dot(left, right):
    return lax.dot_general(
        left, right, (((0,), (0,)), ((), ())), preferred_element_type=jnp.float32
    )


def outer_dot(left, right):
    return lax.dot_general(
        left, right, (((1,), (1,)), ((), ())), preferred_element_type=jnp.float32
    )


def scores_of(query_part, key_part, query_where, key_where, query_seg, key_seg, scale):
    raw = (
        jnp.einsum("tkgd,pkd->kgtp", query_part, key_part, preferred_element_type=jnp.float32)
        * scale
    )
    allowed = (query_seg[:, None] == key_seg[None, :]) & (
        query_where[:, None] >= key_where[None, :]
    )
    return (raw, allowed)


def grad_block(
    query_part,
    grad_part,
    logsum_part,
    delta_part,
    key_part,
    value_part,
    query_where,
    key_where,
    query_seg,
    key_seg,
    scale,
):
    raw, allowed = scores_of(
        query_part, key_part, query_where, key_where, query_seg, key_seg, scale
    )
    prob = jnp.where(allowed, jnp.exp(raw - logsum_part[..., None]), 0.0)
    prob_grad = jnp.einsum(
        "tkgd,pkd->kgtp", grad_part, value_part, preferred_element_type=jnp.float32
    )
    score_grad = (prob * (prob_grad - delta_part[..., None])).astype(jnp.bfloat16)
    query_grad = (
        jnp.einsum("kgtp,pkd->tkgd", score_grad, key_part, preferred_element_type=jnp.float32)
        * scale
    )
    key_grad = (
        jnp.einsum("kgtp,tkgd->pkd", score_grad, query_part, preferred_element_type=jnp.float32)
        * scale
    )
    value_grad = jnp.einsum(
        "kgtp,tkgd->pkd", prob.astype(jnp.bfloat16), grad_part, preferred_element_type=jnp.float32
    )
    return (query_grad, key_grad, value_grad)


def conv_local(extended, taps, fits_one, fits_two):
    rows = extended.shape[0] - 2
    return (
        taps[2] * extended[2:]
        + taps[1] * extended[1 : rows + 1] * fits_one
        + taps[0] * extended[:rows] * fits_two
    )


def feed_forward(hidden, gain, gate_weight, lift_weight, drop_weight):
    fnormed = root_mean_square_scale(hidden, gain).astype(jnp.bfloat16)
    gate_act = jnp.dot(fnormed, gate_weight, preferred_element_type=jnp.float32)
    lift_act = jnp.dot(fnormed, lift_weight, preferred_element_type=jnp.float32)
    inner = (jax.nn.silu(gate_act) * lift_act).astype(jnp.bfloat16)
    result = hidden + jnp.dot(inner, drop_weight, preferred_element_type=jnp.float32)
    return (result, (fnormed, gate_act, lift_act, inner))


def feed_back(grad, hidden, gain, kept, gate_weight, lift_weight, drop_weight):
    fnormed, gate_act, lift_act, inner = kept
    grad_low = grad.astype(jnp.bfloat16)
    drop_grad = inner_dot(inner, grad_low)
    inner_grad = outer_dot(grad_low, drop_weight)
    _, pull_gate = jax.vjp(
        lambda gate_in, lift_in: jax.nn.silu(gate_in) * lift_in, gate_act, lift_act
    )
    gate_grad, lift_grad = pull_gate(inner_grad)
    gate_low = gate_grad.astype(jnp.bfloat16)
    lift_low = lift_grad.astype(jnp.bfloat16)
    gate_wgrad = inner_dot(fnormed, gate_low)
    lift_wgrad = inner_dot(fnormed, lift_low)
    normed_grad = outer_dot(gate_low, gate_weight) + outer_dot(lift_low, lift_weight)
    _, pull_norm = jax.vjp(root_mean_square_scale, hidden, gain)
    hidden_grad, gain_grad = pull_norm(normed_grad)
    return (grad + hidden_grad, (gain_grad, gate_wgrad, lift_wgrad, drop_grad))


def per_device(
    tokens,
    lengths,
    cotangent,
    mixgain,
    mixentry,
    mixtaps,
    mixexit,
    lowgain,
    lowgate,
    lowlift,
    lowdrop,
    attgain,
    attquery,
    attkeys,
    attvalues,
    querygain,
    keysgain,
    attexit,
    topgain,
    topgate,
    toplift,
    topdrop,
):
    rows = tokens.shape[0]
    width_model = tokens.shape[1]
    head_size = querygain.shape[0]
    query_heads = attquery.shape[1] // head_size
    kv_heads = attkeys.shape[1] // head_size
    shared_gradient = query_heads // kv_heads
    scale = 1.0 / math.sqrt(head_size)
    place = lax.axis_index("ctx")
    first = lengths[0, 0]
    second = first + lengths[0, 1]
    mine = place * rows + jnp.arange(rows, dtype=jnp.int32)
    my_seg = segment_of(mine, first, second)
    begin = jnp.where(my_seg == 0, 0, jnp.where(my_seg == 1, first, second))
    position_index = mine - begin
    last_row = place * rows + rows - 1
    mixgain_f = mixgain.astype(jnp.float32)
    taps_f = mixtaps.astype(jnp.float32)
    lowgain_f = lowgain.astype(jnp.float32)
    attgain_f = attgain.astype(jnp.float32)
    querygain_f = querygain.astype(jnp.float32)
    keysgain_f = keysgain.astype(jnp.float32)
    topgain_f = topgain.astype(jnp.float32)
    hidden = tokens.astype(jnp.float32)
    normed_one = root_mean_square_scale(hidden, mixgain_f).astype(jnp.bfloat16)
    mixed = jnp.dot(normed_one, mixentry, preferred_element_type=jnp.float32)
    part_b = mixed[:, :width_model]
    part_c = mixed[:, width_model : 2 * width_model]
    part_x = mixed[:, 2 * width_model :]
    product = (part_b * part_x).astype(jnp.bfloat16)
    borrowed = passed_along(product[rows - 2 :], "ctx", 1)
    extended = jnp.concatenate([borrowed, product], axis=0).astype(jnp.float32)
    fits_one = ((mine >= 1) & (segment_of(mine - 1, first, second) == my_seg)).astype(jnp.float32)[
        :, None
    ]
    fits_two = ((mine >= 2) & (segment_of(mine - 2, first, second) == my_seg)).astype(jnp.float32)[
        :, None
    ]
    conved = conv_local(extended, taps_f, fits_one, fits_two)
    gated = (part_c * conved).astype(jnp.bfloat16)
    hidden_one = hidden + jnp.dot(gated, mixexit, preferred_element_type=jnp.float32)
    hidden_two, kept_low = feed_forward(hidden_one, lowgain_f, lowgate, lowlift, lowdrop)
    normed_two = root_mean_square_scale(hidden_two, attgain_f).astype(jnp.bfloat16)
    query_unrotated = jnp.dot(normed_two, attquery, preferred_element_type=jnp.float32)
    key_unrotated = jnp.dot(normed_two, attkeys, preferred_element_type=jnp.float32)
    value_projected = jnp.dot(normed_two, attvalues, preferred_element_type=jnp.float32)
    query_low = head_prep(query_unrotated, querygain_f, position_index, query_heads).astype(
        jnp.bfloat16
    )
    key_low = head_prep(key_unrotated, keysgain_f, position_index, kv_heads).astype(jnp.bfloat16)
    value_low = value_projected.astype(jnp.bfloat16).reshape(rows, kv_heads, head_size)
    query_grouped = query_low.reshape(rows, kv_heads, shared_gradient, head_size)

    def stat_visit(carry, keys_in, start, offset, width):
        top, total = carry
        key_part = lax.dynamic_slice_in_dim(keys_in, offset, width, 0)
        key_where = start + offset + jnp.arange(width, dtype=jnp.int32)
        raw, allowed = scores_of(
            query_grouped,
            key_part,
            mine,
            key_where,
            my_seg,
            segment_of(key_where, first, second),
            scale,
        )
        new_top = jnp.maximum(top, jnp.max(jnp.where(allowed, raw, NEGATIVE), axis=-1))
        weights = jnp.where(allowed, jnp.exp(raw - new_top[..., None]), 0.0)
        total = total * jnp.exp(top - new_top) + jnp.sum(weights, axis=-1)
        return (new_top, total)

    stat_state = (
        jnp.full((kv_heads, shared_gradient, rows), NEGATIVE, jnp.float32),
        jnp.zeros((kv_heads, shared_gradient, rows), jnp.float32),
    )
    piece = lax.all_gather(key_low, "ctx", axis=0, tiled=True)
    start = jnp.int32(0)
    count = piece.shape[0]

    def stat_running(inner):
        return sweep(
            inner, count, lambda acc, offset, width: stat_visit(acc, piece, start, offset, width)
        )

    top, total = lax.cond(start > last_row, lambda inner: inner, stat_running, stat_state)
    logsum = top + jnp.log(total)

    def forward_visit(accum, keys_in, values_in, start, offset, width):
        key_part = lax.dynamic_slice_in_dim(keys_in, offset, width, 0)
        value_part = lax.dynamic_slice_in_dim(values_in, offset, width, 0)
        key_where = start + offset + jnp.arange(width, dtype=jnp.int32)
        raw, allowed = scores_of(
            query_grouped,
            key_part,
            mine,
            key_where,
            my_seg,
            segment_of(key_where, first, second),
            scale,
        )
        prob_low = jnp.where(allowed, jnp.exp(raw - logsum[..., None]), 0.0).astype(jnp.bfloat16)
        return accum + jnp.einsum(
            "kgtp,pkd->kgtd", prob_low, value_part, preferred_element_type=jnp.float32
        )

    forward_start = jnp.int32(0)
    keys_in = lax.all_gather(key_low, "ctx", axis=0, tiled=True)
    values_in = lax.all_gather(value_low, "ctx", axis=0, tiled=True)
    forward_count = keys_in.shape[0]

    def forward_running(inner):
        return sweep(
            inner,
            forward_count,
            lambda acc, offset, width: forward_visit(
                acc, keys_in, values_in, forward_start, offset, width
            ),
        )

    accum = lax.cond(
        forward_start > last_row,
        lambda inner: inner,
        forward_running,
        jnp.zeros((kv_heads, shared_gradient, rows, head_size), jnp.float32),
    )
    attended = accum.transpose(2, 0, 1, 3).reshape(rows, -1)
    attended_low = attended.astype(jnp.bfloat16)
    hidden_three = hidden_two + jnp.dot(attended_low, attexit, preferred_element_type=jnp.float32)
    output, kept_top = feed_forward(hidden_three, topgain_f, topgate, toplift, topdrop)
    grad = cotangent.astype(jnp.float32)
    grad, top_grads = feed_back(grad, hidden_three, topgain_f, kept_top, topgate, toplift, topdrop)
    grad_low = grad.astype(jnp.bfloat16)
    attexit_grad = inner_dot(attended_low, grad_low)
    out_grads = (
        outer_dot(grad_low, attexit)
        .astype(jnp.bfloat16)
        .reshape(rows, kv_heads, shared_gradient, head_size)
    )
    delta = jnp.einsum(
        "tkgd,tkgd->kgt",
        out_grads.astype(jnp.float32),
        attended.reshape(rows, kv_heads, shared_gradient, head_size),
    )
    cycle_size = lax.axis_size("ctx")

    def cycle_visit(state, keys_in, values_in, start, offset, width):
        query_acc, key_acc, value_acc = state
        key_part = lax.dynamic_slice_in_dim(keys_in, offset, width, 0)
        value_part = lax.dynamic_slice_in_dim(values_in, offset, width, 0)
        key_where = start + offset + jnp.arange(width, dtype=jnp.int32)
        query_grad, key_grad, value_grad = grad_block(
            query_grouped,
            out_grads,
            logsum,
            delta,
            key_part,
            value_part,
            mine,
            key_where,
            my_seg,
            segment_of(key_where, first, second),
            scale,
        )
        key_acc = lax.dynamic_update_slice_in_dim(
            key_acc, lax.dynamic_slice_in_dim(key_acc, offset, width, 0) + key_grad, offset, 0
        )
        value_acc = lax.dynamic_update_slice_in_dim(
            value_acc, lax.dynamic_slice_in_dim(value_acc, offset, width, 0) + value_grad, offset, 0
        )
        return (query_acc + query_grad, key_acc, value_acc)

    def cycle_step(step, carry):
        keys_cur, values_cur, key_acc, value_acc, query_acc = carry
        anchor = (place - step + cycle_size) % cycle_size
        start = anchor * rows

        def cycle_running(state):
            return sweep(
                state,
                rows,
                lambda acc, offset, width: cycle_visit(
                    acc, keys_cur, values_cur, start, offset, width
                ),
            )

        query_acc, key_acc, value_acc = lax.cond(
            start > last_row, lambda state: state, cycle_running, (query_acc, key_acc, value_acc)
        )
        keys_cur, values_cur = passed_along((keys_cur, values_cur), "ctx", 1)
        key_acc, value_acc = (
            passed_along_2(key_acc.astype(jnp.bfloat16), "ctx", 1).astype(key_acc.dtype),
            passed_along_2(value_acc.astype(jnp.bfloat16), "ctx", 1).astype(value_acc.dtype),
        )
        return (keys_cur, values_cur, key_acc, value_acc, query_acc)

    cycle_state = (
        key_low,
        value_low,
        jnp.zeros((rows, kv_heads, head_size), jnp.float32),
        jnp.zeros((rows, kv_heads, head_size), jnp.float32),
        jnp.zeros((rows, kv_heads, shared_gradient, head_size), jnp.float32),
    )
    _, _, key_grads, value_grads, query_acc = lax.fori_loop(0, cycle_size, cycle_step, cycle_state)
    _, pull_query = jax.vjp(
        lambda raw, gain: head_prep(raw, gain, position_index, query_heads),
        query_unrotated,
        querygain_f,
    )
    query_raw_grad, querygain_grad = pull_query(query_acc.reshape(rows, query_heads, head_size))
    _, pull_key = jax.vjp(
        lambda raw, gain: head_prep(raw, gain, position_index, kv_heads), key_unrotated, keysgain_f
    )
    key_raw_grad, keysgain_grad = pull_key(key_grads)
    query_raw_low = query_raw_grad.astype(jnp.bfloat16)
    key_raw_low = key_raw_grad.astype(jnp.bfloat16)
    value_raw_low = value_grads.reshape(rows, -1).astype(jnp.bfloat16)
    attquery_grad = inner_dot(normed_two, query_raw_low)
    attkeys_grad = inner_dot(normed_two, key_raw_low)
    attvalues_grad = inner_dot(normed_two, value_raw_low)
    normed_two_grad = (
        outer_dot(query_raw_low, attquery)
        + outer_dot(key_raw_low, attkeys)
        + outer_dot(value_raw_low, attvalues)
    )
    _, pull_att = jax.vjp(root_mean_square_scale, hidden_two, attgain_f)
    hidden_two_grad, attgain_grad = pull_att(normed_two_grad)
    grad = grad + hidden_two_grad
    grad, low_grads = feed_back(grad, hidden_one, lowgain_f, kept_low, lowgate, lowlift, lowdrop)
    grad_low = grad.astype(jnp.bfloat16)
    mixexit_grad = inner_dot(gated, grad_low)
    gated_grad = outer_dot(grad_low, mixexit)
    part_c_grad = gated_grad * conved
    conved_grad = gated_grad * part_c
    _, pull_conv = jax.vjp(
        lambda ext, taps: conv_local(ext, taps, fits_one, fits_two), extended, taps_f
    )
    extended_grad, mixtaps_grad = pull_conv(conved_grad)
    returned_rim = passed_along(extended_grad[:2], "ctx", -1)
    product_grad = extended_grad[2:].at[rows - 2 :].add(returned_rim)
    mixed_grad = jnp.concatenate(
        [product_grad * part_x, part_c_grad, product_grad * part_b], axis=1
    ).astype(jnp.bfloat16)
    mixentry_grad = inner_dot(normed_one, mixed_grad)
    normed_one_grad = outer_dot(mixed_grad, mixentry)
    _, pull_mix = jax.vjp(root_mean_square_scale, hidden, mixgain_f)
    hidden_grad, mixgain_grad = pull_mix(normed_one_grad)
    tokens_grad = grad + hidden_grad
    lowgain_grad, lowgate_grad, lowlift_grad, lowdrop_grad = low_grads
    topgain_grad, topgate_grad, toplift_grad, topdrop_grad = top_grads
    shares = (
        lax.psum_scatter(mixentry_grad, "ctx", scatter_dimension=0, tiled=True),
        lax.psum_scatter(mixexit_grad, "ctx", scatter_dimension=0, tiled=True),
        lax.psum_scatter(lowgate_grad, "ctx", scatter_dimension=0, tiled=True),
        lax.psum_scatter(lowlift_grad, "ctx", scatter_dimension=0, tiled=True),
        lax.psum_scatter(lowdrop_grad, "ctx", scatter_dimension=0, tiled=True),
        lax.psum_scatter(attquery_grad, "ctx", scatter_dimension=0, tiled=True),
        lax.psum_scatter(attkeys_grad, "ctx", scatter_dimension=0, tiled=True),
        lax.psum_scatter(attvalues_grad, "ctx", scatter_dimension=0, tiled=True),
        lax.psum_scatter(attexit_grad, "ctx", scatter_dimension=0, tiled=True),
        lax.psum_scatter(topgate_grad, "ctx", scatter_dimension=0, tiled=True),
        lax.psum_scatter(toplift_grad, "ctx", scatter_dimension=0, tiled=True),
        lax.psum_scatter(topdrop_grad, "ctx", scatter_dimension=0, tiled=True),
    )
    smalls = lax.psum(
        (
            mixgain_grad,
            mixtaps_grad,
            lowgain_grad,
            attgain_grad,
            querygain_grad,
            keysgain_grad,
            topgain_grad,
        ),
        "ctx",
    )
    summed = (
        lax.psum(shares[0].astype(jnp.bfloat16), "dp").astype(jnp.float32),
        lax.psum(shares[1].astype(jnp.bfloat16), "dp").astype(jnp.float32),
        lax.psum(shares[2].astype(jnp.bfloat16), "dp").astype(jnp.float32),
        lax.psum(shares[3].astype(jnp.bfloat16), "dp").astype(jnp.float32),
        lax.psum(shares[4].astype(jnp.bfloat16), "dp").astype(jnp.float32),
        lax.psum(shares[5].astype(jnp.bfloat16), "dp").astype(jnp.float32),
        lax.psum(shares[6].astype(jnp.bfloat16), "dp").astype(jnp.float32),
        lax.psum(shares[7].astype(jnp.bfloat16), "dp").astype(jnp.float32),
        lax.psum(shares[8].astype(jnp.bfloat16), "dp").astype(jnp.float32),
        lax.psum(shares[9].astype(jnp.bfloat16), "dp").astype(jnp.float32),
        lax.psum(shares[10].astype(jnp.bfloat16), "dp").astype(jnp.float32),
        lax.psum(shares[11].astype(jnp.bfloat16), "dp").astype(jnp.float32),
        lax.psum(smalls[0].astype(jnp.bfloat16), "dp").astype(jnp.float32),
        lax.psum(smalls[1].astype(jnp.bfloat16), "dp").astype(jnp.float32),
        lax.psum(smalls[2].astype(jnp.bfloat16), "dp").astype(jnp.float32),
        lax.psum(smalls[3].astype(jnp.bfloat16), "dp").astype(jnp.float32),
        lax.psum(smalls[4].astype(jnp.bfloat16), "dp").astype(jnp.float32),
        lax.psum(smalls[5].astype(jnp.bfloat16), "dp").astype(jnp.float32),
        lax.psum(smalls[6].astype(jnp.bfloat16), "dp").astype(jnp.float32),
    )
    return (
        output,
        tokens_grad,
        summed[12],
        summed[0],
        summed[13],
        summed[1],
        summed[14],
        summed[2],
        summed[3],
        summed[4],
        summed[15],
        summed[5],
        summed[6],
        summed[7],
        summed[16],
        summed[17],
        summed[8],
        summed[18],
        summed[9],
        summed[10],
        summed[11],
    )


LANES = 128
BF = jnp.bfloat16
F32 = jnp.float32
ONES_NT = (((1,), (1,)), ((), ()))
ONES_TN = (((0,), (0,)), ((), ()))
VMEM_LIMIT = 60 * 1024 * 1024
PIECE = 16
SUB = 2 * PIECE
STRIP = 256
RING = 16
LAG = 4
LINE_LAG = 4
CORE_LAG = 1
AHEAD = 8
LINE_FIRST = 6
SMALL_ROWS = ((0, 0), (1, 0), (4, 0), (5, 0), (6, 0), (7, 0), (7, LANES))


def vmem_specs(count):
    return [pl.BlockSpec(memory_space=pltpu.VMEM)] * count


def lane_of(shape):
    return lax.broadcasted_iota(jnp.int32, shape, len(shape) - 1)


def row_of(ref):
    return ref[...].astype(F32).reshape(1, ref.shape[0])


def same_head(head):
    row = lax.broadcasted_iota(jnp.int32, (LANES, LANES), 0) // head
    column = lax.broadcasted_iota(jnp.int32, (LANES, LANES), 1) // head
    return jnp.where(row == column, 1.0 / head, 0.0).astype(BF)


def head_mean(value, blocks):
    high = value.astype(BF)
    low = (value - high.astype(F32)).astype(BF)
    return (jnp.dot(high, blocks, preferred_element_type=F32) + jnp.dot(low, blocks, preferred_element_type=F32))


def twice(ref):
    row = row_of(ref)
    return jnp.concatenate([row, row], axis=1)


def other_half(value, head):
    lane = lane_of(value.shape)
    ahead = pltpu.roll(value, LANES - head // 2, 1)
    behind = pltpu.roll(value, head // 2, 1)
    return jnp.where(lane % head < head // 2, ahead, behind)


def swap_heads(value, head):
    return pltpu.roll(value, head, 1)


def three_parts(value):
    high = value.astype(BF)
    rest = value - high.astype(F32)
    middle = rest.astype(BF)
    low = (rest - middle.astype(F32)).astype(BF)
    return high.astype(F32), middle.astype(F32), low.astype(F32)


def project_kernel(head, hid_ref, gain_ref, wq_ref, wk_ref, wv_ref, cos_ref, sin_ref, qg_ref, kg_ref,
                   msg_ref, normt_ref, qraw_ref, kraw_ref):
    hid = hid_ref[...]
    scale = lax.rsqrt(jnp.mean(hid * hid, axis=-1, keepdims=True) + EPS)
    normed = hid * scale * row_of(gain_ref)
    normt_ref[...] = turned(normed)
    normed = normed.astype(BF)
    blocks = same_head(head)
    query_gain, keys_gain = twice(qg_ref), twice(kg_ref)
    cosine, sine = cos_ref[...], sin_ref[...]
    half_rows = msg_ref.shape[1]
    lane = lane_of(cosine.shape)

    def prepared(raw, gain):
        unit = raw * lax.rsqrt(head_mean(raw * raw, blocks) + EPS) * gain
        return unit * cosine + other_half(unit, head) * sine

    def put(dest, start, tile):
        low = tile.astype(BF)
        for part in range(2):
            msg_ref[2 * dest + part, :, start:start + LANES] = low[part * half_rows:(part + 1) * half_rows]

    qraw = jnp.dot(normed, wq_ref[...], preferred_element_type=F32)
    qraw_ref[...] = qraw
    for tile in range(qraw.shape[1] // LANES):
        put(tile, 0, prepared(qraw[:, tile * LANES:(tile + 1) * LANES], query_gain))
    kraw = jnp.dot(normed, wk_ref[...], preferred_element_type=F32)
    kraw_ref[...] = kraw
    vraw = jnp.dot(normed, wv_ref[...], preferred_element_type=F32)
    for tile in range(kraw.shape[1] // LANES):
        keys = prepared(kraw[:, tile * LANES:(tile + 1) * LANES], keys_gain)
        values = vraw[:, tile * LANES:(tile + 1) * LANES]
        put(2 * tile, LANES, jnp.where(lane < head, keys, swap_heads(values, head)))
        put(2 * tile + 1, LANES, jnp.where(lane < head, swap_heads(keys, head), values))


def project_back_kernel(head, backq_ref, backk_ref, hid_ref, gain_ref, wq_ref, wk_ref, wv_ref, cos_ref, sin_ref, qg_ref,
                        kg_ref, qraw_ref, kraw_ref, grad_ref,
                        rawq_ref, keep_ref, send_ref, two_ref, again_ref, qgain_ref, kgain_ref):
    query_gain, keys_gain = twice(qg_ref), twice(kg_ref)
    blocks = same_head(head)
    cosine, sine = cos_ref[...], sin_ref[...]
    lane = lane_of(cosine.shape)

    def fetch(source, dest):
        return jnp.concatenate([source[2 * dest], source[2 * dest + 1]], axis=0).astype(F32)

    def through(grad, raw, gain):
        scale = lax.rsqrt(head_mean(raw * raw, blocks) + EPS)
        unit = raw * scale
        turned = grad * cosine - other_half(grad, head) * sine
        gain_part = jnp.sum(turned * unit, axis=0, keepdims=True)
        inward = turned * gain
        return scale * (inward - unit * head_mean(inward * unit, blocks)), gain_part

    width_q = wq_ref.shape[1]
    width_k = wk_ref.shape[1]
    gain_total = jnp.zeros((1, LANES), F32)
    for tile in range(width_q // LANES):
        got, part = through(fetch(backq_ref, tile), qraw_ref[:, tile * LANES:(tile + 1) * LANES], query_gain)
        gain_total = gain_total + part
        rawq_ref[:, tile * LANES:(tile + 1) * LANES] = got.astype(BF)
    qgain_ref[...] = gain_total
    gain_total = jnp.zeros((1, LANES), F32)
    key_tiles, value_tiles = [], []
    for tile in range(width_k // LANES):
        even, odd = fetch(backk_ref, 2 * tile), fetch(backk_ref, 2 * tile + 1)
        keys = jnp.where(lane < head, even, swap_heads(odd, head))
        values = jnp.where(lane < head, swap_heads(even, head), odd)
        got, part = through(keys, kraw_ref[:, tile * LANES:(tile + 1) * LANES], keys_gain)
        gain_total = gain_total + part
        key_tiles.append(got.astype(BF))
        value_tiles.append(values.astype(BF))
    kgain_ref[...] = gain_total
    keys, values = jnp.concatenate(key_tiles, axis=1), jnp.concatenate(value_tiles, axis=1)
    keep_ref[...], send_ref[...] = kept_first(keys, values)
    normed_grad = nt_dot(rawq_ref[...], wq_ref[...]) + nt_dot(keys, wk_ref[...]) + nt_dot(values, wv_ref[...])
    hid = hid_ref[...]
    scale = lax.rsqrt(jnp.mean(hid * hid, axis=-1, keepdims=True) + EPS)
    unit = hid * scale
    again_ref[...] = jnp.sum(normed_grad * unit, axis=0, keepdims=True)
    inward = normed_grad * row_of(gain_ref)
    two_ref[...] = grad_ref[...] + scale * (inward - unit * jnp.mean(inward * unit, axis=-1, keepdims=True))


def allowed_block(row_axis, key_axis, shape, first, second, part, base, start, rows, half_rows):
    row = lax.broadcasted_iota(jnp.int32, shape, row_axis)
    token = (base + row // (2 * half_rows)) * rows + part * half_rows + row % half_rows
    key = start + lax.broadcasted_iota(jnp.int32, shape, key_axis)
    begin = jnp.where(token >= second, second, jnp.where(token >= first, first, 0))
    return (key >= begin) & (key <= token)


MESH = pl.DeviceIdType.MESH


def turned(value):
    return value.astype(F32).T.astype(BF)


def norm_scale(hidden):
    return lax.rsqrt(jnp.mean(hidden * hidden, axis=-1, keepdims=True) + EPS)


def norm_pull(normed_grad, hidden, gain):
    scale = norm_scale(hidden)
    unit = hidden * scale
    inward = normed_grad * gain
    back = scale * (inward - unit * jnp.mean(inward * unit, axis=-1, keepdims=True))
    return back, jnp.sum(normed_grad * unit, axis=0, keepdims=True)


def kept_first(one, two):
    first = lax.axis_index("dp") == 0
    return jnp.where(first, one, two), jnp.where(first, two, one)


def nt_dot(left, right):
    return lax.dot_general(left, right, ONES_NT, preferred_element_type=F32)


def nn_dot(left, right):
    return jnp.dot(left, right, preferred_element_type=F32)


def activation_pull(gate_act, lift_act, sigma, inner_grad):
    gate_grad = inner_grad * lift_act * sigma * (1 + gate_act * (1 - sigma))
    return gate_grad.astype(BF), (inner_grad * gate_act * sigma).astype(BF)


def low_kernel(hid_ref, gain_ref, gate_ref, lift_ref, drop_ref,
               out_ref, normt_ref, gact_ref, lact_ref, innert_ref, norm_ref):
    step = pl.program_id(0)

    @pl.when(step == 0)
    def _():
        hid = hid_ref[...]
        normed = hid * norm_scale(hid) * row_of(gain_ref)
        norm_ref[...] = normed.astype(BF)
        normt_ref[...] = turned(normed)
        out_ref[...] = hid

    normed = norm_ref[...]
    gate_act = nn_dot(normed, gate_ref[...])
    lift_act = nn_dot(normed, lift_ref[...])
    inner = gate_act * jax.nn.sigmoid(gate_act) * lift_act
    gact_ref[...] = gate_act.astype(BF)
    lact_ref[...] = lift_act.astype(BF)
    innert_ref[...] = turned(inner)
    out_ref[...] += nn_dot(inner.astype(BF), drop_ref[...])


def low_back_kernel(grad_ref, hid_ref, gain_ref, gact_ref, lact_ref, gate_ref, lift_ref, drop_ref,
                    out_ref, again_ref, low_ref, outlow_ref, glow_ref, llow_ref, acc_ref):
    step = pl.program_id(0)

    @pl.when(step == 0)
    def _():
        low_ref[...] = grad_ref[...].astype(BF)
        acc_ref[...] = jnp.zeros_like(acc_ref)

    gate_act, lift_act = gact_ref[...].astype(F32), lact_ref[...].astype(F32)
    inner_grad = nt_dot(low_ref[...], drop_ref[...])
    gate_low, lift_low = activation_pull(gate_act, lift_act, jax.nn.sigmoid(gate_act), inner_grad)
    glow_ref[...], llow_ref[...] = kept_first(gate_low, lift_low)
    acc_ref[...] += nt_dot(gate_low, gate_ref[...]) + nt_dot(lift_low, lift_ref[...])

    @pl.when(step == pl.num_programs(0) - 1)
    def _():
        back, gain_part = norm_pull(acc_ref[...], hid_ref[...], row_of(gain_ref))
        again_ref[...] = gain_part
        out = grad_ref[...] + back
        out_ref[...] = out
        outlow_ref[...] = out.astype(BF)


def top_kernel(got_ref, two_ref, exit_ref, cot_ref, gain_ref, gate_ref, lift_ref, drop_ref,
               out_ref, grad_ref, gradlow_ref, send_ref, attt_ref, again_ref, normt_ref, innert_ref, keep_ref,
               senda_ref, sendb_ref, hid_ref, norm_ref, acc_ref):
    step = pl.program_id(0)
    half_rows = got_ref.shape[1]

    @pl.when(step == 0)
    def _():
        tiles = []
        for tile in range(got_ref.shape[0] // 2):
            tiles.append(jnp.concatenate([got_ref[2 * tile], got_ref[2 * tile + 1]], axis=0))
        attended = jnp.concatenate(tiles, axis=1)
        attt_ref[...] = turned(attended)
        hid = two_ref[...] + nn_dot(attended, exit_ref[...])
        hid_ref[...] = hid
        normed = hid * norm_scale(hid) * row_of(gain_ref)
        norm_ref[...] = normed.astype(BF)
        normt_ref[...] = turned(normed)
        out_ref[...] = hid
        acc_ref[...] = jnp.zeros_like(acc_ref)

    normed = norm_ref[...]
    gate_act = nn_dot(normed, gate_ref[...])
    lift_act = nn_dot(normed, lift_ref[...])
    sigma = jax.nn.sigmoid(gate_act)
    inner = gate_act * sigma * lift_act
    innert_ref[...] = turned(inner)
    out_ref[...] += nn_dot(inner.astype(BF), drop_ref[...])
    inner_grad = nt_dot(cot_ref[...], drop_ref[...])
    gate_low, lift_low = activation_pull(gate_act, lift_act, sigma, inner_grad)
    keep_ref[...], sent_part = kept_first(gate_low, lift_low)
    senda_ref[...], sendb_ref[...] = sent_part[:half_rows], sent_part[half_rows:]
    acc_ref[...] += nt_dot(gate_low, gate_ref[...]) + nt_dot(lift_low, lift_ref[...])

    @pl.when(step == pl.num_programs(0) - 1)
    def _():
        back, gain_part = norm_pull(acc_ref[...], hid_ref[...], row_of(gain_ref))
        again_ref[...] = gain_part
        grad = cot_ref[...].astype(F32) + back
        grad_ref[...] = grad
        low = grad.astype(BF)
        gradlow_ref[...] = low
        sent = nt_dot(low, exit_ref[...]).astype(BF)
        for tile in range(send_ref.shape[0] // 2):
            for part in range(2):
                send_ref[2 * tile + part] = sent[part * half_rows:(part + 1) * half_rows,
                                                 tile * LANES:(tile + 1) * LANES]


TILE = 512
WIDE_TILE = 1152


def whole_block(shape):
    return pl.BlockSpec(shape, lambda step, rank=len(shape): (0,) * rank)


def column_block(rows, tile=TILE):
    return pl.BlockSpec((rows, tile), lambda step: (0, step))


def row_block(columns, tile=TILE):
    return pl.BlockSpec((tile, columns), lambda step: (step, 0))


def call_tiled(kernel, tiles, ins, outs, scratch, flops, moved, name):
    return pl.pallas_call(
        kernel,
        grid=(tiles,),
        in_specs=[spec for _, spec in ins],
        out_specs=tuple(spec for _, spec in outs),
        out_shape=tuple(shape for shape, _ in outs),
        scratch_shapes=scratch,
        compiler_params=pltpu.CompilerParams(vmem_limit_bytes=VMEM_LIMIT, dimension_semantics=("arbitrary",)),
        cost_estimate=pl.CostEstimate(flops=flops, bytes_accessed=moved, transcendentals=0),
        name=name,
    )(*[value for value, _ in ins])


def feed_low(hidden, gain, gate, lift, drop):
    rows, width = hidden.shape
    ff = gate.shape[1]
    S = jax.ShapeDtypeStruct
    return call_tiled(
        low_kernel, ff // WIDE_TILE,
        [(hidden, whole_block((rows, width))), (gain, whole_block((width,))), (gate, column_block(width, WIDE_TILE)),
         (lift, column_block(width, WIDE_TILE)), (drop, row_block(width, WIDE_TILE))],
        [(S((rows, width), F32), whole_block((rows, width))), (S((width, rows), BF), whole_block((width, rows))),
         (S((rows, ff), BF), column_block(rows, WIDE_TILE)), (S((rows, ff), BF), column_block(rows, WIDE_TILE)),
         (S((ff, rows), BF), row_block(rows, WIDE_TILE))],
        [pltpu.VMEM((rows, width), BF)], 6 * rows * width * ff, 38 << 20, "feed_low")


def feed_low_back(grad, hidden, gain, gact, lact, gate, lift, drop):
    rows, width = hidden.shape
    ff = gate.shape[1]
    S = jax.ShapeDtypeStruct
    full = whole_block((rows, width))
    return call_tiled(
        low_back_kernel, ff // WIDE_TILE,
        [(grad, full), (hidden, full), (gain, whole_block((width,))), (gact, column_block(rows, WIDE_TILE)),
         (lact, column_block(rows, WIDE_TILE)), (gate, column_block(width, WIDE_TILE)), (lift, column_block(width, WIDE_TILE)),
         (drop, row_block(width, WIDE_TILE))],
        [(S((rows, width), F32), full), (S((1, width), F32), whole_block((1, width))), (S((rows, width), BF), full),
         (S((rows, width), BF), full), (S((rows, ff), BF), column_block(rows, WIDE_TILE)), (S((rows, ff), BF), column_block(rows, WIDE_TILE))],
        [pltpu.VMEM((rows, width), F32)], 1 << 20, 1 << 10, "feed_low_back")


def feed_top(got, two, exit_weight, cotangent, gain, gate, lift, drop):
    rows, width = two.shape
    ff = gate.shape[1]
    S = jax.ShapeDtypeStruct
    full = whole_block((rows, width))
    flat = whole_block((1, width))
    standing = whole_block((width, rows))
    return call_tiled(
        top_kernel, ff // TILE,
        [(got, whole_block(got.shape)), (two, full), (exit_weight, whole_block(exit_weight.shape)), (cotangent, full),
         (gain, whole_block((width,))), (gate, column_block(width)), (lift, column_block(width)), (drop, row_block(width))],
        [(S((rows, width), F32), full), (S((rows, width), F32), full), (S((rows, width), BF), full),
         (S(got.shape, BF), whole_block(got.shape)), (S((width, rows), BF), standing), (S((1, width), F32), flat),
         (S((width, rows), BF), standing), (S((ff, rows), BF), row_block(rows)), (S((rows, ff), BF), column_block(rows)),
         (S((rows // 2, ff), BF), column_block(rows // 2)), (S((rows // 2, ff), BF), column_block(rows // 2))],
        [pltpu.VMEM((rows, width), F32), pltpu.VMEM((rows, width), BF), pltpu.VMEM((rows, width), F32)],
        12 * rows * width * ff, 45 << 20, "feed_top")


MIX_TILE = 256
HALO = 16


def shifted(value, steps):
    return pltpu.roll(value, steps, 0)


def mix_kernel(tok_ref, prev_ref, pos_ref, gain_ref, taps_ref, entb_ref, entc_ref, entx_ref, exit_ref,
               out_ref, normt_ref, gatedt_ref, b_ref, c_ref, x_ref, conv_ref, prod_ref, norm_ref):
    step = pl.program_id(0)

    @pl.when(step == 0)
    def _():
        hid = tok_ref[...].astype(F32)
        normed = hid * norm_scale(hid) * row_of(gain_ref)
        norm_ref[HALO:] = normed.astype(BF)
        normt_ref[...] = turned(normed)
        before = prev_ref[...].astype(F32)
        norm_ref[:HALO] = (before * norm_scale(before) * row_of(gain_ref)).astype(BF)
        out_ref[...] = hid

    taps = taps_ref[...].astype(F32)
    part_b = nn_dot(norm_ref[...], entb_ref[...])
    part_x = nn_dot(norm_ref[...], entx_ref[...])
    part_c = nn_dot(norm_ref[HALO:], entc_ref[...])
    product = (part_b * part_x).astype(BF)
    prod_ref[...] = product
    product = product.astype(F32)
    one = jnp.where(pos_ref[:-HALO] >= 1.0, shifted(product, 1)[HALO:], 0.0)
    two = jnp.where(pos_ref[:-HALO] >= 2.0, shifted(product, 2)[HALO:], 0.0)
    conved = taps[2:3] * product[HALO:] + taps[1:2] * one + taps[0:1] * two
    gated = part_c * conved
    b_ref[...] = part_b[HALO:].astype(BF)
    c_ref[...] = part_c.astype(BF)
    x_ref[...] = part_x[HALO:].astype(BF)
    conv_ref[...] = conved.astype(BF)
    gatedt_ref[...] = turned(gated)
    out_ref[...] += nn_dot(gated.astype(BF), exit_ref[...])


def mix_back_kernel(grad_ref, low_ref, next_ref, cnext_ref, pos_ref, tok_ref, gain_ref, taps_ref, b_ref, c_ref, x_ref,
                    conv_ref, prod_ref, entb_ref, entc_ref, entx_ref, exit_ref,
                    out_ref, again_ref, taps_out_ref, mixed_ref, acc_ref):
    step = pl.program_id(0)
    rows, width = grad_ref.shape
    tile = b_ref.shape[1]

    @pl.when(step == 0)
    def _():
        acc_ref[...] = jnp.zeros_like(acc_ref)

    taps = taps_ref[...].astype(F32)
    lows = jnp.concatenate([low_ref[...], next_ref[...]], axis=0)
    gated_grad = nt_dot(lows, exit_ref[...])
    gate = jnp.concatenate([c_ref[...], cnext_ref[...]], axis=0).astype(F32)
    conved_grad = gated_grad * gate
    first = jnp.where(pos_ref[...] >= 1.0, conved_grad, 0.0)
    second = jnp.where(pos_ref[...] >= 2.0, conved_grad, 0.0)
    ahead_one = shifted(first, rows + HALO - 1)[:rows]
    ahead_two = shifted(second, rows + HALO - 2)[:rows]
    own = conved_grad[:rows]
    product_grad = taps[2:3] * own + taps[1:2] * ahead_one + taps[0:1] * ahead_two
    product = prod_ref[...].astype(F32)
    total = lambda value: jnp.sum(value, axis=0, keepdims=True)
    taps_out_ref[0:1] = total(shifted(product, 2)[HALO:] * second[:rows])
    taps_out_ref[1:2] = total(shifted(product, 1)[HALO:] * first[:rows])
    taps_out_ref[2:3] = total(product[HALO:] * own)
    b_low = (product_grad * x_ref[...].astype(F32)).astype(BF)
    c_low = (gated_grad[:rows] * conv_ref[...].astype(F32)).astype(BF)
    x_low = (product_grad * b_ref[...].astype(F32)).astype(BF)
    for place, value in enumerate((b_low, c_low, x_low)):
        mixed_ref[:, pl.ds(pl.multiple_of(place * width + step * tile, tile), tile)] = value
    acc_ref[...] += nt_dot(b_low, entb_ref[...]) + nt_dot(c_low, entc_ref[...]) + nt_dot(x_low, entx_ref[...])

    @pl.when(step == pl.num_programs(0) - 1)
    def _():
        back, gain_part = norm_pull(acc_ref[...], tok_ref[...].astype(F32), row_of(gain_ref))
        again_ref[...] = gain_part
        out_ref[...] = grad_ref[...] + back


def mix_specs(width):
    tiles = width // MIX_TILE
    entry = [pl.BlockSpec((width, MIX_TILE), lambda step, part=part: (0, part * tiles + step)) for part in range(3)]
    return tiles, entry, row_block(width, MIX_TILE)


def mix_forward(tokens, before, position, gain, taps, entry, exit_weight):
    rows, width = tokens.shape
    tiles, entry_specs, exit_spec = mix_specs(width)
    S = jax.ShapeDtypeStruct
    full = whole_block((rows, width))
    columns = column_block(rows, MIX_TILE)
    return call_tiled(
        mix_kernel, tiles,
        [(tokens, full), (before, whole_block(before.shape)), (position, whole_block(position.shape)),
         (gain, whole_block((width,))), (taps, column_block(3, MIX_TILE)), *[(entry, spec) for spec in entry_specs],
         (exit_weight, exit_spec)],
        [(S((rows, width), F32), full), (S((width, rows), BF), whole_block((width, rows))),
         (S((width, rows), BF), row_block(rows, MIX_TILE))] + [(S((rows, width), BF), columns)] * 4
        + [(S((rows + HALO, width), BF), column_block(rows + HALO, MIX_TILE))],
        [pltpu.VMEM((rows + HALO, width), BF)], 8 * rows * width * width, 12 << 20, "mix")


def mix_backward(grad, low, after, gate_after, position, tokens, gain, taps, kept, entry, exit_weight):
    rows, width = grad.shape
    tiles, entry_specs, exit_spec = mix_specs(width)
    S = jax.ShapeDtypeStruct
    full = whole_block((rows, width))
    flat = whole_block((1, width))
    columns = column_block(rows, MIX_TILE)
    part_b, part_c, part_x, conved, product = kept
    return call_tiled(
        mix_back_kernel, tiles,
        [(grad, full), (low, full), (after, whole_block(after.shape)), (gate_after, column_block(HALO, MIX_TILE)),
         (position, whole_block(position.shape)), (tokens, full), (gain, whole_block((width,))), (taps, column_block(3, MIX_TILE)),
         (part_b, columns), (part_c, columns), (part_x, columns), (conved, columns),
         (product, column_block(rows + HALO, MIX_TILE)), *[(entry, spec) for spec in entry_specs],
         (exit_weight, exit_spec)],
        [(S((rows, width), F32), full), (S((1, width), F32), flat), (S((3, width), F32), column_block(3, MIX_TILE)),
         (S((rows, 3 * width), BF), whole_block((rows, 3 * width)))],
        [pltpu.VMEM((rows, width), F32)], 8 * rows * width * width, 16 << 20, "mix_back")


def sweep_keys(visit, index, tail, part, base, rows, half_rows, keys, sources):
    lowest = base * rows + part * half_rows
    end = (base + sources - 1) * rows + (part + 1) * half_rows
    count = (end + keys - 1) // keys
    free = jnp.where(end > tail, 0, jnp.maximum((lowest + 1) // keys - 1, 0))
    lax.fori_loop(0, free, lambda step, _: visit(step + 1, False), None)
    lax.fori_loop(0, count - free, lambda step, _: visit(jnp.where(step == 0, 0, free + step), True), None)


def greet(me, count):
    barrier = pltpu.get_barrier_semaphore()

    def hello(step, _):
        pl.semaphore_signal(barrier, inc=1, device_id={"ctx": lax.rem(me + step, count)}, device_id_type=MESH)

    lax.fori_loop(1, count, hello, None)
    pl.semaphore_signal(barrier, inc=1, device_id={"dp": 1 - lax.axis_index("dp")}, device_id_type=MESH)
    pl.semaphore_wait(barrier, count)


def hosted_copies(kinds, sources, landings, sends, recvs):
    y = lax.axis_index("dp")
    copies = []
    for number, (kind, source, landing) in enumerate(zip(kinds, sources, landings)):
        if kind == "rows":
            height = landing.shape[2]
            source = source.at[:, :, pl.ds(pl.multiple_of((1 - y) * height, PIECE), height), :]
        if kind == "columns":
            width = landing.shape[1]
            source = source.at[:, pl.ds(pl.multiple_of((1 - y) * width, STRIP), width)]
        copies.append(pltpu.make_async_remote_copy(
            src_ref=source, dst_ref=landing, send_sem=sends.at[number], recv_sem=recvs.at[number],
            device_id={"dp": 1 - y}, device_id_type=MESH))
    return copies


def hosted_shapes(hosted):
    shapes = []
    for kind, value in hosted:
        shape = list(value.shape)
        if kind == "rows":
            shape[2] //= 2
        if kind == "columns":
            shape[1] //= 2
        shapes.append(jax.ShapeDtypeStruct(tuple(shape), value.dtype))
    return shapes


def attend_kernel(head, rows, keys, sources, count, kinds, *refs):
    extra = len(kinds)
    (info_ref, msg_ref), guests, refs = refs[:2], refs[2:2 + extra], refs[2 + extra:]
    (got_ref, out_ref, aug_ref, all_ref), landings, refs = refs[:4], refs[4:4 + extra], refs[4 + extra:]
    (land, kv, tiles, arrive, ones_ref, acc_ref, msend, mrecv, fsend, frecv, gsend, grecv, hsend, hrecv) = refs
    first = info_ref[0, 0]
    second = first + info_ref[0, 1]
    me = lax.axis_index("ctx")
    part = me % 2
    twin = {"ctx": me + 1 - 2 * part}
    half_rows = msg_ref.shape[1]
    wide = sources * 2 * half_rows
    span = sources * rows
    factor = math.log2(math.e) / math.sqrt(head)
    lane = lane_of((half_rows, LANES))
    greet(me, count)

    def remote(src, dst, send, recv, where):
        return pltpu.make_async_remote_copy(src_ref=src, dst_ref=dst, send_sem=send, recv_sem=recv,
                                            device_id=where, device_id_type=MESH)

    def msg_copy(owner, dest):
        return remote(msg_ref.at[dest], land.at[owner], msend.at[dest], mrecv.at[owner], {"ctx": dest})

    def share_copy(source):
        return remote(kv.at[source, part], kv.at[source, part], fsend.at[source], frecv.at[source], twin)

    def tile_copy(owner, dest):
        return remote(tiles.at[dest], arrive.at[owner], gsend.at[dest], grecv.at[owner], {"ctx": dest})

    def start_msg(step, _):
        msg_copy(me, lax.rem(me + step, count)).start()

    lax.fori_loop(1, count, start_msg, None)
    hosted = hosted_copies(kinds, guests, landings, hsend, hrecv)
    for copy in hosted:
        copy.start()
    land[me] = msg_ref[me]

    def share(source):
        @pl.when(source != me)
        def _():
            msg_copy(source, me).wait_recv()

        kv[source, part] = land[source, :, LANES:]
        share_copy(source).start()

    def compute(index):
        base = index * sources
        stack = []
        for source in range(sources):
            share_copy(base + source).wait_recv()
            both = kv[base + source].reshape(rows, LANES)
            place = pl.ds(pl.multiple_of((base + source) * rows, rows), rows)
            all_ref[place] = both
            ones_ref[place] = jnp.where(lane_of(both.shape) < head, jnp.ones_like(both), both)
            tile = land[base + source, :, :LANES].astype(F32) * factor
            stack.append(jnp.where(lane < head, tile, 0.0))
            stack.append(jnp.where(lane < head, swap_heads(tile, head), 0.0))
        queries = jnp.concatenate(stack, axis=0).astype(BF)
        acc_ref[...] = jnp.zeros_like(acc_ref)

        def visit(step, masked):
            start = pl.multiple_of(step * keys, keys)
            here = pl.ds(start, keys)
            raised = jnp.exp2(lax.dot_general(queries, all_ref[here], ONES_NT, preferred_element_type=F32))
            if masked:
                ok = allowed_block(0, 1, (wide, keys), first, second, part, base, start, rows, half_rows)
                raised = jnp.where(ok, raised, 0.0)
            acc_ref[...] += jnp.dot(raised.astype(BF), ones_ref[here], preferred_element_type=F32)

        sweep_keys(visit, index, count * rows - rows, part, base, rows, half_rows, keys, sources)
        for source in range(sources):
            tile = land[base + source, :, :LANES].astype(F32) * factor
            outs = []
            for which in range(2):
                place = (2 * source + which) * half_rows
                acc = acc_ref[place:place + half_rows]
                turn = swap_heads(acc, head)
                outs.append(turn / acc if which == 0 else acc / turn)
                high, middle, low = three_parts(-math.log2(math.e) * jnp.log(turn))
                query = tile if which == 0 else swap_heads(tile, head)
                extra = jnp.where(lane == head, high, jnp.where(lane == head + 1, middle,
                                                                jnp.where(lane == head + 2, low, 0.0)))
                aug_ref[base + source, which] = jnp.where(lane < head, query, extra).astype(BF)
            out = jnp.where(lane < head, outs[0], outs[1])
            out_ref[base + source] = out
            tiles[base + source] = out.astype(BF)

            @pl.when(base + source != me)
            def _(source=source):
                tile_copy(me, base + source).start()

    def block(index, _):
        @pl.when(index < count // sources)
        def _():
            for source in range(sources):
                share(index * sources + source)

        @pl.when(index > 0)
        def _():
            compute(index - 1)

    lax.fori_loop(0, count // sources + 1, block, None)
    arrive[me] = tiles[me]

    def drain(other, _):
        share_copy(other).wait_send()

        @pl.when(other != me)
        def _():
            msg_copy(me, other).wait_send()
            tile_copy(me, other).wait_send()
            tile_copy(other, me).wait_recv()

    lax.fori_loop(0, count, drain, None)
    got_ref[...] = arrive[...]
    for copy in hosted:
        copy.wait()


def attend_back_kernel(head, rows, keys, sources, count, kinds, *refs):
    extra = len(kinds)
    (info_ref, aug_ref, out_ref, kv_ref, msg_ref), guests, refs = refs[:5], refs[5:5 + extra], refs[5 + extra:]
    (gotq_ref, gotk_ref), landings, refs = refs[:2], refs[2:2 + extra], refs[2 + extra:]
    (land, tiles, away, near, sums, arrive_q, arrive_k, kone_ref, vone_ref, kturn_ref, dk_ref, dv_ref, acc_ref,
     msend, mrecv, fsend, frecv, gsend, grecv, ksend, krecv, hsend, hrecv) = refs
    first = info_ref[0, 0]
    second = first + info_ref[0, 1]
    me = lax.axis_index("ctx")
    part = me % 2
    twin = {"ctx": me + 1 - 2 * part}
    half_rows = msg_ref.shape[1]
    wide = sources * 2 * half_rows
    shrink = 1.0 / math.sqrt(head)
    lane = lane_of((half_rows, LANES))
    greet(me, count)

    def remote(src, dst, send, recv, where):
        return pltpu.make_async_remote_copy(src_ref=src, dst_ref=dst, send_sem=send, recv_sem=recv,
                                            device_id=where, device_id_type=MESH)

    def msg_copy(owner, dest):
        return remote(msg_ref.at[dest], land.at[owner], msend.at[dest], mrecv.at[owner], {"ctx": dest})

    def share_copy(source):
        return remote(away.at[source], near.at[source], fsend.at[source], frecv.at[source], twin)

    def q_copy(owner, dest):
        return remote(tiles.at[dest], arrive_q.at[owner], gsend.at[dest], grecv.at[owner], {"ctx": dest})

    def k_copy(owner, dest):
        return remote(sums.at[dest], arrive_k.at[owner], ksend.at[dest], krecv.at[owner], {"ctx": dest})

    def start_msg(step, _):
        msg_copy(me, lax.rem(me + count - step, count)).start()

    lax.fori_loop(1, count, start_msg, None)
    hosted = hosted_copies(kinds, guests, landings, hsend, hrecv)
    for copy in hosted:
        copy.start()
    land[me] = msg_ref[me]
    whole = lane_of(kv_ref.shape)
    vone_ref[...] = jnp.where(whole < head, jnp.ones_like(kv_ref), kv_ref[...])
    kone_ref[...] = jnp.where(whole < head, kv_ref[...], jnp.ones_like(kv_ref))
    kturn_ref[...] = turned(kv_ref[...])
    dk_ref[...] = jnp.zeros_like(dk_ref)
    dv_ref[...] = jnp.zeros_like(dv_ref)

    def rows_of(source, which):
        return pl.ds(pl.multiple_of(source * rows + which * half_rows, half_rows), half_rows)

    def key_tile(source, which):
        here = rows_of(source, which)
        return jnp.where(lane < head, dk_ref[here] * math.log(2.0), dv_ref[here])

    def compute(index):
        base = index * sources
        stack_q, stack_d = [], []
        for source in range(sources):
            @pl.when(base + source != me)
            def _(source=source):
                msg_copy(base + source, me).wait_recv()

            grad = land[base + source].astype(F32)
            spread = grad * out_ref[base + source]
            for which in range(2):
                stack_q.append(aug_ref[base + source, which])
                mine = (lane < head) if which == 0 else (lane >= head)
                delta = jnp.sum(jnp.where(mine, spread, 0.0), axis=1, keepdims=True)
                high, middle, low = three_parts(-delta)
                extra = jnp.where(lane == 0, high, jnp.where(lane == 1, middle, jnp.where(lane == 2, low, 0.0)))
                moved = swap_heads(grad, head) if which == 0 else grad
                stack_d.append(jnp.where(lane < head, extra, moved).astype(BF))
        queries = jnp.concatenate(stack_q, axis=0)
        grads = jnp.concatenate(stack_d, axis=0)
        acc_ref[...] = jnp.zeros_like(acc_ref)

        def visit(step, masked):
            start = pl.multiple_of(step * keys, keys)
            here = pl.ds(start, keys)
            raw = lax.dot_general(kone_ref[here], queries, ONES_NT, preferred_element_type=F32)
            if masked:
                ok = allowed_block(1, 0, (keys, wide), first, second, part, base, start, rows, half_rows)
                prob = jnp.where(ok, jnp.exp2(jnp.where(ok, raw, 0.0)), 0.0)
            else:
                prob = jnp.exp2(raw)
            along = lax.dot_general(vone_ref[here], grads, ONES_NT, preferred_element_type=F32)
            score = (prob * along).astype(BF)
            dv_ref[here] += jnp.dot(prob.astype(BF), grads, preferred_element_type=F32)
            dk_ref[here] += jnp.dot(score, queries, preferred_element_type=F32)
            acc_ref[...] += jnp.dot(kturn_ref[:, here], score, preferred_element_type=F32)

        sweep_keys(visit, index, count * rows - rows, part, base, rows, half_rows, keys, sources)
        acc = acc_ref[...].T
        for source in range(sources):
            place = 2 * source * half_rows
            one = acc[place:place + half_rows]
            two = acc[place + half_rows:place + 2 * half_rows]
            tiles[base + source] = (jnp.where(lane < head, one, swap_heads(two, head)) * shrink).astype(BF)

            @pl.when(base + source != me)
            def _(source=source):
                q_copy(me, base + source).start()

            away[base + source] = key_tile(base + source, 1 - part).astype(BF)
            share_copy(base + source).start()

    def finish(index):
        for source in range(sources):
            block = index * sources + source
            share_copy(block).wait_recv()
            sums[block] = (key_tile(block, part) + near[block].astype(F32)).astype(BF)

            @pl.when(block != me)
            def _(block=block):
                k_copy(me, block).start()

    def sweep(step, _):
        index = count // sources - 1 - step

        @pl.when(index >= 0)
        def _():
            compute(jnp.maximum(index, 0))

        @pl.when(step > 0)
        def _():
            finish(index + 1)

    lax.fori_loop(0, count // sources + 1, sweep, None)
    arrive_q[me] = tiles[me]
    arrive_k[me] = sums[me]

    def drain(other, _):
        share_copy(other).wait_send()

        @pl.when(other != me)
        def _():
            msg_copy(me, other).wait_send()
            q_copy(me, other).wait_send()
            k_copy(me, other).wait_send()
            q_copy(other, me).wait_recv()
            k_copy(other, me).wait_recv()

    lax.fori_loop(0, count, drain, None)
    gotq_ref[...] = arrive_q[...]
    gotk_ref[...] = arrive_k[...]
    for copy in hosted:
        copy.wait()


def exchange_attend(msg, info, head, rows, hosted, collective_id):
    count, half_rows = msg.shape[0], msg.shape[1]
    keys, sources = 512, 2
    group = count * rows
    dma = pltpu.SemaphoreType.DMA((count,))
    S = jax.ShapeDtypeStruct
    tile = (count, half_rows, LANES)
    kinds = [kind for kind, _ in hosted]
    guests = [value for _, value in hosted]
    hdma = pltpu.SemaphoreType.DMA((len(hosted),))
    anywhere = [pl.BlockSpec(memory_space=pl.ANY)] * len(hosted)
    return pl.pallas_call(
        functools.partial(attend_kernel, head, rows, keys, sources, count, kinds),
        out_shape=(S(tile, BF), S(tile, F32), S((count, 2, half_rows, LANES), BF), S((group, LANES), BF),
                   *hosted_shapes(hosted)),
        in_specs=[pl.BlockSpec(memory_space=pltpu.SMEM)] + vmem_specs(1) + anywhere,
        out_specs=tuple(vmem_specs(4) + anywhere),
        scratch_shapes=[pltpu.VMEM((count, half_rows, 2 * LANES), BF), pltpu.VMEM((count, 2, half_rows, LANES), BF),
                        pltpu.VMEM(tile, BF), pltpu.VMEM(tile, BF), pltpu.VMEM((group, LANES), BF),
                        pltpu.VMEM((sources * rows, LANES), F32)] + [dma] * 6 + [hdma] * 2,
        compiler_params=pltpu.CompilerParams(collective_id=collective_id, has_side_effects=True,
                                             vmem_limit_bytes=VMEM_LIMIT),
        cost_estimate=pl.CostEstimate(flops=2 * group * group * LANES, bytes_accessed=6 << 20, transcendentals=0),
        name="attend",
    )(info, msg, *guests)


def exchange_attend_back(msg, info, augmented, attended, all_kv, head, rows, hosted, collective_id):
    count, half_rows = msg.shape[0], msg.shape[1]
    keys, sources = 512, 2
    group = count * rows
    dma = pltpu.SemaphoreType.DMA((count,))
    S = jax.ShapeDtypeStruct
    tile = (count, half_rows, LANES)
    kinds = [kind for kind, _ in hosted]
    guests = [value for _, value in hosted]
    hdma = pltpu.SemaphoreType.DMA((len(hosted),))
    anywhere = [pl.BlockSpec(memory_space=pl.ANY)] * len(hosted)
    long = (group, LANES)
    return pl.pallas_call(
        functools.partial(attend_back_kernel, head, rows, keys, sources, count, kinds),
        out_shape=(S(tile, BF), S(tile, BF), *hosted_shapes(hosted)),
        in_specs=[pl.BlockSpec(memory_space=pltpu.SMEM)] + vmem_specs(4) + anywhere,
        out_specs=tuple(vmem_specs(2) + anywhere),
        scratch_shapes=[pltpu.VMEM(tile, BF)] * 7 + [
            pltpu.VMEM(long, BF), pltpu.VMEM(long, BF), pltpu.VMEM((LANES, group), BF), pltpu.VMEM(long, F32),
            pltpu.VMEM(long, F32), pltpu.VMEM((LANES, sources * rows), F32)] + [dma] * 8 + [hdma] * 2,
        compiler_params=pltpu.CompilerParams(collective_id=collective_id, has_side_effects=True,
                                             vmem_limit_bytes=VMEM_LIMIT),
        cost_estimate=pl.CostEstimate(flops=5 * group * group * LANES, bytes_accessed=8 << 20, transcendentals=0),
        name="attend_back",
    )(info, augmented, attended, all_kv, msg, *guests)


def sum_kernel(jobs, sides, weights, lines, *refs):
    count = len(jobs)
    refs = list(refs)
    take = lambda number: [refs.pop(0) for _ in range(number)]
    lefts, lefts_y, rights = take(sides), take(sides), take(count)
    sent = [refs.pop(0) if job["late"] and job["kind"] == "pair" else None for job in jobs]
    early_y = [None if job["late"] else take(job["parts"]) for job in jobs]
    small_refs = take(len(SMALL_ROWS))
    outs, (small_out,) = take(weights), take(1)
    lefts_s, lefts_ys, rights_s, rights_ys = take(sides), take(sides), take(count), take(count)
    rights_y = [take(1) if job["late"] else early for job, early in zip(jobs, early_y)]
    (lbuf, rbuf, xp, xr, x2r, zp, us, ur, ds_, dr, fs, fr, cs, cr, stage, sm_s, sm_r,
     lsem, rsem, xs, xv, x2s, x2v, uss, urv, dss, drv, fss, frv, css, crv, osem, sms, smv, els, elv, ers, erv, yrs, yrv) = refs
    steps = sum(job["total"] for job in jobs)
    last = steps - 1
    tokens = lbuf.shape[-1] // 4
    me = lax.axis_index("ctx")
    y = lax.axis_index("dp")
    z = me // 4
    x = (me // 2) % 2
    c = me % 2
    top = lines - 1
    twin = {"ctx": me + 1 - 2 * c}
    across_x = {"ctx": me + 2 - 4 * x}
    across_y = {"dp": 1 - y}
    above = {"ctx": jnp.minimum(me + 4, 4 * top + me % 4)}
    below = {"ctx": jnp.maximum(me - 4, me % 4)}
    near = {"ctx": me + 4 - 8 * (z % 2)}
    far = {"ctx": me + 8 - 16 * (z // 2)}
    rounds = [twin, across_x, across_y, near, far]

    for buf in (ur, dr, zp):
        buf[...] = jnp.zeros_like(buf)
    sm_s[0] = jnp.zeros(sm_s.shape[1:], F32)
    for (row, column), ref in zip(SMALL_ROWS, small_refs):
        sm_s[0, row:row + ref.shape[0], column:column + ref.shape[1]] = ref[...]

    barrier = pltpu.get_barrier_semaphore()
    for where in (twin, across_x, across_y, far):
        pl.semaphore_signal(barrier, inc=1, device_id=where, device_id_type=MESH)

    @pl.when(z < top)
    def _():
        pl.semaphore_signal(barrier, inc=1, device_id=above, device_id_type=MESH)

    @pl.when(z > 0)
    def _():
        pl.semaphore_signal(barrier, inc=1, device_id=below, device_id_type=MESH)

    pl.semaphore_wait(barrier, 4 + (z < top).astype(jnp.int32) + (z > 0).astype(jnp.int32))

    def remote(src, dst, send, recv, where):
        return pltpu.make_async_remote_copy(src_ref=src, dst_ref=dst, send_sem=send, recv_sem=recv,
                                            device_id=where, device_id_type=MESH)

    def row_base(number):
        height = lefts_s[number].shape[2]
        return y * height if height < lefts[number].shape[2] else 0

    def column_base(number):
        width = 2 * rights_s[number].shape[1]
        return y * width if jobs[number]["kind"] == "quarter" else 0

    def left_copies(number):
        height = lefts_s[number].shape[2]
        rows = pl.ds(pl.multiple_of(row_base(number), PIECE), height)
        return [
            remote(lefts[number].at[:, :, rows, :], lefts_s[number], els.at[number, 0], elv.at[number, 0], twin),
            remote(lefts_y[number], lefts_ys[number], els.at[number, 1], elv.at[number, 1], twin),
        ]

    def right_own(number):
        width = rights_s[number].shape[1]
        start = pl.multiple_of(column_base(number) + (1 - c) * width, STRIP)
        return remote(rights[number].at[:, pl.ds(start, width)], rights_s[number], ers.at[number, 0],
                      erv.at[number, 0], twin)

    def right_forward(number):
        width = rights_s[number].shape[1]
        columns = pl.ds(pl.multiple_of((1 - c) * width, STRIP), width)
        tall = tokens // len(rights_y[number])
        return [remote(source.at[:, columns], rights_ys[number].at[pl.ds(part * tall, tall)],
                       ers.at[number, 1 + part], erv.at[number, 1 + part], twin)
                for part, source in enumerate(rights_y[number])]

    def right_cross(number, piece=None):
        width = 2 * rights_s[number].shape[1]
        kind = jobs[number]["kind"]
        source = sent[number] if kind == "pair" else rights[number]
        start = (1 - y) * width if kind == "quarter" else 0
        rows, inside = slice(None), 0
        size = width
        if piece is not None:
            rows = pl.ds(pl.multiple_of((piece & 1) * (tokens // 2), PIECE), tokens // 2)
            inside, size = (piece >> 1) * STRIP, STRIP
        place = pl.ds(pl.multiple_of(inside, STRIP), size)
        if piece is None:
            landing = rights_y[number][0]
        else:
            landing = rights_y[number][0].at[rows, place]
        return remote(source.at[rows, pl.ds(pl.multiple_of(start + inside, STRIP), size)], landing,
                      yrs.at[number], yrv.at[number], across_y)

    def x_copy(j):
        s = j & (RING - 1)
        return remote(xp.at[s, 1 - x], xr.at[s], xs.at[s], xv.at[s], across_x)

    def x2_copy(j):
        s = j & (RING - 1)
        return remote(zp.at[j & (2 * RING - 1), z, 1 - x], x2r.at[s], x2s.at[s], x2v.at[s], across_x)

    def line_first(j):
        return lax.rem(j, LINE_FIRST) == LINE_FIRST - 1

    def either(j, act):
        both = line_first(j)
        pl.when(both)(lambda: act(True))
        pl.when(jnp.logical_not(both))(lambda: act(False))

    def up_copy(j, both):
        s = j & (RING - 1)
        src, dst = (us.at[s], ur.at[s]) if both else (us.at[s, :, 0], ur.at[s, :, 0])
        return remote(src, dst, uss.at[s], urv.at[s], above)

    def down_copy(j, both):
        s = j & (RING - 1)
        src, dst = (ds_.at[s], dr.at[s]) if both else (ds_.at[s, :, 0], dr.at[s, :, 0])
        return remote(src, dst, dss.at[s], drv.at[s], below)

    def f_copy(j):
        s = j & (RING - 1)
        return remote(fs.at[s], fr.at[s], fss.at[s], frv.at[s], across_y)

    def c_copy(j):
        s = j & (RING - 1)
        return remote(cs.at[s], cr.at[s], css.at[s], crv.at[s], twin)

    def small_copy(k):
        return remote(sm_s.at[k], sm_r.at[k], sms.at[k], smv.at[k], rounds[k])

    def loads(number):
        job = jobs[number]
        left, s = job["left"], number % 2
        height, width = lefts_s[left].shape[2], rights_s[number].shape[1]
        own_rows = pl.ds(pl.multiple_of(row_base(left), PIECE), height)
        own_columns = pl.ds(pl.multiple_of(column_base(number) + c * width, STRIP), width)
        mine = pl.ds(pl.multiple_of(c * width, STRIP), width)
        copies = []
        for place, source in enumerate([lefts[left].at[:, :, own_rows, :], lefts_s[left], lefts_y[left],
                                        lefts_ys[left]]):
            copies.append(pltpu.make_async_copy(
                source, lbuf.at[s, :, :, pl.ds(0, height), pl.ds(place * tokens, tokens)], lsem.at[s, place]))
        tall = tokens // len(rights_y[number])
        pieces = [(0, rights[number].at[:, own_columns]), (tokens, rights_s[number]), (3 * tokens, rights_ys[number])]
        pieces += [(2 * tokens + part * tall, source.at[:, mine]) for part, source in enumerate(rights_y[number])]
        for place, (start, source) in enumerate(pieces):
            copies.append(pltpu.make_async_copy(
                source, rbuf.at[s, pl.ds(start, source.shape[0]), pl.ds(0, width)], rsem.at[s, place]))
        return copies

    def each_job(j, visit):
        begin = 0
        for number, job in enumerate(jobs):
            @pl.when((j >= begin) & (j < begin + job["total"]))
            def _(number=number, begin=begin):
                visit(number, j - begin)
            begin += job["total"]

    def begins():
        begin = 0
        for number, job in enumerate(jobs):
            yield number, job, begin
            begin += job["total"]

    def out_copies(number, k, j):
        job = jobs[number]
        o = j & (RING - 1)
        row = pl.multiple_of(lax.rem(k, job["subs"]) * PIECE, PIECE)
        column = pl.multiple_of(lax.div(k, job["subs"]) * STRIP, STRIP)
        width = rights_s[number].shape[1]
        copies = []
        for line in range(2):
            for core in range(2):
                out = outs[job["outs"][line if job["kind"] == "pair" else 0]]
                rows, columns = row, core * width + column
                if job["kind"] == "quarter":
                    columns = line * 2 * width + columns
                if job["kind"] == "drop":
                    rows = line * lefts_s[job["left"]].shape[2] + row
                copies.append(pltpu.make_async_copy(
                    stage.at[o, line, core],
                    out.at[pl.ds(pl.multiple_of(rows, PIECE), PIECE), pl.ds(pl.multiple_of(columns, STRIP), STRIP)],
                    osem.at[o, line, core]))
        return copies

    def out_wait(j):
        for copy in out_copies(0, 0, j):
            copy.wait()

    started = []
    for number, job, begin in begins():
        if job["left"] not in started:
            started.append(job["left"])
            for copy in left_copies(job["left"]):
                copy.start()
        right_own(number).start()
        if not job["late"]:
            for copy in right_forward(number):
                copy.start()

    def step(t, _):
        slot = t & (RING - 1)

        for number, job, begin in begins():
            if job["late"]:
                ago = t - job["issue"]
                piece = ago - (ago >> 2)
                pieces = 4 * rights_s[number].shape[1] // STRIP

                @pl.when((ago >= 0) & (ago & 3 != 3) & (piece < pieces))
                def _(number=number, piece=piece):
                    right_cross(number, piece).start()

                @pl.when(t == begin - job["ahead"])
                def _(number=number):
                    right_cross(number).wait()
                    for copy in right_forward(number):
                        copy.start()

        done, before = [], 0
        for number, job, begin in begins():
            fresh = job["left"] not in done
            done.append(job["left"])

            @pl.when(t == max(before, begin - AHEAD))
            def _(number=number, job=job, fresh=fresh):
                if fresh:
                    for copy in left_copies(job["left"]):
                        copy.wait()
                right_own(number).wait()
                for copy in right_forward(number):
                    copy.wait()
                for copy in loads(number):
                    copy.start()

            before = begin

        for number, job, begin in begins():
            @pl.when(t == begin)
            def _(number=number):
                for copy in loads(number):
                    copy.wait()

        for k in range(len(rounds) + 1):
            @pl.when(t == LAG * k)
            def _(k=k):
                if k > 0:
                    small_copy(k - 1).wait()
                    total = sm_s[k - 1] + sm_r[k - 1]
                    if k == len(rounds):
                        small_out[...] = total
                    else:
                        sm_s[k] = total
                if k < len(rounds):
                    small_copy(k).start()

        @pl.when(t < steps)
        def _():
            which, begin_now, subs_now = 0, 0, jobs[0]["subs"]
            for number, job, begin in begins():
                here = t >= begin
                begin_now = jnp.where(here, begin, begin_now)
                subs_now = jnp.where(here, job["subs"], subs_now)
                which = jnp.where(here, number % 2, which)
            row = lax.rem(t - begin_now, subs_now) * PIECE
            column = lax.div(t - begin_now, subs_now) * STRIP
            rows = pl.ds(pl.multiple_of(row, PIECE), PIECE)
            left = lbuf[which, :, :, rows, :].reshape(2 * lines * SUB, 4 * tokens)
            right = rbuf[which, :, pl.ds(pl.multiple_of(column, STRIP), STRIP)]
            got = jnp.dot(left, right, preferred_element_type=F32).astype(BF)
            @pl.when(line_first(t))
            def _():
                for line in range(lines):
                    for side in range(2):
                        row = (2 * line + side) * SUB
                        zp[t & (2 * RING - 1), line, side] = got[row:row + SUB]

            @pl.when(jnp.logical_not(line_first(t)))
            def _():
                for line in range(lines):
                    for side in range(2):
                        row = (2 * line + side) * SUB
                        xp[slot, side, line] = got[row:row + SUB]
                x_copy(t).start()

        @pl.when((t >= LAG) & (t - LAG <= last) & jnp.logical_not(line_first(jnp.maximum(t - LAG, 0))))
        def _():
            x_copy(t - LAG).wait()
            s = (t - LAG) & (RING - 1)
            zp[(t - LAG) & (2 * RING - 1), :, 0] = xp[s, x] + xr[s]

        ju = t - LAG - LINE_LAG * z

        @pl.when((ju >= 0) & (ju <= last))
        def _():
            s = ju & (RING - 1)
            held = ju & (2 * RING - 1)

            @pl.when(z > 0)
            def _():
                either(ju, lambda both: up_copy(ju, both).wait_recv())
                zp[held, z] = zp[held, z] + ur[s, 0]

            @pl.when(z < top)
            def _():
                @pl.when(ju >= RING)
                def _():
                    either(ju - RING, lambda both: up_copy(ju - RING, both).wait_send())

                for m in range(top):
                    own = zp[held, jnp.minimum(z + 1 + m, top)]
                    if m + 1 < top:
                        own = own + ur[s, m + 1]
                    us[s, m] = own
                either(ju, lambda both: up_copy(ju, both).start())

        jd = t - LAG - LINE_LAG * (top - z)

        @pl.when((jd >= 0) & (jd <= last))
        def _():
            s = jd & (RING - 1)
            held = jd & (2 * RING - 1)

            @pl.when(z < top)
            def _():
                either(jd, lambda both: down_copy(jd, both).wait_recv())
                zp[held, z] = zp[held, z] + dr[s, 0]

            @pl.when(z > 0)
            def _():
                @pl.when(jd >= RING)
                def _():
                    either(jd - RING, lambda both: down_copy(jd - RING, both).wait_send())

                for m in range(top):
                    own = zp[held, jnp.maximum(z - 1 - m, 0)]
                    if m + 1 < top:
                        own = own + dr[s, m + 1]
                    ds_[s, m] = own
                either(jd, lambda both: down_copy(jd, both).start())

        jx = t - LAG - LINE_LAG * top

        @pl.when((jx >= 0) & (jx <= last) & line_first(jnp.maximum(jx, 0)))
        def _():
            x2_copy(jx).start()

        jf = jx - LAG

        @pl.when((jf >= 0) & (jf <= last))
        def _():
            s = jf & (RING - 1)
            held = jf & (2 * RING - 1)

            def gather(both):
                if both:
                    x2_copy(jf).wait()
                    fs[s] = zp[held, z, x] + x2r[s]
                else:
                    fs[s] = zp[held, z, 0]

            either(jf, gather)
            f_copy(jf).start()

        jo = jf - LAG

        @pl.when((jo >= 0) & (jo <= last))
        def _():
            f_copy(jo).wait()
            s = jo & (RING - 1)
            mine = pl.ds(pl.multiple_of(c * PIECE, PIECE), PIECE)
            away = pl.ds(pl.multiple_of((1 - c) * PIECE, PIECE), PIECE)
            cs[s, y] = fs[s, away]
            cs[s, 1 - y] = fr[s, away]
            c_copy(jo).start()
            stage[s, y, c] = fs[s, mine].astype(F32)
            stage[s, 1 - y, c] = fr[s, mine].astype(F32)

        jc = jo - CORE_LAG

        @pl.when((jc >= 0) & (jc <= last))
        def _():
            c_copy(jc).wait()
            s = jc & (RING - 1)
            stage[s, 0, 1 - c] = cr[s, 0].astype(F32)
            stage[s, 1, 1 - c] = cr[s, 1].astype(F32)

            def start(number, k):
                for copy in out_copies(number, k, jc):
                    copy.start()

            each_job(jc, start)

            @pl.when(jc >= LAG)
            def _():
                out_wait(jc - LAG)

    lax.fori_loop(0, last + 3 * LAG + LINE_LAG * top + CORE_LAG + 1, step, None)
    for back in range(LAG):
        out_wait(last - back)
    for back in range(RING):
        j = last - back

        @pl.when(z < top)
        def _(j=j):
            up_copy(j, j % LINE_FIRST == LINE_FIRST - 1).wait_send()

        @pl.when(z > 0)
        def _(j=j):
            down_copy(j, j % LINE_FIRST == LINE_FIRST - 1).wait_send()


def sum_over_chips(lefts, works, small, lines, collective_id):
    S = jax.ShapeDtypeStruct
    jobs, landing_r, landing_y, outs, sent, early = [], [], [], [], [], []
    shaped = [own.reshape(2 * lines, 2, own.shape[0] // (4 * lines), own.shape[1]) for own, _ in lefts]
    crossed = [cross for _, cross in lefts]
    tokens = shaped[0].shape[-1]
    for work in works:
        job = {name: work[name] for name in ("left", "kind", "late", "issue", "ahead")}
        columns = work["own"].shape[1]
        width = columns // 4 if job["kind"] == "quarter" else columns // 2
        height = crossed[job["left"]].shape[2]
        job["subs"], job["strips"] = height // PIECE, width // STRIP
        job["total"] = job["subs"] * job["strips"]
        job["outs"] = []
        for _ in range(2 if job["kind"] == "pair" else 1):
            job["outs"].append(len(outs))
            outs.append(S((shaped[job["left"]].shape[2], columns), F32))
        landing_r.append(S((tokens, width), BF))
        if job["late"]:
            landing_y.append(S((tokens, 2 * width), BF))
            if job["kind"] == "pair":
                sent.append(work["cross"])
        else:
            job["parts"] = len(work["cross"])
            early.extend(work["cross"])
        jobs.append(job)
    steps = sum(job["total"] for job in jobs)
    flat = (8, small[0].shape[1])
    top = lines - 1
    dma = pltpu.SemaphoreType.DMA
    ring = lambda *shape: pltpu.VMEM((RING,) + shape, BF)
    scratch = [
        pltpu.VMEM((2, 2 * lines, 2, max(value.shape[2] for value in crossed), 4 * tokens), BF),
        pltpu.VMEM((2, 4 * tokens, max(value.shape[1] for value in landing_r)), BF),
        ring(2, lines, SUB, STRIP), ring(lines, SUB, STRIP), ring(SUB, STRIP),
        pltpu.VMEM((2 * RING, lines, 2, SUB, STRIP), BF),
        ring(top, 2, SUB, STRIP), ring(top, 2, SUB, STRIP), ring(top, 2, SUB, STRIP), ring(top, 2, SUB, STRIP),
        ring(SUB, STRIP), ring(SUB, STRIP), ring(2, PIECE, STRIP), ring(2, PIECE, STRIP),
        pltpu.VMEM((RING, 2, 2, PIECE, STRIP), F32),
        pltpu.VMEM((5,) + flat, F32),
        pltpu.VMEM((5,) + flat, F32),
        dma((2, 4)), dma((2, 5)),
    ] + [dma((RING,))] * 12 + [
        dma((RING, 2, 2)), dma((5,)), dma((5,)),
        dma((len(lefts), 2)), dma((len(lefts), 2)), dma((len(works), 3)), dma((len(works), 3)),
        dma((len(works),)), dma((len(works),)),
    ]
    anywhere = pl.BlockSpec(memory_space=pl.ANY)
    inside = pl.BlockSpec(memory_space=pltpu.VMEM)
    landings = [S(value.shape, BF) for value in crossed] * 2 + landing_r * 2 + landing_y
    operands = shaped + crossed + [work["own"] for work in works] + sent + early
    flops = 2 * steps * 2 * lines * SUB * STRIP * 4 * tokens
    got = pl.pallas_call(
        functools.partial(sum_kernel, jobs, len(lefts), len(outs), lines),
        out_shape=tuple(outs) + (S(flat, F32),) + tuple(landings),
        in_specs=[anywhere] * len(operands) + [inside] * len(small),
        out_specs=tuple([anywhere] * len(outs) + [inside] + [anywhere] * len(landings)),
        scratch_shapes=scratch,
        compiler_params=pltpu.CompilerParams(collective_id=collective_id, has_side_effects=True,
                                             vmem_limit_bytes=VMEM_LIMIT),
        cost_estimate=pl.CostEstimate(flops=flops, bytes_accessed=steps * 1_100_000, transcendentals=0),
        name="sum_over_chips",
    )(*operands, *small)
    return got[:len(outs)], got[len(outs)]


def hand_over_kernel(count, head, *refs):
    sources, small_ref, results = refs[:count], refs[count], refs[count + 1:2 * count + 1]
    mix_ref, taps_ref, low_ref, att_ref, top_ref, query_ref, keys_ref = refs[2 * count + 1:2 * count + 8]
    holds, (ins, outs) = refs[2 * count + 8:3 * count + 8], refs[3 * count + 8:]
    arrive = [pltpu.make_async_copy(source, hold, ins.at[number])
              for number, (source, hold) in enumerate(zip(sources, holds))]
    leave = [pltpu.make_async_copy(hold, result, outs.at[number])
             for number, (hold, result) in enumerate(zip(holds, results))]
    for copy in arrive:
        copy.start()
    mix_ref[...] = small_ref[0]
    taps_ref[...] = small_ref[1:4]
    low_ref[...] = small_ref[4]
    att_ref[...] = small_ref[5]
    top_ref[...] = small_ref[6]
    query_ref[...] = small_ref[7, :head] + small_ref[7, head:LANES]
    keys_ref[...] = small_ref[7, LANES:LANES + head] + small_ref[7, LANES + head:2 * LANES]
    for first, then in zip(arrive, leave):
        first.wait()
        then.start()
    for copy in leave:
        copy.wait()


def hand_over(grads, small, head):
    count, width = len(grads), small.shape[1]
    S = jax.ShapeDtypeStruct
    anywhere = [pl.BlockSpec(memory_space=pl.ANY)] * count
    smalls = (S((width,), F32), S((3, width), F32), S((width,), F32), S((width,), F32), S((width,), F32),
              S((head,), F32), S((head,), F32))
    got = pl.pallas_call(
        functools.partial(hand_over_kernel, count, head),
        out_shape=tuple(S(value.shape, F32) for value in grads) + smalls,
        in_specs=anywhere + vmem_specs(1),
        out_specs=tuple(anywhere + vmem_specs(len(smalls))),
        scratch_shapes=[pltpu.VMEM(value.shape, F32) for value in grads] + [pltpu.SemaphoreType.DMA((count,))] * 2,
        compiler_params=pltpu.CompilerParams(vmem_limit_bytes=VMEM_LIMIT),
        name="hand_over",
    )(*grads, small)
    return got[:count], got[count:]


def call_plain(kernel, outs, args, smem=0, scratch=(), flops=0, moved=0, name=None):
    specs = [pl.BlockSpec(memory_space=pltpu.SMEM)] * smem + vmem_specs(len(args) - smem)
    many = isinstance(outs, (tuple, list))
    return pl.pallas_call(
        kernel,
        out_shape=tuple(outs) if many else outs,
        in_specs=specs,
        out_specs=tuple(vmem_specs(len(outs))) if many else vmem_specs(1)[0],
        scratch_shapes=list(scratch),
        compiler_params=pltpu.CompilerParams(vmem_limit_bytes=VMEM_LIMIT),
        cost_estimate=pl.CostEstimate(flops=flops, bytes_accessed=moved, transcendentals=0),
        name=name,
    )(*args)


def shape_of(shape, kind):
    return jax.ShapeDtypeStruct(shape, kind)


def sibling(value):
    count = lax.axis_size("ctx")
    return lax.ppermute(value, "ctx", [(i, i ^ 1) for i in range(count)])


def fast_device(tokens, lengths, cotangent, mixgain, mixentry, mixtaps, mixexit, lowgain, lowgate, lowlift,
                lowdrop, attgain, attquery, attkeys, attvalues, querygain, keysgain, attexit, topgain, topgate,
                toplift, topdrop):
    rows, width = tokens.shape
    head = querygain.shape[0]
    devices = lax.axis_size("ctx")
    lines = devices // 4
    half_rows = rows // 2
    place = lax.axis_index("ctx")
    core = place % 2
    first = lengths[0, 0]
    second = first + lengths[0, 1]
    where = place * rows + jnp.arange(rows + HALO, dtype=jnp.int32)
    begin = jnp.where(where >= second, second, jnp.where(where >= first, first, 0))
    spots = (where - begin).astype(F32)[:, None]
    spot = jnp.arange(LANES, dtype=jnp.int32) % (head // 2)
    angle = spots[:rows] * (THETA ** (-spot.astype(F32) * 2.0 / head))[None, :]
    cosine = jnp.cos(angle)
    sine = jnp.sin(angle) * jnp.where(jnp.arange(LANES) % head < head // 2, -1.0, 1.0)[None, :]

    before = passed_along(tokens[rows - HALO:], "ctx", 1)
    (hidden_one, normed_one_t, gated_t, part_b, part_c, part_x, conved, product) = mix_forward(
        tokens, before, spots, mixgain, mixtaps, mixentry, mixexit)
    gate_after = passed_along(part_c[:HALO], "ctx", -1)
    hidden_two, lownorm_t, gact_low, lact_low, lowinner_t = feed_low(
        hidden_one, lowgain, lowgate, lowlift, lowdrop)

    heads_q, heads_k = attquery.shape[1] // head, attkeys.shape[1] // head
    msg, normed_two_t, query_raw, key_raw = call_plain(
        functools.partial(project_kernel, head),
        (shape_of((devices, half_rows, 2 * LANES), BF), shape_of((width, rows), BF),
         shape_of((rows, attquery.shape[1]), F32), shape_of((rows, attkeys.shape[1]), F32)),
        (hidden_two, attgain, attquery, attkeys, attvalues, cosine, sine, querygain, keysgain),
        flops=2 * rows * width * 2 * width, moved=6 << 20, name="project")
    upright = lambda value: value.reshape(devices // 2, 2, value.shape[0] // devices, rows)
    over_dp = lambda value: lax.ppermute(value, "dp", [(0, 1), (1, 0)])
    msg, gated_y, normed_one_y, cotangent_y, gate_after = lax.optimization_barrier(
        (msg, over_dp(gated_t), over_dp(normed_one_t), over_dp(cotangent), gate_after))
    gated_y, normed_one_y = upright(gated_y), upright(normed_one_y)
    got, attended_f, augmented, all_kv, lowinner_y, lownorm_y = exchange_attend(
        msg, lengths, head, rows, [("rows", upright(lowinner_t)), ("whole", upright(lownorm_t))], 2)
    (output, grad, grad_low3, send, attended_t, topgain_grad, topnorm_t, topinner_t, keep_top, send_top_a,
     send_top_b) = feed_top(
        got, hidden_two, attexit, cotangent, topgain, topgate, toplift, topdrop)
    send, normed_two_y = lax.optimization_barrier((send, over_dp(normed_two_t)))
    normed_two_y = upright(normed_two_y)
    back_q, back_k, topinner_y, topnorm_y, attended_y, grad_low3_y = exchange_attend_back(
        send, lengths, augmented, attended_f, all_kv, head, rows,
        [("rows", upright(topinner_t)), ("whole", upright(topnorm_t)), ("whole", upright(attended_t)),
         ("columns", grad_low3)], 3)
    back_q, send_top_a, send_top_b = lax.optimization_barrier((back_q, send_top_a, send_top_b))
    top_y_one = over_dp(send_top_a)
    rawq_low, keep_kv, send_kv, grad_two, attgain_grad, querygain_grad, keysgain_grad = call_plain(
        functools.partial(project_back_kernel, head),
        (shape_of((rows, attquery.shape[1]), BF), shape_of((rows, attkeys.shape[1]), BF),
         shape_of((rows, attkeys.shape[1]), BF), shape_of((rows, width), F32), shape_of((1, width), F32),
         shape_of((1, LANES), F32), shape_of((1, LANES), F32)),
        (back_q, back_k, hidden_two, attgain, attquery, attkeys, attvalues, cosine, sine, querygain, keysgain,
         query_raw, key_raw, grad),
        flops=1 << 20, moved=1 << 10, name="project_back")
    grad, lowgain_grad, gb_low, grad_low1, keep_low, send_low = feed_low_back(
        grad_two, hidden_one, lowgain, gact_low, lact_low, lowgate, lowlift, lowdrop)
    grad, grad_low1, top_y_one = lax.optimization_barrier((grad, grad_low1, top_y_one))
    after = passed_along(grad_low1[:HALO], "ctx", -1)
    tokens_grad, mixgain_grad, mixtaps_grad, mixed_grad = mix_backward(
        grad, grad_low1, after, gate_after, spots, tokens, mixgain, mixtaps,
        (part_b, part_c, part_x, conved, product), mixentry, mixexit)
    mixgain_grad, tokens_grad, top_y_two = lax.optimization_barrier(
        (mixgain_grad, tokens_grad, over_dp(send_top_b)))

    lefts = [(attended_t, attended_y), (topinner_t, topinner_y), (topnorm_t, topnorm_y), (normed_two_t, normed_two_y),
             (lowinner_t, lowinner_y), (lownorm_t, lownorm_y), (gated_t, gated_y), (normed_one_t, normed_one_y)]

    def work(left, kind, own, cross=None, issue=-1, ahead=12):
        return dict(left=left, kind=kind, own=own, cross=cross, late=issue >= 0, issue=issue, ahead=ahead)

    works = [work(0, "quarter", grad_low3, (grad_low3_y,)), work(1, "drop", cotangent, (cotangent_y,)),
             work(2, "pair", keep_top, (top_y_one, top_y_two)), work(3, "quarter", rawq_low, issue=0),
             work(3, "pair", keep_kv, send_kv, issue=5), work(4, "drop", gb_low, issue=10),
             work(5, "pair", keep_low, send_low, issue=20), work(6, "quarter", grad_low1, issue=68),
             work(7, "quarter", mixed_grad, issue=73)]
    small = (mixgain_grad, mixtaps_grad, lowgain_grad, attgain_grad, topgain_grad, querygain_grad, keysgain_grad)
    grads, small = sum_over_chips(lefts, works, small, lines, 1)
    grads, smalls = hand_over(grads, small, head)
    (attexit_grad, topdrop_grad, topgate_grad, toplift_grad, attquery_grad, attkeys_grad, attvalues_grad, lowdrop_grad,
     lowgate_grad, lowlift_grad, mixexit_grad, mixentry_grad) = grads
    (mixgain_grad, mixtaps_grad, lowgain_grad, attgain_grad, topgain_grad, querygain_grad, keysgain_grad) = smalls
    return (output, tokens_grad, mixgain_grad, mixentry_grad, mixtaps_grad, mixexit_grad, lowgain_grad, lowgate_grad,
            lowlift_grad, lowdrop_grad, attgain_grad, attquery_grad, attkeys_grad, attvalues_grad, querygain_grad,
            keysgain_grad, attexit_grad, topgain_grad, topgate_grad, toplift_grad, topdrop_grad)


def solution(mesh):
    placed = (P(("dp", "ctx"), None), P("dp", None), P(("dp", "ctx"), None)) + (P(),) * 19
    split = {0: P(("dp", "ctx"), None), 1: P(("dp", "ctx"), None)}
    whole = (2, 4, 6, 10, 14, 15, 17)
    outs = tuple(split.get(i, P() if i in whole else P("ctx", None)) for i in range(21))
    small = mesh.shape["ctx"] == 16 and mesh.shape["dp"] == 2
    return jax.shard_map(fast_device if small else per_device, mesh=mesh, in_specs=placed, out_specs=outs,
                         check_vma=False)
```
